32 devices in a mesh: tokens: 8 (over y, x, core), heads: 4 (over z).
Axes of the slice: x: 2, y: 2, z: 4, core: 2. Of those that a mesh axis runs over, the one named last changes fastest.
Arguments:
- inputs: bfloat16 [4096, 2048], P('tokens'), may hold values from -6 to 6
- segments: int32 [4096], P('tokens'), may hold values from 0 to 7, as said below
- pre_gain: bfloat16 [2048], P('tokens'), may hold values from 0.099609375 to 1.8984375
- mid_gain: bfloat16 [2048], P('tokens'), may hold values from 0.099609375 to 1.8984375
- query_weight: bfloat16 [2048, 2048], P('tokens', 'heads'), may hold values from -0.125 to 0.125
- key_weight: bfloat16 [2048, 256], P('tokens', 'heads'), may hold values from -0.125 to 0.125
- value_weight: bfloat16 [2048, 256], P('tokens', 'heads'), may hold values from -0.125 to 0.125
- out_weight: bfloat16 [2048, 2048], P('heads', 'tokens'), may hold values from -0.5 to 0.5
- gate_weight: bfloat16 [2048, 5632], P('tokens', 'heads'), may hold values from -0.125 to 0.125
- up_weight: bfloat16 [2048, 5632], P('tokens', 'heads'), may hold values from -0.125 to 0.125
- down_weight: bfloat16 [5632, 2048], P('heads', 'tokens'), may hold values from -0.109375 to 0.109375
- cotangent: bfloat16 [4096, 2048], P('tokens'), may hold values from -6 to 6
Outputs:
- layer_out: bfloat16 [4096, 2048], P('tokens')
- grad_input: bfloat16 [4096, 2048], P('tokens')
- grad_pre: float32 [2048], P('tokens')
- grad_mid: float32 [2048], P('tokens')
- grad_query: float32 [2048, 2048], P('tokens', 'heads')
- grad_key: float32 [2048, 256], P('tokens', 'heads')
- grad_value: float32 [2048, 256], P('tokens', 'heads')
- grad_out: float32 [2048, 2048], P('heads', 'tokens')
- grad_gate: float32 [2048, 5632], P('tokens', 'heads')
- grad_up: float32 [2048, 5632], P('tokens', 'heads')
- grad_down: float32 [5632, 2048], P('heads', 'tokens')
The draws below stay inside these ranges and needn't reach their ends.
Inputs may be any that keep to these rules, and one draw needn't show every extreme that they name: `segments`: segment ids never fall and rise by at most 1 from one token to the next; row r holds exactly the four documents 4 r to 4 r + 3, of uneven lengths; in one row drawn from the seed a document begins within the row's first 512 tokens and ends within its last 512.
All inputs are finite; a program needn't handle non-finite values.
Results may differ from the reference program's by a relative error of at most 0.025.
Values may be sent and summed in bfloat16 or wider, within the bound.
A program may use at most 192 MiB of HBM per device.

```python
import math
import jax
import jax.numpy as jnp
from jax import lax

D = 2048
HEADS = 32
KVH = 4
HD = 64
FF = 5632
ROW = 2048
TOK_DEV = 512
TOKENS = 4096


def draw_segments(key, part):
    key = jax.random.fold_in(key, 7)
    keys = jax.random.split(key, 7)
    row_total = TOKENS // ROW
    third = ROW // 3
    chosen = jax.random.randint(keys[0], (), 0, row_total)
    drawn_one = jax.random.randint(keys[1], (row_total,), 1, third)
    drawn_two = jax.random.randint(keys[2], (row_total,), third, 2 * third)
    drawn_three = jax.random.randint(keys[3], (row_total,), 2 * third, ROW)
    wide_one = jax.random.randint(keys[4], (row_total,), 1, TOK_DEV // 2)
    wide_two = jax.random.randint(keys[5], (row_total,), ROW - TOK_DEV, ROW - TOK_DEV // 2)
    wide_three = jax.random.randint(keys[6], (row_total,), ROW - TOK_DEV // 2, ROW)
    row_ids = jnp.arange(row_total, dtype=jnp.int32)
    picked = row_ids == chosen
    first_cut = jnp.where(picked, wide_one, drawn_one)
    second_cut = jnp.where(picked, wide_two, drawn_two)
    third_cut = jnp.where(picked, wide_three, drawn_three)
    places = jnp.arange(TOKENS, dtype=jnp.int32)
    row_of = places // ROW
    inside = places % ROW
    count = (inside >= first_cut[row_of]).astype(jnp.int32) + (inside >= second_cut[row_of]).astype(jnp.int32) + (inside >= third_cut[row_of]).astype(jnp.int32)
    return (4 * row_of + count).astype(jnp.int32)


def strengthened(array, stream_key, source, target, parts, factor):
    owner, partner = [(jnp.arange(array.shape[position]) // (array.shape[position] // parts)).reshape([-1 if axis == position else 1 for axis in range(array.ndim)]) for position in (source, target)]
    chosen = jax.random.permutation(stream_key, parts)[partner]
    strong = (owner == chosen) | (owner == (partner + parts // 2) % parts)
    return jnp.where(strong, factor * array, array)


def levels(key, extent, shards, low, top_value):
    level = 1.0
    for dim, parts in shards:
        draws = jax.random.uniform(jax.random.fold_in(jax.random.fold_in(key, 6), dim), (parts,), jnp.float32, low / len(shards), top_value / len(shards))
        level = level * jnp.repeat(jnp.exp(draws), extent[dim] // parts).reshape((-1,) + (1,) * (len(extent) - 1 - dim))
    return level


def scatter_about(key, extent, spread, most, shards=(), kind=jnp.bfloat16):
    level = levels(key, extent, shards, -0.22, 0.18) if shards else 1.0
    entries = jax.random.normal(key, extent, jnp.float32) * spread * level
    return jnp.minimum(jnp.maximum(entries, -most), most).astype(kind)


def heavy_noise(key, shape, spread, reach, pieces, heavy, kind=jnp.bfloat16):
    drawn = spread * jax.random.normal(key, shape, jnp.float32)
    if pieces:
        drawn = drawn * levels(key, shape, pieces, -0.22, 0.18)
    return jnp.clip(strengthened(drawn, jax.random.fold_in(key, 3), *heavy), -reach, reach).astype(kind)


def setup_inputs(seed: int = 0) -> dict:
    arg_keys = jax.random.split(jax.random.key(seed), 13)
    return {
        "inputs": heavy_noise(arg_keys[0], (TOKENS, D), 1.0, 6.0, ((0, 8),), (0, 1, 8, 2.0)),
        "segments": draw_segments(jax.random.fold_in(arg_keys[12], 71), 0),
        "pre_gain": jnp.clip(1.0 + 0.18 * jax.random.normal(arg_keys[2], (D,), jnp.float32), 0.099609375, 1.8984375).astype(jnp.bfloat16),
        "mid_gain": jnp.clip(1.0 + 0.18 * jax.random.normal(arg_keys[3], (D,), jnp.float32), 0.099609375, 1.8984375).astype(jnp.bfloat16),
        "query_weight": scatter_about(arg_keys[4], (D, HEADS * HD), D ** -0.5, 0.125, ((0, 8), (1, 4))),
        "key_weight": scatter_about(arg_keys[5], (D, KVH * HD), D ** -0.5, 0.125, ((0, 8), (1, 4))),
        "value_weight": scatter_about(arg_keys[6], (D, KVH * HD), D ** -0.5, 0.125, ((0, 8), (1, 4))),
        "out_weight": scatter_about(arg_keys[7], (HEADS * HD, D), (HEADS * HD // 16) ** -0.5, 0.5, ((0, 4), (1, 8))),
        "gate_weight": scatter_about(arg_keys[8], (D, FF), D ** -0.5, 0.125, ((0, 8), (1, 4))),
        "up_weight": scatter_about(arg_keys[9], (D, FF), D ** -0.5, 0.125, ((0, 8), (1, 4))),
        "down_weight": scatter_about(arg_keys[10], (FF, D), (FF // 2) ** -0.5, 0.109375, ((0, 4), (1, 8))),
        "cotangent": heavy_noise(arg_keys[11], (TOKENS, D), 1.0, 6.0, ((0, 8),), (0, 1, 8, 2.0)),
    }


@jax.custom_vjp
def low(v):
    return lax.optimization_barrier(v.astype(jnp.bfloat16)).astype(jnp.float32)

@jax.custom_vjp
def low_back(v):
    return v

def low_keep(v):
    return (low(v), None)

def low_pass(kept, grad):
    return (grad,)

def back_keep(v):
    return (v, None)

def back_low(kept, grad):
    return (low(grad),)
low.defvjp(low_keep, low_pass)
low_back.defvjp(back_keep, back_low)

def rms_scale(vectors):
    return lax.rsqrt(lax.optimization_barrier(jnp.mean(vectors * vectors, axis=-1, keepdims=True)) + 1e-05)

def rotate(vectors, cos_table, sin_table):
    middle_index = vectors.shape[-1] // 2
    former = vectors[..., :middle_index]
    latter = vectors[..., middle_index:]
    return jnp.concatenate([former * cos_table - latter * sin_table, latter * cos_table + former * sin_table], axis=-1)

def doc_positions(segments):
    places = jnp.arange(segments.shape[0], dtype=jnp.int32)
    starts_here = jnp.concatenate([jnp.ones((1,), dtype=jnp.bool_), segments[1:] != segments[:-1]])
    opening = lax.cummax(jnp.where(starts_here, places, 0).astype(jnp.int32), axis=0)
    return places - opening

def angle_tables(positions):
    half_size = HD // 2
    inverse = 10000.0 ** (-jnp.arange(half_size, dtype=jnp.float32) / half_size)
    turned = positions.astype(jnp.float32)[:, None] * inverse[None, :]
    return (jnp.cos(turned)[:, None, :], jnp.sin(turned)[:, None, :])

def forward(inputs, pre_gain, mid_gain, query_weight, key_weight, value_weight, out_weight, gate_weight, up_weight, down_weight, cos_table, sin_table, segments):
    highest = lax.Precision.HIGHEST
    length = inputs.shape[0]
    group = HEADS // KVH
    normed = low(inputs * rms_scale(inputs) * pre_gain)
    queries = low_back(jnp.dot(normed, query_weight, precision=highest)).reshape(length, HEADS, HD)
    key_rows = low_back(jnp.dot(normed, key_weight, precision=highest)).reshape(length, KVH, HD)
    value_rows = low_back(low(jnp.dot(normed, value_weight, precision=highest))).reshape(length, KVH, HD)
    query_rot = low(rotate(queries, cos_table, sin_table) * HD ** (-0.5)).reshape(length, KVH, group, HD)
    key_rot = low(rotate(key_rows, cos_table, sin_table))
    span = math.gcd(length, 512)
    places = jnp.arange(length, dtype=jnp.int32)

    def attend(block_index):
        opening = (block_index * span).astype(jnp.int32)
        block_queries = lax.dynamic_slice_in_dim(query_rot, opening, span, 0)
        block_ids = lax.dynamic_slice_in_dim(segments, opening, span, 0)
        block_places = opening + jnp.arange(span, dtype=jnp.int32)
        allowed = (block_ids[:, None] == segments[None, :]) & (block_places[:, None] >= places[None, :])
        scores = low_back(jnp.einsum('qkgd,skd->kgqs', block_queries, key_rot, precision=highest))
        scores = jnp.where(allowed[None, None], scores, -1e+30)
        weights = jnp.exp(scores - lax.optimization_barrier(jnp.max(scores, axis=-1, keepdims=True)))
        shares = low(weights / lax.optimization_barrier(jnp.sum(weights, axis=-1, keepdims=True)))
        mixed = jnp.einsum('kgqs,skd->qkgd', shares, value_rows, precision=highest)
        return mixed.reshape(span, HEADS * HD)
    attended = lax.map(jax.checkpoint(attend), jnp.arange(length // span, dtype=jnp.int32))
    attended = low_back(low(attended.reshape(length, HEADS * HD)))
    attn_out = low_back(jnp.dot(attended, out_weight, precision=highest))
    middle = inputs + attn_out
    normed_mid = low(middle * rms_scale(middle) * mid_gain)
    gate_rows = low_back(jnp.dot(normed_mid, gate_weight, precision=highest))
    up_rows = low_back(jnp.dot(normed_mid, up_weight, precision=highest))
    hidden = low(jax.nn.silu(gate_rows) * up_rows)
    return middle + jnp.dot(hidden, down_weight, precision=highest)

def reference(inputs, segments, pre_gain, mid_gain, query_weight, key_weight, value_weight, out_weight, gate_weight, up_weight, down_weight, cotangent):
    cos_table, sin_table = angle_tables(doc_positions(segments))
    members = (inputs, pre_gain, mid_gain, query_weight, key_weight, value_weight, out_weight, gate_weight, up_weight, down_weight)
    params = tuple((member.astype(jnp.float32) for member in members))

    def layer(*params_in):
        return forward(*params_in, cos_table, sin_table, segments)
    result, pullback = jax.vjp(layer, *params)
    gradients = pullback(cotangent.astype(jnp.float32))
    return (result.astype(jnp.bfloat16), gradients[0].astype(jnp.bfloat16), gradients[1], gradients[2], gradients[3], gradients[4], gradients[5], gradients[6], gradients[7], gradients[8], gradients[9])
```

```python
import functools
import math

import jax
import jax.numpy as jnp
from jax import lax
from jax.experimental import pallas as pl
from jax.experimental.pallas import tpu as pltpu
from jax.sharding import PartitionSpec as P

ROW = 2048


def rms_scale(vectors):
    return lax.rsqrt(jnp.mean(vectors * vectors, axis=-1, keepdims=True) + 1e-05)


def rotate(vectors, cos_table, sin_table):
    middle_index = vectors.shape[-1] // 2
    former = vectors[..., :middle_index]
    latter = vectors[..., middle_index:]
    return jnp.concatenate(
        [former * cos_table - latter * sin_table, latter * cos_table + former * sin_table], axis=-1
    )


def unrotate(gradient, cos_table, sin_table):
    middle_index = gradient.shape[-1] // 2
    former = gradient[..., :middle_index]
    latter = gradient[..., middle_index:]
    return jnp.concatenate(
        [former * cos_table + latter * sin_table, latter * cos_table - former * sin_table], axis=-1
    )


def norm_back(gradient, vectors, scale_rows, gain_row):
    shaped = vectors * scale_rows
    weighted = gradient * gain_row
    back_vectors = scale_rows * (
        weighted - shaped * jnp.mean(weighted * shaped, axis=-1, keepdims=True)
    )
    return (back_vectors, jnp.sum(gradient * shaped, axis=0))


def shards_any(
    inputs,
    segments,
    pre_gain,
    mid_gain,
    query_weight,
    key_weight,
    value_weight,
    out_weight,
    gate_weight,
    up_weight,
    down_weight,
    cotangent,
):
    row_count = inputs.shape[0]
    head_size = key_weight.shape[1]
    heads_here = query_weight.shape[1] // head_size
    myself = lax.axis_index("tokens")
    gathered = (
        lax.all_gather(pre_gain, "tokens", axis=0, tiled=True),
        lax.all_gather(mid_gain, "tokens", axis=0, tiled=True),
        lax.all_gather(query_weight, "tokens", axis=0, tiled=True),
        lax.all_gather(key_weight, "tokens", axis=0, tiled=True),
        lax.all_gather(value_weight, "tokens", axis=0, tiled=True),
        lax.all_gather(out_weight, "tokens", axis=1, tiled=True),
        lax.all_gather(gate_weight, "tokens", axis=0, tiled=True),
        lax.all_gather(up_weight, "tokens", axis=0, tiled=True),
        lax.all_gather(down_weight, "tokens", axis=1, tiled=True),
    )
    (
        pre_full,
        mid_full,
        query_full,
        key_full,
        value_full,
        out_full,
        gate_full,
        up_full,
        down_full,
    ) = gathered
    pre_row = pre_full.astype(jnp.float32)
    mid_row = mid_full.astype(jnp.float32)
    all_ids = lax.all_gather(segments, "tokens", axis=0, tiled=True)
    length = all_ids.shape[0]
    places = jnp.arange(length, dtype=jnp.int32)
    starts_here = jnp.concatenate([jnp.ones((1,), dtype=jnp.bool_), all_ids[1:] != all_ids[:-1]])
    opening = lax.cummax(jnp.where(starts_here, places, 0), axis=0)
    own_first = myself * row_count
    positions = lax.dynamic_slice_in_dim(places - opening, own_first, row_count)
    own_places = own_first + jnp.arange(row_count, dtype=jnp.int32)
    half_size = head_size // 2
    inverse = 10000.0 ** (-jnp.arange(half_size, dtype=jnp.float32) / half_size)
    turned = positions.astype(jnp.float32)[:, None] * inverse[None, :]
    cos_table = jnp.cos(turned)[:, None, :]
    sin_table = jnp.sin(turned)[:, None, :]
    inputs_f = inputs.astype(jnp.float32)
    pre_scale = rms_scale(inputs_f)
    normed = (inputs_f * pre_scale * pre_row).astype(jnp.bfloat16)
    queries = jnp.dot(normed, query_full, preferred_element_type=jnp.float32).reshape(
        row_count, heads_here, head_size
    )
    query_rot = (rotate(queries, cos_table, sin_table) * head_size ** (-0.5)).astype(jnp.bfloat16)
    key_rows = jnp.dot(normed, key_full, preferred_element_type=jnp.float32)[:, None, :]
    key_rot = rotate(key_rows, cos_table, sin_table)[:, 0, :].astype(jnp.bfloat16)
    value_low = jnp.dot(normed, value_full, preferred_element_type=jnp.float32).astype(jnp.bfloat16)
    key_all, value_all = (
        lax.all_gather(key_rot, "tokens", axis=0, tiled=True),
        lax.all_gather(value_low, "tokens", axis=0, tiled=True),
    )
    span = math.gcd(ROW, 1024)
    row_start = own_first // ROW * ROW
    block_first = row_start // span
    block_total = (own_first + row_count + span - 1) // span

    def key_block(block_index):
        opening_row = block_index * span
        block_keys = lax.dynamic_slice_in_dim(key_all, opening_row, span)
        block_values = lax.dynamic_slice_in_dim(value_all, opening_row, span)
        block_ids = lax.dynamic_slice_in_dim(all_ids, opening_row, span)
        block_places = opening_row + jnp.arange(span, dtype=jnp.int32)
        allowed = (segments[:, None] == block_ids[None, :]) & (
            own_places[:, None] >= block_places[None, :]
        )
        scores = jnp.einsum(
            "qhd,kd->qhk", query_rot, block_keys, preferred_element_type=jnp.float32
        )
        return (opening_row, block_keys, block_values, allowed[:, None, :], scores)

    def forward_step(block_index, state_now):
        row_peak, row_total, running = state_now
        opening_row, block_keys, block_values, allowed, scores = key_block(block_index)
        new_peak = jnp.maximum(row_peak, jnp.max(jnp.where(allowed, scores, -1e30), axis=-1))
        factor = jnp.exp(row_peak - new_peak)
        weights = jnp.where(allowed, jnp.exp(scores - new_peak[..., None]), 0.0)
        row_total = row_total * factor + jnp.sum(weights, axis=-1)
        running = running * factor[..., None] + jnp.einsum(
            "qhk,kd->qhd",
            weights.astype(jnp.bfloat16),
            block_values,
            preferred_element_type=jnp.float32,
        )
        return (new_peak, row_total, running)

    start_state = (
        jnp.full((row_count, heads_here), -1e30, jnp.float32),
        jnp.zeros((row_count, heads_here), jnp.float32),
        jnp.zeros((row_count, heads_here, head_size), jnp.float32),
    )
    row_peak, row_total, running = lax.fori_loop(
        block_first, block_total, forward_step, start_state
    )
    attended = running / row_total[..., None]
    log_total = row_peak + jnp.log(row_total)
    attended_low = attended.astype(jnp.bfloat16).reshape(row_count, heads_here * head_size)
    attn_term = jnp.dot(attended_low, out_full, preferred_element_type=jnp.float32)
    middle = inputs_f + lax.psum(attn_term.astype(jnp.bfloat16), "heads").astype(jnp.float32)
    mid_scale = rms_scale(middle)
    normed_mid = (middle * mid_scale * mid_row).astype(jnp.bfloat16)
    gate_rows = jnp.dot(normed_mid, gate_full, preferred_element_type=jnp.float32)
    up_rows = jnp.dot(normed_mid, up_full, preferred_element_type=jnp.float32)
    sigmoid_rows = jax.nn.sigmoid(gate_rows)
    silu_rows = gate_rows * sigmoid_rows
    hidden = (silu_rows * up_rows).astype(jnp.bfloat16)
    mlp_term = jnp.dot(hidden, down_full, preferred_element_type=jnp.float32)
    layer_out = (
        middle + lax.psum(mlp_term.astype(jnp.bfloat16), "heads").astype(jnp.float32)
    ).astype(jnp.bfloat16)
    grad_down = jnp.einsum("tf,td->fd", hidden, cotangent, preferred_element_type=jnp.float32)
    back_hidden = jnp.einsum("td,fd->tf", cotangent, down_full, preferred_element_type=jnp.float32)
    back_gate = (
        back_hidden * up_rows * sigmoid_rows * (1.0 + gate_rows * (1.0 - sigmoid_rows))
    ).astype(jnp.bfloat16)
    back_up = (back_hidden * silu_rows).astype(jnp.bfloat16)
    grad_gate = jnp.einsum("tc,tf->cf", normed_mid, back_gate, preferred_element_type=jnp.float32)
    grad_up = jnp.einsum("tc,tf->cf", normed_mid, back_up, preferred_element_type=jnp.float32)
    mid_term = jnp.einsum(
        "tf,cf->tc", back_gate, gate_full, preferred_element_type=jnp.float32
    ) + jnp.einsum("tf,cf->tc", back_up, up_full, preferred_element_type=jnp.float32)
    back_normed_mid = lax.psum(mid_term.astype(jnp.bfloat16), "heads").astype(jnp.float32)
    back_middle, grad_mid = norm_back(back_normed_mid, middle, mid_scale, mid_row)
    back_middle = back_middle + cotangent.astype(jnp.float32)
    back_attn = back_middle.astype(jnp.bfloat16)
    grad_out = jnp.einsum("tc,td->cd", attended_low, back_attn, preferred_element_type=jnp.float32)
    back_attended = (
        jnp.einsum("td,cd->tc", back_attn, out_full, preferred_element_type=jnp.float32)
        .astype(jnp.bfloat16)
        .reshape(row_count, heads_here, head_size)
    )
    row_delta = jnp.sum(back_attended.astype(jnp.float32) * attended, axis=-1)

    def backward_step(block_index, state_now):
        back_rows, back_pairs = state_now
        opening_row, block_keys, block_values, allowed, scores = key_block(block_index)
        chances = jnp.where(allowed, jnp.exp(scores - log_total[..., None]), 0.0)
        back_values = jnp.einsum(
            "qhk,qhd->kd",
            chances.astype(jnp.bfloat16),
            back_attended,
            preferred_element_type=jnp.float32,
        )
        back_chances = jnp.einsum(
            "qhd,kd->qhk", back_attended, block_values, preferred_element_type=jnp.float32
        )
        back_scores = (chances * (back_chances - row_delta[..., None])).astype(jnp.bfloat16)
        back_rows = back_rows + jnp.einsum(
            "qhk,kd->qhd", back_scores, block_keys, preferred_element_type=jnp.float32
        )
        back_keys = jnp.einsum(
            "qhk,qhd->kd", back_scores, query_rot, preferred_element_type=jnp.float32
        )
        old_piece = lax.dynamic_slice_in_dim(back_pairs, opening_row, span)
        fresh_piece = old_piece + jnp.concatenate([back_keys, back_values], axis=-1)
        back_pairs = lax.dynamic_update_slice_in_dim(back_pairs, fresh_piece, opening_row, 0)
        return (back_rows, back_pairs)

    start_back = (
        jnp.zeros((row_count, heads_here, head_size), jnp.float32),
        jnp.zeros((length, 2 * head_size), jnp.float32),
    )
    back_rows, back_pairs = lax.fori_loop(block_first, block_total, backward_step, start_back)
    own_pairs = lax.psum_scatter(
        back_pairs.astype(jnp.bfloat16), "tokens", scatter_dimension=0, tiled=True
    ).astype(jnp.float32)
    back_query = (
        (unrotate(back_rows, cos_table, sin_table) * head_size ** (-0.5))
        .astype(jnp.bfloat16)
        .reshape(row_count, heads_here * head_size)
    )
    back_key = unrotate(own_pairs[:, None, :head_size], cos_table, sin_table)[:, 0, :].astype(
        jnp.bfloat16
    )
    back_value = own_pairs[:, head_size:].astype(jnp.bfloat16)
    grad_query = jnp.einsum("tc,tq->cq", normed, back_query, preferred_element_type=jnp.float32)
    grad_key = jnp.einsum("tc,tq->cq", normed, back_key, preferred_element_type=jnp.float32)
    grad_value = jnp.einsum("tc,tq->cq", normed, back_value, preferred_element_type=jnp.float32)
    pre_term = jnp.einsum("tq,cq->tc", back_query, query_full, preferred_element_type=jnp.float32)
    pre_term = pre_term + jnp.einsum(
        "tq,cq->tc", back_key, key_full, preferred_element_type=jnp.float32
    )
    pre_term = pre_term + jnp.einsum(
        "tq,cq->tc", back_value, value_full, preferred_element_type=jnp.float32
    )
    back_normed = lax.psum(pre_term.astype(jnp.bfloat16), "heads").astype(jnp.float32)
    back_inputs, grad_pre = norm_back(back_normed, inputs_f, pre_scale, pre_row)
    grad_input = (back_middle + back_inputs).astype(jnp.bfloat16)
    summed = (
        lax.psum_scatter(
            grad_pre.astype(jnp.bfloat16), "tokens", scatter_dimension=0, tiled=True
        ).astype(jnp.float32),
        lax.psum_scatter(
            grad_mid.astype(jnp.bfloat16), "tokens", scatter_dimension=0, tiled=True
        ).astype(jnp.float32),
        lax.psum_scatter(
            grad_query.astype(jnp.bfloat16), "tokens", scatter_dimension=0, tiled=True
        ).astype(jnp.float32),
        lax.psum_scatter(
            grad_key.astype(jnp.bfloat16), "tokens", scatter_dimension=0, tiled=True
        ).astype(jnp.float32),
        lax.psum_scatter(
            grad_value.astype(jnp.bfloat16), "tokens", scatter_dimension=0, tiled=True
        ).astype(jnp.float32),
        lax.psum_scatter(
            grad_out.astype(jnp.bfloat16), "tokens", scatter_dimension=1, tiled=True
        ).astype(jnp.float32),
        lax.psum_scatter(
            grad_gate.astype(jnp.bfloat16), "tokens", scatter_dimension=0, tiled=True
        ).astype(jnp.float32),
        lax.psum_scatter(
            grad_up.astype(jnp.bfloat16), "tokens", scatter_dimension=0, tiled=True
        ).astype(jnp.float32),
        lax.psum_scatter(
            grad_down.astype(jnp.bfloat16), "tokens", scatter_dimension=1, tiled=True
        ).astype(jnp.float32),
    )
    (
        grad_pre,
        grad_mid,
        grad_query,
        grad_key,
        grad_value,
        grad_out,
        grad_gate,
        grad_up,
        grad_down,
    ) = summed
    return (
        layer_out,
        grad_input,
        grad_pre,
        grad_mid,
        grad_query,
        grad_key,
        grad_value,
        grad_out,
        grad_gate,
        grad_up,
        grad_down,
    )


MESH_ID = pl.DeviceIdType.MESH
VMEM_BYTES = 60 * 2**20


def token_device(flip):
    return (jnp.bitwise_xor(lax.axis_index("tokens"), flip), lax.axis_index("heads"))


def remote(src, dst, send, recv, device):
    return pltpu.make_async_remote_copy(
        src_ref=src, dst_ref=dst, send_sem=send, recv_sem=recv, device_id=device, device_id_type=MESH_ID
    )


def greet_cube():
    barrier = pltpu.get_barrier_semaphore()
    for flip in (1, 2, 4):
        pl.semaphore_signal(barrier, inc=1, device_id=token_device(flip), device_id_type=MESH_ID)
    pl.semaphore_wait(barrier, 3)


def block_of(ref, axis, index, half=None):
    size = ref.shape[axis] // 8
    start = pl.multiple_of(index * size, size)
    if axis == 0:
        if half is None:
            return ref.at[pl.ds(start, size), :]
        return ref.at[pl.ds(pl.multiple_of(start + half * (size // 2), size // 2), size // 2), :]
    if half is None:
        return ref.at[:, pl.ds(start, size)]
    rows = ref.shape[0] // 2
    return ref.at[pl.ds(half * rows, rows), pl.ds(start, size)]


class Gather:
    COPIES = 9

    def __init__(self, shard, full, axis, send, recv):
        self.shard, self.full, self.axis, self.send, self.recv = shard, full, axis, send, recv
        self.me = lax.axis_index("tokens")

    def copy(self, slot, flip_block, flip_target, half=None):
        index = jnp.bitwise_xor(self.me, flip_block)
        src = self.shard if flip_block == 0 else block_of(self.full, self.axis, index, half)
        return remote(
            src,
            block_of(self.full, self.axis, index, half),
            self.send.at[slot],
            self.recv.at[slot],
            token_device(flip_target),
        )

    def copies(self, slot):
        return self.copy(
            slot,
            *(
                (0, 2),
                (0, 4),
                (0, 1),
                (2, 4, 0),
                (4, 2, 1),
                (2, 1),
                (4, 1),
                (6, 1, 0),
                (6, 1, 1),
            )[slot],
        )

    def start(self, local):
        for slot in (0, 1, 2):
            self.copies(slot).start()
        mine = pltpu.make_async_copy(self.shard, block_of(self.full, self.axis, self.me), local)
        mine.start()
        mine.wait()

    def relay(self):
        self.copies(0).wait_recv()
        self.copies(3).start()
        self.copies(1).wait_recv()
        self.copies(4).start()
        self.copies(5).start()
        self.copies(6).start()

    def finish_relay(self):
        self.copies(3).wait_recv()
        self.copies(7).start()
        self.copies(4).wait_recv()
        self.copies(8).start()

    def finish(self):
        for slot in (2, 5, 6, 7, 8):
            self.copies(slot).wait_recv()
        for slot in range(self.COPIES):
            self.copies(slot).wait_send()


def gather_kernel(axes, *refs):
    count = len(axes)
    shards_in, fulls = refs[:count], refs[count : 2 * count]
    send, recv, local = refs[2 * count :]
    greet_cube()
    parts = [
        Gather(shards_in[i], fulls[i], axes[i], send.at[i], recv.at[i]) for i in range(count)
    ]
    ahead = 2
    for i in range(count + ahead + 1):
        if i < count:
            parts[i].start(local.at[i])
        if 0 <= i - ahead < count:
            parts[i - ahead].relay()
        if 0 <= i - ahead - 1 < count:
            parts[i - ahead - 1].finish_relay()
    for part in parts:
        part.finish()


def gather_weights(arrays, axes, collective_id):
    count = len(arrays)
    shapes = [
        tuple(size * 8 if d == axis else size for d, size in enumerate(array.shape))
        for array, axis in zip(arrays, axes)
    ]
    return pl.pallas_call(
        functools.partial(gather_kernel, axes),
        out_shape=[jax.ShapeDtypeStruct(s, a.dtype) for s, a in zip(shapes, arrays)],
        in_specs=[pl.BlockSpec(memory_space=pl.ANY)] * count,
        out_specs=[pl.BlockSpec(memory_space=pl.ANY)] * count,
        scratch_shapes=[
            pltpu.SemaphoreType.DMA((count, Gather.COPIES)),
            pltpu.SemaphoreType.DMA((count, Gather.COPIES)),
            pltpu.SemaphoreType.DMA((count,)),
        ],
        compiler_params=pltpu.CompilerParams(collective_id=collective_id, has_side_effects=True),
        name="gather_weights",
    )(*arrays)


def greet_chain(chain):
    here = lax.axis_index("heads")
    barrier = pltpu.get_barrier_semaphore()
    for step in (-1, 1):
        near = here + step

        @pl.when((near >= 0) & (near < chain))
        def _():
            pl.semaphore_signal(
                barrier,
                inc=1,
                device_id=(lax.axis_index("tokens"), near),
                device_id_type=MESH_ID,
            )

    edge = (here == 0) | (here == chain - 1)

    @pl.when(edge)
    def _():
        pl.semaphore_wait(barrier, 1)

    @pl.when(jnp.logical_not(edge))
    def _():
        pl.semaphore_wait(barrier, 2)


class ChainSum:
    def __init__(self, chain, upward, term, passing, total, first_row, rows, sems):
        self.chain, self.term, self.passing, self.total = chain, term, passing, total
        self.first_row, self.rows = first_row, rows
        here = lax.axis_index("heads")
        self.rank = here if upward else chain - 1 - here
        move = 1 if upward else -1
        clip = lambda h: jnp.clip(h, 0, chain - 1)
        tokens = lax.axis_index("tokens")
        self.ahead = (tokens, clip(here + move))
        self.behind = (tokens, clip(here - move))
        self.sems = sems
        self.first = self.rank == 0
        self.last = self.rank == chain - 1

    def place(self, i):
        return pl.ds(self.first_row + i * self.rows, self.rows)

    def out_copy(self, i, first):
        place = self.place(i)
        src = self.term if first else self.passing
        return remote(
            src.at[place], self.passing.at[place], self.sems.at[0, i], self.sems.at[1, i], self.ahead
        )

    def back_copy(self, i):
        place = self.place(i)
        return remote(
            self.total.at[place], self.total.at[place], self.sems.at[2, i], self.sems.at[3, i], self.behind
        )

    def add(self, i):
        place = self.place(i)
        return self.term[place, :].astype(jnp.float32) + self.passing[place, :].astype(jnp.float32)

    def out_step(self, i):
        @pl.when(self.first)
        def _():
            self.out_copy(i, True).start()

        @pl.when(jnp.logical_not(self.first))
        def _():
            self.out_copy(i, False).wait_recv()

        @pl.when(jnp.logical_not(self.first | self.last))
        def _():
            self.passing[self.place(i), :] = self.add(i).astype(self.passing.dtype)
            self.out_copy(i, False).start()

        @pl.when(self.last)
        def _():
            self.total[self.place(i), :] = self.add(i).astype(self.total.dtype)
            self.back_copy(i).start()

    def back_step(self, i):
        @pl.when(jnp.logical_not(self.last))
        def _():
            self.back_copy(i).wait_recv()

        @pl.when(jnp.logical_not(self.first | self.last))
        def _():
            self.back_copy(i).start()

    def finish(self, count):
        for i in range(count):

            @pl.when(jnp.logical_not(self.last))
            def _():
                self.out_copy(i, False).wait_send()

            @pl.when(jnp.logical_not(self.first))
            def _():
                self.back_copy(i).wait_send()


def chain_kernel(chain, count, lag, term, out, passing, total, sems):
    greet_chain(chain)
    half = term.shape[0] // 2
    rows = half // count
    sums = [
        ChainSum(chain, upward, term, passing, total, first, rows, sems.at[k])
        for k, (upward, first) in enumerate(((True, 0), (False, half)))
    ]
    for i in range(count + lag):
        if i < count:
            for part in sums:
                part.out_step(i)
        if i >= lag:
            for part in sums:
                part.back_step(i - lag)
    for part in sums:
        part.finish(count)
    out[...] = total[...]


def chain_sum(term, chain, collective_id, count=8, lag=4):
    return pl.pallas_call(
        functools.partial(chain_kernel, chain, count, lag),
        out_shape=jax.ShapeDtypeStruct(term.shape, term.dtype),
        in_specs=[pl.BlockSpec(memory_space=pltpu.VMEM)],
        out_specs=pl.BlockSpec(memory_space=pltpu.VMEM),
        scratch_shapes=[
            pltpu.VMEM(term.shape, term.dtype),
            pltpu.VMEM(term.shape, term.dtype),
            pltpu.SemaphoreType.DMA((2, 4, count)),
        ],
        compiler_params=pltpu.CompilerParams(
            collective_id=collective_id, has_side_effects=True, vmem_limit_bytes=VMEM_BYTES
        ),
        name="chain_sum",
    )(term)


class Scatter:
    COPIES = 10

    def __init__(self, grad, axis, own, sib, near, sems, local):
        self.grad, self.axis, self.own, self.sib, self.near = grad, axis, own, sib, near
        self.sems, self.local = sems, local
        self.me = lax.axis_index("tokens")

    def sib_copy(self, k):
        index = jnp.bitwise_xor(self.me, 2 * k + 1)
        return remote(
            block_of(self.grad, self.axis, index),
            self.sib.at[k],
            self.sems.at[0, k],
            self.sems.at[1, k],
            token_device(1),
        )

    def own_copy(self, k):
        index = jnp.bitwise_xor(self.me, 2 * k)
        return pltpu.make_async_copy(
            block_of(self.grad, self.axis, index), self.own.at[k], self.local.at[k]
        )

    def half(self, ref, k, half):
        rows = ref.shape[1] // 2
        return ref.at[k, pl.ds(half * rows, rows)]

    def chip_copy(self, slot):
        k, half, flip = ((1, 0, 2), (3, 0, 2), (2, 1, 4), (3, 1, 4), (2, 0, 4), (1, 1, 2))[slot]
        return remote(
            self.half(self.own, k, half),
            self.near.at[slot],
            self.sems.at[0, 4 + slot],
            self.sems.at[1, 4 + slot],
            token_device(flip),
        )

    def start(self):
        for k in (3, 1, 2, 0):
            self.sib_copy(k).start()
            self.own_copy(k).start()

    def cores(self):
        for k in (3, 1, 2, 0):
            self.sib_copy(k).wait_recv()
            self.own_copy(k).wait()
            self.own[k] = (
                self.own[k].astype(jnp.float32) + self.sib[k].astype(jnp.float32)
            ).astype(self.own.dtype)
            for slot in {3: (1, 3), 1: (0,), 2: (2,), 0: ()}[k]:
                self.chip_copy(slot).start()

    def add_near(self, k, half, slot):
        rows = self.own.shape[1] // 2
        place = pl.ds(half * rows, rows)
        self.own[k, place] = (
            self.own[k, place].astype(jnp.float32) + self.near[slot].astype(jnp.float32)
        ).astype(self.own.dtype)

    def second(self):
        self.chip_copy(1).wait_recv()
        self.add_near(2, 0, 1)
        self.chip_copy(4).start()
        self.chip_copy(3).wait_recv()
        self.add_near(1, 1, 3)
        self.chip_copy(5).start()

    def finish(self, out):
        rows = self.own.shape[1] // 2
        for half, slots in ((0, (0, 4)), (1, (2, 5))):
            place = pl.ds(half * rows, rows)
            total = self.own[0, place].astype(jnp.float32)
            for slot in slots:
                self.chip_copy(slot).wait_recv()
                total = total + self.near[slot].astype(jnp.float32)
            out[place, :] = total
        for k in range(4):
            self.sib_copy(k).wait_send()
        for slot in range(6):
            self.chip_copy(slot).wait_send()


def scatter_kernel(axes, *refs):
    count = len(axes)
    grads, outs = refs[:count], refs[count : 2 * count]
    owns = refs[2 * count : 3 * count]
    sibs = refs[3 * count : 4 * count]
    nears = refs[4 * count : 5 * count]
    sems, local = refs[5 * count :]
    greet_cube()
    parts = [
        Scatter(grads[i], axes[i], owns[i], sibs[i], nears[i], sems.at[i], local.at[i])
        for i in range(count)
    ]
    for i in range(count + 2):
        if i < count:
            parts[i].start()
        if 0 <= i - 1 < count:
            parts[i - 1].cores()
        if 0 <= i - 2 < count:
            parts[i - 2].second()
    for part, out in zip(parts, outs):
        part.finish(out)


def scatter_sums(arrays, axes, collective_id):
    count = len(arrays)
    blocks = [
        tuple(size // 8 if d == axis else size for d, size in enumerate(array.shape))
        for array, axis in zip(arrays, axes)
    ]
    return pl.pallas_call(
        functools.partial(scatter_kernel, axes),
        out_shape=[jax.ShapeDtypeStruct(s, jnp.float32) for s in blocks],
        in_specs=[pl.BlockSpec(memory_space=pl.ANY)] * count,
        out_specs=[pl.BlockSpec(memory_space=pltpu.VMEM)] * count,
        scratch_shapes=[pltpu.VMEM((4,) + s, a.dtype) for s, a in zip(blocks, arrays)]
        + [pltpu.VMEM((4,) + s, a.dtype) for s, a in zip(blocks, arrays)]
        + [pltpu.VMEM((6, s[0] // 2, s[1]), a.dtype) for s, a in zip(blocks, arrays)]
        + [
            pltpu.SemaphoreType.DMA((count, 2, Scatter.COPIES)),
            pltpu.SemaphoreType.DMA((count, 4)),
        ],
        compiler_params=pltpu.CompilerParams(
            collective_id=collective_id, has_side_effects=True, vmem_limit_bytes=VMEM_BYTES
        ),
        name="scatter_sums",
    )(*arrays)


def shards_cube(
    chain,
    inputs,
    segments,
    pre_gain,
    mid_gain,
    query_weight,
    key_weight,
    value_weight,
    out_weight,
    gate_weight,
    up_weight,
    down_weight,
    cotangent,
):
    row_count = inputs.shape[0]
    head_size = key_weight.shape[1]
    heads_here = query_weight.shape[1] // head_size
    myself = lax.axis_index("tokens")
    small = jnp.stack(
        [
            segments.astype(jnp.float32),
            jnp.concatenate([pre_gain, mid_gain]).astype(jnp.float32),
        ]
    )
    small = jnp.concatenate([small, jnp.zeros((14, row_count), jnp.float32)])
    in_weight = jnp.concatenate([query_weight, key_weight, value_weight], axis=1)
    small_full, in_full, out_full, gate_full, up_full, down_full = gather_weights(
        (small, in_weight, out_weight, gate_weight, up_weight, down_weight), (0, 0, 1, 0, 0, 1), 0
    )
    query_width = query_weight.shape[1]
    query_full = in_full[:, :query_width]
    key_full = in_full[:, query_width : query_width + head_size]
    value_full = in_full[:, query_width + head_size :]
    small_full = small_full.reshape(8, 16, row_count)
    all_ids = small_full[:, 0].reshape(-1).astype(jnp.int32)
    pre_row = small_full[:, 1, : row_count // 2].reshape(-1)
    mid_row = small_full[:, 1, row_count // 2 :].reshape(-1)
    length = all_ids.shape[0]
    places = jnp.arange(length, dtype=jnp.int32)
    starts_here = jnp.concatenate([jnp.ones((1,), dtype=jnp.bool_), all_ids[1:] != all_ids[:-1]])
    opening = lax.cummax(jnp.where(starts_here, places, 0), axis=0)
    own_first = myself * row_count
    positions = lax.dynamic_slice_in_dim(places - opening, own_first, row_count)
    own_places = own_first + jnp.arange(row_count, dtype=jnp.int32)
    half_size = head_size // 2
    inverse = 10000.0 ** (-jnp.arange(half_size, dtype=jnp.float32) / half_size)
    turned = positions.astype(jnp.float32)[:, None] * inverse[None, :]
    cos_table = jnp.cos(turned)[:, None, :]
    sin_table = jnp.sin(turned)[:, None, :]
    inputs_f = inputs.astype(jnp.float32)
    pre_scale = rms_scale(inputs_f)
    normed = (inputs_f * pre_scale * pre_row).astype(jnp.bfloat16)
    queries = jnp.dot(normed, query_full, preferred_element_type=jnp.float32).reshape(
        row_count, heads_here, head_size
    )
    query_rot = (rotate(queries, cos_table, sin_table) * head_size ** (-0.5)).astype(jnp.bfloat16)
    key_rows = jnp.dot(normed, key_full, preferred_element_type=jnp.float32)[:, None, :]
    key_rot = rotate(key_rows, cos_table, sin_table)[:, 0, :].astype(jnp.bfloat16)
    value_low = jnp.dot(normed, value_full, preferred_element_type=jnp.float32).astype(jnp.bfloat16)
    key_all, value_all = (
        lax.all_gather(key_rot, "tokens", axis=0, tiled=True),
        lax.all_gather(value_low, "tokens", axis=0, tiled=True),
    )
    span = math.gcd(ROW, 1024)
    row_start = own_first // ROW * ROW
    block_first = row_start // span
    block_total = (own_first + row_count + span - 1) // span

    def key_block(block_index):
        opening_row = block_index * span
        block_keys = lax.dynamic_slice_in_dim(key_all, opening_row, span)
        block_values = lax.dynamic_slice_in_dim(value_all, opening_row, span)
        block_ids = lax.dynamic_slice_in_dim(all_ids, opening_row, span)
        block_places = opening_row + jnp.arange(span, dtype=jnp.int32)
        allowed = (segments[:, None] == block_ids[None, :]) & (
            own_places[:, None] >= block_places[None, :]
        )
        scores = jnp.einsum(
            "qhd,kd->qhk", query_rot, block_keys, preferred_element_type=jnp.float32
        )
        return (opening_row, block_keys, block_values, allowed[:, None, :], scores)

    def forward_step(block_index, state_now):
        row_peak, row_total, running = state_now
        opening_row, block_keys, block_values, allowed, scores = key_block(block_index)
        new_peak = jnp.maximum(row_peak, jnp.max(jnp.where(allowed, scores, -1e30), axis=-1))
        factor = jnp.exp(row_peak - new_peak)
        weights = jnp.where(allowed, jnp.exp(scores - new_peak[..., None]), 0.0)
        row_total = row_total * factor + jnp.sum(weights, axis=-1)
        running = running * factor[..., None] + jnp.einsum(
            "qhk,kd->qhd",
            weights.astype(jnp.bfloat16),
            block_values,
            preferred_element_type=jnp.float32,
        )
        return (new_peak, row_total, running)

    start_state = (
        jnp.full((row_count, heads_here), -1e30, jnp.float32),
        jnp.zeros((row_count, heads_here), jnp.float32),
        jnp.zeros((row_count, heads_here, head_size), jnp.float32),
    )
    row_peak, row_total, running = lax.fori_loop(
        block_first, block_total, forward_step, start_state
    )
    attended = running / row_total[..., None]
    log_total = row_peak + jnp.log(row_total)
    attended_low = attended.astype(jnp.bfloat16).reshape(row_count, heads_here * head_size)
    attn_term = jnp.dot(attended_low, out_full, preferred_element_type=jnp.float32)
    middle = inputs_f + chain_sum(attn_term.astype(jnp.bfloat16), chain, 1).astype(jnp.float32)
    mid_scale = rms_scale(middle)
    normed_mid = (middle * mid_scale * mid_row).astype(jnp.bfloat16)
    gate_rows = jnp.dot(normed_mid, gate_full, preferred_element_type=jnp.float32)
    up_rows = jnp.dot(normed_mid, up_full, preferred_element_type=jnp.float32)
    sigmoid_rows = jax.nn.sigmoid(gate_rows)
    silu_rows = gate_rows * sigmoid_rows
    hidden = (silu_rows * up_rows).astype(jnp.bfloat16)
    mlp_term = jnp.dot(hidden, down_full, preferred_element_type=jnp.float32)
    layer_out = (
        middle + chain_sum(mlp_term.astype(jnp.bfloat16), chain, 2).astype(jnp.float32)
    ).astype(jnp.bfloat16)
    grad_down = jnp.einsum("tf,td->fd", hidden, cotangent, preferred_element_type=jnp.float32)
    back_hidden = jnp.einsum("td,fd->tf", cotangent, down_full, preferred_element_type=jnp.float32)
    back_gate = (
        back_hidden * up_rows * sigmoid_rows * (1.0 + gate_rows * (1.0 - sigmoid_rows))
    ).astype(jnp.bfloat16)
    back_up = (back_hidden * silu_rows).astype(jnp.bfloat16)
    grad_gate = jnp.einsum("tc,tf->cf", normed_mid, back_gate, preferred_element_type=jnp.float32)
    grad_up = jnp.einsum("tc,tf->cf", normed_mid, back_up, preferred_element_type=jnp.float32)
    mid_term = jnp.einsum(
        "tf,cf->tc", back_gate, gate_full, preferred_element_type=jnp.float32
    ) + jnp.einsum("tf,cf->tc", back_up, up_full, preferred_element_type=jnp.float32)
    back_normed_mid = chain_sum(mid_term.astype(jnp.bfloat16), chain, 3).astype(jnp.float32)
    back_middle, grad_mid = norm_back(back_normed_mid, middle, mid_scale, mid_row)
    back_middle = back_middle + cotangent.astype(jnp.float32)
    back_attn = back_middle.astype(jnp.bfloat16)
    grad_out = jnp.einsum("tc,td->cd", attended_low, back_attn, preferred_element_type=jnp.float32)
    back_attended = (
        jnp.einsum("td,cd->tc", back_attn, out_full, preferred_element_type=jnp.float32)
        .astype(jnp.bfloat16)
        .reshape(row_count, heads_here, head_size)
    )
    row_delta = jnp.sum(back_attended.astype(jnp.float32) * attended, axis=-1)

    def backward_step(block_index, state_now):
        back_rows, back_pairs = state_now
        opening_row, block_keys, block_values, allowed, scores = key_block(block_index)
        chances = jnp.where(allowed, jnp.exp(scores - log_total[..., None]), 0.0)
        back_values = jnp.einsum(
            "qhk,qhd->kd",
            chances.astype(jnp.bfloat16),
            back_attended,
            preferred_element_type=jnp.float32,
        )
        back_chances = jnp.einsum(
            "qhd,kd->qhk", back_attended, block_values, preferred_element_type=jnp.float32
        )
        back_scores = (chances * (back_chances - row_delta[..., None])).astype(jnp.bfloat16)
        back_rows = back_rows + jnp.einsum(
            "qhk,kd->qhd", back_scores, block_keys, preferred_element_type=jnp.float32
        )
        back_keys = jnp.einsum(
            "qhk,qhd->kd", back_scores, query_rot, preferred_element_type=jnp.float32
        )
        old_piece = lax.dynamic_slice_in_dim(back_pairs, opening_row, span)
        fresh_piece = old_piece + jnp.concatenate([back_keys, back_values], axis=-1)
        back_pairs = lax.dynamic_update_slice_in_dim(back_pairs, fresh_piece, opening_row, 0)
        return (back_rows, back_pairs)

    start_back = (
        jnp.zeros((row_count, heads_here, head_size), jnp.float32),
        jnp.zeros((length, 2 * head_size), jnp.float32),
    )
    back_rows, back_pairs = lax.fori_loop(block_first, block_total, backward_step, start_back)
    own_pairs = lax.psum_scatter(
        back_pairs.astype(jnp.bfloat16), "tokens", scatter_dimension=0, tiled=True
    ).astype(jnp.float32)
    back_query = (
        (unrotate(back_rows, cos_table, sin_table) * head_size ** (-0.5))
        .astype(jnp.bfloat16)
        .reshape(row_count, heads_here * head_size)
    )
    back_key = unrotate(own_pairs[:, None, :head_size], cos_table, sin_table)[:, 0, :].astype(
        jnp.bfloat16
    )
    back_value = own_pairs[:, head_size:].astype(jnp.bfloat16)
    grad_query = jnp.einsum("tc,tq->cq", normed, back_query, preferred_element_type=jnp.float32)
    grad_key = jnp.einsum("tc,tq->cq", normed, back_key, preferred_element_type=jnp.float32)
    grad_value = jnp.einsum("tc,tq->cq", normed, back_value, preferred_element_type=jnp.float32)
    pre_term = jnp.einsum("tq,cq->tc", back_query, query_full, preferred_element_type=jnp.float32)
    pre_term = pre_term + jnp.einsum(
        "tq,cq->tc", back_key, key_full, preferred_element_type=jnp.float32
    )
    pre_term = pre_term + jnp.einsum(
        "tq,cq->tc", back_value, value_full, preferred_element_type=jnp.float32
    )
    back_normed = chain_sum(pre_term.astype(jnp.bfloat16), chain, 4).astype(jnp.float32)
    back_inputs, grad_pre = norm_back(back_normed, inputs_f, pre_scale, pre_row)
    grad_input = (back_middle + back_inputs).astype(jnp.bfloat16)
    grad_in = jnp.concatenate([grad_query, grad_key, grad_value], axis=1).astype(jnp.bfloat16)
    grad_gate, grad_up, grad_down, grad_in, grad_out = scatter_sums(
        (
            grad_gate.astype(jnp.bfloat16),
            grad_up.astype(jnp.bfloat16),
            grad_down.astype(jnp.bfloat16),
            grad_in,
            grad_out.astype(jnp.bfloat16),
        ),
        (0, 0, 1, 0, 1),
        5,
    )
    grad_query = grad_in[:, :query_width]
    grad_key = grad_in[:, query_width : query_width + head_size]
    grad_value = grad_in[:, query_width + head_size :]
    grad_pre, grad_mid = (
        lax.psum_scatter(part.astype(jnp.bfloat16), "tokens", scatter_dimension=0, tiled=True).astype(jnp.float32)
        for part in (grad_pre, grad_mid)
    )
    return (
        layer_out,
        grad_input,
        grad_pre,
        grad_mid,
        grad_query,
        grad_key,
        grad_value,
        grad_out,
        grad_gate,
        grad_up,
        grad_down,
    )


def solution(mesh):
    sizes = dict(mesh.shape)
    plan = shards_any
    if sizes["tokens"] == 8:
        plan = functools.partial(shards_cube, sizes["heads"])
    return jax.shard_map(
        plan,
        mesh=mesh,
        in_specs=(
            P("tokens", None),
            P("tokens"),
            P("tokens"),
            P("tokens"),
            P("tokens", "heads"),
            P("tokens", "heads"),
            P("tokens", "heads"),
            P("heads", "tokens"),
            P("tokens", "heads"),
            P("tokens", "heads"),
            P("heads", "tokens"),
            P("tokens", None),
        ),
        out_specs=(
            P("tokens", None),
            P("tokens", None),
            P("tokens"),
            P("tokens"),
            P("tokens", "heads"),
            P("tokens", "heads"),
            P("tokens", "heads"),
            P("heads", "tokens"),
            P("tokens", "heads"),
            P("tokens", "heads"),
            P("heads", "tokens"),
        ),
        check_vma=False,
    )
```

```python
import functools
import math

import jax
import jax.numpy as jnp
from jax import lax
from jax.experimental import pallas as pl
from jax.experimental.pallas import tpu as pltpu
from jax.sharding import PartitionSpec as P

ROW = 2048


def rms_scale(vectors):
    return lax.rsqrt(jnp.mean(vectors * vectors, axis=-1, keepdims=True) + 1e-05)


def rotate(vectors, cos_table, sin_table):
    middle_index = vectors.shape[-1] // 2
    former = vectors[..., :middle_index]
    latter = vectors[..., middle_index:]
    return jnp.concatenate(
        [former * cos_table - latter * sin_table, latter * cos_table + former * sin_table], axis=-1
    )


def unrotate(gradient, cos_table, sin_table):
    middle_index = gradient.shape[-1] // 2
    former = gradient[..., :middle_index]
    latter = gradient[..., middle_index:]
    return jnp.concatenate(
        [former * cos_table + latter * sin_table, latter * cos_table - former * sin_table], axis=-1
    )


def norm_back(gradient, vectors, scale_rows, gain_row):
    shaped = vectors * scale_rows
    weighted = gradient * gain_row
    back_vectors = scale_rows * (
        weighted - shaped * jnp.mean(weighted * shaped, axis=-1, keepdims=True)
    )
    return (back_vectors, jnp.sum(gradient * shaped, axis=0))


def shards_any(
    inputs,
    segments,
    pre_gain,
    mid_gain,
    query_weight,
    key_weight,
    value_weight,
    out_weight,
    gate_weight,
    up_weight,
    down_weight,
    cotangent,
):
    row_count = inputs.shape[0]
    head_size = key_weight.shape[1]
    heads_here = query_weight.shape[1] // head_size
    myself = lax.axis_index("tokens")
    gathered = (
        lax.all_gather(pre_gain, "tokens", axis=0, tiled=True),
        lax.all_gather(mid_gain, "tokens", axis=0, tiled=True),
        lax.all_gather(query_weight, "tokens", axis=0, tiled=True),
        lax.all_gather(key_weight, "tokens", axis=0, tiled=True),
        lax.all_gather(value_weight, "tokens", axis=0, tiled=True),
        lax.all_gather(out_weight, "tokens", axis=1, tiled=True),
        lax.all_gather(gate_weight, "tokens", axis=0, tiled=True),
        lax.all_gather(up_weight, "tokens", axis=0, tiled=True),
        lax.all_gather(down_weight, "tokens", axis=1, tiled=True),
    )
    (
        pre_full,
        mid_full,
        query_full,
        key_full,
        value_full,
        out_full,
        gate_full,
        up_full,
        down_full,
    ) = gathered
    pre_row = pre_full.astype(jnp.float32)
    mid_row = mid_full.astype(jnp.float32)
    all_ids = lax.all_gather(segments, "tokens", axis=0, tiled=True)
    length = all_ids.shape[0]
    places = jnp.arange(length, dtype=jnp.int32)
    starts_here = jnp.concatenate([jnp.ones((1,), dtype=jnp.bool_), all_ids[1:] != all_ids[:-1]])
    opening = lax.cummax(jnp.where(starts_here, places, 0), axis=0)
    own_first = myself * row_count
    positions = lax.dynamic_slice_in_dim(places - opening, own_first, row_count)
    own_places = own_first + jnp.arange(row_count, dtype=jnp.int32)
    half_size = head_size // 2
    inverse = 10000.0 ** (-jnp.arange(half_size, dtype=jnp.float32) / half_size)
    turned = positions.astype(jnp.float32)[:, None] * inverse[None, :]
    cos_table = jnp.cos(turned)[:, None, :]
    sin_table = jnp.sin(turned)[:, None, :]
    inputs_f = inputs.astype(jnp.float32)
    pre_scale = rms_scale(inputs_f)
    normed = (inputs_f * pre_scale * pre_row).astype(jnp.bfloat16)
    queries = jnp.dot(normed, query_full, preferred_element_type=jnp.float32).reshape(
        row_count, heads_here, head_size
    )
    query_rot = (rotate(queries, cos_table, sin_table) * head_size ** (-0.5)).astype(jnp.bfloat16)
    key_rows = jnp.dot(normed, key_full, preferred_element_type=jnp.float32)[:, None, :]
    key_rot = rotate(key_rows, cos_table, sin_table)[:, 0, :].astype(jnp.bfloat16)
    value_low = jnp.dot(normed, value_full, preferred_element_type=jnp.float32).astype(jnp.bfloat16)
    key_all, value_all = (
        lax.all_gather(key_rot, "tokens", axis=0, tiled=True),
        lax.all_gather(value_low, "tokens", axis=0, tiled=True),
    )
    span = math.gcd(ROW, 1024)
    row_start = own_first // ROW * ROW
    block_first = row_start // span
    block_total = (own_first + row_count + span - 1) // span

    def key_block(block_index):
        opening_row = block_index * span
        block_keys = lax.dynamic_slice_in_dim(key_all, opening_row, span)
        block_values = lax.dynamic_slice_in_dim(value_all, opening_row, span)
        block_ids = lax.dynamic_slice_in_dim(all_ids, opening_row, span)
        block_places = opening_row + jnp.arange(span, dtype=jnp.int32)
        allowed = (segments[:, None] == block_ids[None, :]) & (
            own_places[:, None] >= block_places[None, :]
        )
        scores = jnp.einsum(
            "qhd,kd->qhk", query_rot, block_keys, preferred_element_type=jnp.float32
        )
        return (opening_row, block_keys, block_values, allowed[:, None, :], scores)

    def forward_step(block_index, state_now):
        row_peak, row_total, running = state_now
        opening_row, block_keys, block_values, allowed, scores = key_block(block_index)
        new_peak = jnp.maximum(row_peak, jnp.max(jnp.where(allowed, scores, -1e30), axis=-1))
        factor = jnp.exp(row_peak - new_peak)
        weights = jnp.where(allowed, jnp.exp(scores - new_peak[..., None]), 0.0)
        row_total = row_total * factor + jnp.sum(weights, axis=-1)
        running = running * factor[..., None] + jnp.einsum(
            "qhk,kd->qhd",
            weights.astype(jnp.bfloat16),
            block_values,
            preferred_element_type=jnp.float32,
        )
        return (new_peak, row_total, running)

    start_state = (
        jnp.full((row_count, heads_here), -1e30, jnp.float32),
        jnp.zeros((row_count, heads_here), jnp.float32),
        jnp.zeros((row_count, heads_here, head_size), jnp.float32),
    )
    row_peak, row_total, running = lax.fori_loop(
        block_first, block_total, forward_step, start_state
    )
    attended = running / row_total[..., None]
    log_total = row_peak + jnp.log(row_total)
    attended_low = attended.astype(jnp.bfloat16).reshape(row_count, heads_here * head_size)
    attn_term = jnp.dot(attended_low, out_full, preferred_element_type=jnp.float32)
    middle = inputs_f + lax.psum(attn_term.astype(jnp.bfloat16), "heads").astype(jnp.float32)
    mid_scale = rms_scale(middle)
    normed_mid = (middle * mid_scale * mid_row).astype(jnp.bfloat16)
    gate_rows = jnp.dot(normed_mid, gate_full, preferred_element_type=jnp.float32)
    up_rows = jnp.dot(normed_mid, up_full, preferred_element_type=jnp.float32)
    sigmoid_rows = jax.nn.sigmoid(gate_rows)
    silu_rows = gate_rows * sigmoid_rows
    hidden = (silu_rows * up_rows).astype(jnp.bfloat16)
    mlp_term = jnp.dot(hidden, down_full, preferred_element_type=jnp.float32)
    layer_out = (
        middle + lax.psum(mlp_term.astype(jnp.bfloat16), "heads").astype(jnp.float32)
    ).astype(jnp.bfloat16)
    grad_down = jnp.einsum("tf,td->fd", hidden, cotangent, preferred_element_type=jnp.float32)
    back_hidden = jnp.einsum("td,fd->tf", cotangent, down_full, preferred_element_type=jnp.float32)
    back_gate = (
        back_hidden * up_rows * sigmoid_rows * (1.0 + gate_rows * (1.0 - sigmoid_rows))
    ).astype(jnp.bfloat16)
    back_up = (back_hidden * silu_rows).astype(jnp.bfloat16)
    grad_gate = jnp.einsum("tc,tf->cf", normed_mid, back_gate, preferred_element_type=jnp.float32)
    grad_up = jnp.einsum("tc,tf->cf", normed_mid, back_up, preferred_element_type=jnp.float32)
    mid_term = jnp.einsum(
        "tf,cf->tc", back_gate, gate_full, preferred_element_type=jnp.float32
    ) + jnp.einsum("tf,cf->tc", back_up, up_full, preferred_element_type=jnp.float32)
    back_normed_mid = lax.psum(mid_term.astype(jnp.bfloat16), "heads").astype(jnp.float32)
    back_middle, grad_mid = norm_back(back_normed_mid, middle, mid_scale, mid_row)
    back_middle = back_middle + cotangent.astype(jnp.float32)
    back_attn = back_middle.astype(jnp.bfloat16)
    grad_out = jnp.einsum("tc,td->cd", attended_low, back_attn, preferred_element_type=jnp.float32)
    back_attended = (
        jnp.einsum("td,cd->tc", back_attn, out_full, preferred_element_type=jnp.float32)
        .astype(jnp.bfloat16)
        .reshape(row_count, heads_here, head_size)
    )
    row_delta = jnp.sum(back_attended.astype(jnp.float32) * attended, axis=-1)

    def backward_step(block_index, state_now):
        back_rows, back_pairs = state_now
        opening_row, block_keys, block_values, allowed, scores = key_block(block_index)
        chances = jnp.where(allowed, jnp.exp(scores - log_total[..., None]), 0.0)
        back_values = jnp.einsum(
            "qhk,qhd->kd",
            chances.astype(jnp.bfloat16),
            back_attended,
            preferred_element_type=jnp.float32,
        )
        back_chances = jnp.einsum(
            "qhd,kd->qhk", back_attended, block_values, preferred_element_type=jnp.float32
        )
        back_scores = (chances * (back_chances - row_delta[..., None])).astype(jnp.bfloat16)
        back_rows = back_rows + jnp.einsum(
            "qhk,kd->qhd", back_scores, block_keys, preferred_element_type=jnp.float32
        )
        back_keys = jnp.einsum(
            "qhk,qhd->kd", back_scores, query_rot, preferred_element_type=jnp.float32
        )
        old_piece = lax.dynamic_slice_in_dim(back_pairs, opening_row, span)
        fresh_piece = old_piece + jnp.concatenate([back_keys, back_values], axis=-1)
        back_pairs = lax.dynamic_update_slice_in_dim(back_pairs, fresh_piece, opening_row, 0)
        return (back_rows, back_pairs)

    start_back = (
        jnp.zeros((row_count, heads_here, head_size), jnp.float32),
        jnp.zeros((length, 2 * head_size), jnp.float32),
    )
    back_rows, back_pairs = lax.fori_loop(block_first, block_total, backward_step, start_back)
    own_pairs = lax.psum_scatter(
        back_pairs.astype(jnp.bfloat16), "tokens", scatter_dimension=0, tiled=True
    ).astype(jnp.float32)
    back_query = (
        (unrotate(back_rows, cos_table, sin_table) * head_size ** (-0.5))
        .astype(jnp.bfloat16)
        .reshape(row_count, heads_here * head_size)
    )
    back_key = unrotate(own_pairs[:, None, :head_size], cos_table, sin_table)[:, 0, :].astype(
        jnp.bfloat16
    )
    back_value = own_pairs[:, head_size:].astype(jnp.bfloat16)
    grad_query = jnp.einsum("tc,tq->cq", normed, back_query, preferred_element_type=jnp.float32)
    grad_key = jnp.einsum("tc,tq->cq", normed, back_key, preferred_element_type=jnp.float32)
    grad_value = jnp.einsum("tc,tq->cq", normed, back_value, preferred_element_type=jnp.float32)
    pre_term = jnp.einsum("tq,cq->tc", back_query, query_full, preferred_element_type=jnp.float32)
    pre_term = pre_term + jnp.einsum(
        "tq,cq->tc", back_key, key_full, preferred_element_type=jnp.float32
    )
    pre_term = pre_term + jnp.einsum(
        "tq,cq->tc", back_value, value_full, preferred_element_type=jnp.float32
    )
    back_normed = lax.psum(pre_term.astype(jnp.bfloat16), "heads").astype(jnp.float32)
    back_inputs, grad_pre = norm_back(back_normed, inputs_f, pre_scale, pre_row)
    grad_input = (back_middle + back_inputs).astype(jnp.bfloat16)
    summed = (
        lax.psum_scatter(
            grad_pre.astype(jnp.bfloat16), "tokens", scatter_dimension=0, tiled=True
        ).astype(jnp.float32),
        lax.psum_scatter(
            grad_mid.astype(jnp.bfloat16), "tokens", scatter_dimension=0, tiled=True
        ).astype(jnp.float32),
        lax.psum_scatter(
            grad_query.astype(jnp.bfloat16), "tokens", scatter_dimension=0, tiled=True
        ).astype(jnp.float32),
        lax.psum_scatter(
            grad_key.astype(jnp.bfloat16), "tokens", scatter_dimension=0, tiled=True
        ).astype(jnp.float32),
        lax.psum_scatter(
            grad_value.astype(jnp.bfloat16), "tokens", scatter_dimension=0, tiled=True
        ).astype(jnp.float32),
        lax.psum_scatter(
            grad_out.astype(jnp.bfloat16), "tokens", scatter_dimension=1, tiled=True
        ).astype(jnp.float32),
        lax.psum_scatter(
            grad_gate.astype(jnp.bfloat16), "tokens", scatter_dimension=0, tiled=True
        ).astype(jnp.float32),
        lax.psum_scatter(
            grad_up.astype(jnp.bfloat16), "tokens", scatter_dimension=0, tiled=True
        ).astype(jnp.float32),
        lax.psum_scatter(
            grad_down.astype(jnp.bfloat16), "tokens", scatter_dimension=1, tiled=True
        ).astype(jnp.float32),
    )
    (
        grad_pre,
        grad_mid,
        grad_query,
        grad_key,
        grad_value,
        grad_out,
        grad_gate,
        grad_up,
        grad_down,
    ) = summed
    return (
        layer_out,
        grad_input,
        grad_pre,
        grad_mid,
        grad_query,
        grad_key,
        grad_value,
        grad_out,
        grad_gate,
        grad_up,
        grad_down,
    )


MESH_ID = pl.DeviceIdType.MESH
VMEM_BYTES = 60 * 2**20


def token_device(flip):
    return (jnp.bitwise_xor(lax.axis_index("tokens"), flip), lax.axis_index("heads"))


def remote(src, dst, send, recv, device):
    return pltpu.make_async_remote_copy(
        src_ref=src, dst_ref=dst, send_sem=send, recv_sem=recv, device_id=device, device_id_type=MESH_ID
    )


def greet_cube():
    barrier = pltpu.get_barrier_semaphore()
    for flip in (1, 2, 4):
        pl.semaphore_signal(barrier, inc=1, device_id=token_device(flip), device_id_type=MESH_ID)
    pl.semaphore_wait(barrier, 3)


def block_of(ref, axis, index, half=None):
    size = ref.shape[axis] // 8
    start = pl.multiple_of(index * size, size)
    if axis == 0:
        if half is None:
            return ref.at[pl.ds(start, size), :]
        return ref.at[pl.ds(pl.multiple_of(start + half * (size // 2), size // 2), size // 2), :]
    if half is None:
        return ref.at[:, pl.ds(start, size)]
    rows = ref.shape[0] // 2
    return ref.at[pl.ds(half * rows, rows), pl.ds(start, size)]


class Gather:
    COPIES = 9

    def __init__(self, shard, full, axis, send, recv, local):
        self.shard, self.full, self.axis = shard, full, axis
        self.send, self.recv, self.local = send, recv, local
        self.me = lax.axis_index("tokens")

    def copy(self, slot, flip_block, flip_target, half=None):
        index = jnp.bitwise_xor(self.me, flip_block)
        src = self.shard if flip_block == 0 else block_of(self.full, self.axis, index, half)
        return remote(
            src,
            block_of(self.full, self.axis, index, half),
            self.send.at[slot],
            self.recv.at[slot],
            token_device(flip_target),
        )

    def copies(self, slot):
        return self.copy(
            slot,
            *(
                (0, 2),
                (0, 4),
                (0, 1),
                (2, 4, 0),
                (4, 2, 1),
                (2, 1),
                (4, 1),
                (6, 1, 0),
                (6, 1, 1),
            )[slot],
        )

    def own_copy(self):
        return pltpu.make_async_copy(
            self.shard, block_of(self.full, self.axis, self.me), self.local
        )

    def start(self):
        for slot in (0, 1, 2):
            self.copies(slot).start()
        self.own_copy().start()

    def relay(self):
        self.copies(0).wait_recv()
        self.copies(3).start()
        self.copies(1).wait_recv()
        self.copies(4).start()
        self.copies(5).start()
        self.copies(6).start()

    def finish_relay(self):
        self.copies(3).wait_recv()
        self.copies(7).start()
        self.copies(4).wait_recv()
        self.copies(8).start()

    def finish(self):
        for slot in (2, 5, 6, 7, 8):
            self.copies(slot).wait_recv()
        for slot in range(self.COPIES):
            self.copies(slot).wait_send()
        self.own_copy().wait()


def greet_chain(chain):
    here = lax.axis_index("heads")
    barrier = pltpu.get_barrier_semaphore()
    for step in (-1, 1):
        near = here + step

        @pl.when((near >= 0) & (near < chain))
        def _():
            pl.semaphore_signal(
                barrier,
                inc=1,
                device_id=(lax.axis_index("tokens"), near),
                device_id_type=MESH_ID,
            )

    edge = (here == 0) | (here == chain - 1)

    @pl.when(edge)
    def _():
        pl.semaphore_wait(barrier, 1)

    @pl.when(jnp.logical_not(edge))
    def _():
        pl.semaphore_wait(barrier, 2)


class ChainSum:
    def __init__(self, chain, upward, term, passing, total, base, count, sems):
        self.chain, self.term, self.passing, self.total = chain, term, passing, total
        self.base, self.count = base, count
        here = lax.axis_index("heads")
        self.rank = here if upward else chain - 1 - here
        move = 1 if upward else -1
        tokens = lax.axis_index("tokens")
        self.ahead = (tokens, jnp.clip(here + move, 0, chain - 1))
        self.behind = (tokens, jnp.clip(here - move, 0, chain - 1))
        self.sems = sems
        self.first = self.rank == 0
        self.last = self.rank == chain - 1

    def out_copy(self, i, first):
        src = self.term if first else self.passing
        at = self.base + i
        return remote(
            src.at[at], self.passing.at[at], self.sems.at[0, i], self.sems.at[1, i], self.ahead
        )

    def back_copy(self, i):
        at = self.base + i
        return remote(
            self.total.at[at], self.total.at[at], self.sems.at[2, i], self.sems.at[3, i], self.behind
        )

    def add(self, i):
        at = self.base + i
        return self.term[at].astype(jnp.float32) + self.passing[at].astype(jnp.float32)

    def step(self, now):
        i = now - self.rank
        valid = (i >= 0) & (i < self.count)

        @pl.when(valid & self.first)
        def _():
            self.out_copy(i, True).start()

        @pl.when(valid & jnp.logical_not(self.first))
        def _():
            self.out_copy(i, False).wait_recv()

        @pl.when(valid & jnp.logical_not(self.first | self.last))
        def _():
            self.passing[self.base + i] = self.add(i).astype(self.passing.dtype)
            self.out_copy(i, False).start()

        @pl.when(valid & self.last)
        def _():
            self.total[self.base + i] = self.add(i).astype(self.total.dtype)
            self.back_copy(i).start()

        j = now - (2 * (self.chain - 1) - self.rank)
        back = (j >= 0) & (j < self.count) & jnp.logical_not(self.last)

        @pl.when(back)
        def _():
            self.back_copy(j).wait_recv()

        @pl.when(back & jnp.logical_not(self.first))
        def _():
            self.back_copy(j).start()

    def steps(self):
        return self.count + 2 * (self.chain - 1)

    def finish(self):
        @pl.when(jnp.logical_not(self.last))
        def _():
            for i in range(self.count):
                self.out_copy(i, False).wait_send()

        @pl.when(jnp.logical_not(self.first))
        def _():
            for i in range(self.count):
                self.back_copy(i).wait_send()


def chain_kernel(chain, count, term, out, passing, total, sems):
    greet_chain(chain)
    sums = [
        ChainSum(chain, upward, term, passing, total, base, count, sems.at[k])
        for k, (upward, base) in enumerate(((True, 0), (False, count)))
    ]

    @pl.loop(0, sums[0].steps())
    def _(now):
        for part in sums:
            part.step(now)

    for part in sums:
        part.finish()
    out[...] = total[...]


def chain_sum(term, chain, collective_id, count=8):
    shape = (2 * count, term.shape[0] // (2 * count), term.shape[1])
    return pl.pallas_call(
        functools.partial(chain_kernel, chain, count),
        out_shape=jax.ShapeDtypeStruct(shape, term.dtype),
        in_specs=[pl.BlockSpec(memory_space=pltpu.VMEM)],
        out_specs=pl.BlockSpec(memory_space=pltpu.VMEM),
        scratch_shapes=[
            pltpu.VMEM(shape, term.dtype),
            pltpu.VMEM(shape, term.dtype),
            pltpu.SemaphoreType.DMA((2, 4, count)),
        ],
        compiler_params=pltpu.CompilerParams(
            collective_id=collective_id, has_side_effects=True, vmem_limit_bytes=VMEM_BYTES
        ),
        name="chain_sum",
    )(term.reshape(shape)).reshape(term.shape)


def lanes(shape):
    return lax.broadcasted_iota(jnp.int32, shape, len(shape) - 1)


def turn(vectors, cos_table, sin_table):
    near = jnp.where(
        lanes(vectors.shape) % 64 < 32, pltpu.roll(vectors, 96, 1), pltpu.roll(vectors, 32, 1)
    )
    return vectors * cos_table + near * sin_table


def token_column(row):
    return jnp.broadcast_to(row, (128, row.shape[1])).T


def key_marks(column, first_id):
    lane = lanes(column.shape) % 64
    one_hot = (column - first_id).astype(jnp.int32) == lane
    return jnp.where(one_hot | ((lane >= 4) & (lane < 7)), 1.0, 0.0)


def query_marks(column, first_id):
    lane = lanes(column.shape) % 64
    other = (column - first_id).astype(jnp.int32) != lane
    return jnp.where(other & (lane < 4), -1e30, 0.0)


def nt_dot(left, right):
    return lax.dot_general(
        left, right, (((1,), (1,)), ((), ())), preferred_element_type=jnp.float32
    )


def attend_kernel(
    chain, places, x, small, in_shard, out_shard, gate_shard, up_shard, down_shard, inverse,
    gate_full, up_full, down_full, in_full, out_full, attn_sum, normed, query, pairs, attended, log_total,
    cos_table, sin_table, small_all, in_here, out_here, pre_row, key_side, value_side, marks, scores, peak,
    mixed, near_pairs, term, passing, total, small_sems, gather_sems, local_sems, pair_sems, chain_sems,
):
    count = term.shape[0] // 2
    tokens = x.shape[0]
    me = lax.axis_index("tokens")
    place = lax.rem(me, places)
    here = lax.axis_index("heads")
    barrier = pltpu.get_barrier_semaphore()
    for flip in range(1, 8):
        pl.semaphore_signal(barrier, inc=1, device_id=token_device(flip), device_id_type=MESH_ID)
    for step in (-1, 1):
        near = here + step

        @pl.when((near >= 0) & (near < chain))
        def _():
            pl.semaphore_signal(barrier, inc=1, device_id=(me, near), device_id_type=MESH_ID)

    edge = (here == 0) | (here == chain - 1)

    @pl.when(edge)
    def _():
        pl.semaphore_wait(barrier, 8)

    @pl.when(jnp.logical_not(edge))
    def _():
        pl.semaphore_wait(barrier, 9)

    def small_copy(flip):
        return remote(
            small,
            small_all.at[me],
            small_sems.at[0, flip - 1],
            small_sems.at[1, flip - 1],
            token_device(flip),
        )

    for flip in range(1, 8):
        small_copy(flip).start()

    def gather(k, shard, full, axis):
        return Gather(shard, full, axis, gather_sems.at[0, k], gather_sems.at[1, k], local_sems.at[k])

    gather_in = gather(0, in_shard, in_here, 0)
    gather_out = gather(1, out_shard, out_here, 1)
    big = [
        gather(2, gate_shard, gate_full, 0),
        gather(3, up_shard, up_full, 0),
        gather(4, down_shard, down_full, 1),
    ]
    gather_in.start()
    small_all[me] = small[...]

    x_f = x[...].astype(jnp.float32)
    pre_scale = lax.rsqrt(jnp.mean(x_f * x_f, axis=1, keepdims=True) + 1e-05)

    for flip in range(1, 8):
        small_copy(flip).wait_recv()
    width = x.shape[1] // 8
    for k in range(8):
        pre_row[:, k * width : (k + 1) * width] = jnp.broadcast_to(
            small_all[k, 1:2, :width], (8, width)
        )
    gather_in.relay()
    gather_out.start()
    normed[...] = (x[...].astype(jnp.float32) * pre_scale * pre_row[0:1, :]).astype(jnp.bfloat16)
    gather_in.finish_relay()

    first_device = me - place
    first_id = (first_device // places * 4).astype(jnp.float32)
    own = token_column(small_all[me, 0:1, :])
    before = jnp.zeros((tokens, 1), jnp.float32)
    for k in range(places):
        others = small_all[first_device + k, 0:1, :]
        before = before + jnp.sum(
            jnp.where(others < own[:, 0:1], 1.0, 0.0), axis=1, keepdims=True
        )
        column = token_column(others)
        marks[pl.ds(k * tokens, tokens), :] = key_marks(column, first_id)
    row_index = lax.broadcasted_iota(jnp.int32, (tokens, 128), 0) + place * tokens
    turned = (row_index.astype(jnp.float32) - before) * inverse[0:1, :]
    cos_table[...] = jnp.cos(turned)
    sin_signed = jnp.sin(turned)
    sin_table[...] = jnp.where(lanes(sin_signed.shape) % 64 < 32, -sin_signed, sin_signed)
    gather_out.relay()
    big[0].copies(1).start()
    gather_in.finish()

    wide = in_here.shape[1]
    heads_wide = wide - 128
    for low in range(0, wide, 256):
        high = min(low + 256, wide)
        made = jnp.dot(normed[...], in_here[:, low:high], preferred_element_type=jnp.float32)
        for group in range(low, high, 128):
            part = made[:, group - low : group - low + 128]
            spun = turn(part, cos_table[...], sin_table[...])
            if group < heads_wide:
                query[:, group : group + 128] = (spun * 0.125).astype(jnp.bfloat16)
            else:
                near_pairs[place] = jnp.where(lanes(part.shape) < 64, spun, part).astype(jnp.bfloat16)

    def pair_copy(flip):
        return remote(
            near_pairs.at[place],
            near_pairs.at[place],
            pair_sems.at[0, flip - 1],
            pair_sems.at[1, flip - 1],
            token_device(flip),
        )

    for flip in range(1, places):
        pair_copy(flip).start()
    big[0].copies(0).start()
    big[0].copies(2).start()
    big[0].own_copy().start()
    big[1].copies(1).start()
    gather_out.finish_relay()
    for flip in range(1, places):
        pair_copy(flip).wait_recv()
    big[1].copies(0).start()
    big[1].copies(2).start()
    big[1].own_copy().start()
    big[2].start()

    for k in range(places):
        pair = near_pairs[k].astype(jnp.float32)
        swapped = pltpu.roll(pair, 64, 1)
        lane = lanes(pair.shape)
        mark = marks[pl.ds(k * tokens, tokens), :]
        block = pl.ds(k * tokens, tokens)
        key_side[0, block] = jnp.where(lane < 64, pair, mark).astype(jnp.bfloat16)
        key_side[1, block] = jnp.where(lane < 64, mark, swapped).astype(jnp.bfloat16)
        value_side[0, block] = jnp.where(lane < 64, swapped, 1.0).astype(jnp.bfloat16)
        value_side[1, block] = jnp.where(lane < 64, 1.0, pair).astype(jnp.bfloat16)
        pairs[block] = near_pairs[k]

    lane = lanes((tokens, 128))
    own_marks = query_marks(own, first_id)

    @pl.loop(0, query.shape[1] // 128)
    def _(group):
        at = pl.ds(pl.multiple_of(group * 128, 128), 128)
        both = query[:, at].astype(jnp.float32)
        halves = []
        for e in range(2):
            mine = (lane < 64) if e == 0 else (lane >= 64)
            side = jnp.where(mine, both, own_marks).astype(jnp.bfloat16)

            def look(k, masked):
                found = nt_dot(side, key_side[e, pl.ds(pl.multiple_of(k * tokens, tokens), tokens)])
                if masked:
                    rows = lax.broadcasted_iota(jnp.int32, found.shape, 0)
                    found = jnp.where(lanes(found.shape) <= rows, found, -1e30)
                scores[k] = found
                best = found[:, :128]
                for part in range(128, tokens, 128):
                    best = jnp.maximum(best, found[:, part : part + 128])
                return best

            peak[...] = look(place, True)

            @pl.loop(0, place)
            def _(k):
                peak[...] = jnp.maximum(peak[...], look(k, False))

            top = jnp.max(peak[...], axis=1, keepdims=True)

            def blend(k):
                weights = jnp.exp(scores[k] - top).astype(jnp.bfloat16)
                return jnp.dot(
                    weights,
                    value_side[e, pl.ds(pl.multiple_of(k * tokens, tokens), tokens)],
                    preferred_element_type=jnp.float32,
                )

            mixed[...] = blend(place)

            @pl.loop(0, place)
            def _(k):
                mixed[...] += blend(k)

            out = mixed[...]
            rolled = pltpu.roll(out, 64, 1)
            sums = jnp.where(mine, rolled, out)
            halves.append(out / sums)
            log_total[...] = jnp.where(
                lane == 2 * group + e, top + jnp.log(sums), log_total[...]
            )
        attended[:, at] = jnp.where(lane < 64, halves[0], halves[1])

    gather_out.finish()
    low = attended[...].astype(jnp.bfloat16)
    each = term.shape[2]
    for k in range(0, 2 * count, 2):
        made = jnp.dot(
            low, out_here[:, k * each : (k + 2) * each], preferred_element_type=jnp.float32
        ).astype(jnp.bfloat16)
        term[k] = made[:, :each]
        term[k + 1] = made[:, each:]
    in_out = [
        pltpu.make_async_copy(in_here, in_full, local_sems.at[5]),
        pltpu.make_async_copy(out_here, out_full, local_sems.at[6]),
    ]
    for copy in in_out:
        copy.start()
    sums = [
        ChainSum(chain, upward, term, passing, total, base, count, chain_sems.at[k])
        for k, (upward, base) in enumerate(((True, 0), (False, count)))
    ]
    steps = sums[0].steps()
    stops = [0, steps // 4, steps // 2, steps * 3 // 4, steps]
    work = [big[0].relay, big[1].relay, big[0].finish_relay, lambda: None]
    for begin, end, job in zip(stops[:-1], stops[1:], work):

        @pl.loop(begin, end)
        def _(now):
            for part in sums:
                part.step(now)

        job()
    big[2].relay()
    big[1].finish_relay()
    attn_sum[...] = total[...]
    big[2].finish_relay()
    for part in sums:
        part.finish()
    for part in big:
        part.finish()
    for copy in in_out:
        copy.wait()
    for flip in range(1, 8):
        small_copy(flip).wait_send()
    for flip in range(1, places):
        pair_copy(flip).wait_send()


def attend(chain, places, x, small, in_weight, out_weight, gate_weight, up_weight, down_weight, inverse):
    tokens, width = x.shape
    count = 8
    wide = in_weight.shape[1]
    heads_wide = wide - 128
    bf16, f32 = jnp.bfloat16, jnp.float32
    row = places * tokens
    each = width // (2 * count)
    anywhere, vmem = pl.BlockSpec(memory_space=pl.ANY), pl.BlockSpec(memory_space=pltpu.VMEM)
    shape = jax.ShapeDtypeStruct
    chunks = (2 * count, tokens, each)
    return pl.pallas_call(
        functools.partial(attend_kernel, chain, places),
        out_shape=[
            shape((gate_weight.shape[0] * 8, gate_weight.shape[1]), bf16),
            shape((up_weight.shape[0] * 8, up_weight.shape[1]), bf16),
            shape((down_weight.shape[0], down_weight.shape[1] * 8), bf16),
            shape((in_weight.shape[0] * 8, wide), bf16),
            shape((out_weight.shape[0], out_weight.shape[1] * 8), bf16),
            shape(chunks, bf16),
            shape((tokens, width), bf16),
            shape((tokens, heads_wide), bf16),
            shape((row, 128), bf16),
            shape((tokens, heads_wide), f32),
            shape((tokens, 128), f32),
            shape((tokens, 128), f32),
            shape((tokens, 128), f32),
            shape((8,) + small.shape, f32),
        ],
        in_specs=[vmem, vmem] + [anywhere] * 5 + [vmem],
        out_specs=[anywhere] * 5 + [vmem] * 8 + [vmem],
        scratch_shapes=[
            pltpu.VMEM((in_weight.shape[0] * 8, wide), bf16),
            pltpu.VMEM((out_weight.shape[0], out_weight.shape[1] * 8), bf16),
            pltpu.VMEM((8, width), f32),
            pltpu.VMEM((2, row, 128), bf16),
            pltpu.VMEM((2, row, 128), bf16),
            pltpu.VMEM((row, 128), f32),
            pltpu.VMEM((places, tokens, tokens), f32),
            pltpu.VMEM((tokens, 128), f32),
            pltpu.VMEM((tokens, 128), f32),
            pltpu.VMEM((places, tokens, 128), bf16),
            pltpu.VMEM(chunks, bf16),
            pltpu.VMEM(chunks, bf16),
            pltpu.VMEM(chunks, bf16),
            pltpu.SemaphoreType.DMA((2, 7)),
            pltpu.SemaphoreType.DMA((2, 5, Gather.COPIES)),
            pltpu.SemaphoreType.DMA((7,)),
            pltpu.SemaphoreType.DMA((2, places)),
            pltpu.SemaphoreType.DMA((2, 4, count)),
        ],
        compiler_params=pltpu.CompilerParams(
            collective_id=0, has_side_effects=True, vmem_limit_bytes=VMEM_BYTES
        ),
        name="attend_forward",
    )(x, small, in_weight, out_weight, gate_weight, up_weight, down_weight, inverse)


class Scatter:
    COPIES = 10

    def __init__(self, grad, axis, own, sib, near, sems, local):
        self.grad, self.axis, self.own, self.sib, self.near = grad, axis, own, sib, near
        self.sems, self.local = sems, local
        self.me = lax.axis_index("tokens")

    def sib_copy(self, k):
        index = jnp.bitwise_xor(self.me, 2 * k + 1)
        return remote(
            block_of(self.grad, self.axis, index),
            self.sib.at[k],
            self.sems.at[0, k],
            self.sems.at[1, k],
            token_device(1),
        )

    def own_copy(self, k):
        index = jnp.bitwise_xor(self.me, 2 * k)
        return pltpu.make_async_copy(
            block_of(self.grad, self.axis, index), self.own.at[k], self.local.at[k]
        )

    def half(self, ref, k, half):
        rows = ref.shape[1] // 2
        return ref.at[k, pl.ds(half * rows, rows)]

    def chip_copy(self, slot):
        k, half, flip = ((1, 0, 2), (3, 0, 2), (2, 1, 4), (3, 1, 4), (2, 0, 4), (1, 1, 2))[slot]
        return remote(
            self.half(self.own, k, half),
            self.near.at[slot],
            self.sems.at[0, 4 + slot],
            self.sems.at[1, 4 + slot],
            token_device(flip),
        )

    def start(self):
        for k in (3, 1, 2, 0):
            self.sib_copy(k).start()
            self.own_copy(k).start()

    def cores(self):
        for k in (3, 1, 2, 0):
            self.sib_copy(k).wait_recv()
            self.own_copy(k).wait()
            self.own[k] = (
                self.own[k].astype(jnp.float32) + self.sib[k].astype(jnp.float32)
            ).astype(self.own.dtype)
            for slot in {3: (1, 3), 1: (0,), 2: (2,), 0: ()}[k]:
                self.chip_copy(slot).start()

    def add_near(self, k, half, slot):
        rows = self.own.shape[1] // 2
        place = pl.ds(half * rows, rows)
        self.own[k, place] = (
            self.own[k, place].astype(jnp.float32) + self.near[slot].astype(jnp.float32)
        ).astype(self.own.dtype)

    def second(self):
        self.chip_copy(1).wait_recv()
        self.add_near(2, 0, 1)
        self.chip_copy(4).start()
        self.chip_copy(3).wait_recv()
        self.add_near(1, 1, 3)
        self.chip_copy(5).start()

    def finish(self, out):
        rows = self.own.shape[1] // 2
        for half, slots in ((0, (0, 4)), (1, (2, 5))):
            place = pl.ds(half * rows, rows)
            total = self.own[0, place].astype(jnp.float32)
            for slot in slots:
                self.chip_copy(slot).wait_recv()
                total = total + self.near[slot].astype(jnp.float32)
            out[place, :] = total
        for k in range(4):
            self.sib_copy(k).wait_send()
        for slot in range(6):
            self.chip_copy(slot).wait_send()


def scatter_kernel(axes, *refs):
    count = len(axes)
    grads, outs = refs[:count], refs[count : 2 * count]
    owns = refs[2 * count : 3 * count]
    sibs = refs[3 * count : 4 * count]
    nears = refs[4 * count : 5 * count]
    sems, local = refs[5 * count :]
    greet_cube()
    parts = [
        Scatter(grads[i], axes[i], owns[i], sibs[i], nears[i], sems.at[i], local.at[i])
        for i in range(count)
    ]
    for i in range(count + 2):
        if i < count:
            parts[i].start()
        if 0 <= i - 1 < count:
            parts[i - 1].cores()
        if 0 <= i - 2 < count:
            parts[i - 2].second()
    for part, out in zip(parts, outs):
        part.finish(out)


def scatter_sums(arrays, axes, collective_id):
    count = len(arrays)
    blocks = [
        tuple(size // 8 if d == axis else size for d, size in enumerate(array.shape))
        for array, axis in zip(arrays, axes)
    ]
    return pl.pallas_call(
        functools.partial(scatter_kernel, axes),
        out_shape=[jax.ShapeDtypeStruct(s, jnp.float32) for s in blocks],
        in_specs=[pl.BlockSpec(memory_space=pl.ANY)] * count,
        out_specs=[pl.BlockSpec(memory_space=pltpu.VMEM)] * count,
        scratch_shapes=[pltpu.VMEM((4,) + s, a.dtype) for s, a in zip(blocks, arrays)]
        + [pltpu.VMEM((4,) + s, a.dtype) for s, a in zip(blocks, arrays)]
        + [pltpu.VMEM((6, s[0] // 2, s[1]), a.dtype) for s, a in zip(blocks, arrays)]
        + [
            pltpu.SemaphoreType.DMA((count, 2, Scatter.COPIES)),
            pltpu.SemaphoreType.DMA((count, 4)),
        ],
        compiler_params=pltpu.CompilerParams(
            collective_id=collective_id, has_side_effects=True, vmem_limit_bytes=VMEM_BYTES
        ),
        name="scatter_sums",
    )(*arrays)


def shards_cube(
    chain,
    inputs,
    segments,
    pre_gain,
    mid_gain,
    query_weight,
    key_weight,
    value_weight,
    out_weight,
    gate_weight,
    up_weight,
    down_weight,
    cotangent,
):
    row_count = inputs.shape[0]
    head_size = key_weight.shape[1]
    query_width = query_weight.shape[1]
    heads_here = query_width // head_size
    places = ROW // row_count
    small = jnp.stack(
        [
            segments.astype(jnp.float32),
            jnp.concatenate([pre_gain, mid_gain]).astype(jnp.float32),
        ]
    )
    small = jnp.concatenate([small, jnp.zeros((6, row_count), jnp.float32)])
    in_weight = jnp.concatenate([query_weight, key_weight, value_weight], axis=1)
    half_size = head_size // 2
    inverse = 10000.0 ** (-jnp.arange(half_size, dtype=jnp.float32) / half_size)
    inverse = jnp.broadcast_to(jnp.tile(inverse, 128 // half_size)[None], (8, 128))
    (
        gate_full,
        up_full,
        down_full,
        in_full,
        out_full,
        attn_sum,
        normed,
        query_rot,
        pairs,
        attended,
        log_total,
        cos_wide,
        sin_wide,
        small_full,
    ) = attend(
        chain, places, inputs, small, in_weight, out_weight, gate_weight, up_weight, down_weight, inverse
    )
    query_full = in_full[:, :query_width]
    key_full = in_full[:, query_width : query_width + head_size]
    value_full = in_full[:, query_width + head_size :]
    all_ids = small_full[:, 0].reshape(-1).astype(jnp.int32)
    pre_row = small_full[:, 1, : row_count // 2].reshape(-1)
    mid_row = small_full[:, 1, row_count // 2 :].reshape(-1)
    myself = lax.axis_index("tokens")
    own_first = myself * row_count
    own_places = own_first + jnp.arange(row_count, dtype=jnp.int32)
    row_start = own_first // ROW * ROW
    length = all_ids.shape[0]
    span = math.gcd(ROW, 1024)
    block_first = row_start // span
    block_total = (own_first + row_count + span - 1) // span
    key_all = lax.dynamic_update_slice_in_dim(
        jnp.zeros((length, head_size), jnp.bfloat16), pairs[:, :head_size], row_start, 0
    )
    value_all = lax.dynamic_update_slice_in_dim(
        jnp.zeros((length, head_size), jnp.bfloat16), pairs[:, head_size:], row_start, 0
    )
    cos_table = cos_wide[:, None, :half_size]
    sin_table = sin_wide[:, None, half_size : 2 * half_size]
    inputs_f = inputs.astype(jnp.float32)
    pre_scale = rms_scale(inputs_f)
    attended_low = attended.astype(jnp.bfloat16)
    attended = attended.reshape(row_count, heads_here, head_size)
    query_rot = query_rot.reshape(row_count, heads_here, head_size)
    log_total = log_total[:, :heads_here]

    def key_block(block_index):
        opening_row = block_index * span
        block_keys = lax.dynamic_slice_in_dim(key_all, opening_row, span)
        block_values = lax.dynamic_slice_in_dim(value_all, opening_row, span)
        block_ids = lax.dynamic_slice_in_dim(all_ids, opening_row, span)
        block_places = opening_row + jnp.arange(span, dtype=jnp.int32)
        allowed = (segments[:, None] == block_ids[None, :]) & (
            own_places[:, None] >= block_places[None, :]
        )
        scores = jnp.einsum(
            "qhd,kd->qhk", query_rot, block_keys, preferred_element_type=jnp.float32
        )
        return (opening_row, block_keys, block_values, allowed[:, None, :], scores)

    attn_term = attn_sum.transpose(1, 0, 2).reshape(row_count, -1)
    middle = inputs_f + attn_term.astype(jnp.float32)
    mid_scale = rms_scale(middle)
    normed_mid = (middle * mid_scale * mid_row).astype(jnp.bfloat16)
    gate_rows = jnp.dot(normed_mid, gate_full, preferred_element_type=jnp.float32)
    up_rows = jnp.dot(normed_mid, up_full, preferred_element_type=jnp.float32)
    sigmoid_rows = jax.nn.sigmoid(gate_rows)
    silu_rows = gate_rows * sigmoid_rows
    hidden = (silu_rows * up_rows).astype(jnp.bfloat16)
    mlp_term = jnp.dot(hidden, down_full, preferred_element_type=jnp.float32)
    layer_out = (
        middle + chain_sum(mlp_term.astype(jnp.bfloat16), chain, 2).astype(jnp.float32)
    ).astype(jnp.bfloat16)
    grad_down = jnp.einsum("tf,td->fd", hidden, cotangent, preferred_element_type=jnp.float32)
    back_hidden = jnp.einsum("td,fd->tf", cotangent, down_full, preferred_element_type=jnp.float32)
    back_gate = (
        back_hidden * up_rows * sigmoid_rows * (1.0 + gate_rows * (1.0 - sigmoid_rows))
    ).astype(jnp.bfloat16)
    back_up = (back_hidden * silu_rows).astype(jnp.bfloat16)
    grad_gate = jnp.einsum("tc,tf->cf", normed_mid, back_gate, preferred_element_type=jnp.float32)
    grad_up = jnp.einsum("tc,tf->cf", normed_mid, back_up, preferred_element_type=jnp.float32)
    mid_term = jnp.einsum(
        "tf,cf->tc", back_gate, gate_full, preferred_element_type=jnp.float32
    ) + jnp.einsum("tf,cf->tc", back_up, up_full, preferred_element_type=jnp.float32)
    back_normed_mid = chain_sum(mid_term.astype(jnp.bfloat16), chain, 3).astype(jnp.float32)
    back_middle, grad_mid = norm_back(back_normed_mid, middle, mid_scale, mid_row)
    back_middle = back_middle + cotangent.astype(jnp.float32)
    back_attn = back_middle.astype(jnp.bfloat16)
    grad_out = jnp.einsum("tc,td->cd", attended_low, back_attn, preferred_element_type=jnp.float32)
    back_attended = (
        jnp.einsum("td,cd->tc", back_attn, out_full, preferred_element_type=jnp.float32)
        .astype(jnp.bfloat16)
        .reshape(row_count, heads_here, head_size)
    )
    row_delta = jnp.sum(back_attended.astype(jnp.float32) * attended, axis=-1)

    def backward_step(block_index, state_now):
        back_rows, back_pairs = state_now
        opening_row, block_keys, block_values, allowed, scores = key_block(block_index)
        chances = jnp.where(allowed, jnp.exp(scores - log_total[..., None]), 0.0)
        back_values = jnp.einsum(
            "qhk,qhd->kd",
            chances.astype(jnp.bfloat16),
            back_attended,
            preferred_element_type=jnp.float32,
        )
        back_chances = jnp.einsum(
            "qhd,kd->qhk", back_attended, block_values, preferred_element_type=jnp.float32
        )
        back_scores = (chances * (back_chances - row_delta[..., None])).astype(jnp.bfloat16)
        back_rows = back_rows + jnp.einsum(
            "qhk,kd->qhd", back_scores, block_keys, preferred_element_type=jnp.float32
        )
        back_keys = jnp.einsum(
            "qhk,qhd->kd", back_scores, query_rot, preferred_element_type=jnp.float32
        )
        old_piece = lax.dynamic_slice_in_dim(back_pairs, opening_row, span)
        fresh_piece = old_piece + jnp.concatenate([back_keys, back_values], axis=-1)
        back_pairs = lax.dynamic_update_slice_in_dim(back_pairs, fresh_piece, opening_row, 0)
        return (back_rows, back_pairs)

    start_back = (
        jnp.zeros((row_count, heads_here, head_size), jnp.float32),
        jnp.zeros((length, 2 * head_size), jnp.float32),
    )
    back_rows, back_pairs = lax.fori_loop(block_first, block_total, backward_step, start_back)
    own_pairs = lax.psum_scatter(
        back_pairs.astype(jnp.bfloat16), "tokens", scatter_dimension=0, tiled=True
    ).astype(jnp.float32)
    back_query = (
        (unrotate(back_rows, cos_table, sin_table) * head_size ** (-0.5))
        .astype(jnp.bfloat16)
        .reshape(row_count, heads_here * head_size)
    )
    back_key = unrotate(own_pairs[:, None, :head_size], cos_table, sin_table)[:, 0, :].astype(
        jnp.bfloat16
    )
    back_value = own_pairs[:, head_size:].astype(jnp.bfloat16)
    grad_query = jnp.einsum("tc,tq->cq", normed, back_query, preferred_element_type=jnp.float32)
    grad_key = jnp.einsum("tc,tq->cq", normed, back_key, preferred_element_type=jnp.float32)
    grad_value = jnp.einsum("tc,tq->cq", normed, back_value, preferred_element_type=jnp.float32)
    pre_term = jnp.einsum("tq,cq->tc", back_query, query_full, preferred_element_type=jnp.float32)
    pre_term = pre_term + jnp.einsum(
        "tq,cq->tc", back_key, key_full, preferred_element_type=jnp.float32
    )
    pre_term = pre_term + jnp.einsum(
        "tq,cq->tc", back_value, value_full, preferred_element_type=jnp.float32
    )
    back_normed = chain_sum(pre_term.astype(jnp.bfloat16), chain, 4).astype(jnp.float32)
    back_inputs, grad_pre = norm_back(back_normed, inputs_f, pre_scale, pre_row)
    grad_input = (back_middle + back_inputs).astype(jnp.bfloat16)
    grad_in = jnp.concatenate([grad_query, grad_key, grad_value], axis=1).astype(jnp.bfloat16)
    grad_gate, grad_up, grad_down, grad_in, grad_out = scatter_sums(
        (
            grad_gate.astype(jnp.bfloat16),
            grad_up.astype(jnp.bfloat16),
            grad_down.astype(jnp.bfloat16),
            grad_in,
            grad_out.astype(jnp.bfloat16),
        ),
        (0, 0, 1, 0, 1),
        5,
    )
    grad_query = grad_in[:, :query_width]
    grad_key = grad_in[:, query_width : query_width + head_size]
    grad_value = grad_in[:, query_width + head_size :]
    grad_pre, grad_mid = (
        lax.psum_scatter(part.astype(jnp.bfloat16), "tokens", scatter_dimension=0, tiled=True).astype(jnp.float32)
        for part in (grad_pre, grad_mid)
    )
    return (
        layer_out,
        grad_input,
        grad_pre,
        grad_mid,
        grad_query,
        grad_key,
        grad_value,
        grad_out,
        grad_gate,
        grad_up,
        grad_down,
    )


def solution(mesh):
    sizes = dict(mesh.shape)
    plan = shards_any
    if sizes["tokens"] == 8:
        plan = functools.partial(shards_cube, sizes["heads"])
    return jax.shard_map(
        plan,
        mesh=mesh,
        in_specs=(
            P("tokens", None),
            P("tokens"),
            P("tokens"),
            P("tokens"),
            P("tokens", "heads"),
            P("tokens", "heads"),
            P("tokens", "heads"),
            P("heads", "tokens"),
            P("tokens", "heads"),
            P("tokens", "heads"),
            P("heads", "tokens"),
            P("tokens", None),
        ),
        out_specs=(
            P("tokens", None),
            P("tokens", None),
            P("tokens"),
            P("tokens"),
            P("tokens", "heads"),
            P("tokens", "heads"),
            P("tokens", "heads"),
            P("heads", "tokens"),
            P("tokens", "heads"),
            P("tokens", "heads"),
            P("heads", "tokens"),
        ),
        check_vma=False,
    )
```

```python
import functools
import math

import jax
import jax.numpy as jnp
from jax import lax
from jax.experimental import pallas as pl
from jax.experimental.pallas import tpu as pltpu
from jax.sharding import PartitionSpec as P

ROW = 2048


def rms_scale(vectors):
    return lax.rsqrt(jnp.mean(vectors * vectors, axis=-1, keepdims=True) + 1e-05)


def rotate(vectors, cos_table, sin_table):
    middle_index = vectors.shape[-1] // 2
    former = vectors[..., :middle_index]
    latter = vectors[..., middle_index:]
    return jnp.concatenate(
        [former * cos_table - latter * sin_table, latter * cos_table + former * sin_table], axis=-1
    )


def unrotate(gradient, cos_table, sin_table):
    middle_index = gradient.shape[-1] // 2
    former = gradient[..., :middle_index]
    latter = gradient[..., middle_index:]
    return jnp.concatenate(
        [former * cos_table + latter * sin_table, latter * cos_table - former * sin_table], axis=-1
    )


def norm_back(gradient, vectors, scale_rows, gain_row):
    shaped = vectors * scale_rows
    weighted = gradient * gain_row
    back_vectors = scale_rows * (
        weighted - shaped * jnp.mean(weighted * shaped, axis=-1, keepdims=True)
    )
    return (back_vectors, jnp.sum(gradient * shaped, axis=0))


def shards_any(
    inputs,
    segments,
    pre_gain,
    mid_gain,
    query_weight,
    key_weight,
    value_weight,
    out_weight,
    gate_weight,
    up_weight,
    down_weight,
    cotangent,
):
    row_count = inputs.shape[0]
    head_size = key_weight.shape[1]
    heads_here = query_weight.shape[1] // head_size
    myself = lax.axis_index("tokens")
    gathered = (
        lax.all_gather(pre_gain, "tokens", axis=0, tiled=True),
        lax.all_gather(mid_gain, "tokens", axis=0, tiled=True),
        lax.all_gather(query_weight, "tokens", axis=0, tiled=True),
        lax.all_gather(key_weight, "tokens", axis=0, tiled=True),
        lax.all_gather(value_weight, "tokens", axis=0, tiled=True),
        lax.all_gather(out_weight, "tokens", axis=1, tiled=True),
        lax.all_gather(gate_weight, "tokens", axis=0, tiled=True),
        lax.all_gather(up_weight, "tokens", axis=0, tiled=True),
        lax.all_gather(down_weight, "tokens", axis=1, tiled=True),
    )
    (
        pre_full,
        mid_full,
        query_full,
        key_full,
        value_full,
        out_full,
        gate_full,
        up_full,
        down_full,
    ) = gathered
    pre_row = pre_full.astype(jnp.float32)
    mid_row = mid_full.astype(jnp.float32)
    all_ids = lax.all_gather(segments, "tokens", axis=0, tiled=True)
    length = all_ids.shape[0]
    places = jnp.arange(length, dtype=jnp.int32)
    starts_here = jnp.concatenate([jnp.ones((1,), dtype=jnp.bool_), all_ids[1:] != all_ids[:-1]])
    opening = lax.cummax(jnp.where(starts_here, places, 0), axis=0)
    own_first = myself * row_count
    positions = lax.dynamic_slice_in_dim(places - opening, own_first, row_count)
    own_places = own_first + jnp.arange(row_count, dtype=jnp.int32)
    half_size = head_size // 2
    inverse = 10000.0 ** (-jnp.arange(half_size, dtype=jnp.float32) / half_size)
    turned = positions.astype(jnp.float32)[:, None] * inverse[None, :]
    cos_table = jnp.cos(turned)[:, None, :]
    sin_table = jnp.sin(turned)[:, None, :]
    inputs_f = inputs.astype(jnp.float32)
    pre_scale = rms_scale(inputs_f)
    normed = (inputs_f * pre_scale * pre_row).astype(jnp.bfloat16)
    queries = jnp.dot(normed, query_full, preferred_element_type=jnp.float32).reshape(
        row_count, heads_here, head_size
    )
    query_rot = (rotate(queries, cos_table, sin_table) * head_size ** (-0.5)).astype(jnp.bfloat16)
    key_rows = jnp.dot(normed, key_full, preferred_element_type=jnp.float32)[:, None, :]
    key_rot = rotate(key_rows, cos_table, sin_table)[:, 0, :].astype(jnp.bfloat16)
    value_low = jnp.dot(normed, value_full, preferred_element_type=jnp.float32).astype(jnp.bfloat16)
    key_all, value_all = (
        lax.all_gather(key_rot, "tokens", axis=0, tiled=True),
        lax.all_gather(value_low, "tokens", axis=0, tiled=True),
    )
    span = math.gcd(ROW, 1024)
    row_start = own_first // ROW * ROW
    block_first = row_start // span
    block_total = (own_first + row_count + span - 1) // span

    def key_block(block_index):
        opening_row = block_index * span
        block_keys = lax.dynamic_slice_in_dim(key_all, opening_row, span)
        block_values = lax.dynamic_slice_in_dim(value_all, opening_row, span)
        block_ids = lax.dynamic_slice_in_dim(all_ids, opening_row, span)
        block_places = opening_row + jnp.arange(span, dtype=jnp.int32)
        allowed = (segments[:, None] == block_ids[None, :]) & (
            own_places[:, None] >= block_places[None, :]
        )
        scores = jnp.einsum(
            "qhd,kd->qhk", query_rot, block_keys, preferred_element_type=jnp.float32
        )
        return (opening_row, block_keys, block_values, allowed[:, None, :], scores)

    def forward_step(block_index, state_now):
        row_peak, row_total, running = state_now
        opening_row, block_keys, block_values, allowed, scores = key_block(block_index)
        new_peak = jnp.maximum(row_peak, jnp.max(jnp.where(allowed, scores, -1e30), axis=-1))
        factor = jnp.exp(row_peak - new_peak)
        weights = jnp.where(allowed, jnp.exp(scores - new_peak[..., None]), 0.0)
        row_total = row_total * factor + jnp.sum(weights, axis=-1)
        running = running * factor[..., None] + jnp.einsum(
            "qhk,kd->qhd",
            weights.astype(jnp.bfloat16),
            block_values,
            preferred_element_type=jnp.float32,
        )
        return (new_peak, row_total, running)

    start_state = (
        jnp.full((row_count, heads_here), -1e30, jnp.float32),
        jnp.zeros((row_count, heads_here), jnp.float32),
        jnp.zeros((row_count, heads_here, head_size), jnp.float32),
    )
    row_peak, row_total, running = lax.fori_loop(
        block_first, block_total, forward_step, start_state
    )
    attended = running / row_total[..., None]
    log_total = row_peak + jnp.log(row_total)
    attended_low = attended.astype(jnp.bfloat16).reshape(row_count, heads_here * head_size)
    attn_term = jnp.dot(attended_low, out_full, preferred_element_type=jnp.float32)
    middle = inputs_f + lax.psum(attn_term.astype(jnp.bfloat16), "heads").astype(jnp.float32)
    mid_scale = rms_scale(middle)
    normed_mid = (middle * mid_scale * mid_row).astype(jnp.bfloat16)
    gate_rows = jnp.dot(normed_mid, gate_full, preferred_element_type=jnp.float32)
    up_rows = jnp.dot(normed_mid, up_full, preferred_element_type=jnp.float32)
    sigmoid_rows = jax.nn.sigmoid(gate_rows)
    silu_rows = gate_rows * sigmoid_rows
    hidden = (silu_rows * up_rows).astype(jnp.bfloat16)
    mlp_term = jnp.dot(hidden, down_full, preferred_element_type=jnp.float32)
    layer_out = (
        middle + lax.psum(mlp_term.astype(jnp.bfloat16), "heads").astype(jnp.float32)
    ).astype(jnp.bfloat16)
    grad_down = jnp.einsum("tf,td->fd", hidden, cotangent, preferred_element_type=jnp.float32)
    back_hidden = jnp.einsum("td,fd->tf", cotangent, down_full, preferred_element_type=jnp.float32)
    back_gate = (
        back_hidden * up_rows * sigmoid_rows * (1.0 + gate_rows * (1.0 - sigmoid_rows))
    ).astype(jnp.bfloat16)
    back_up = (back_hidden * silu_rows).astype(jnp.bfloat16)
    grad_gate = jnp.einsum("tc,tf->cf", normed_mid, back_gate, preferred_element_type=jnp.float32)
    grad_up = jnp.einsum("tc,tf->cf", normed_mid, back_up, preferred_element_type=jnp.float32)
    mid_term = jnp.einsum(
        "tf,cf->tc", back_gate, gate_full, preferred_element_type=jnp.float32
    ) + jnp.einsum("tf,cf->tc", back_up, up_full, preferred_element_type=jnp.float32)
    back_normed_mid = lax.psum(mid_term.astype(jnp.bfloat16), "heads").astype(jnp.float32)
    back_middle, grad_mid = norm_back(back_normed_mid, middle, mid_scale, mid_row)
    back_middle = back_middle + cotangent.astype(jnp.float32)
    back_attn = back_middle.astype(jnp.bfloat16)
    grad_out = jnp.einsum("tc,td->cd", attended_low, back_attn, preferred_element_type=jnp.float32)
    back_attended = (
        jnp.einsum("td,cd->tc", back_attn, out_full, preferred_element_type=jnp.float32)
        .astype(jnp.bfloat16)
        .reshape(row_count, heads_here, head_size)
    )
    row_delta = jnp.sum(back_attended.astype(jnp.float32) * attended, axis=-1)

    def backward_step(block_index, state_now):
        back_rows, back_pairs = state_now
        opening_row, block_keys, block_values, allowed, scores = key_block(block_index)
        chances = jnp.where(allowed, jnp.exp(scores - log_total[..., None]), 0.0)
        back_values = jnp.einsum(
            "qhk,qhd->kd",
            chances.astype(jnp.bfloat16),
            back_attended,
            preferred_element_type=jnp.float32,
        )
        back_chances = jnp.einsum(
            "qhd,kd->qhk", back_attended, block_values, preferred_element_type=jnp.float32
        )
        back_scores = (chances * (back_chances - row_delta[..., None])).astype(jnp.bfloat16)
        back_rows = back_rows + jnp.einsum(
            "qhk,kd->qhd", back_scores, block_keys, preferred_element_type=jnp.float32
        )
        back_keys = jnp.einsum(
            "qhk,qhd->kd", back_scores, query_rot, preferred_element_type=jnp.float32
        )
        old_piece = lax.dynamic_slice_in_dim(back_pairs, opening_row, span)
        fresh_piece = old_piece + jnp.concatenate([back_keys, back_values], axis=-1)
        back_pairs = lax.dynamic_update_slice_in_dim(back_pairs, fresh_piece, opening_row, 0)
        return (back_rows, back_pairs)

    start_back = (
        jnp.zeros((row_count, heads_here, head_size), jnp.float32),
        jnp.zeros((length, 2 * head_size), jnp.float32),
    )
    back_rows, back_pairs = lax.fori_loop(block_first, block_total, backward_step, start_back)
    own_pairs = lax.psum_scatter(
        back_pairs.astype(jnp.bfloat16), "tokens", scatter_dimension=0, tiled=True
    ).astype(jnp.float32)
    back_query = (
        (unrotate(back_rows, cos_table, sin_table) * head_size ** (-0.5))
        .astype(jnp.bfloat16)
        .reshape(row_count, heads_here * head_size)
    )
    back_key = unrotate(own_pairs[:, None, :head_size], cos_table, sin_table)[:, 0, :].astype(
        jnp.bfloat16
    )
    back_value = own_pairs[:, head_size:].astype(jnp.bfloat16)
    grad_query = jnp.einsum("tc,tq->cq", normed, back_query, preferred_element_type=jnp.float32)
    grad_key = jnp.einsum("tc,tq->cq", normed, back_key, preferred_element_type=jnp.float32)
    grad_value = jnp.einsum("tc,tq->cq", normed, back_value, preferred_element_type=jnp.float32)
    pre_term = jnp.einsum("tq,cq->tc", back_query, query_full, preferred_element_type=jnp.float32)
    pre_term = pre_term + jnp.einsum(
        "tq,cq->tc", back_key, key_full, preferred_element_type=jnp.float32
    )
    pre_term = pre_term + jnp.einsum(
        "tq,cq->tc", back_value, value_full, preferred_element_type=jnp.float32
    )
    back_normed = lax.psum(pre_term.astype(jnp.bfloat16), "heads").astype(jnp.float32)
    back_inputs, grad_pre = norm_back(back_normed, inputs_f, pre_scale, pre_row)
    grad_input = (back_middle + back_inputs).astype(jnp.bfloat16)
    summed = (
        lax.psum_scatter(
            grad_pre.astype(jnp.bfloat16), "tokens", scatter_dimension=0, tiled=True
        ).astype(jnp.float32),
        lax.psum_scatter(
            grad_mid.astype(jnp.bfloat16), "tokens", scatter_dimension=0, tiled=True
        ).astype(jnp.float32),
        lax.psum_scatter(
            grad_query.astype(jnp.bfloat16), "tokens", scatter_dimension=0, tiled=True
        ).astype(jnp.float32),
        lax.psum_scatter(
            grad_key.astype(jnp.bfloat16), "tokens", scatter_dimension=0, tiled=True
        ).astype(jnp.float32),
        lax.psum_scatter(
            grad_value.astype(jnp.bfloat16), "tokens", scatter_dimension=0, tiled=True
        ).astype(jnp.float32),
        lax.psum_scatter(
            grad_out.astype(jnp.bfloat16), "tokens", scatter_dimension=1, tiled=True
        ).astype(jnp.float32),
        lax.psum_scatter(
            grad_gate.astype(jnp.bfloat16), "tokens", scatter_dimension=0, tiled=True
        ).astype(jnp.float32),
        lax.psum_scatter(
            grad_up.astype(jnp.bfloat16), "tokens", scatter_dimension=0, tiled=True
        ).astype(jnp.float32),
        lax.psum_scatter(
            grad_down.astype(jnp.bfloat16), "tokens", scatter_dimension=1, tiled=True
        ).astype(jnp.float32),
    )
    (
        grad_pre,
        grad_mid,
        grad_query,
        grad_key,
        grad_value,
        grad_out,
        grad_gate,
        grad_up,
        grad_down,
    ) = summed
    return (
        layer_out,
        grad_input,
        grad_pre,
        grad_mid,
        grad_query,
        grad_key,
        grad_value,
        grad_out,
        grad_gate,
        grad_up,
        grad_down,
    )


MESH_ID = pl.DeviceIdType.MESH
VMEM_BYTES = 63 * 2**20


def token_device(flip):
    return (jnp.bitwise_xor(lax.axis_index("tokens"), flip), lax.axis_index("heads"))


def remote(src, dst, send, recv, device):
    return pltpu.make_async_remote_copy(
        src_ref=src, dst_ref=dst, send_sem=send, recv_sem=recv, device_id=device, device_id_type=MESH_ID
    )


def block_of(ref, axis, index, half=None):
    size = ref.shape[axis] // 8
    start = pl.multiple_of(index * size, size)
    if axis == 0:
        if half is None:
            return ref.at[pl.ds(start, size), :]
        return ref.at[pl.ds(pl.multiple_of(start + half * (size // 2), size // 2), size // 2), :]
    if half is None:
        return ref.at[:, pl.ds(start, size)]
    rows = ref.shape[0] // 2
    return ref.at[pl.ds(half * rows, rows), pl.ds(start, size)]


class Gather:
    COPIES = 9

    def __init__(self, shard, full, axis, send, recv, local):
        self.shard, self.full, self.axis = shard, full, axis
        self.send, self.recv, self.local = send, recv, local
        self.me = lax.axis_index("tokens")

    def copy(self, slot, flip_block, flip_target, half=None):
        index = jnp.bitwise_xor(self.me, flip_block)
        src = self.shard if flip_block == 0 else block_of(self.full, self.axis, index, half)
        return remote(
            src,
            block_of(self.full, self.axis, index, half),
            self.send.at[slot],
            self.recv.at[slot],
            token_device(flip_target),
        )

    def copies(self, slot):
        return self.copy(
            slot,
            *(
                (0, 2),
                (0, 4),
                (0, 1),
                (2, 4, 0),
                (4, 2, 1),
                (2, 1),
                (4, 1),
                (6, 1, 0),
                (6, 1, 1),
            )[slot],
        )

    def own_copy(self):
        return pltpu.make_async_copy(
            self.shard, block_of(self.full, self.axis, self.me), self.local
        )

    def start(self):
        for slot in (0, 1, 2):
            self.copies(slot).start()
        self.own_copy().start()

    def relay(self):
        self.copies(0).wait_recv()
        self.copies(3).start()
        self.copies(1).wait_recv()
        self.copies(4).start()
        self.copies(5).start()
        self.copies(6).start()

    def finish_relay(self):
        self.copies(3).wait_recv()
        self.copies(7).start()
        self.copies(4).wait_recv()
        self.copies(8).start()

    def finish(self):
        for slot in (2, 5, 6, 7, 8):
            self.copies(slot).wait_recv()
        for slot in range(self.COPIES):
            self.copies(slot).wait_send()
        self.own_copy().wait()


class ChainSum:
    def __init__(self, chain, upward, term, passing, total, base, count, sems):
        self.chain, self.term, self.passing, self.total = chain, term, passing, total
        self.base, self.count = base, count
        here = lax.axis_index("heads")
        self.rank = here if upward else chain - 1 - here
        move = 1 if upward else -1
        tokens = lax.axis_index("tokens")
        self.ahead = (tokens, jnp.clip(here + move, 0, chain - 1))
        self.behind = (tokens, jnp.clip(here - move, 0, chain - 1))
        self.sems = sems
        self.first = self.rank == 0
        self.last = self.rank == chain - 1

    def out_copy(self, i, first):
        src = self.term if first else self.passing
        at = self.base + i
        return remote(
            src.at[at], self.passing.at[at], self.sems.at[0, i], self.sems.at[1, i], self.ahead
        )

    def back_copy(self, i):
        at = self.base + i
        return remote(
            self.total.at[at], self.total.at[at], self.sems.at[2, i], self.sems.at[3, i], self.behind
        )

    def add(self, i):
        at = self.base + i
        return self.term[at].astype(jnp.float32) + self.passing[at].astype(jnp.float32)

    def step(self, now):
        i = now - self.rank
        valid = (i >= 0) & (i < self.count)

        @pl.when(valid & self.first)
        def _():
            self.out_copy(i, True).start()

        @pl.when(valid & jnp.logical_not(self.first))
        def _():
            self.out_copy(i, False).wait_recv()

        @pl.when(valid & jnp.logical_not(self.first | self.last))
        def _():
            self.passing[self.base + i] = self.add(i).astype(self.passing.dtype)
            self.out_copy(i, False).start()

        @pl.when(valid & self.last)
        def _():
            self.total[self.base + i] = self.add(i).astype(self.total.dtype)
            self.back_copy(i).start()

        j = now - (2 * (self.chain - 1) - self.rank)
        back = (j >= 0) & (j < self.count) & jnp.logical_not(self.last)

        @pl.when(back)
        def _():
            self.back_copy(j).wait_recv()

        @pl.when(back & jnp.logical_not(self.first))
        def _():
            self.back_copy(j).start()

    def steps(self):
        return self.count + 2 * (self.chain - 1)

    def finish(self):
        @pl.when(jnp.logical_not(self.last))
        def _():
            for i in range(self.count):
                self.out_copy(i, False).wait_send()

        @pl.when(jnp.logical_not(self.first))
        def _():
            for i in range(self.count):
                self.back_copy(i).wait_send()


def lanes(shape):
    return lax.broadcasted_iota(jnp.int32, shape, len(shape) - 1)


def turn(vectors, cos_table, sin_table):
    near = jnp.where(
        lanes(vectors.shape) % 64 < 32, pltpu.roll(vectors, 96, 1), pltpu.roll(vectors, 32, 1)
    )
    return vectors * cos_table + near * sin_table


def token_column(row):
    return jnp.broadcast_to(row, (128, row.shape[1])).T


def key_marks(column, first_id):
    lane = lanes(column.shape) % 64
    one_hot = (column - first_id).astype(jnp.int32) == lane
    return jnp.where(one_hot | ((lane >= 4) & (lane < 7)), 1.0, 0.0)


def query_marks(column, first_id):
    lane = lanes(column.shape) % 64
    other = (column - first_id).astype(jnp.int32) != lane
    return jnp.where(other & (lane < 4), -1e30, 0.0)


def nt_dot(left, right):
    return lax.dot_general(
        left, right, (((1,), (1,)), ((), ())), preferred_element_type=jnp.float32
    )


def attend_kernel(
    chain, places, x, small, in_shard, out_shard, gate_shard, up_shard, down_shard, inverse,
    gate_full, up_full, down_full, in_full, out_full, attn_sum, normed, query, pairs, attended, log_total,
    cos_table, sin_table, small_all, in_here, out_here, pre_row, key_side, value_side, marks, scores, peak,
    mixed, near_pairs, term, passing, total, small_sems, gather_sems, local_sems, pair_sems, chain_sems,
):
    count = term.shape[0] // 2
    tokens = x.shape[0]
    me = lax.axis_index("tokens")
    place = lax.rem(me, places)
    here = lax.axis_index("heads")
    barrier = pltpu.get_barrier_semaphore()
    for flip in range(1, 8):
        pl.semaphore_signal(barrier, inc=1, device_id=token_device(flip), device_id_type=MESH_ID)
    for step in (-1, 1):
        near = here + step

        @pl.when((near >= 0) & (near < chain))
        def _():
            pl.semaphore_signal(barrier, inc=1, device_id=(me, near), device_id_type=MESH_ID)

    edge = (here == 0) | (here == chain - 1)

    @pl.when(edge)
    def _():
        pl.semaphore_wait(barrier, 8)

    @pl.when(jnp.logical_not(edge))
    def _():
        pl.semaphore_wait(barrier, 9)

    def small_copy(flip):
        return remote(
            small,
            small_all.at[me],
            small_sems.at[0, flip - 1],
            small_sems.at[1, flip - 1],
            token_device(flip),
        )

    for flip in range(1, 8):
        small_copy(flip).start()

    def gather(k, shard, full, axis):
        return Gather(shard, full, axis, gather_sems.at[0, k], gather_sems.at[1, k], local_sems.at[k])

    gather_in = gather(0, in_shard, in_here, 0)
    gather_out = gather(1, out_shard, out_here, 1)
    big = [
        gather(2, gate_shard, gate_full, 0),
        gather(3, up_shard, up_full, 0),
        gather(4, down_shard, down_full, 1),
    ]
    gather_in.start()
    small_all[me] = small[...]

    x_f = x[...].astype(jnp.float32)
    pre_scale = lax.rsqrt(jnp.mean(x_f * x_f, axis=1, keepdims=True) + 1e-05)

    for flip in range(1, 8):
        small_copy(flip).wait_recv()
    width = x.shape[1] // 8
    for k in range(8):
        pre_row[:, k * width : (k + 1) * width] = jnp.broadcast_to(
            small_all[k, 1:2, :width], (8, width)
        )
    gather_in.relay()
    gather_out.start()
    normed[...] = (x[...].astype(jnp.float32) * pre_scale * pre_row[0:1, :]).astype(jnp.bfloat16)
    gather_in.finish_relay()

    first_device = me - place
    first_id = (first_device // places * 4).astype(jnp.float32)
    own = token_column(small_all[me, 0:1, :])
    before = jnp.zeros((tokens, 1), jnp.float32)
    for k in range(places):
        others = small_all[first_device + k, 0:1, :]
        before = before + jnp.sum(
            jnp.where(others < own[:, 0:1], 1.0, 0.0), axis=1, keepdims=True
        )
        column = token_column(others)
        marks[pl.ds(k * tokens, tokens), :] = key_marks(column, first_id)
    row_index = lax.broadcasted_iota(jnp.int32, (tokens, 128), 0) + place * tokens
    turned = (row_index.astype(jnp.float32) - before) * inverse[0:1, :]
    cos_table[...] = jnp.cos(turned)
    sin_signed = jnp.sin(turned)
    sin_table[...] = jnp.where(lanes(sin_signed.shape) % 64 < 32, -sin_signed, sin_signed)
    gather_out.relay()
    big[0].copies(1).start()
    gather_in.finish()

    wide = in_here.shape[1]
    heads_wide = wide - 128
    for low in range(0, wide, 256):
        high = min(low + 256, wide)
        made = jnp.dot(normed[...], in_here[:, low:high], preferred_element_type=jnp.float32)
        for group in range(low, high, 128):
            part = made[:, group - low : group - low + 128]
            spun = turn(part, cos_table[...], sin_table[...])
            if group < heads_wide:
                query[:, group : group + 128] = (spun * 0.125).astype(jnp.bfloat16)
            else:
                near_pairs[place] = jnp.where(lanes(part.shape) < 64, spun, part).astype(jnp.bfloat16)

    def pair_copy(flip):
        return remote(
            near_pairs.at[place],
            near_pairs.at[place],
            pair_sems.at[0, flip - 1],
            pair_sems.at[1, flip - 1],
            token_device(flip),
        )

    for flip in range(1, places):
        pair_copy(flip).start()
    big[0].copies(0).start()
    big[0].copies(2).start()
    big[0].own_copy().start()
    big[1].copies(1).start()
    gather_out.finish_relay()
    for flip in range(1, places):
        pair_copy(flip).wait_recv()
    big[1].copies(0).start()
    big[1].copies(2).start()
    big[1].own_copy().start()
    big[2].start()

    for k in range(places):
        pair = near_pairs[k].astype(jnp.float32)
        swapped = pltpu.roll(pair, 64, 1)
        lane = lanes(pair.shape)
        mark = marks[pl.ds(k * tokens, tokens), :]
        block = pl.ds(k * tokens, tokens)
        key_side[0, block] = jnp.where(lane < 64, pair, mark).astype(jnp.bfloat16)
        key_side[1, block] = jnp.where(lane < 64, mark, swapped).astype(jnp.bfloat16)
        value_side[0, block] = jnp.where(lane < 64, swapped, 1.0).astype(jnp.bfloat16)
        value_side[1, block] = jnp.where(lane < 64, 1.0, pair).astype(jnp.bfloat16)
        pairs[block] = near_pairs[k]

    lane = lanes((tokens, 128))
    own_marks = query_marks(own, first_id)

    @pl.loop(0, query.shape[1] // 128)
    def _(group):
        at = pl.ds(pl.multiple_of(group * 128, 128), 128)
        both = query[:, at].astype(jnp.float32)
        halves = []
        for e in range(2):
            mine = (lane < 64) if e == 0 else (lane >= 64)
            side = jnp.where(mine, both, own_marks).astype(jnp.bfloat16)

            def look(k, masked):
                found = nt_dot(side, key_side[e, pl.ds(pl.multiple_of(k * tokens, tokens), tokens)])
                if masked:
                    rows = lax.broadcasted_iota(jnp.int32, found.shape, 0)
                    found = jnp.where(lanes(found.shape) <= rows, found, -1e30)
                scores[k] = found
                best = found[:, :128]
                for part in range(128, tokens, 128):
                    best = jnp.maximum(best, found[:, part : part + 128])
                return best

            peak[...] = look(place, True)

            @pl.loop(0, place)
            def _(k):
                peak[...] = jnp.maximum(peak[...], look(k, False))

            top = jnp.max(peak[...], axis=1, keepdims=True)

            def blend(k):
                weights = jnp.exp(scores[k] - top).astype(jnp.bfloat16)
                return jnp.dot(
                    weights,
                    value_side[e, pl.ds(pl.multiple_of(k * tokens, tokens), tokens)],
                    preferred_element_type=jnp.float32,
                )

            mixed[...] = blend(place)

            @pl.loop(0, place)
            def _(k):
                mixed[...] += blend(k)

            out = mixed[...]
            rolled = pltpu.roll(out, 64, 1)
            sums = jnp.where(mine, rolled, out)
            halves.append(out / sums)
            log_total[...] = jnp.where(
                lane == 2 * group + e, top + jnp.log(sums), log_total[...]
            )
        attended[:, at] = jnp.where(lane < 64, halves[0], halves[1])

    gather_out.finish()
    low = attended[...].astype(jnp.bfloat16)
    each = term.shape[2]
    for k in range(0, 2 * count, 2):
        made = jnp.dot(
            low, out_here[:, k * each : (k + 2) * each], preferred_element_type=jnp.float32
        ).astype(jnp.bfloat16)
        term[k] = made[:, :each]
        term[k + 1] = made[:, each:]
    in_out = [
        pltpu.make_async_copy(in_here, in_full, local_sems.at[5]),
        pltpu.make_async_copy(out_here, out_full, local_sems.at[6]),
    ]
    for copy in in_out:
        copy.start()
    sums = [
        ChainSum(chain, upward, term, passing, total, base, count, chain_sems.at[k])
        for k, (upward, base) in enumerate(((True, 0), (False, count)))
    ]
    steps = sums[0].steps()
    stops = [0, steps // 4, steps // 2, steps * 3 // 4, steps]
    work = [big[0].relay, big[1].relay, big[0].finish_relay, lambda: None]
    for begin, end, job in zip(stops[:-1], stops[1:], work):

        @pl.loop(begin, end)
        def _(now):
            for part in sums:
                part.step(now)

        job()
    big[2].relay()
    big[1].finish_relay()
    attn_sum[...] = total[...]
    big[2].finish_relay()
    for part in sums:
        part.finish()
    for part in big:
        part.finish()
    for copy in in_out:
        copy.wait()
    for flip in range(1, 8):
        small_copy(flip).wait_send()
    for flip in range(1, places):
        pair_copy(flip).wait_send()


def attend(chain, places, x, small, in_weight, out_weight, gate_weight, up_weight, down_weight, inverse):
    tokens, width = x.shape
    count = 8
    wide = in_weight.shape[1]
    heads_wide = wide - 128
    bf16, f32 = jnp.bfloat16, jnp.float32
    row = places * tokens
    each = width // (2 * count)
    anywhere, vmem = pl.BlockSpec(memory_space=pl.ANY), pl.BlockSpec(memory_space=pltpu.VMEM)
    shape = jax.ShapeDtypeStruct
    chunks = (2 * count, tokens, each)
    return pl.pallas_call(
        functools.partial(attend_kernel, chain, places),
        out_shape=[
            shape((gate_weight.shape[0] * 8, gate_weight.shape[1]), bf16),
            shape((up_weight.shape[0] * 8, up_weight.shape[1]), bf16),
            shape((down_weight.shape[0], down_weight.shape[1] * 8), bf16),
            shape((in_weight.shape[0] * 8, wide), bf16),
            shape((out_weight.shape[0], out_weight.shape[1] * 8), bf16),
            shape(chunks, bf16),
            shape((tokens, width), bf16),
            shape((tokens, heads_wide), bf16),
            shape((row, 128), bf16),
            shape((tokens, heads_wide), f32),
            shape((tokens, 128), f32),
            shape((tokens, 128), f32),
            shape((tokens, 128), f32),
            shape((8,) + small.shape, f32),
        ],
        in_specs=[vmem, vmem] + [anywhere] * 5 + [vmem],
        out_specs=[anywhere] * 5 + [vmem] * 8 + [vmem],
        scratch_shapes=[
            pltpu.VMEM((in_weight.shape[0] * 8, wide), bf16),
            pltpu.VMEM((out_weight.shape[0], out_weight.shape[1] * 8), bf16),
            pltpu.VMEM((8, width), f32),
            pltpu.VMEM((2, row, 128), bf16),
            pltpu.VMEM((2, row, 128), bf16),
            pltpu.VMEM((row, 128), f32),
            pltpu.VMEM((places, tokens, tokens), f32),
            pltpu.VMEM((tokens, 128), f32),
            pltpu.VMEM((tokens, 128), f32),
            pltpu.VMEM((places, tokens, 128), bf16),
            pltpu.VMEM(chunks, bf16),
            pltpu.VMEM(chunks, bf16),
            pltpu.VMEM(chunks, bf16),
            pltpu.SemaphoreType.DMA((2, 7)),
            pltpu.SemaphoreType.DMA((2, 5, Gather.COPIES)),
            pltpu.SemaphoreType.DMA((7,)),
            pltpu.SemaphoreType.DMA((2, places)),
            pltpu.SemaphoreType.DMA((2, 4, count)),
        ],
        compiler_params=pltpu.CompilerParams(
            collective_id=0, has_side_effects=True, vmem_limit_bytes=VMEM_BYTES
        ),
        name="attend_forward",
    )(x, small, in_weight, out_weight, gate_weight, up_weight, down_weight, inverse)


def greet(flips, chain):
    me, here = lax.axis_index("tokens"), lax.axis_index("heads")
    barrier = pltpu.get_barrier_semaphore()
    for flip in flips:
        pl.semaphore_signal(barrier, inc=1, device_id=token_device(flip), device_id_type=MESH_ID)
    for step in (-1, 1):
        near = here + step

        @pl.when((near >= 0) & (near < chain))
        def _():
            pl.semaphore_signal(barrier, inc=1, device_id=(me, near), device_id_type=MESH_ID)

    edge = (here == 0) | (here == chain - 1)

    @pl.when(edge)
    def _():
        pl.semaphore_wait(barrier, len(flips) + 1)

    @pl.when(jnp.logical_not(edge))
    def _():
        pl.semaphore_wait(barrier, len(flips) + 2)


class Reduce:
    COPIES = 6

    def __init__(self, own, near, sems):
        self.own, self.near, self.sems = own, near, sems

    def copy(self, slot):
        k, half, flip = ((1, 0, 2), (3, 0, 2), (2, 1, 4), (3, 1, 4), (2, 0, 4), (1, 1, 2))[slot]
        rows = self.own.shape[1] // 2
        return remote(
            self.own.at[k, pl.ds(half * rows, rows)],
            self.near.at[slot],
            self.sems.at[0, slot],
            self.sems.at[1, slot],
            token_device(flip),
        )

    def put(self, k, block):
        self.own[k] = block.astype(self.own.dtype)
        self.send(k)

    def send(self, k):
        for slot in {3: (1, 3), 1: (0,), 2: (2,), 0: ()}[k]:
            self.copy(slot).start()

    def add_near(self, k, half, slot):
        rows = self.own.shape[1] // 2
        place = pl.ds(half * rows, rows)
        self.own[k, place] = (
            self.own[k, place].astype(jnp.float32) + self.near[slot].astype(jnp.float32)
        ).astype(self.own.dtype)

    def second(self):
        self.copy(1).wait_recv()
        self.add_near(2, 0, 1)
        self.copy(4).start()
        self.copy(3).wait_recv()
        self.add_near(1, 1, 3)
        self.copy(5).start()

    def finish(self, out):
        rows = self.own.shape[1] // 2
        for half, slots in ((0, (0, 4)), (1, (2, 5))):
            place = pl.ds(half * rows, rows)
            total = self.own[0, place].astype(jnp.float32)
            for slot in slots:
                self.copy(slot).wait_recv()
                total = total + self.near[slot].astype(jnp.float32)
            out[place, :] = total
        for slot in range(self.COPIES):
            self.copy(slot).wait_send()


def tn_dot(left, right):
    return lax.dot_general(
        left, right, (((0,), (0,)), ((), ())), preferred_element_type=jnp.float32
    )


def tiles_of(length, size):
    return [(low, min(low + size, length)) for low in range(0, length, size)]


def feed_kernel(
    chain, x, attn_sum, small_all, cotangent, gate_full, up_full, down_full, back_attn, hidden, mlp_term,
    grad_gate, grad_up, grad_mid, gate, up, down, mid_row, normed, back_gate, back_up, term, passing, total,
    own_gate, near_gate, own_up, near_up, load_sems, swap_sems, chain_sems, reduce_sems,
):
    count = term.shape[0] // 2
    each = term.shape[2]
    tokens, width = x.shape
    inner = gate.shape[1]
    me = lax.axis_index("tokens")
    tiles = tiles_of(inner, 512)
    loads = []
    for k, (low, high) in enumerate(tiles):
        cut = pl.ds(low, high - low)
        loads.append(
            (
                pltpu.make_async_copy(gate_full.at[:, cut], gate.at[:, cut], load_sems.at[0, k]),
                pltpu.make_async_copy(up_full.at[:, cut], up.at[:, cut], load_sems.at[1, k]),
                pltpu.make_async_copy(down_full.at[cut, :], down.at[cut, :], load_sems.at[2, k]),
            )
        )
    for group in loads:
        for load in group:
            load.start()
    greet((1, 2, 4), chain)

    def swap(k, ref, cut):
        mine, theirs = pl.ds(0, tokens), pl.ds(tokens, tokens)
        return remote(
            ref.at[mine, cut],
            ref.at[theirs, cut],
            swap_sems.at[0, k],
            swap_sems.at[1, k],
            token_device(1),
        )

    span = width // 8
    for k in range(8):
        mid_row[:, k * span : (k + 1) * span] = jnp.broadcast_to(
            small_all[k, 1:2, span : 2 * span], (8, span)
        )

    def middle_at(c):
        cut = slice(c * each, (c + 1) * each)
        return x[:, cut].astype(jnp.float32) + attn_sum[c].astype(jnp.float32)

    squares = jnp.zeros((tokens, each), jnp.float32)
    for c in range(2 * count):
        part = middle_at(c)
        squares = squares + part * part
    mid_scale = lax.rsqrt(jnp.sum(squares, axis=1, keepdims=True) / width + 1e-05)
    for c in range(2 * count):
        cut = slice(c * each, (c + 1) * each)
        normed[:tokens, cut] = (middle_at(c) * mid_scale * mid_row[0:1, cut]).astype(jnp.bfloat16)
    swaps = [swap(0, normed, pl.ds(0, width))]
    swaps[0].start()

    for k, (low, high) in enumerate(tiles):
        for load in loads[k]:
            load.wait()
        gate_rows = jnp.dot(
            normed[:tokens, :], gate[:, low:high], preferred_element_type=jnp.float32
        )
        up_rows = jnp.dot(normed[:tokens, :], up[:, low:high], preferred_element_type=jnp.float32)
        back_hidden = nt_dot(cotangent[...], down[low:high, :])
        sigmoid = jax.nn.sigmoid(gate_rows)
        silu = gate_rows * sigmoid
        hidden[:, low:high] = (silu * up_rows).astype(jnp.bfloat16)
        back_gate[:tokens, low:high] = (
            back_hidden * up_rows * sigmoid * (1.0 + gate_rows * (1.0 - sigmoid))
        ).astype(jnp.bfloat16)
        back_up[:tokens, low:high] = (back_hidden * silu).astype(jnp.bfloat16)
        for j, ref in enumerate((back_gate, back_up)):
            swaps.append(swap(1 + 2 * k + j, ref, pl.ds(low, high - low)))
            swaps[-1].start()

    def mid_pair(c):
        cut = pl.ds(c * each, 2 * each)
        made = nt_dot(back_gate[:tokens, :], gate[cut, :]) + nt_dot(back_up[:tokens, :], up[cut, :])
        made = made.astype(jnp.bfloat16)
        term[c] = made[:, :each]
        term[c + 1] = made[:, each:]

    def mlp_pair(c):
        made = jnp.dot(
            hidden[...], down[:, c * each : (c + 2) * each], preferred_element_type=jnp.float32
        ).astype(jnp.bfloat16)
        pair = c // 2
        rows, low = pl.ds(pair % 4 * tokens, tokens), pair // 4 * 2 * each
        gate[rows, low : low + 2 * each] = made
        for k in range(2):
            copy = pltpu.make_async_copy(
                gate.at[rows, pl.ds(low + k * each, each)], mlp_term.at[c + k], load_sems.at[3, c + k]
            )
            copy.start()
            stores.append(copy)

    stores = []
    gate_sum = Reduce(own_gate, near_gate, reduce_sems.at[0])
    up_sum = Reduce(own_up, near_up, reduce_sems.at[1])

    def block(part, k):
        index = jnp.bitwise_xor(me, 2 * k)
        cut = pl.ds(pl.multiple_of(index * span, span), span)
        ref = back_gate if part is gate_sum else back_up
        part.put(k, tn_dot(normed[:, cut], ref[...]))

    def received(indices):
        for k in indices:
            swaps[k].wait_recv()

    pairs_of = lambda n: lambda: (mid_pair(2 * n), mid_pair(count + 2 * n))
    grad = lambda part, *ks: lambda: [block(part, k) for k in ks]
    mlp = lambda *cs: lambda: [mlp_pair(2 * c) for c in cs]
    gates, ups = range(1, len(swaps), 2), range(2, len(swaps), 2)
    work = {now: [] for now in range(count + 2 * (chain - 1))}

    def plan(now, *jobs):
        work[min(now, len(work) - 1)].extend(jobs)

    for n in range(count // 2):
        plan(2 * n, pairs_of(n))
    plan(1, lambda: received([0, *gates]), grad(gate_sum, 3))
    plan(3, grad(gate_sum, 1, 2))
    plan(5, grad(gate_sum, 0), lambda: received(ups), grad(up_sum, 3))
    plan(7, grad(up_sum, 1), gate_sum.second)
    plan(8, grad(up_sum, 2))
    plan(9, grad(up_sum, 0))
    plan(10, mlp(0, 1, 2, 3))
    plan(11, up_sum.second)
    plan(12, mlp(4, 5, 6, 7))

    sums = [
        ChainSum(chain, upward, term, passing, total, base, count, chain_sems.at[k])
        for k, (upward, base) in enumerate(((True, 0), (False, count)))
    ]
    for now, jobs in work.items():
        for job in jobs:
            job()
        for part in sums:
            part.step(now)
    gate_sum.finish(grad_gate)

    weighed = jnp.zeros((tokens, each), jnp.float32)
    for c in range(2 * count):
        cut = slice(c * each, (c + 1) * each)
        back = total[c].astype(jnp.float32)
        hat = middle_at(c) * mid_scale
        weighed = weighed + back * mid_row[0:1, cut] * hat
        grad_mid[:, cut] = jnp.broadcast_to(jnp.sum(back * hat, axis=0, keepdims=True), (8, each))
    mean = jnp.sum(weighed, axis=1, keepdims=True) / width
    for c in range(2 * count):
        cut = slice(c * each, (c + 1) * each)
        u = total[c].astype(jnp.float32) * mid_row[0:1, cut]
        hat = middle_at(c) * mid_scale
        back_attn[:, cut] = (
            cotangent[:, cut].astype(jnp.float32) + mid_scale * (u - hat * mean)
        ).astype(jnp.bfloat16)
    up_sum.finish(grad_up)
    for part in sums:
        part.finish()
    for copy in swaps:
        copy.wait_send()
    for copy in stores:
        copy.wait()


def feed(chain, x, attn_sum, small_all, cotangent, gate_full, up_full, down_full):
    tokens, width = x.shape
    inner = gate_full.shape[1]
    count = attn_sum.shape[0] // 2
    span = width // 8
    bf16, f32 = jnp.bfloat16, jnp.float32
    anywhere, vmem = pl.BlockSpec(memory_space=pl.ANY), pl.BlockSpec(memory_space=pltpu.VMEM)
    shape = jax.ShapeDtypeStruct
    tiles = len(tiles_of(inner, 512))
    return pl.pallas_call(
        functools.partial(feed_kernel, chain),
        out_shape=[
            shape((tokens, width), bf16),
            shape((tokens, inner), bf16),
            shape(attn_sum.shape, bf16),
            shape((span, inner), f32),
            shape((span, inner), f32),
            shape((8, width), f32),
        ],
        in_specs=[vmem] * 4 + [anywhere] * 3,
        out_specs=[vmem, vmem, anywhere, vmem, vmem, vmem],
        scratch_shapes=[
            pltpu.VMEM((width, inner), bf16),
            pltpu.VMEM((width, inner), bf16),
            pltpu.VMEM((inner, width), bf16),
            pltpu.VMEM((8, width), f32),
            pltpu.VMEM((2 * tokens, width), bf16),
            pltpu.VMEM((2 * tokens, inner), bf16),
            pltpu.VMEM((2 * tokens, inner), bf16),
            pltpu.VMEM(attn_sum.shape, bf16),
            pltpu.VMEM(attn_sum.shape, bf16),
            pltpu.VMEM(attn_sum.shape, bf16),
            pltpu.VMEM((4, span, inner), bf16),
            pltpu.VMEM((6, span // 2, inner), bf16),
            pltpu.VMEM((4, span, inner), bf16),
            pltpu.VMEM((6, span // 2, inner), bf16),
            pltpu.SemaphoreType.DMA((4, max(tiles, 2 * count))),
            pltpu.SemaphoreType.DMA((2, 1 + 2 * tiles)),
            pltpu.SemaphoreType.DMA((2, 4, count)),
            pltpu.SemaphoreType.DMA((2, 2, Reduce.COPIES)),
        ],
        compiler_params=pltpu.CompilerParams(
            collective_id=1, has_side_effects=True, vmem_limit_bytes=VMEM_BYTES
        ),
        name="feed_forward",
    )(x, attn_sum, small_all, cotangent, gate_full, up_full, down_full)


def split_marks(values, at):
    high = values.astype(jnp.bfloat16).astype(jnp.float32)
    rest = values - high
    middle = rest.astype(jnp.bfloat16).astype(jnp.float32)
    low = rest - middle
    return jnp.where(at == 4, high, jnp.where(at == 5, middle, jnp.where(at == 6, low, 0.0)))


def return_kernel(
    chain, places, small_all, query, pairs, log_total, cos_table, sin_table,
    mid_part, attended_in, x_in, attn_sum, back_in, in_full, out_full, mlp_term, hidden_in, cotangent, normed_in, layer_out, grad_input, grad_down,
    grad_in, grad_out, gains, in_here, out_here, key_side, value_side, query_side, back_side, back_att,
    back_rows, back_keys, back_values, pair_out, pair_near, normed, back_attn, hidden, cotangents, att_low,
    back_all, pre_row, pre_part, gains_near, mlp_sum, mlp_passing, mlp_total, term, passing, total, own_down,
    near_down, own_in, near_in, own_out, near_out, load_sems, swap_sems, pair_sems, gain_sems, chain_sems,
    reduce_sems, store_sems,
):
    count = term.shape[0] // 2
    each = term.shape[2]
    tokens, width = x_in.shape
    span = width // 8
    groups = query.shape[1] // 128
    me = lax.axis_index("tokens")
    place = lax.rem(me, places)
    first_device = me - place
    mine, theirs = pl.ds(0, tokens), pl.ds(tokens, tokens)

    def load(k, src, dst):
        copy = pltpu.make_async_copy(src, dst, load_sems.at[k])
        copy.start()
        return copy

    attended = back_rows
    load_attended = load(8 + 2 * count, attended_in, attended)
    load_back = load(6, back_in, back_attn.at[mine, :])
    load_out = load(0, out_full, out_here)
    load_in = load(1, in_full, in_here)
    load_cot = load(2, cotangent, cotangents.at[mine, :])
    load_hidden = load(3, hidden_in, hidden.at[mine, :])
    load_normed = load(4, normed_in, normed.at[mine, :])
    load_mlp = load(5, mlp_term, mlp_sum)
    greet(range(1, 8), chain)

    def swap(k, ref):
        copy = remote(
            ref.at[mine, :],
            ref.at[theirs, :],
            swap_sems.at[0, k],
            swap_sems.at[1, k],
            token_device(1),
        )
        copy.start()
        return copy

    def gain_copy(which, src, flip):
        other = jnp.bitwise_xor(me, flip)
        return remote(
            src.at[:, pl.ds(pl.multiple_of(other * span, span), span)],
            gains_near.at[me, :, pl.ds(which * span, span)],
            gain_sems.at[0, which, flip - 1],
            gain_sems.at[1, which, flip - 1],
            token_device(flip),
        )

    for flip in range(1, 8):
        gain_copy(1, mid_part, flip).start()
    load_back.wait()
    load_attended.wait()
    att_low[mine, :] = attended[...].astype(jnp.bfloat16)
    swap_back = swap(0, back_attn)
    swap_att = swap(1, att_low)

    lane = lanes((tokens, 128))
    at = lane % 64
    first_id = (first_device // places * 4).astype(jnp.float32)
    for k in range(places):
        mark = key_marks(token_column(small_all[first_device + k, 0:1, :]), first_id)
        block = pl.ds(k * tokens, tokens)
        pair = pairs[block].astype(jnp.float32)
        swapped = pltpu.roll(pair, 64, 1)
        key_side[0, block] = jnp.where(lane < 64, pair, mark).astype(jnp.bfloat16)
        key_side[1, block] = jnp.where(lane < 64, mark, swapped).astype(jnp.bfloat16)
        value_side[0, block] = jnp.where(lane < 64, swapped, 1.0).astype(jnp.bfloat16)
        value_side[1, block] = jnp.where(lane < 64, 1.0, pair).astype(jnp.bfloat16)
    own_marks = query_marks(token_column(small_all[me, 0:1, :]), first_id)

    load_out.wait()
    back_att[...] = nt_dot(back_attn[mine, :], out_here[...]).astype(jnp.bfloat16)
    load_cot.wait()
    swap_cot = swap(2, cotangents)
    load_hidden.wait()
    swap_hidden = swap(3, hidden)
    for group in range(groups):
        cut = slice(group * 128, (group + 1) * 128)
        back = back_att[:, cut].astype(jnp.float32)
        both = query[:, cut].astype(jnp.float32)
        shared = back * attended[:, cut]
        for e in range(2):
            head = 2 * group + e
            used = (lane < 64) if e == 0 else (lane >= 64)
            delta = jnp.sum(jnp.where(used, shared, 0.0), axis=1, keepdims=True)
            peak = jnp.sum(jnp.where(lane == head, log_total[...], 0.0), axis=1, keepdims=True)
            back_side[head] = jnp.where(
                used, back, split_marks(jnp.broadcast_to(-delta, lane.shape), at)
            ).astype(jnp.bfloat16)
            query_side[head] = jnp.where(
                used, both, own_marks + split_marks(jnp.broadcast_to(-peak, lane.shape), at)
            ).astype(jnp.bfloat16)
    load_normed.wait()
    swap_normed = swap(4, normed)
    load_mlp.wait()
    load_in.wait()

    mlp_sums = [
        ChainSum(chain, upward, mlp_sum, mlp_passing, mlp_total, base, count, chain_sems.at[0, k])
        for k, (upward, base) in enumerate(((True, 0), (False, count)))
    ]
    back_rows[...] = jnp.zeros_like(back_rows)

    def key_step(k, diagonal):
        back_keys[...] = jnp.zeros_like(back_keys)
        back_values[...] = jnp.zeros_like(back_values)

        @pl.loop(0, groups)
        def _(group):
            cut = pl.ds(pl.multiple_of(group * 128, 128), 128)
            for low in (0, tokens // 2):
                keys_here = pl.ds(pl.multiple_of(k * tokens + low, tokens // 2), tokens // 2)
                part = pl.ds(low, tokens // 2)
                first = low if diagonal else 0
                seen = pl.ds(first, tokens - first)
                rows = []
                for e in range(2):
                    head = 2 * group + e
                    found = nt_dot(key_side[e, keys_here], query_side[head, seen])
                    chances = jnp.exp(found)
                    if diagonal:
                        keys = lax.broadcasted_iota(jnp.int32, found.shape, 0) + (low - first)
                        chances = jnp.where(keys <= lanes(found.shape), chances, 0.0)
                    moved = chances * nt_dot(value_side[e, keys_here], back_side[head, seen])
                    chances = chances.astype(jnp.bfloat16)
                    moved = moved.astype(jnp.bfloat16)
                    back_values[e, part] += jnp.dot(
                        chances, back_att[seen, cut], preferred_element_type=jnp.float32
                    )
                    back_keys[e, part] += jnp.dot(
                        moved, query[seen, cut], preferred_element_type=jnp.float32
                    )
                    rows.append(tn_dot(moved, key_side[e, keys_here]))
                back_rows[seen, cut] += jnp.where(lanes(rows[0].shape) < 64, rows[0], rows[1])

            @pl.when(group % 2 == 1)
            def _():
                for part in mlp_sums:
                    part.step(2 * k + group // 2)

        keys = back_keys[0] + pltpu.roll(back_keys[1], 64, 1)
        values = pltpu.roll(back_values[0], 64, 1) + back_values[1]
        return jnp.where(lane < 64, keys, values)

    def pair_copy(source, target):
        return remote(
            pair_out.at[target],
            pair_near.at[source],
            pair_sems.at[0, target],
            pair_sems.at[1, source],
            (first_device + target, lax.axis_index("heads")),
        )

    @pl.loop(0, place)
    def _(k):
        pair_out[k] = key_step(k, False).astype(jnp.bfloat16)
        pair_copy(place, k).start()

    own_pair = key_step(place, True)
    pair_out[place] = own_pair.astype(jnp.bfloat16)
    early = 2 * places

    @pl.loop(2 * (place + 1), early)
    def _(now):
        for part in mlp_sums:
            part.step(now)

    for group in range(groups):
        cut = slice(group * 128, (group + 1) * 128)
        back_all[mine, cut] = (
            turn(back_rows[:, cut], cos_table[...], -sin_table[...]) * 0.125
        ).astype(jnp.bfloat16)
    back_keys[0] = own_pair
    for k in range(1, places):

        @pl.when(k > place)
        def _():
            remote(
                pair_out.at[k],
                pair_near.at[k],
                pair_sems.at[0, k],
                pair_sems.at[1, k],
                (first_device + k, lax.axis_index("heads")),
            ).wait_recv()
            back_keys[0] += pair_near[k].astype(jnp.float32)

    summed = back_keys[0]
    spun = turn(summed, cos_table[...], -sin_table[...])
    back_all[mine, pl.ds(groups * 128, 128)] = jnp.where(lane < 64, spun, summed).astype(
        jnp.bfloat16
    )
    swap_all = swap(5, back_all)

    def pre_pair(c):
        cut = pl.ds(c * each, 2 * each)
        made = nt_dot(back_all[mine, :], in_here[cut, :]).astype(jnp.bfloat16)
        term[c] = made[:, :each]
        term[c + 1] = made[:, each:]

    def cut_of(k):
        index = jnp.bitwise_xor(me, 2 * k)
        return pl.ds(pl.multiple_of(index * span, span), span)

    down_sum = Reduce(own_down, near_down, reduce_sems.at[0])
    in_sum = Reduce(own_in, near_in, reduce_sems.at[1])
    out_sum = Reduce(own_out, near_out, reduce_sems.at[2])

    def down_block(k):
        for low, high in tiles_of(hidden.shape[1], 512):
            own_down[k, low:high] = tn_dot(hidden[:, low:high], cotangents[:, cut_of(k)]).astype(
                own_down.dtype
            )
        down_sum.send(k)

    def in_block(k):
        in_sum.put(k, tn_dot(normed[:, cut_of(k)], back_all[...]))

    def out_block(k):
        out_sum.put(k, tn_dot(att_low[...], back_attn[:, cut_of(k)]))

    def late_loads():
        copies = [pltpu.make_async_copy(x_in, cotangents.at[theirs, :], load_sems.at[7])]
        for c in range(2 * count):
            copies.append(
                pltpu.make_async_copy(
                    attn_sum.at[c],
                    cotangents.at[mine, pl.ds(c * each, each)],
                    load_sems.at[8 + c],
                )
            )
        return copies

    def load_late():
        swap_cot.wait_send()
        for copy in late_loads():
            copy.start()

    def x_at(c):
        return cotangents[theirs, c * each : (c + 1) * each].astype(jnp.float32)

    def middle_at(c):
        return x_at(c) + cotangents[mine, c * each : (c + 1) * each].astype(jnp.float32)

    stores = []

    def store(c, src, out):
        copy = pltpu.make_async_copy(
            src.at[c], out.at[:, pl.ds(c * each, each)], store_sems.at[len(stores)]
        )
        copy.start()
        stores.append(copy)

    def finish_mlp():
        for part in mlp_sums:
            part.finish()
        for copy in late_loads():
            copy.wait()
        for c in range(2 * count):
            mlp_sum[c] = (middle_at(c) + mlp_total[c].astype(jnp.float32)).astype(jnp.bfloat16)
            store(c, mlp_sum, layer_out)

    def scale_rows():
        for k in range(8):
            pre_row[:, k * span : (k + 1) * span] = jnp.broadcast_to(
                small_all[k, 1:2, :span], (8, span)
            )

    steps = count + 2 * (chain - 1)
    work = {now: [] for now in range(steps)}

    def plan(now, *jobs):
        work[min(now, steps - 1)].extend(jobs)

    pre = lambda n: lambda: (pre_pair(2 * n), pre_pair(count + 2 * n))
    blocks = lambda make, *ks: lambda: [make(k) for k in ks]
    received = lambda *copies: lambda: [copy.wait_recv() for copy in copies]
    for n in range(count // 2):
        plan(2 * n, pre(n))
    plan(1, received(swap_cot, swap_hidden), blocks(down_block, 3, 1))
    plan(3, blocks(down_block, 2, 0), load_late)
    plan(4, received(swap_back, swap_att), blocks(out_block, 3, 1, 2, 0))
    plan(5, received(swap_normed, swap_all), blocks(in_block, 3, 1, 2, 0))
    plan(7, down_sum.second)
    plan(8, finish_mlp)
    plan(9, out_sum.second)
    plan(10, in_sum.second, scale_rows)
    plan(11, lambda: down_sum.finish(grad_down))
    plan(12, lambda: out_sum.finish(grad_out))
    sums = [
        ChainSum(chain, upward, term, passing, total, base, count, chain_sems.at[1, k])
        for k, (upward, base) in enumerate(((True, 0), (False, count)))
    ]
    for now, jobs in work.items():
        for job in jobs:
            job()
        if early + now < steps:
            for part in mlp_sums:
                part.step(early + now)
        for part in sums:
            part.step(now)
    for part in sums:
        part.finish()

    squares = jnp.zeros((tokens, each), jnp.float32)
    for c in range(2 * count):
        part = x_at(c)
        squares = squares + part * part
    pre_scale = lax.rsqrt(jnp.sum(squares, axis=1, keepdims=True) / width + 1e-05)
    weighed = jnp.zeros((tokens, each), jnp.float32)
    for c in range(2 * count):
        cut = slice(c * each, (c + 1) * each)
        back = total[c].astype(jnp.float32)
        hat = x_at(c) * pre_scale
        weighed = weighed + back * pre_row[0:1, cut] * hat
        pre_part[:, cut] = jnp.broadcast_to(jnp.sum(back * hat, axis=0, keepdims=True), (8, each))
    for flip in range(1, 8):
        gain_copy(0, pre_part, flip).start()
    mean = jnp.sum(weighed, axis=1, keepdims=True) / width
    for c in range(2 * count):
        cut = slice(c * each, (c + 1) * each)
        u = total[c].astype(jnp.float32) * pre_row[0:1, cut]
        hat = x_at(c) * pre_scale
        term[c] = (
            back_attn[mine, cut].astype(jnp.float32) + pre_scale * (u - hat * mean)
        ).astype(jnp.bfloat16)
        store(c, term, grad_input)
    in_sum.finish(grad_in)
    own = pl.ds(pl.multiple_of(me * span, span), span)
    gains_near[me, :, :span] = pre_part[:, own]
    gains_near[me, :, span:] = mid_part[:, own]
    for flip in range(1, 8):
        for which, src in enumerate((pre_part, mid_part)):
            gain_copy(which, src, flip).wait_recv()
    gains[...] = jnp.sum(gains_near[...], axis=0)
    for flip in range(1, 8):
        for which, src in enumerate((pre_part, mid_part)):
            gain_copy(which, src, flip).wait_send()
    for copy in (swap_back, swap_att, swap_hidden, swap_normed, swap_all):
        copy.wait_send()

    @pl.loop(0, place)
    def _(k):
        pair_copy(place, k).wait_send()

    for copy in stores:
        copy.wait()


def way_back(
    chain, places, x, attn_sum, small_all, back_attn, query, pairs, attended, log_total, cos_table, sin_table,
    mid_part, in_full, out_full, mlp_term, hidden, cotangent, normed,
):
    tokens, width = x.shape
    inner = hidden.shape[1]
    heads_wide = query.shape[1]
    wide = in_full.shape[1]
    chunks = attn_sum.shape
    count = chunks[0] // 2
    span = width // 8
    row = places * tokens
    bf16, f32 = jnp.bfloat16, jnp.float32
    anywhere, vmem = pl.BlockSpec(memory_space=pl.ANY), pl.BlockSpec(memory_space=pltpu.VMEM)
    shape = jax.ShapeDtypeStruct
    return pl.pallas_call(
        functools.partial(return_kernel, chain, places),
        out_shape=[
            shape((tokens, width), bf16),
            shape((tokens, width), bf16),
            shape((inner, span), f32),
            shape((span, wide), f32),
            shape((heads_wide, span), f32),
            shape((8, 2 * span), f32),
        ],
        in_specs=[vmem] * 7 + [anywhere] * 10,
        out_specs=[anywhere] * 2 + [vmem] * 4,
        scratch_shapes=[
            pltpu.VMEM((width, wide), bf16),
            pltpu.VMEM((heads_wide, width), bf16),
            pltpu.VMEM((2, row, 128), bf16),
            pltpu.VMEM((2, row, 128), bf16),
            pltpu.VMEM((heads_wide // 64, tokens, 128), bf16),
            pltpu.VMEM((heads_wide // 64, tokens, 128), bf16),
            pltpu.VMEM((tokens, heads_wide), bf16),
            pltpu.VMEM((tokens, heads_wide), f32),
            pltpu.VMEM((2, tokens, 128), f32),
            pltpu.VMEM((2, tokens, 128), f32),
            pltpu.VMEM((places, tokens, 128), bf16),
            pltpu.VMEM((places, tokens, 128), bf16),
            pltpu.VMEM((2 * tokens, width), bf16),
            pltpu.VMEM((2 * tokens, width), bf16),
            pltpu.VMEM((2 * tokens, inner), bf16),
            pltpu.VMEM((2 * tokens, width), bf16),
            pltpu.VMEM((2 * tokens, heads_wide), bf16),
            pltpu.VMEM((2 * tokens, wide), bf16),
            pltpu.VMEM((8, width), f32),
            pltpu.VMEM((8, width), f32),
            pltpu.VMEM((8, 8, 2 * span), f32),
            pltpu.VMEM(chunks, bf16),
            pltpu.VMEM(chunks, bf16),
            pltpu.VMEM(chunks, bf16),
            pltpu.VMEM(chunks, bf16),
            pltpu.VMEM(chunks, bf16),
            pltpu.VMEM(chunks, bf16),
            pltpu.VMEM((4, inner, span), bf16),
            pltpu.VMEM((6, inner // 2, span), bf16),
            pltpu.VMEM((4, span, wide), bf16),
            pltpu.VMEM((6, span // 2, wide), bf16),
            pltpu.VMEM((4, heads_wide, span), bf16),
            pltpu.VMEM((6, heads_wide // 2, span), bf16),
            pltpu.SemaphoreType.DMA((9 + 2 * count,)),
            pltpu.SemaphoreType.DMA((2, 6)),
            pltpu.SemaphoreType.DMA((2, places)),
            pltpu.SemaphoreType.DMA((2, 2, 7)),
            pltpu.SemaphoreType.DMA((2, 2, 4, count)),
            pltpu.SemaphoreType.DMA((3, 2, Reduce.COPIES)),
            pltpu.SemaphoreType.DMA((4 * count,)),
        ],
        compiler_params=pltpu.CompilerParams(
            collective_id=2, has_side_effects=True, vmem_limit_bytes=VMEM_BYTES
        ),
        name="way_back",
    )(
        small_all, query, pairs, log_total, cos_table, sin_table,
        mid_part, attended, x, attn_sum, back_attn, in_full, out_full, mlp_term, hidden, cotangent, normed,
    )


def shards_cube(
    chain,
    inputs,
    segments,
    pre_gain,
    mid_gain,
    query_weight,
    key_weight,
    value_weight,
    out_weight,
    gate_weight,
    up_weight,
    down_weight,
    cotangent,
):
    row_count = inputs.shape[0]
    head_size = key_weight.shape[1]
    query_width = query_weight.shape[1]
    heads_here = query_width // head_size
    places = ROW // row_count
    small = jnp.stack(
        [
            segments.astype(jnp.float32),
            jnp.concatenate([pre_gain, mid_gain]).astype(jnp.float32),
        ]
    )
    small = jnp.concatenate([small, jnp.zeros((6, row_count), jnp.float32)])
    in_weight = jnp.concatenate([query_weight, key_weight, value_weight], axis=1)
    half_size = head_size // 2
    inverse = 10000.0 ** (-jnp.arange(half_size, dtype=jnp.float32) / half_size)
    inverse = jnp.broadcast_to(jnp.tile(inverse, 128 // half_size)[None], (8, 128))
    (
        gate_full,
        up_full,
        down_full,
        in_full,
        out_full,
        attn_sum,
        normed,
        query_rot,
        pairs,
        attended,
        log_total,
        cos_wide,
        sin_wide,
        small_full,
    ) = attend(
        chain, places, inputs, small, in_weight, out_weight, gate_weight, up_weight, down_weight, inverse
    )
    back_attn, hidden, mlp_term, grad_gate, grad_up, grad_mid = feed(
        chain, inputs, attn_sum, small_full, cotangent, gate_full, up_full, down_full
    )
    layer_out, grad_input, grad_down, grad_in, grad_out, gains = way_back(
        chain,
        places,
        inputs,
        attn_sum,
        small_full,
        back_attn,
        query_rot,
        pairs,
        attended,
        log_total,
        cos_wide,
        sin_wide,
        grad_mid,
        in_full,
        out_full,
        mlp_term,
        hidden,
        cotangent,
        normed,
    )
    grad_pre, grad_mid = jnp.split(gains[0], 2)
    grad_query = grad_in[:, :query_width]
    grad_key = grad_in[:, query_width : query_width + head_size]
    grad_value = grad_in[:, query_width + head_size :]
    return (
        layer_out,
        grad_input,
        grad_pre,
        grad_mid,
        grad_query,
        grad_key,
        grad_value,
        grad_out,
        grad_gate,
        grad_up,
        grad_down,
    )


def solution(mesh):
    sizes = dict(mesh.shape)
    plan = shards_any
    if sizes["tokens"] == 8:
        plan = functools.partial(shards_cube, sizes["heads"])
    return jax.shard_map(
        plan,
        mesh=mesh,
        in_specs=(
            P("tokens", None),
            P("tokens"),
            P("tokens"),
            P("tokens"),
            P("tokens", "heads"),
            P("tokens", "heads"),
            P("tokens", "heads"),
            P("heads", "tokens"),
            P("tokens", "heads"),
            P("tokens", "heads"),
            P("heads", "tokens"),
            P("tokens", None),
        ),
        out_specs=(
            P("tokens", None),
            P("tokens", None),
            P("tokens"),
            P("tokens"),
            P("tokens", "heads"),
            P("tokens", "heads"),
            P("tokens", "heads"),
            P("heads", "tokens"),
            P("tokens", "heads"),
            P("tokens", "heads"),
            P("heads", "tokens"),
        ),
        check_vma=False,
    )
```

```python
import functools
import math

import jax
import jax.numpy as jnp
import numpy as np
from jax import lax
from jax.experimental import pallas as pl
from jax.experimental.pallas import tpu as pltpu
from jax.sharding import PartitionSpec as P

ROW = 2048


def rms_scale(vectors):
    return lax.rsqrt(jnp.mean(vectors * vectors, axis=-1, keepdims=True) + 1e-05)


def rotate(vectors, cos_table, sin_table):
    middle_index = vectors.shape[-1] // 2
    former = vectors[..., :middle_index]
    latter = vectors[..., middle_index:]
    return jnp.concatenate(
        [former * cos_table - latter * sin_table, latter * cos_table + former * sin_table], axis=-1
    )


def unrotate(gradient, cos_table, sin_table):
    middle_index = gradient.shape[-1] // 2
    former = gradient[..., :middle_index]
    latter = gradient[..., middle_index:]
    return jnp.concatenate(
        [former * cos_table + latter * sin_table, latter * cos_table - former * sin_table], axis=-1
    )


def norm_back(gradient, vectors, scale_rows, gain_row):
    shaped = vectors * scale_rows
    weighted = gradient * gain_row
    back_vectors = scale_rows * (
        weighted - shaped * jnp.mean(weighted * shaped, axis=-1, keepdims=True)
    )
    return (back_vectors, jnp.sum(gradient * shaped, axis=0))


def shards_any(
    inputs,
    segments,
    pre_gain,
    mid_gain,
    query_weight,
    key_weight,
    value_weight,
    out_weight,
    gate_weight,
    up_weight,
    down_weight,
    cotangent,
):
    row_count = inputs.shape[0]
    head_size = key_weight.shape[1]
    heads_here = query_weight.shape[1] // head_size
    myself = lax.axis_index("tokens")
    gathered = (
        lax.all_gather(pre_gain, "tokens", axis=0, tiled=True),
        lax.all_gather(mid_gain, "tokens", axis=0, tiled=True),
        lax.all_gather(query_weight, "tokens", axis=0, tiled=True),
        lax.all_gather(key_weight, "tokens", axis=0, tiled=True),
        lax.all_gather(value_weight, "tokens", axis=0, tiled=True),
        lax.all_gather(out_weight, "tokens", axis=1, tiled=True),
        lax.all_gather(gate_weight, "tokens", axis=0, tiled=True),
        lax.all_gather(up_weight, "tokens", axis=0, tiled=True),
        lax.all_gather(down_weight, "tokens", axis=1, tiled=True),
    )
    (
        pre_full,
        mid_full,
        query_full,
        key_full,
        value_full,
        out_full,
        gate_full,
        up_full,
        down_full,
    ) = gathered
    pre_row = pre_full.astype(jnp.float32)
    mid_row = mid_full.astype(jnp.float32)
    all_ids = lax.all_gather(segments, "tokens", axis=0, tiled=True)
    length = all_ids.shape[0]
    places = jnp.arange(length, dtype=jnp.int32)
    starts_here = jnp.concatenate([jnp.ones((1,), dtype=jnp.bool_), all_ids[1:] != all_ids[:-1]])
    opening = lax.cummax(jnp.where(starts_here, places, 0), axis=0)
    own_first = myself * row_count
    positions = lax.dynamic_slice_in_dim(places - opening, own_first, row_count)
    own_places = own_first + jnp.arange(row_count, dtype=jnp.int32)
    half_size = head_size // 2
    inverse = 10000.0 ** (-jnp.arange(half_size, dtype=jnp.float32) / half_size)
    turned = positions.astype(jnp.float32)[:, None] * inverse[None, :]
    cos_table = jnp.cos(turned)[:, None, :]
    sin_table = jnp.sin(turned)[:, None, :]
    inputs_f = inputs.astype(jnp.float32)
    pre_scale = rms_scale(inputs_f)
    normed = (inputs_f * pre_scale * pre_row).astype(jnp.bfloat16)
    queries = jnp.dot(normed, query_full, preferred_element_type=jnp.float32).reshape(
        row_count, heads_here, head_size
    )
    query_rot = (rotate(queries, cos_table, sin_table) * head_size ** (-0.5)).astype(jnp.bfloat16)
    key_rows = jnp.dot(normed, key_full, preferred_element_type=jnp.float32)[:, None, :]
    key_rot = rotate(key_rows, cos_table, sin_table)[:, 0, :].astype(jnp.bfloat16)
    value_low = jnp.dot(normed, value_full, preferred_element_type=jnp.float32).astype(jnp.bfloat16)
    key_all, value_all = (
        lax.all_gather(key_rot, "tokens", axis=0, tiled=True),
        lax.all_gather(value_low, "tokens", axis=0, tiled=True),
    )
    span = math.gcd(ROW, 1024)
    row_start = own_first // ROW * ROW
    block_first = row_start // span
    block_total = (own_first + row_count + span - 1) // span

    def key_block(block_index):
        opening_row = block_index * span
        block_keys = lax.dynamic_slice_in_dim(key_all, opening_row, span)
        block_values = lax.dynamic_slice_in_dim(value_all, opening_row, span)
        block_ids = lax.dynamic_slice_in_dim(all_ids, opening_row, span)
        block_places = opening_row + jnp.arange(span, dtype=jnp.int32)
        allowed = (segments[:, None] == block_ids[None, :]) & (
            own_places[:, None] >= block_places[None, :]
        )
        scores = jnp.einsum(
            "qhd,kd->qhk", query_rot, block_keys, preferred_element_type=jnp.float32
        )
        return (opening_row, block_keys, block_values, allowed[:, None, :], scores)

    def forward_step(block_index, state_now):
        row_peak, row_total, running = state_now
        opening_row, block_keys, block_values, allowed, scores = key_block(block_index)
        new_peak = jnp.maximum(row_peak, jnp.max(jnp.where(allowed, scores, -1e30), axis=-1))
        factor = jnp.exp(row_peak - new_peak)
        weights = jnp.where(allowed, jnp.exp(scores - new_peak[..., None]), 0.0)
        row_total = row_total * factor + jnp.sum(weights, axis=-1)
        running = running * factor[..., None] + jnp.einsum(
            "qhk,kd->qhd",
            weights.astype(jnp.bfloat16),
            block_values,
            preferred_element_type=jnp.float32,
        )
        return (new_peak, row_total, running)

    start_state = (
        jnp.full((row_count, heads_here), -1e30, jnp.float32),
        jnp.zeros((row_count, heads_here), jnp.float32),
        jnp.zeros((row_count, heads_here, head_size), jnp.float32),
    )
    row_peak, row_total, running = lax.fori_loop(
        block_first, block_total, forward_step, start_state
    )
    attended = running / row_total[..., None]
    log_total = row_peak + jnp.log(row_total)
    attended_low = attended.astype(jnp.bfloat16).reshape(row_count, heads_here * head_size)
    attn_term = jnp.dot(attended_low, out_full, preferred_element_type=jnp.float32)
    middle = inputs_f + lax.psum(attn_term.astype(jnp.bfloat16), "heads").astype(jnp.float32)
    mid_scale = rms_scale(middle)
    normed_mid = (middle * mid_scale * mid_row).astype(jnp.bfloat16)
    gate_rows = jnp.dot(normed_mid, gate_full, preferred_element_type=jnp.float32)
    up_rows = jnp.dot(normed_mid, up_full, preferred_element_type=jnp.float32)
    sigmoid_rows = jax.nn.sigmoid(gate_rows)
    silu_rows = gate_rows * sigmoid_rows
    hidden = (silu_rows * up_rows).astype(jnp.bfloat16)
    mlp_term = jnp.dot(hidden, down_full, preferred_element_type=jnp.float32)
    layer_out = (
        middle + lax.psum(mlp_term.astype(jnp.bfloat16), "heads").astype(jnp.float32)
    ).astype(jnp.bfloat16)
    grad_down = jnp.einsum("tf,td->fd", hidden, cotangent, preferred_element_type=jnp.float32)
    back_hidden = jnp.einsum("td,fd->tf", cotangent, down_full, preferred_element_type=jnp.float32)
    back_gate = (
        back_hidden * up_rows * sigmoid_rows * (1.0 + gate_rows * (1.0 - sigmoid_rows))
    ).astype(jnp.bfloat16)
    back_up = (back_hidden * silu_rows).astype(jnp.bfloat16)
    grad_gate = jnp.einsum("tc,tf->cf", normed_mid, back_gate, preferred_element_type=jnp.float32)
    grad_up = jnp.einsum("tc,tf->cf", normed_mid, back_up, preferred_element_type=jnp.float32)
    mid_term = jnp.einsum(
        "tf,cf->tc", back_gate, gate_full, preferred_element_type=jnp.float32
    ) + jnp.einsum("tf,cf->tc", back_up, up_full, preferred_element_type=jnp.float32)
    back_normed_mid = lax.psum(mid_term.astype(jnp.bfloat16), "heads").astype(jnp.float32)
    back_middle, grad_mid = norm_back(back_normed_mid, middle, mid_scale, mid_row)
    back_middle = back_middle + cotangent.astype(jnp.float32)
    back_attn = back_middle.astype(jnp.bfloat16)
    grad_out = jnp.einsum("tc,td->cd", attended_low, back_attn, preferred_element_type=jnp.float32)
    back_attended = (
        jnp.einsum("td,cd->tc", back_attn, out_full, preferred_element_type=jnp.float32)
        .astype(jnp.bfloat16)
        .reshape(row_count, heads_here, head_size)
    )
    row_delta = jnp.sum(back_attended.astype(jnp.float32) * attended, axis=-1)

    def backward_step(block_index, state_now):
        back_rows, back_pairs = state_now
        opening_row, block_keys, block_values, allowed, scores = key_block(block_index)
        chances = jnp.where(allowed, jnp.exp(scores - log_total[..., None]), 0.0)
        back_values = jnp.einsum(
            "qhk,qhd->kd",
            chances.astype(jnp.bfloat16),
            back_attended,
            preferred_element_type=jnp.float32,
        )
        back_chances = jnp.einsum(
            "qhd,kd->qhk", back_attended, block_values, preferred_element_type=jnp.float32
        )
        back_scores = (chances * (back_chances - row_delta[..., None])).astype(jnp.bfloat16)
        back_rows = back_rows + jnp.einsum(
            "qhk,kd->qhd", back_scores, block_keys, preferred_element_type=jnp.float32
        )
        back_keys = jnp.einsum(
            "qhk,qhd->kd", back_scores, query_rot, preferred_element_type=jnp.float32
        )
        old_piece = lax.dynamic_slice_in_dim(back_pairs, opening_row, span)
        fresh_piece = old_piece + jnp.concatenate([back_keys, back_values], axis=-1)
        back_pairs = lax.dynamic_update_slice_in_dim(back_pairs, fresh_piece, opening_row, 0)
        return (back_rows, back_pairs)

    start_back = (
        jnp.zeros((row_count, heads_here, head_size), jnp.float32),
        jnp.zeros((length, 2 * head_size), jnp.float32),
    )
    back_rows, back_pairs = lax.fori_loop(block_first, block_total, backward_step, start_back)
    own_pairs = lax.psum_scatter(
        back_pairs.astype(jnp.bfloat16), "tokens", scatter_dimension=0, tiled=True
    ).astype(jnp.float32)
    back_query = (
        (unrotate(back_rows, cos_table, sin_table) * head_size ** (-0.5))
        .astype(jnp.bfloat16)
        .reshape(row_count, heads_here * head_size)
    )
    back_key = unrotate(own_pairs[:, None, :head_size], cos_table, sin_table)[:, 0, :].astype(
        jnp.bfloat16
    )
    back_value = own_pairs[:, head_size:].astype(jnp.bfloat16)
    grad_query = jnp.einsum("tc,tq->cq", normed, back_query, preferred_element_type=jnp.float32)
    grad_key = jnp.einsum("tc,tq->cq", normed, back_key, preferred_element_type=jnp.float32)
    grad_value = jnp.einsum("tc,tq->cq", normed, back_value, preferred_element_type=jnp.float32)
    pre_term = jnp.einsum("tq,cq->tc", back_query, query_full, preferred_element_type=jnp.float32)
    pre_term = pre_term + jnp.einsum(
        "tq,cq->tc", back_key, key_full, preferred_element_type=jnp.float32
    )
    pre_term = pre_term + jnp.einsum(
        "tq,cq->tc", back_value, value_full, preferred_element_type=jnp.float32
    )
    back_normed = lax.psum(pre_term.astype(jnp.bfloat16), "heads").astype(jnp.float32)
    back_inputs, grad_pre = norm_back(back_normed, inputs_f, pre_scale, pre_row)
    grad_input = (back_middle + back_inputs).astype(jnp.bfloat16)
    summed = (
        lax.psum_scatter(
            grad_pre.astype(jnp.bfloat16), "tokens", scatter_dimension=0, tiled=True
        ).astype(jnp.float32),
        lax.psum_scatter(
            grad_mid.astype(jnp.bfloat16), "tokens", scatter_dimension=0, tiled=True
        ).astype(jnp.float32),
        lax.psum_scatter(
            grad_query.astype(jnp.bfloat16), "tokens", scatter_dimension=0, tiled=True
        ).astype(jnp.float32),
        lax.psum_scatter(
            grad_key.astype(jnp.bfloat16), "tokens", scatter_dimension=0, tiled=True
        ).astype(jnp.float32),
        lax.psum_scatter(
            grad_value.astype(jnp.bfloat16), "tokens", scatter_dimension=0, tiled=True
        ).astype(jnp.float32),
        lax.psum_scatter(
            grad_out.astype(jnp.bfloat16), "tokens", scatter_dimension=1, tiled=True
        ).astype(jnp.float32),
        lax.psum_scatter(
            grad_gate.astype(jnp.bfloat16), "tokens", scatter_dimension=0, tiled=True
        ).astype(jnp.float32),
        lax.psum_scatter(
            grad_up.astype(jnp.bfloat16), "tokens", scatter_dimension=0, tiled=True
        ).astype(jnp.float32),
        lax.psum_scatter(
            grad_down.astype(jnp.bfloat16), "tokens", scatter_dimension=1, tiled=True
        ).astype(jnp.float32),
    )
    (
        grad_pre,
        grad_mid,
        grad_query,
        grad_key,
        grad_value,
        grad_out,
        grad_gate,
        grad_up,
        grad_down,
    ) = summed
    return (
        layer_out,
        grad_input,
        grad_pre,
        grad_mid,
        grad_query,
        grad_key,
        grad_value,
        grad_out,
        grad_gate,
        grad_up,
        grad_down,
    )


MESH_ID = pl.DeviceIdType.MESH
VMEM_BYTES = 63 * 2**20


def token_device(flip):
    return (jnp.bitwise_xor(lax.axis_index("tokens"), flip), lax.axis_index("heads"))


def remote(src, dst, send, recv, device):
    return pltpu.make_async_remote_copy(
        src_ref=src, dst_ref=dst, send_sem=send, recv_sem=recv, device_id=device, device_id_type=MESH_ID
    )


def block_of(ref, axis, index, half=None):
    size = ref.shape[axis] // 8
    start = pl.multiple_of(index * size, size)
    if axis == 0:
        if half is None:
            return ref.at[pl.ds(start, size), :]
        return ref.at[pl.ds(pl.multiple_of(start + half * (size // 2), size // 2), size // 2), :]
    if half is None:
        return ref.at[:, pl.ds(start, size)]
    rows = ref.shape[0] // 2
    return ref.at[pl.ds(half * rows, rows), pl.ds(start, size)]


class Gather:
    COPIES = 9

    def __init__(self, shard, full, axis, send, recv, local):
        self.shard, self.full, self.axis = shard, full, axis
        self.send, self.recv, self.local = send, recv, local
        self.me = lax.axis_index("tokens")

    def copy(self, slot, flip_block, flip_target, half=None):
        index = jnp.bitwise_xor(self.me, flip_block)
        src = self.shard if flip_block == 0 else block_of(self.full, self.axis, index, half)
        return remote(
            src,
            block_of(self.full, self.axis, index, half),
            self.send.at[slot],
            self.recv.at[slot],
            token_device(flip_target),
        )

    def copies(self, slot):
        return self.copy(
            slot,
            *(
                (0, 2),
                (0, 4),
                (0, 1),
                (2, 4, 0),
                (4, 2, 1),
                (2, 1),
                (4, 1),
                (6, 1, 0),
                (6, 1, 1),
            )[slot],
        )

    def own_copy(self):
        return pltpu.make_async_copy(
            self.shard, block_of(self.full, self.axis, self.me), self.local
        )

    def start(self):
        for slot in (0, 1, 2):
            self.copies(slot).start()
        self.own_copy().start()

    def relay_x(self):
        self.copies(0).wait_recv()
        self.copies(3).start()
        self.copies(5).start()

    def relay_y(self):
        self.copies(1).wait_recv()
        self.copies(4).start()
        self.copies(6).start()

    def relay(self):
        self.relay_x()
        self.relay_y()

    def finish_relay(self):
        self.copies(3).wait_recv()
        self.copies(7).start()
        self.copies(4).wait_recv()
        self.copies(8).start()

    def finish(self):
        for slot in (2, 5, 6, 7, 8):
            self.copies(slot).wait_recv()
        for slot in range(self.COPIES):
            self.copies(slot).wait_send()
        self.own_copy().wait()


class LineSum:
    FIRST, SECOND = 1, 3

    def __init__(self, term, passing, total, sems):
        self.term, self.passing, self.total, self.sems = term, passing, total, sems
        self.count = term.shape[0]
        here, tokens = lax.axis_index("heads"), lax.axis_index("tokens")
        self.inner = (here == 1) | (here == 2)
        self.mate = (tokens, jnp.where(here < 2, 1 - here, 5 - here))
        self.across = (tokens, jnp.where(self.inner, 3 - here, here))

    def out_copy(self, i):
        return remote(
            self.term.at[i], self.passing.at[i], self.sems.at[0, i], self.sems.at[1, i], self.mate
        )

    def across_copy(self, i):
        return remote(
            self.passing.at[i], self.total.at[i], self.sems.at[2, i], self.sems.at[3, i], self.across
        )

    def back_copy(self, i):
        return remote(
            self.total.at[i], self.total.at[i], self.sems.at[4, i], self.sems.at[5, i], self.mate
        )

    def add(self, out, left, right):
        out[...] = (left[...].astype(jnp.float32) + right[...].astype(jnp.float32)).astype(out.dtype)

    def step(self, now):
        now = jnp.int32(now)
        i, j = now - self.FIRST, now - self.SECOND

        @pl.when(jnp.logical_not(self.inner) & (now < self.count))
        def _():
            self.out_copy(now).start()

        @pl.when(self.inner & (i >= 0) & (i < self.count))
        def _():
            self.out_copy(i).wait_recv()
            self.add(self.passing.at[i], self.passing.at[i], self.term.at[i])
            self.across_copy(i).start()

        @pl.when(self.inner & (j >= 0) & (j < self.count))
        def _():
            self.across_copy(j).wait_recv()
            self.add(self.total.at[j], self.total.at[j], self.passing.at[j])
            self.back_copy(j).start()

    def steps(self):
        return self.count + self.SECOND

    def receive(self, i):
        @pl.when(jnp.logical_not(self.inner))
        def _():
            self.back_copy(i).wait_recv()

    def receive_all(self):
        @pl.when(jnp.logical_not(self.inner))
        def _():
            @pl.loop(0, self.count)
            def _(i):
                self.back_copy(i).wait_recv()

    def finish(self):
        @pl.when(self.inner)
        def _():
            @pl.loop(0, self.count)
            def _(i):
                self.across_copy(i).wait_send()
                self.back_copy(i).wait_send()

        @pl.when(jnp.logical_not(self.inner))
        def _():
            @pl.loop(0, self.count)
            def _(i):
                self.out_copy(i).wait_send()


def lanes(shape):
    return lax.broadcasted_iota(jnp.int32, shape, len(shape) - 1)


def turn(vectors, cos_table, sin_table):
    near = jnp.where(
        lanes(vectors.shape) % 64 < 32, pltpu.roll(vectors, 96, 1), pltpu.roll(vectors, 32, 1)
    )
    return vectors * cos_table + near * sin_table


def token_column(row):
    return jnp.broadcast_to(row, (128, row.shape[1])).T


def key_marks(column, first_id):
    lane = lanes(column.shape) % 64
    one_hot = (column - first_id).astype(jnp.int32) == lane
    return jnp.where(one_hot | ((lane >= 4) & (lane < 7)), 1.0, 0.0)


def query_marks(column, first_id):
    lane = lanes(column.shape) % 64
    other = (column - first_id).astype(jnp.int32) != lane
    return jnp.where(other & (lane < 4), -1e30, 0.0)


def nt_dot(left, right):
    return lax.dot_general(
        left, right, (((1,), (1,)), ((), ())), preferred_element_type=jnp.float32
    )


def attend_kernel(
    chain, places, x, small, key_shard, value_shard, inverse, query_shard, out_shard, gate_shard, up_shard,
    down_shard, gate_full, up_full, down_full, query_full, pair_full, out_full, attn_sum, normed_out, query_out,
    pairs, attended_out, log_out, cos_out, sin_out, small_out, small_all, query_here, pair_here, pair_shard,
    out_here, pre_row, normed, query, attended, log_total, cos_table, sin_table, key_side, value_side, marks,
    scores, peak, mixed, near_pairs, term, passing, total, small_sems, gather_sems, local_sems, pair_sems,
    chain_sems, store_sems,
):
    count = term.shape[0] // 2
    tokens = x.shape[0]
    heads = query.shape[1] // 64
    me = lax.axis_index("tokens")
    place = lax.rem(me, places)
    far = place >= 2
    greet(range(1, 8), chain)

    def small_copy(flip):
        return remote(
            small,
            small_all.at[me],
            small_sems.at[0, flip - 1],
            small_sems.at[1, flip - 1],
            token_device(flip),
        )

    def gather(k, shard, full, axis):
        return Gather(shard, full, axis, gather_sems.at[0, k], gather_sems.at[1, k], local_sems.at[k])

    gather_query = gather(0, query_shard, query_here, 0)
    gather_pair = gather(1, pair_shard, pair_here, 0)
    gather_out = gather(2, out_shard, out_here, 1)
    gate, up, down = (
        gather(3, gate_shard, gate_full, 0),
        gather(4, up_shard, up_full, 0),
        gather(5, down_shard, down_full, 1),
    )
    stores = []

    def store(src, out):
        copy = pltpu.make_async_copy(src, out, store_sems.at[len(stores)])
        copy.start()
        stores.append(copy)

    for flip in range(1, 8):
        small_copy(flip).start()
    gather_query.start()
    both = jnp.concatenate(
        [key_shard[...].astype(jnp.float32), value_shard[...].astype(jnp.float32)], axis=0
    )
    pair_shard[...] = both.T.astype(jnp.bfloat16)
    gather_pair.start()
    small_all[me] = small[...]
    x_f = x[...].astype(jnp.float32)
    pre_scale = lax.rsqrt(jnp.mean(x_f * x_f, axis=1, keepdims=True) + 1e-05)

    for flip in range(1, 8):
        small_copy(flip).wait_recv()
    store(small_all, small_out)
    width = x.shape[1] // 8
    for k in range(8):
        pre_row[:, k * width : (k + 1) * width] = jnp.broadcast_to(
            small_all[k, 1:2, :width], (8, width)
        )
    gather_query.relay()
    gather_pair.relay()
    normed[...] = (x[...].astype(jnp.float32) * pre_scale * pre_row[0:1, :]).astype(jnp.bfloat16)
    store(normed, normed_out)

    first_device = me - place
    first_id = (first_device // places * 4).astype(jnp.float32)
    own = token_column(small_all[me, 0:1, :])
    before = jnp.zeros((tokens, 1), jnp.float32)
    for k in range(places):
        others = small_all[first_device + k, 0:1, :]
        before = before + jnp.sum(
            jnp.where(others < own[:, 0:1], 1.0, 0.0), axis=1, keepdims=True
        )
        column = token_column(others)
        marks[pl.ds(k * tokens, tokens), :] = key_marks(column, first_id)
    row_index = lax.broadcasted_iota(jnp.int32, (tokens, 128), 0) + place * tokens
    turned = (row_index.astype(jnp.float32) - before) * inverse[0:1, :]
    cos_table[...] = jnp.cos(turned)
    sin_signed = jnp.sin(turned)
    sin_table[...] = jnp.where(lanes(sin_signed.shape) % 64 < 32, -sin_signed, sin_signed)
    store(cos_table, cos_out)
    store(sin_table, sin_out)
    gather_query.finish_relay()
    gather_pair.finish_relay()
    gather_out.copies(1).start()
    gather_out.copies(2).start()
    gather_out.own_copy().start()
    gather_query.finish()
    gather_pair.finish()

    made = jnp.dot(normed[...], pair_here[...], preferred_element_type=jnp.float32)
    spun = turn(made, cos_table[...], sin_table[...])
    near_pairs[place] = jnp.where(lanes(made.shape) < 64, spun, made).astype(jnp.bfloat16)

    def pair_copy(slot, flip):
        at = place - 2 if slot == 2 else place
        return remote(
            near_pairs.at[at],
            near_pairs.at[at],
            pair_sems.at[0, slot],
            pair_sems.at[1, slot],
            token_device(flip),
        )

    pair_copy(0, 1).start()

    @pl.when(jnp.logical_not(far))
    def _():
        pair_copy(1, 2).start()

    gather_out.copies(0).start()
    gate.copies(1).start()
    gate.copies(2).start()
    gate.own_copy().start()
    for low in range(0, query.shape[1], 256):
        made = jnp.dot(
            normed[...], query_here[:, low : low + 256], preferred_element_type=jnp.float32
        )
        for group in range(low, low + 256, 128):
            spun = turn(made[:, group - low : group - low + 128], cos_table[...], sin_table[...])
            query[:, group : group + 128] = (spun * 0.125).astype(jnp.bfloat16)
    store(query, query_out)
    store(query_here, query_full)
    store(pair_here, pair_full)
    pair_copy(0, 1).wait_recv()

    @pl.when(far)
    def _():
        pair_copy(1, 2).wait_recv()
        pair_copy(2, 1).start()
        pair_copy(2, 1).wait_recv()

    for k in range(places):

        @pl.when(k <= place)
        def _():
            pair = near_pairs[k].astype(jnp.float32)
            swapped = pltpu.roll(pair, 64, 1)
            lane = lanes(pair.shape)
            mark = marks[pl.ds(k * tokens, tokens), :]
            block = pl.ds(k * tokens, tokens)
            key_side[0, block] = jnp.where(lane < 64, pair, mark).astype(jnp.bfloat16)
            key_side[1, block] = jnp.where(lane < 64, mark, swapped).astype(jnp.bfloat16)
            value_side[0, block] = jnp.where(lane < 64, swapped, 1.0).astype(jnp.bfloat16)
            value_side[1, block] = jnp.where(lane < 64, 1.0, pair).astype(jnp.bfloat16)

    store(near_pairs, pairs)
    lane = lanes((tokens, 128))
    own_marks = query_marks(own, first_id)

    def side_of(head):
        at = head // 2 * 128
        mine = (lane < 64) if head % 2 == 0 else (lane >= 64)
        return jnp.where(mine, query[:, at : at + 128].astype(jnp.float32), own_marks).astype(
            jnp.bfloat16
        )

    def keys_at(k):
        return pl.ds(pl.multiple_of(k * tokens, tokens), tokens)

    def look(head, side, k, masked):
        e = head % 2
        found = nt_dot(side, key_side[e, keys_at(k)])
        if masked:
            rows = lax.broadcasted_iota(jnp.int32, found.shape, 0)
            found = jnp.where(lanes(found.shape) <= rows, found, -1e30)
        scores[e, k] = found
        best = found[:, :128]
        for part in range(128, tokens, 128):
            best = jnp.maximum(best, found[:, part : part + 128])
        peak[e] = best if masked else jnp.maximum(peak[e], best)

    def blend(head, k, first):
        e = head % 2
        parts = [
            jnp.exp(scores[e, k, :, part : part + 128] - peak[e]).astype(jnp.bfloat16)
            for part in range(0, tokens, 128)
        ]
        made = jnp.dot(
            jnp.concatenate(parts, axis=1),
            value_side[e, keys_at(k)],
            preferred_element_type=jnp.float32,
        )
        mixed[e] = made if first else mixed[e] + made

    def settle(head):
        e = head % 2
        peak[e] = jnp.broadcast_to(jnp.max(peak[e], axis=1, keepdims=True), lane.shape)

    def finish_head(head):
        e = head % 2
        mine = (lane < 64) if e == 0 else (lane >= 64)
        at = slice(head // 2 * 128, head // 2 * 128 + 128)
        out = mixed[e]
        sums = jnp.where(mine, pltpu.roll(out, 64, 1), out)
        share = out / sums
        attended[:, at] = share if e == 0 else jnp.where(lane < 64, attended[:, at], share)
        noted = peak[e] + jnp.log(sums)
        log_total[...] = noted if head == 0 else jnp.where(lane == head, noted, log_total[...])

    for head in range(heads + 1):
        side = side_of(head) if head < heads else None
        if head < heads:
            look(head, side, place, True)
        if head > 0:
            blend(head - 1, place, True)

        @pl.loop(0, place)
        def _(k):
            if head < heads:
                look(head, side, k, False)
            if head > 0:
                blend(head - 1, k, False)

        if head > 0:
            finish_head(head - 1)
        if head < heads:
            settle(head)
        if head == 2:
            gather_out.relay()
            gate.copies(0).start()
            up.copies(1).start()
            up.copies(2).start()
            up.own_copy().start()
    store(attended, attended_out)
    store(log_total, log_out)
    gather_out.finish_relay()

    gather_out.finish()
    low = attended[...].astype(jnp.bfloat16)
    each = term.shape[2]
    for k in range(0, 2 * count, 2):
        made = jnp.dot(
            low, out_here[:, k * each : (k + 2) * each], preferred_element_type=jnp.float32
        ).astype(jnp.bfloat16)
        term[k] = made[:, :each]
        term[k + 1] = made[:, each:]
    store(out_here, out_full)

    gate.relay_y()
    up.copies(0).start()
    down.start()
    line = LineSum(term, passing, total, chain_sems)
    work = {now: [] for now in range(line.steps())}
    for now, job in (
        (1, gate.relay_x),
        (4, up.relay_y),
        (8, down.relay_y),
        (9, up.relay_x),
        (11, gate.finish_relay),
        (13, down.relay_x),
        (16, up.finish_relay),
    ):
        work[now].append(job)
    for now, jobs in work.items():
        for job in jobs:
            job()
        line.step(now)
    line.receive_all()
    store(total, attn_sum)
    down.finish_relay()
    line.finish()
    for part in (gate, up, down):
        part.finish()
    for flip in range(1, 8):
        small_copy(flip).wait_send()
    pair_copy(0, 1).wait_send()

    @pl.when(far)
    def _():
        pair_copy(2, 1).wait_send()

    @pl.when(jnp.logical_not(far))
    def _():
        pair_copy(1, 2).wait_send()

    for copy in stores:
        copy.wait()


def attend(
    chain, places, x, small, key_weight, value_weight, inverse, query_weight, out_weight, gate_weight, up_weight,
    down_weight,
):
    tokens, width = x.shape
    count = 8
    heads_wide = query_weight.shape[1]
    bf16, f32 = jnp.bfloat16, jnp.float32
    row = places * tokens
    each = width // (2 * count)
    anywhere, vmem = pl.BlockSpec(memory_space=pl.ANY), pl.BlockSpec(memory_space=pltpu.VMEM)
    shape = jax.ShapeDtypeStruct
    chunks = (2 * count, tokens, each)
    out_shape = [
        shape((gate_weight.shape[0] * 8, gate_weight.shape[1]), bf16),
        shape((up_weight.shape[0] * 8, up_weight.shape[1]), bf16),
        shape((down_weight.shape[0], down_weight.shape[1] * 8), bf16),
        shape((width, heads_wide), bf16),
        shape((width, 128), bf16),
        shape((heads_wide, width), bf16),
        shape(chunks, bf16),
        shape((tokens, width), bf16),
        shape((tokens, heads_wide), bf16),
        shape((places, tokens, 128), bf16),
        shape((tokens, heads_wide), f32),
        shape((tokens, 128), f32),
        shape((tokens, 128), f32),
        shape((tokens, 128), f32),
        shape((8,) + small.shape, f32),
    ]
    return pl.pallas_call(
        functools.partial(attend_kernel, chain, places),
        out_shape=out_shape,
        in_specs=[vmem] * 5 + [anywhere] * 5,
        out_specs=[anywhere] * len(out_shape),
        scratch_shapes=[
            pltpu.VMEM((8,) + small.shape, f32),
            pltpu.VMEM((width, heads_wide), bf16),
            pltpu.VMEM((width, 128), bf16),
            pltpu.VMEM((width // 8, 128), bf16),
            pltpu.VMEM((heads_wide, width), bf16),
            pltpu.VMEM((8, width), f32),
            pltpu.VMEM((tokens, width), bf16),
            pltpu.VMEM((tokens, heads_wide), bf16),
            pltpu.VMEM((tokens, heads_wide), f32),
            pltpu.VMEM((tokens, 128), f32),
            pltpu.VMEM((tokens, 128), f32),
            pltpu.VMEM((tokens, 128), f32),
            pltpu.VMEM((2, row, 128), bf16),
            pltpu.VMEM((2, row, 128), bf16),
            pltpu.VMEM((row, 128), f32),
            pltpu.VMEM((2, places, tokens, tokens), f32),
            pltpu.VMEM((2, tokens, 128), f32),
            pltpu.VMEM((2, tokens, 128), f32),
            pltpu.VMEM((places, tokens, 128), bf16),
            pltpu.VMEM(chunks, bf16),
            pltpu.VMEM(chunks, bf16),
            pltpu.VMEM(chunks, bf16),
            pltpu.SemaphoreType.DMA((2, 7)),
            pltpu.SemaphoreType.DMA((2, 6, Gather.COPIES)),
            pltpu.SemaphoreType.DMA((6,)),
            pltpu.SemaphoreType.DMA((2, 3)),
            pltpu.SemaphoreType.DMA((6, 2 * count)),
            pltpu.SemaphoreType.DMA((len(out_shape),)),
        ],
        compiler_params=pltpu.CompilerParams(
            collective_id=0, has_side_effects=True, vmem_limit_bytes=VMEM_BYTES
        ),
        name="attend_forward",
    )(
        x, small, key_weight.T, value_weight.T, inverse, query_weight, out_weight, gate_weight, up_weight,
        down_weight,
    )


def greet(flips, chain):
    me, here = lax.axis_index("tokens"), lax.axis_index("heads")
    barrier = pltpu.get_barrier_semaphore()
    for flip in flips:
        pl.semaphore_signal(barrier, inc=1, device_id=token_device(flip), device_id_type=MESH_ID)
    for step in (-1, 1):
        near = here + step

        @pl.when((near >= 0) & (near < chain))
        def _():
            pl.semaphore_signal(barrier, inc=1, device_id=(me, near), device_id_type=MESH_ID)

    edge = (here == 0) | (here == chain - 1)

    @pl.when(edge)
    def _():
        pl.semaphore_wait(barrier, len(flips) + 1)

    @pl.when(jnp.logical_not(edge))
    def _():
        pl.semaphore_wait(barrier, len(flips) + 2)


class Reduce:
    COPIES = 6

    def __init__(self, own, near, sems):
        self.own, self.near, self.sems = own, near, sems

    def copy(self, slot):
        k, half, flip = ((1, 0, 2), (3, 0, 2), (2, 1, 4), (3, 1, 4), (2, 0, 4), (1, 1, 2))[slot]
        rows = self.own.shape[1] // 2
        return remote(
            self.own.at[k, pl.ds(half * rows, rows)],
            self.near.at[slot],
            self.sems.at[0, slot],
            self.sems.at[1, slot],
            token_device(flip),
        )

    def put(self, k, block):
        self.own[k] = block.astype(self.own.dtype)
        self.send(k)

    def send(self, k):
        for slot in {3: (1, 3), 1: (0,), 2: (2,), 0: ()}[k]:
            self.copy(slot).start()

    def add_near(self, k, half, slot):
        rows = self.own.shape[1] // 2
        place = pl.ds(half * rows, rows)
        self.own[k, place] = (
            self.own[k, place].astype(jnp.float32) + self.near[slot].astype(jnp.float32)
        ).astype(self.own.dtype)

    def second(self):
        self.copy(1).wait_recv()
        self.add_near(2, 0, 1)
        self.copy(4).start()
        self.copy(3).wait_recv()
        self.add_near(1, 1, 3)
        self.copy(5).start()

    def finish(self, out):
        rows = self.own.shape[1] // 2
        for half, slots in ((0, (0, 4)), (1, (2, 5))):
            place = pl.ds(half * rows, rows)
            total = self.own[0, place].astype(jnp.float32)
            for slot in slots:
                self.copy(slot).wait_recv()
                total = total + self.near[slot].astype(jnp.float32)
            out[place, :] = total
        for slot in range(self.COPIES):
            self.copy(slot).wait_send()


def tn_dot(left, right):
    return lax.dot_general(
        left, right, (((0,), (0,)), ((), ())), preferred_element_type=jnp.float32
    )


def tiles_of(length, size):
    return [(low, min(low + size, length)) for low in range(0, length, size)]


def feed_kernel(
    chain, x, attn_sum, small_all, cotangent, gate_full, up_full, down_full, back_attn, hidden, mlp_term,
    grad_gate, grad_up, grad_mid, gate, up, down, mid_row, normed, back_gate, back_up, term, passing, total,
    own_gate, near_gate, own_up, near_up, load_sems, swap_sems, chain_sems, reduce_sems,
):
    count = term.shape[0] // 2
    each = term.shape[2]
    tokens, width = x.shape
    inner = gate.shape[1]
    me = lax.axis_index("tokens")
    tiles = tiles_of(inner, 512)
    loads = []
    for k, (low, high) in enumerate(tiles):
        cut = pl.ds(low, high - low)
        loads.append(
            (
                pltpu.make_async_copy(gate_full.at[:, cut], gate.at[:, cut], load_sems.at[0, k]),
                pltpu.make_async_copy(up_full.at[:, cut], up.at[:, cut], load_sems.at[1, k]),
                pltpu.make_async_copy(down_full.at[cut, :], down.at[cut, :], load_sems.at[2, k]),
            )
        )
    for group in loads:
        for load in group:
            load.start()
    greet((1, 2, 4), chain)

    def swap(k, ref, cut):
        mine, theirs = pl.ds(0, tokens), pl.ds(tokens, tokens)
        return remote(
            ref.at[mine, cut],
            ref.at[theirs, cut],
            swap_sems.at[0, k],
            swap_sems.at[1, k],
            token_device(1),
        )

    span = width // 8
    for k in range(8):
        mid_row[:, k * span : (k + 1) * span] = jnp.broadcast_to(
            small_all[k, 1:2, span : 2 * span], (8, span)
        )

    def middle_at(c):
        cut = slice(c * each, (c + 1) * each)
        return x[:, cut].astype(jnp.float32) + attn_sum[c].astype(jnp.float32)

    squares = jnp.zeros((tokens, each), jnp.float32)
    for c in range(2 * count):
        part = middle_at(c)
        squares = squares + part * part
    mid_scale = lax.rsqrt(jnp.sum(squares, axis=1, keepdims=True) / width + 1e-05)
    for c in range(2 * count):
        cut = slice(c * each, (c + 1) * each)
        normed[:tokens, cut] = (middle_at(c) * mid_scale * mid_row[0:1, cut]).astype(jnp.bfloat16)
    swaps = [swap(0, normed, pl.ds(0, width))]
    swaps[0].start()

    for k, (low, high) in enumerate(tiles):
        for load in loads[k]:
            load.wait()
        gate_rows = jnp.dot(
            normed[:tokens, :], gate[:, low:high], preferred_element_type=jnp.float32
        )
        up_rows = jnp.dot(normed[:tokens, :], up[:, low:high], preferred_element_type=jnp.float32)
        back_hidden = nt_dot(cotangent[...], down[low:high, :])
        sigmoid = jax.nn.sigmoid(gate_rows)
        silu = gate_rows * sigmoid
        hidden[:, low:high] = (silu * up_rows).astype(jnp.bfloat16)
        back_gate[:tokens, low:high] = (
            back_hidden * up_rows * sigmoid * (1.0 + gate_rows * (1.0 - sigmoid))
        ).astype(jnp.bfloat16)
        back_up[:tokens, low:high] = (back_hidden * silu).astype(jnp.bfloat16)
        for j, ref in enumerate((back_gate, back_up)):
            swaps.append(swap(1 + 2 * k + j, ref, pl.ds(low, high - low)))
            swaps[-1].start()

    def mid_pair(c):
        cut = pl.ds(c * each, 2 * each)
        made = nt_dot(back_gate[:tokens, :], gate[cut, :]) + nt_dot(back_up[:tokens, :], up[cut, :])
        made = made.astype(jnp.bfloat16)
        term[c] = made[:, :each]
        term[c + 1] = made[:, each:]

    def mlp_pair(c):
        made = jnp.dot(
            hidden[...], down[:, c * each : (c + 2) * each], preferred_element_type=jnp.float32
        ).astype(jnp.bfloat16)
        pair = c // 2
        rows, low = pl.ds(pair % 4 * tokens, tokens), pair // 4 * 2 * each
        gate[rows, low : low + 2 * each] = made
        for k in range(2):
            copy = pltpu.make_async_copy(
                gate.at[rows, pl.ds(low + k * each, each)], mlp_term.at[c + k], load_sems.at[3, c + k]
            )
            copy.start()
            stores.append(copy)

    stores = []
    gate_sum = Reduce(own_gate, near_gate, reduce_sems.at[0])
    up_sum = Reduce(own_up, near_up, reduce_sems.at[1])

    def block(part, k):
        index = jnp.bitwise_xor(me, 2 * k)
        cut = pl.ds(pl.multiple_of(index * span, span), span)
        ref = back_gate if part is gate_sum else back_up
        part.put(k, tn_dot(normed[:, cut], ref[...]))

    def received(indices):
        for k in indices:
            swaps[k].wait_recv()

    pairs_of = lambda n: lambda: mid_pair(2 * n)
    grad = lambda part, *ks: lambda: [block(part, k) for k in ks]
    mlp = lambda *cs: lambda: [mlp_pair(2 * c) for c in cs]
    gates, ups = range(1, len(swaps), 2), range(2, len(swaps), 2)
    work = {now: [] for now in range(2 * count + LineSum.SECOND)}

    def plan(now, *jobs):
        work[min(now, len(work) - 1)].extend(jobs)

    for n in range(count):
        plan(max(0, 2 * n - 1), pairs_of(n))
    plan(2, lambda: received([0, *gates]), grad(gate_sum, 3))
    plan(4, grad(gate_sum, 1))
    plan(6, grad(gate_sum, 2))
    plan(7, lambda: received(ups), grad(gate_sum, 0))
    plan(8, grad(up_sum, 3))
    plan(10, grad(up_sum, 1))
    plan(12, grad(up_sum, 2))
    plan(13, grad(up_sum, 0))
    plan(14, gate_sum.second)
    for n in range(count):
        plan(14 + n // 2, mlp(n))
    plan(18, up_sum.second)
    line = LineSum(term, passing, total, chain_sems)
    for now, jobs in work.items():
        for job in jobs:
            job()
        line.step(now)
    line.receive_all()
    gate_sum.finish(grad_gate)

    weighed = jnp.zeros((tokens, each), jnp.float32)
    for c in range(2 * count):
        cut = slice(c * each, (c + 1) * each)
        back = total[c].astype(jnp.float32)
        hat = middle_at(c) * mid_scale
        weighed = weighed + back * mid_row[0:1, cut] * hat
        grad_mid[:, cut] = jnp.broadcast_to(jnp.sum(back * hat, axis=0, keepdims=True), (8, each))
    mean = jnp.sum(weighed, axis=1, keepdims=True) / width
    for c in range(2 * count):
        cut = slice(c * each, (c + 1) * each)
        u = total[c].astype(jnp.float32) * mid_row[0:1, cut]
        hat = middle_at(c) * mid_scale
        back_attn[:, cut] = (
            cotangent[:, cut].astype(jnp.float32) + mid_scale * (u - hat * mean)
        ).astype(jnp.bfloat16)
    up_sum.finish(grad_up)
    line.finish()
    for copy in swaps:
        copy.wait_send()
    for copy in stores:
        copy.wait()


def feed(chain, x, attn_sum, small_all, cotangent, gate_full, up_full, down_full):
    tokens, width = x.shape
    inner = gate_full.shape[1]
    count = attn_sum.shape[0] // 2
    span = width // 8
    bf16, f32 = jnp.bfloat16, jnp.float32
    anywhere, vmem = pl.BlockSpec(memory_space=pl.ANY), pl.BlockSpec(memory_space=pltpu.VMEM)
    shape = jax.ShapeDtypeStruct
    tiles = len(tiles_of(inner, 512))
    return pl.pallas_call(
        functools.partial(feed_kernel, chain),
        out_shape=[
            shape((tokens, width), bf16),
            shape((tokens, inner), bf16),
            shape(attn_sum.shape, bf16),
            shape((span, inner), f32),
            shape((span, inner), f32),
            shape((8, width), f32),
        ],
        in_specs=[vmem] * 4 + [anywhere] * 3,
        out_specs=[vmem, vmem, anywhere, vmem, vmem, vmem],
        scratch_shapes=[
            pltpu.VMEM((width, inner), bf16),
            pltpu.VMEM((width, inner), bf16),
            pltpu.VMEM((inner, width), bf16),
            pltpu.VMEM((8, width), f32),
            pltpu.VMEM((2 * tokens, width), bf16),
            pltpu.VMEM((2 * tokens, inner), bf16),
            pltpu.VMEM((2 * tokens, inner), bf16),
            pltpu.VMEM(attn_sum.shape, bf16),
            pltpu.VMEM(attn_sum.shape, bf16),
            pltpu.VMEM(attn_sum.shape, bf16),
            pltpu.VMEM((4, span, inner), bf16),
            pltpu.VMEM((6, span // 2, inner), bf16),
            pltpu.VMEM((4, span, inner), bf16),
            pltpu.VMEM((6, span // 2, inner), bf16),
            pltpu.SemaphoreType.DMA((4, max(tiles, 2 * count))),
            pltpu.SemaphoreType.DMA((2, 1 + 2 * tiles)),
            pltpu.SemaphoreType.DMA((6, 2 * count)),
            pltpu.SemaphoreType.DMA((2, 2, Reduce.COPIES)),
        ],
        compiler_params=pltpu.CompilerParams(
            collective_id=1, has_side_effects=True, vmem_limit_bytes=VMEM_BYTES
        ),
        name="feed_forward",
    )(x, attn_sum, small_all, cotangent, gate_full, up_full, down_full)


def split_marks(values, at):
    high = values.astype(jnp.bfloat16).astype(jnp.float32)
    rest = values - high
    middle = rest.astype(jnp.bfloat16).astype(jnp.float32)
    low = rest - middle
    return jnp.where(at == 4, high, jnp.where(at == 5, middle, jnp.where(at == 6, low, 0.0)))


def return_kernel(
    chain, places, small_all, query, pairs, log_total, cos_table, sin_table,
    mid_part, attended_in, x_in, attn_sum, back_in, query_full, pair_full, out_full, mlp_term, hidden_in, cotangent, normed_in, layer_out, grad_input, grad_down,
    grad_query, grad_key, grad_value, grad_out, gains, grad_in, in_here, out_here, key_side, value_side, query_side, back_side, back_att,
    back_rows, back_keys, back_values, pair_out, pair_near, normed, back_attn, hidden, cotangents, att_low,
    back_all, pre_row, pre_part, gains_near, mlp_sum, mlp_passing, mlp_total, term, passing, total, own_down,
    near_down, own_in, near_in, own_out, near_out, load_sems, swap_sems, pair_sems, gain_sems, chain_sems,
    reduce_sems, store_sems,
):
    count = term.shape[0] // 2
    each = term.shape[2]
    tokens, width = x_in.shape
    span = width // 8
    groups = query.shape[1] // 128
    me = lax.axis_index("tokens")
    place = lax.rem(me, places)
    first_device = me - place
    mine, theirs = pl.ds(0, tokens), pl.ds(tokens, tokens)

    def load(k, src, dst):
        copy = pltpu.make_async_copy(src, dst, load_sems.at[k])
        copy.start()
        return copy

    attended = back_rows
    load_attended = load(8 + 2 * count, attended_in, attended)
    load_back = load(6, back_in, back_attn.at[mine, :])
    load_out = load(0, out_full, out_here)
    heads_wide = query.shape[1]
    load_in = load(1, query_full, in_here.at[:, pl.ds(0, heads_wide)])
    load_pair = load(9 + 2 * count, pair_full, in_here.at[:, pl.ds(heads_wide, 128)])
    load_cot = load(2, cotangent, cotangents.at[mine, :])
    load_hidden = load(3, hidden_in, hidden.at[mine, :])
    load_normed = load(4, normed_in, normed.at[mine, :])
    load_mlp = load(5, mlp_term, mlp_sum)
    greet(range(1, 8), chain)

    def swap(k, ref):
        copy = remote(
            ref.at[mine, :],
            ref.at[theirs, :],
            swap_sems.at[0, k],
            swap_sems.at[1, k],
            token_device(1),
        )
        copy.start()
        return copy

    def gain_copy(which, src, flip):
        other = jnp.bitwise_xor(me, flip)
        return remote(
            src.at[:, pl.ds(pl.multiple_of(other * span, span), span)],
            gains_near.at[me, :, pl.ds(which * span, span)],
            gain_sems.at[0, which, flip - 1],
            gain_sems.at[1, which, flip - 1],
            token_device(flip),
        )

    for flip in range(1, 8):
        gain_copy(1, mid_part, flip).start()
    load_back.wait()
    load_attended.wait()
    att_low[mine, :] = attended[...].astype(jnp.bfloat16)
    swap_back = swap(0, back_attn)
    swap_att = swap(1, att_low)

    lane = lanes((tokens, 128))
    at = lane % 64
    first_id = (first_device // places * 4).astype(jnp.float32)
    for k in range(places):
        mark = key_marks(token_column(small_all[first_device + k, 0:1, :]), first_id)
        block = pl.ds(k * tokens, tokens)

        @pl.when(k <= place)
        def _():
            pair = pairs[k].astype(jnp.float32)
            swapped = pltpu.roll(pair, 64, 1)
            key_side[0, block] = jnp.where(lane < 64, pair, mark).astype(jnp.bfloat16)
            key_side[1, block] = jnp.where(lane < 64, mark, swapped).astype(jnp.bfloat16)
            value_side[0, block] = jnp.where(lane < 64, swapped, 1.0).astype(jnp.bfloat16)
            value_side[1, block] = jnp.where(lane < 64, 1.0, pair).astype(jnp.bfloat16)

    own_marks = query_marks(token_column(small_all[me, 0:1, :]), first_id)

    load_out.wait()
    back_att[...] = nt_dot(back_attn[mine, :], out_here[...]).astype(jnp.bfloat16)
    load_cot.wait()
    swap_cot = swap(2, cotangents)
    load_hidden.wait()
    swap_hidden = swap(3, hidden)
    for group in range(groups):
        cut = slice(group * 128, (group + 1) * 128)
        back = back_att[:, cut].astype(jnp.float32)
        both = query[:, cut].astype(jnp.float32)
        shared = back * attended[:, cut]
        for e in range(2):
            head = 2 * group + e
            used = (lane < 64) if e == 0 else (lane >= 64)
            delta = jnp.sum(jnp.where(used, shared, 0.0), axis=1, keepdims=True)
            peak = jnp.sum(jnp.where(lane == head, log_total[...], 0.0), axis=1, keepdims=True)
            back_side[head] = jnp.where(
                used, back, split_marks(jnp.broadcast_to(-delta, lane.shape), at)
            ).astype(jnp.bfloat16)
            query_side[head] = jnp.where(
                used, both, own_marks + split_marks(jnp.broadcast_to(-peak, lane.shape), at)
            ).astype(jnp.bfloat16)
    load_normed.wait()
    swap_normed = swap(4, normed)
    load_mlp.wait()
    load_in.wait()
    load_pair.wait()

    mlp_line = LineSum(mlp_sum, mlp_passing, mlp_total, chain_sems.at[0])
    back_rows[...] = jnp.zeros_like(back_rows)

    def key_step(k, diagonal):
        back_keys[...] = jnp.zeros_like(back_keys)
        back_values[...] = jnp.zeros_like(back_values)

        @pl.loop(0, groups)
        def _(group):
            cut = pl.ds(pl.multiple_of(group * 128, 128), 128)
            for low in (0, tokens // 2):
                keys_here = pl.ds(pl.multiple_of(k * tokens + low, tokens // 2), tokens // 2)
                part = pl.ds(low, tokens // 2)
                first = low if diagonal else 0
                seen = pl.ds(first, tokens - first)
                rows = []
                for e in range(2):
                    head = 2 * group + e
                    found = nt_dot(key_side[e, keys_here], query_side[head, seen])
                    chances = jnp.exp(found)
                    if diagonal:
                        keys = lax.broadcasted_iota(jnp.int32, found.shape, 0) + (low - first)
                        chances = jnp.where(keys <= lanes(found.shape), chances, 0.0)
                    moved = chances * nt_dot(value_side[e, keys_here], back_side[head, seen])
                    chances = chances.astype(jnp.bfloat16)
                    moved = moved.astype(jnp.bfloat16)
                    back_values[e, part] += jnp.dot(
                        chances, back_att[seen, cut], preferred_element_type=jnp.float32
                    )
                    back_keys[e, part] += jnp.dot(
                        moved, query[seen, cut], preferred_element_type=jnp.float32
                    )
                    rows.append(tn_dot(moved, key_side[e, keys_here]))
                back_rows[seen, cut] += jnp.where(lanes(rows[0].shape) < 64, rows[0], rows[1])

            mlp_line.step(groups * k + group)

        keys = back_keys[0] + pltpu.roll(back_keys[1], 64, 1)
        values = pltpu.roll(back_values[0], 64, 1) + back_values[1]
        return jnp.where(lane < 64, keys, values)

    def pair_copy(source, target):
        return remote(
            pair_out.at[target],
            pair_near.at[source],
            pair_sems.at[0, target],
            pair_sems.at[1, source],
            (first_device + target, lax.axis_index("heads")),
        )

    @pl.loop(0, place)
    def _(k):
        pair_out[k] = key_step(k, False).astype(jnp.bfloat16)
        pair_copy(place, k).start()

    own_pair = key_step(place, True)
    pair_out[place] = own_pair.astype(jnp.bfloat16)
    early = groups * places

    @pl.loop(groups * (place + 1), early)
    def _(now):
        mlp_line.step(now)

    for group in range(groups):
        cut = slice(group * 128, (group + 1) * 128)
        back_all[mine, cut] = (
            turn(back_rows[:, cut], cos_table[...], -sin_table[...]) * 0.125
        ).astype(jnp.bfloat16)
    back_keys[0] = own_pair
    for k in range(1, places):

        @pl.when(k > place)
        def _():
            remote(
                pair_out.at[k],
                pair_near.at[k],
                pair_sems.at[0, k],
                pair_sems.at[1, k],
                (first_device + k, lax.axis_index("heads")),
            ).wait_recv()
            back_keys[0] += pair_near[k].astype(jnp.float32)

    summed = back_keys[0]
    spun = turn(summed, cos_table[...], -sin_table[...])
    back_all[mine, pl.ds(groups * 128, 128)] = jnp.where(lane < 64, spun, summed).astype(
        jnp.bfloat16
    )
    swap_all = swap(5, back_all)

    def pre_pair(c):
        cut = pl.ds(c * each, 2 * each)
        made = nt_dot(back_all[mine, :], in_here[cut, :]).astype(jnp.bfloat16)
        term[c] = made[:, :each]
        term[c + 1] = made[:, each:]

    def cut_of(k):
        index = jnp.bitwise_xor(me, 2 * k)
        return pl.ds(pl.multiple_of(index * span, span), span)

    down_sum = Reduce(own_down, near_down, reduce_sems.at[0])
    in_sum = Reduce(own_in, near_in, reduce_sems.at[1])
    out_sum = Reduce(own_out, near_out, reduce_sems.at[2])

    def down_block(k):
        for low, high in tiles_of(hidden.shape[1], 512):
            own_down[k, low:high] = tn_dot(hidden[:, low:high], cotangents[:, cut_of(k)]).astype(
                own_down.dtype
            )
        down_sum.send(k)

    def in_block(k):
        in_sum.put(k, tn_dot(normed[:, cut_of(k)], back_all[...]))

    def out_block(k):
        out_sum.put(k, tn_dot(att_low[...], back_attn[:, cut_of(k)]))

    def late_loads():
        copies = [pltpu.make_async_copy(x_in, cotangents.at[theirs, :], load_sems.at[7])]
        for c in range(2 * count):
            copies.append(
                pltpu.make_async_copy(
                    attn_sum.at[c],
                    cotangents.at[mine, pl.ds(c * each, each)],
                    load_sems.at[8 + c],
                )
            )
        return copies

    def load_late():
        swap_cot.wait_send()
        for copy in late_loads():
            copy.start()

    def x_at(c):
        return cotangents[theirs, c * each : (c + 1) * each].astype(jnp.float32)

    def middle_at(c):
        return x_at(c) + cotangents[mine, c * each : (c + 1) * each].astype(jnp.float32)

    stores = []

    def store(c, src, out):
        copy = pltpu.make_async_copy(
            src.at[c], out.at[:, pl.ds(c * each, each)], store_sems.at[len(stores)]
        )
        copy.start()
        stores.append(copy)

    def finish_mlp():
        mlp_line.receive_all()
        mlp_line.finish()
        for copy in late_loads():
            copy.wait()
        for c in range(2 * count):
            mlp_sum[c] = (middle_at(c) + mlp_total[c].astype(jnp.float32)).astype(jnp.bfloat16)
            store(c, mlp_sum, layer_out)

    def scale_rows():
        for k in range(8):
            pre_row[:, k * span : (k + 1) * span] = jnp.broadcast_to(
                small_all[k, 1:2, :span], (8, span)
            )

    steps = 2 * count + LineSum.SECOND
    work = {now: [] for now in range(steps)}

    def plan(now, *jobs):
        work[min(now, steps - 1)].extend(jobs)

    pre = lambda n: lambda: pre_pair(2 * n)
    blocks = lambda make, *ks: lambda: [make(k) for k in ks]
    received = lambda *copies: lambda: [copy.wait_recv() for copy in copies]
    for n in range(count):
        plan(max(0, 2 * n - 1), pre(n))
    plan(2, received(swap_cot, swap_hidden), blocks(down_block, 3))
    plan(3, blocks(down_block, 1))
    plan(4, blocks(down_block, 2))
    plan(5, blocks(down_block, 0), load_late)
    plan(6, received(swap_back, swap_att), blocks(out_block, 3, 1))
    plan(7, blocks(out_block, 2, 0))
    plan(8, received(swap_normed, swap_all), blocks(in_block, 3, 1))
    plan(9, blocks(in_block, 2, 0))
    plan(10, down_sum.second)
    plan(12, finish_mlp)
    plan(13, out_sum.second)
    plan(14, in_sum.second, scale_rows)
    plan(16, lambda: down_sum.finish(grad_down))
    plan(17, lambda: out_sum.finish(grad_out))
    line = LineSum(term, passing, total, chain_sems.at[1])
    for now, jobs in work.items():
        for job in jobs:
            job()
        if early + now < steps:
            mlp_line.step(early + now)
        line.step(now)
    line.receive_all()
    line.finish()

    squares = jnp.zeros((tokens, each), jnp.float32)
    for c in range(2 * count):
        part = x_at(c)
        squares = squares + part * part
    pre_scale = lax.rsqrt(jnp.sum(squares, axis=1, keepdims=True) / width + 1e-05)
    weighed = jnp.zeros((tokens, each), jnp.float32)
    for c in range(2 * count):
        cut = slice(c * each, (c + 1) * each)
        back = total[c].astype(jnp.float32)
        hat = x_at(c) * pre_scale
        weighed = weighed + back * pre_row[0:1, cut] * hat
        pre_part[:, cut] = jnp.broadcast_to(jnp.sum(back * hat, axis=0, keepdims=True), (8, each))
    for flip in range(1, 8):
        gain_copy(0, pre_part, flip).start()
    mean = jnp.sum(weighed, axis=1, keepdims=True) / width
    for c in range(2 * count):
        cut = slice(c * each, (c + 1) * each)
        u = total[c].astype(jnp.float32) * pre_row[0:1, cut]
        hat = x_at(c) * pre_scale
        term[c] = (
            back_attn[mine, cut].astype(jnp.float32) + pre_scale * (u - hat * mean)
        ).astype(jnp.bfloat16)
        store(c, term, grad_input)
    in_sum.finish(grad_in)
    grad_query[...] = grad_in[:, :heads_wide]
    pair_back = grad_in[:, heads_wide:].T
    grad_key[...] = pair_back[:64]
    grad_value[...] = pair_back[64:]
    own = pl.ds(pl.multiple_of(me * span, span), span)
    gains_near[me, :, :span] = pre_part[:, own]
    gains_near[me, :, span:] = mid_part[:, own]
    for flip in range(1, 8):
        for which, src in enumerate((pre_part, mid_part)):
            gain_copy(which, src, flip).wait_recv()
    gains[...] = jnp.sum(gains_near[...], axis=0)
    for flip in range(1, 8):
        for which, src in enumerate((pre_part, mid_part)):
            gain_copy(which, src, flip).wait_send()
    for copy in (swap_back, swap_att, swap_hidden, swap_normed, swap_all):
        copy.wait_send()

    @pl.loop(0, place)
    def _(k):
        pair_copy(place, k).wait_send()

    for copy in stores:
        copy.wait()


def way_back(
    chain, places, x, attn_sum, small_all, back_attn, query, pairs, attended, log_total, cos_table, sin_table,
    mid_part, query_full, pair_full, out_full, mlp_term, hidden, cotangent, normed,
):
    tokens, width = x.shape
    inner = hidden.shape[1]
    heads_wide = query.shape[1]
    wide = heads_wide + 128
    chunks = attn_sum.shape
    count = chunks[0] // 2
    span = width // 8
    row = places * tokens
    bf16, f32 = jnp.bfloat16, jnp.float32
    anywhere, vmem = pl.BlockSpec(memory_space=pl.ANY), pl.BlockSpec(memory_space=pltpu.VMEM)
    shape = jax.ShapeDtypeStruct
    return pl.pallas_call(
        functools.partial(return_kernel, chain, places),
        out_shape=[
            shape((tokens, width), bf16),
            shape((tokens, width), bf16),
            shape((inner, span), f32),
            shape((span, heads_wide), f32),
            shape((64, span), f32),
            shape((64, span), f32),
            shape((heads_wide, span), f32),
            shape((8, 2 * span), f32),
        ],
        in_specs=[vmem] * 7 + [anywhere] * 11,
        out_specs=[anywhere] * 2 + [vmem] * 6,
        scratch_shapes=[
            pltpu.VMEM((span, wide), f32),
            pltpu.VMEM((width, wide), bf16),
            pltpu.VMEM((heads_wide, width), bf16),
            pltpu.VMEM((2, row, 128), bf16),
            pltpu.VMEM((2, row, 128), bf16),
            pltpu.VMEM((heads_wide // 64, tokens, 128), bf16),
            pltpu.VMEM((heads_wide // 64, tokens, 128), bf16),
            pltpu.VMEM((tokens, heads_wide), bf16),
            pltpu.VMEM((tokens, heads_wide), f32),
            pltpu.VMEM((2, tokens, 128), f32),
            pltpu.VMEM((2, tokens, 128), f32),
            pltpu.VMEM((places, tokens, 128), bf16),
            pltpu.VMEM((places, tokens, 128), bf16),
            pltpu.VMEM((2 * tokens, width), bf16),
            pltpu.VMEM((2 * tokens, width), bf16),
            pltpu.VMEM((2 * tokens, inner), bf16),
            pltpu.VMEM((2 * tokens, width), bf16),
            pltpu.VMEM((2 * tokens, heads_wide), bf16),
            pltpu.VMEM((2 * tokens, wide), bf16),
            pltpu.VMEM((8, width), f32),
            pltpu.VMEM((8, width), f32),
            pltpu.VMEM((8, 8, 2 * span), f32),
            pltpu.VMEM(chunks, bf16),
            pltpu.VMEM(chunks, bf16),
            pltpu.VMEM(chunks, bf16),
            pltpu.VMEM(chunks, bf16),
            pltpu.VMEM(chunks, bf16),
            pltpu.VMEM(chunks, bf16),
            pltpu.VMEM((4, inner, span), bf16),
            pltpu.VMEM((6, inner // 2, span), bf16),
            pltpu.VMEM((4, span, wide), bf16),
            pltpu.VMEM((6, span // 2, wide), bf16),
            pltpu.VMEM((4, heads_wide, span), bf16),
            pltpu.VMEM((6, heads_wide // 2, span), bf16),
            pltpu.SemaphoreType.DMA((10 + 2 * count,)),
            pltpu.SemaphoreType.DMA((2, 6)),
            pltpu.SemaphoreType.DMA((2, places)),
            pltpu.SemaphoreType.DMA((2, 2, 7)),
            pltpu.SemaphoreType.DMA((2, 6, 2 * count)),
            pltpu.SemaphoreType.DMA((3, 2, Reduce.COPIES)),
            pltpu.SemaphoreType.DMA((4 * count,)),
        ],
        compiler_params=pltpu.CompilerParams(
            collective_id=2, has_side_effects=True, vmem_limit_bytes=VMEM_BYTES
        ),
        name="way_back",
    )(
        small_all, query, pairs, log_total, cos_table, sin_table,
        mid_part, attended, x, attn_sum, back_attn, query_full, pair_full, out_full, mlp_term, hidden, cotangent, normed,
    )


def shards_cube(
    chain,
    inputs,
    segments,
    pre_gain,
    mid_gain,
    query_weight,
    key_weight,
    value_weight,
    out_weight,
    gate_weight,
    up_weight,
    down_weight,
    cotangent,
):
    row_count = inputs.shape[0]
    head_size = key_weight.shape[1]
    query_width = query_weight.shape[1]
    heads_here = query_width // head_size
    places = ROW // row_count
    half = row_count // 2
    gains = jnp.pad(pre_gain.astype(jnp.float32), (0, half)) + jnp.pad(
        mid_gain.astype(jnp.float32), (half, 0)
    )
    sublane = lax.broadcasted_iota(jnp.int32, (8, row_count), 0)
    small = jnp.where(
        sublane == 0, segments.astype(jnp.float32)[None], jnp.where(sublane == 1, gains[None], 0.0)
    )
    half_size = head_size // 2
    inverse = 10000.0 ** (-np.arange(half_size, dtype=np.float32) / half_size)
    inverse = jnp.asarray(np.tile(inverse.astype(np.float32), (8, 128 // half_size)))
    (
        gate_full,
        up_full,
        down_full,
        query_full,
        pair_full,
        out_full,
        attn_sum,
        normed,
        query_rot,
        pairs,
        attended,
        log_total,
        cos_wide,
        sin_wide,
        small_full,
    ) = attend(
        chain,
        places,
        inputs,
        small,
        key_weight,
        value_weight,
        inverse,
        query_weight,
        out_weight,
        gate_weight,
        up_weight,
        down_weight,
    )
    back_attn, hidden, mlp_term, grad_gate, grad_up, grad_mid = feed(
        chain, inputs, attn_sum, small_full, cotangent, gate_full, up_full, down_full
    )
    layer_out, grad_input, grad_down, grad_query, grad_key, grad_value, grad_out, gains = way_back(
        chain,
        places,
        inputs,
        attn_sum,
        small_full,
        back_attn,
        query_rot,
        pairs,
        attended,
        log_total,
        cos_wide,
        sin_wide,
        grad_mid,
        query_full,
        pair_full,
        out_full,
        mlp_term,
        hidden,
        cotangent,
        normed,
    )
    grad_pre, grad_mid = jnp.split(gains[0], 2)
    grad_key, grad_value = grad_key.T, grad_value.T
    return (
        layer_out,
        grad_input,
        grad_pre,
        grad_mid,
        grad_query,
        grad_key,
        grad_value,
        grad_out,
        grad_gate,
        grad_up,
        grad_down,
    )


def solution(mesh):
    sizes = dict(mesh.shape)
    plan = shards_any
    if sizes["tokens"] == 8 and sizes["heads"] == 4:
        plan = functools.partial(shards_cube, sizes["heads"])
    return jax.shard_map(
        plan,
        mesh=mesh,
        in_specs=(
            P("tokens", None),
            P("tokens"),
            P("tokens"),
            P("tokens"),
            P("tokens", "heads"),
            P("tokens", "heads"),
            P("tokens", "heads"),
            P("heads", "tokens"),
            P("tokens", "heads"),
            P("tokens", "heads"),
            P("heads", "tokens"),
            P("tokens", None),
        ),
        out_specs=(
            P("tokens", None),
            P("tokens", None),
            P("tokens"),
            P("tokens"),
            P("tokens", "heads"),
            P("tokens", "heads"),
            P("tokens", "heads"),
            P("heads", "tokens"),
            P("tokens", "heads"),
            P("tokens", "heads"),
            P("heads", "tokens"),
        ),
        check_vma=False,
    )
```

```python
import functools
import math

import jax
import jax.numpy as jnp
import numpy as np
from jax import lax
from jax.experimental import pallas as pl
from jax.experimental.pallas import tpu as pltpu
from jax.sharding import PartitionSpec as P

ROW = 2048


def rms_scale(vectors):
    return lax.rsqrt(jnp.mean(vectors * vectors, axis=-1, keepdims=True) + 1e-05)


def rotate(vectors, cos_table, sin_table):
    middle_index = vectors.shape[-1] // 2
    former = vectors[..., :middle_index]
    latter = vectors[..., middle_index:]
    return jnp.concatenate(
        [former * cos_table - latter * sin_table, latter * cos_table + former * sin_table], axis=-1
    )


def unrotate(gradient, cos_table, sin_table):
    middle_index = gradient.shape[-1] // 2
    former = gradient[..., :middle_index]
    latter = gradient[..., middle_index:]
    return jnp.concatenate(
        [former * cos_table + latter * sin_table, latter * cos_table - former * sin_table], axis=-1
    )


def norm_back(gradient, vectors, scale_rows, gain_row):
    shaped = vectors * scale_rows
    weighted = gradient * gain_row
    back_vectors = scale_rows * (
        weighted - shaped * jnp.mean(weighted * shaped, axis=-1, keepdims=True)
    )
    return (back_vectors, jnp.sum(gradient * shaped, axis=0))


def shards_any(
    inputs,
    segments,
    pre_gain,
    mid_gain,
    query_weight,
    key_weight,
    value_weight,
    out_weight,
    gate_weight,
    up_weight,
    down_weight,
    cotangent,
):
    row_count = inputs.shape[0]
    head_size = key_weight.shape[1]
    heads_here = query_weight.shape[1] // head_size
    myself = lax.axis_index("tokens")
    gathered = (
        lax.all_gather(pre_gain, "tokens", axis=0, tiled=True),
        lax.all_gather(mid_gain, "tokens", axis=0, tiled=True),
        lax.all_gather(query_weight, "tokens", axis=0, tiled=True),
        lax.all_gather(key_weight, "tokens", axis=0, tiled=True),
        lax.all_gather(value_weight, "tokens", axis=0, tiled=True),
        lax.all_gather(out_weight, "tokens", axis=1, tiled=True),
        lax.all_gather(gate_weight, "tokens", axis=0, tiled=True),
        lax.all_gather(up_weight, "tokens", axis=0, tiled=True),
        lax.all_gather(down_weight, "tokens", axis=1, tiled=True),
    )
    (
        pre_full,
        mid_full,
        query_full,
        key_full,
        value_full,
        out_full,
        gate_full,
        up_full,
        down_full,
    ) = gathered
    pre_row = pre_full.astype(jnp.float32)
    mid_row = mid_full.astype(jnp.float32)
    all_ids = lax.all_gather(segments, "tokens", axis=0, tiled=True)
    length = all_ids.shape[0]
    places = jnp.arange(length, dtype=jnp.int32)
    starts_here = jnp.concatenate([jnp.ones((1,), dtype=jnp.bool_), all_ids[1:] != all_ids[:-1]])
    opening = lax.cummax(jnp.where(starts_here, places, 0), axis=0)
    own_first = myself * row_count
    positions = lax.dynamic_slice_in_dim(places - opening, own_first, row_count)
    own_places = own_first + jnp.arange(row_count, dtype=jnp.int32)
    half_size = head_size // 2
    inverse = 10000.0 ** (-jnp.arange(half_size, dtype=jnp.float32) / half_size)
    turned = positions.astype(jnp.float32)[:, None] * inverse[None, :]
    cos_table = jnp.cos(turned)[:, None, :]
    sin_table = jnp.sin(turned)[:, None, :]
    inputs_f = inputs.astype(jnp.float32)
    pre_scale = rms_scale(inputs_f)
    normed = (inputs_f * pre_scale * pre_row).astype(jnp.bfloat16)
    queries = jnp.dot(normed, query_full, preferred_element_type=jnp.float32).reshape(
        row_count, heads_here, head_size
    )
    query_rot = (rotate(queries, cos_table, sin_table) * head_size ** (-0.5)).astype(jnp.bfloat16)
    key_rows = jnp.dot(normed, key_full, preferred_element_type=jnp.float32)[:, None, :]
    key_rot = rotate(key_rows, cos_table, sin_table)[:, 0, :].astype(jnp.bfloat16)
    value_low = jnp.dot(normed, value_full, preferred_element_type=jnp.float32).astype(jnp.bfloat16)
    key_all, value_all = (
        lax.all_gather(key_rot, "tokens", axis=0, tiled=True),
        lax.all_gather(value_low, "tokens", axis=0, tiled=True),
    )
    span = math.gcd(ROW, 1024)
    row_start = own_first // ROW * ROW
    block_first = row_start // span
    block_total = (own_first + row_count + span - 1) // span

    def key_block(block_index):
        opening_row = block_index * span
        block_keys = lax.dynamic_slice_in_dim(key_all, opening_row, span)
        block_values = lax.dynamic_slice_in_dim(value_all, opening_row, span)
        block_ids = lax.dynamic_slice_in_dim(all_ids, opening_row, span)
        block_places = opening_row + jnp.arange(span, dtype=jnp.int32)
        allowed = (segments[:, None] == block_ids[None, :]) & (
            own_places[:, None] >= block_places[None, :]
        )
        scores = jnp.einsum(
            "qhd,kd->qhk", query_rot, block_keys, preferred_element_type=jnp.float32
        )
        return (opening_row, block_keys, block_values, allowed[:, None, :], scores)

    def forward_step(block_index, state_now):
        row_peak, row_total, running = state_now
        opening_row, block_keys, block_values, allowed, scores = key_block(block_index)
        new_peak = jnp.maximum(row_peak, jnp.max(jnp.where(allowed, scores, -1e30), axis=-1))
        factor = jnp.exp(row_peak - new_peak)
        weights = jnp.where(allowed, jnp.exp(scores - new_peak[..., None]), 0.0)
        row_total = row_total * factor + jnp.sum(weights, axis=-1)
        running = running * factor[..., None] + jnp.einsum(
            "qhk,kd->qhd",
            weights.astype(jnp.bfloat16),
            block_values,
            preferred_element_type=jnp.float32,
        )
        return (new_peak, row_total, running)

    start_state = (
        jnp.full((row_count, heads_here), -1e30, jnp.float32),
        jnp.zeros((row_count, heads_here), jnp.float32),
        jnp.zeros((row_count, heads_here, head_size), jnp.float32),
    )
    row_peak, row_total, running = lax.fori_loop(
        block_first, block_total, forward_step, start_state
    )
    attended = running / row_total[..., None]
    log_total = row_peak + jnp.log(row_total)
    attended_low = attended.astype(jnp.bfloat16).reshape(row_count, heads_here * head_size)
    attn_term = jnp.dot(attended_low, out_full, preferred_element_type=jnp.float32)
    middle = inputs_f + lax.psum(attn_term.astype(jnp.bfloat16), "heads").astype(jnp.float32)
    mid_scale = rms_scale(middle)
    normed_mid = (middle * mid_scale * mid_row).astype(jnp.bfloat16)
    gate_rows = jnp.dot(normed_mid, gate_full, preferred_element_type=jnp.float32)
    up_rows = jnp.dot(normed_mid, up_full, preferred_element_type=jnp.float32)
    sigmoid_rows = jax.nn.sigmoid(gate_rows)
    silu_rows = gate_rows * sigmoid_rows
    hidden = (silu_rows * up_rows).astype(jnp.bfloat16)
    mlp_term = jnp.dot(hidden, down_full, preferred_element_type=jnp.float32)
    layer_out = (
        middle + lax.psum(mlp_term.astype(jnp.bfloat16), "heads").astype(jnp.float32)
    ).astype(jnp.bfloat16)
    grad_down = jnp.einsum("tf,td->fd", hidden, cotangent, preferred_element_type=jnp.float32)
    back_hidden = jnp.einsum("td,fd->tf", cotangent, down_full, preferred_element_type=jnp.float32)
    back_gate = (
        back_hidden * up_rows * sigmoid_rows * (1.0 + gate_rows * (1.0 - sigmoid_rows))
    ).astype(jnp.bfloat16)
    back_up = (back_hidden * silu_rows).astype(jnp.bfloat16)
    grad_gate = jnp.einsum("tc,tf->cf", normed_mid, back_gate, preferred_element_type=jnp.float32)
    grad_up = jnp.einsum("tc,tf->cf", normed_mid, back_up, preferred_element_type=jnp.float32)
    mid_term = jnp.einsum(
        "tf,cf->tc", back_gate, gate_full, preferred_element_type=jnp.float32
    ) + jnp.einsum("tf,cf->tc", back_up, up_full, preferred_element_type=jnp.float32)
    back_normed_mid = lax.psum(mid_term.astype(jnp.bfloat16), "heads").astype(jnp.float32)
    back_middle, grad_mid = norm_back(back_normed_mid, middle, mid_scale, mid_row)
    back_middle = back_middle + cotangent.astype(jnp.float32)
    back_attn = back_middle.astype(jnp.bfloat16)
    grad_out = jnp.einsum("tc,td->cd", attended_low, back_attn, preferred_element_type=jnp.float32)
    back_attended = (
        jnp.einsum("td,cd->tc", back_attn, out_full, preferred_element_type=jnp.float32)
        .astype(jnp.bfloat16)
        .reshape(row_count, heads_here, head_size)
    )
    row_delta = jnp.sum(back_attended.astype(jnp.float32) * attended, axis=-1)

    def backward_step(block_index, state_now):
        back_rows, back_pairs = state_now
        opening_row, block_keys, block_values, allowed, scores = key_block(block_index)
        chances = jnp.where(allowed, jnp.exp(scores - log_total[..., None]), 0.0)
        back_values = jnp.einsum(
            "qhk,qhd->kd",
            chances.astype(jnp.bfloat16),
            back_attended,
            preferred_element_type=jnp.float32,
        )
        back_chances = jnp.einsum(
            "qhd,kd->qhk", back_attended, block_values, preferred_element_type=jnp.float32
        )
        back_scores = (chances * (back_chances - row_delta[..., None])).astype(jnp.bfloat16)
        back_rows = back_rows + jnp.einsum(
            "qhk,kd->qhd", back_scores, block_keys, preferred_element_type=jnp.float32
        )
        back_keys = jnp.einsum(
            "qhk,qhd->kd", back_scores, query_rot, preferred_element_type=jnp.float32
        )
        old_piece = lax.dynamic_slice_in_dim(back_pairs, opening_row, span)
        fresh_piece = old_piece + jnp.concatenate([back_keys, back_values], axis=-1)
        back_pairs = lax.dynamic_update_slice_in_dim(back_pairs, fresh_piece, opening_row, 0)
        return (back_rows, back_pairs)

    start_back = (
        jnp.zeros((row_count, heads_here, head_size), jnp.float32),
        jnp.zeros((length, 2 * head_size), jnp.float32),
    )
    back_rows, back_pairs = lax.fori_loop(block_first, block_total, backward_step, start_back)
    own_pairs = lax.psum_scatter(
        back_pairs.astype(jnp.bfloat16), "tokens", scatter_dimension=0, tiled=True
    ).astype(jnp.float32)
    back_query = (
        (unrotate(back_rows, cos_table, sin_table) * head_size ** (-0.5))
        .astype(jnp.bfloat16)
        .reshape(row_count, heads_here * head_size)
    )
    back_key = unrotate(own_pairs[:, None, :head_size], cos_table, sin_table)[:, 0, :].astype(
        jnp.bfloat16
    )
    back_value = own_pairs[:, head_size:].astype(jnp.bfloat16)
    grad_query = jnp.einsum("tc,tq->cq", normed, back_query, preferred_element_type=jnp.float32)
    grad_key = jnp.einsum("tc,tq->cq", normed, back_key, preferred_element_type=jnp.float32)
    grad_value = jnp.einsum("tc,tq->cq", normed, back_value, preferred_element_type=jnp.float32)
    pre_term = jnp.einsum("tq,cq->tc", back_query, query_full, preferred_element_type=jnp.float32)
    pre_term = pre_term + jnp.einsum(
        "tq,cq->tc", back_key, key_full, preferred_element_type=jnp.float32
    )
    pre_term = pre_term + jnp.einsum(
        "tq,cq->tc", back_value, value_full, preferred_element_type=jnp.float32
    )
    back_normed = lax.psum(pre_term.astype(jnp.bfloat16), "heads").astype(jnp.float32)
    back_inputs, grad_pre = norm_back(back_normed, inputs_f, pre_scale, pre_row)
    grad_input = (back_middle + back_inputs).astype(jnp.bfloat16)
    summed = (
        lax.psum_scatter(
            grad_pre.astype(jnp.bfloat16), "tokens", scatter_dimension=0, tiled=True
        ).astype(jnp.float32),
        lax.psum_scatter(
            grad_mid.astype(jnp.bfloat16), "tokens", scatter_dimension=0, tiled=True
        ).astype(jnp.float32),
        lax.psum_scatter(
            grad_query.astype(jnp.bfloat16), "tokens", scatter_dimension=0, tiled=True
        ).astype(jnp.float32),
        lax.psum_scatter(
            grad_key.astype(jnp.bfloat16), "tokens", scatter_dimension=0, tiled=True
        ).astype(jnp.float32),
        lax.psum_scatter(
            grad_value.astype(jnp.bfloat16), "tokens", scatter_dimension=0, tiled=True
        ).astype(jnp.float32),
        lax.psum_scatter(
            grad_out.astype(jnp.bfloat16), "tokens", scatter_dimension=1, tiled=True
        ).astype(jnp.float32),
        lax.psum_scatter(
            grad_gate.astype(jnp.bfloat16), "tokens", scatter_dimension=0, tiled=True
        ).astype(jnp.float32),
        lax.psum_scatter(
            grad_up.astype(jnp.bfloat16), "tokens", scatter_dimension=0, tiled=True
        ).astype(jnp.float32),
        lax.psum_scatter(
            grad_down.astype(jnp.bfloat16), "tokens", scatter_dimension=1, tiled=True
        ).astype(jnp.float32),
    )
    (
        grad_pre,
        grad_mid,
        grad_query,
        grad_key,
        grad_value,
        grad_out,
        grad_gate,
        grad_up,
        grad_down,
    ) = summed
    return (
        layer_out,
        grad_input,
        grad_pre,
        grad_mid,
        grad_query,
        grad_key,
        grad_value,
        grad_out,
        grad_gate,
        grad_up,
        grad_down,
    )


MESH_ID = pl.DeviceIdType.MESH
VMEM_BYTES = 63 * 2**20


def token_device(flip):
    return (jnp.bitwise_xor(lax.axis_index("tokens"), flip), lax.axis_index("heads"))


def remote(src, dst, send, recv, device):
    return pltpu.make_async_remote_copy(
        src_ref=src, dst_ref=dst, send_sem=send, recv_sem=recv, device_id=device, device_id_type=MESH_ID
    )


def block_of(ref, axis, index, half=None, part=(0, 1)):
    size = ref.shape[axis] // 8
    start = pl.multiple_of(index * size, size)
    if axis == 0:
        rows = size // part[1]
        start = pl.multiple_of(start + part[0] * rows, rows)
        if half is None:
            return ref.at[pl.ds(start, rows), :]
        rows //= 2
        return ref.at[pl.ds(pl.multiple_of(start + half * rows, rows), rows), :]
    if half is None:
        return ref.at[:, pl.ds(start, size)]
    rows = ref.shape[0] // 2
    return ref.at[pl.ds(half * rows, rows), pl.ds(start, size)]


def in_order(job):
    @pl.when(lax.axis_index("tokens") >= 0)
    def _():
        job()


class Gather:
    COPIES = 9

    def __init__(self, shard, full, axis, send, recv, local, part=(0, 1)):
        self.shard, self.full, self.axis, self.part = shard, full, axis, part
        self.send, self.recv, self.local = send, recv, local
        self.me = lax.axis_index("tokens")

    def copy(self, slot, flip_block, flip_target, half=None):
        index = jnp.bitwise_xor(self.me, flip_block)
        place = block_of(self.full, self.axis, index, half, self.part)
        return remote(
            self.shard if flip_block == 0 else place,
            place,
            self.send.at[slot],
            self.recv.at[slot],
            token_device(flip_target),
        )

    def copies(self, slot):
        return self.copy(
            slot,
            *(
                (0, 2),
                (0, 4),
                (0, 1),
                (2, 4, 0),
                (4, 2, 1),
                (2, 1),
                (4, 1),
                (6, 1, 0),
                (6, 1, 1),
            )[slot],
        )

    def own_copy(self):
        return pltpu.make_async_copy(
            self.shard, block_of(self.full, self.axis, self.me, None, self.part), self.local
        )

    def start(self):
        def job():
            for slot in (0, 1, 2):
                self.copies(slot).start()
            self.own_copy().start()

        in_order(job)

    def relay_x(self):
        def job():
            self.copies(0).wait_recv()
            self.copies(3).start()
            self.copies(5).start()

        in_order(job)

    def relay_y(self):
        def job():
            self.copies(1).wait_recv()
            self.copies(4).start()
            self.copies(6).start()

        in_order(job)

    def relay(self):
        self.relay_x()
        self.relay_y()

    def finish_relay(self):
        def job():
            self.copies(3).wait_recv()
            self.copies(7).start()
            self.copies(4).wait_recv()
            self.copies(8).start()

        in_order(job)

    def finish(self):
        def job():
            for slot in (2, 5, 6, 7, 8):
                self.copies(slot).wait_recv()
            for slot in range(self.COPIES):
                self.copies(slot).wait_send()
            self.own_copy().wait()

        in_order(job)


class LineSum:
    FIRST, SECOND = 1, 3

    def __init__(self, term, passing, total, sems, parts=1):
        self.term, self.passing, self.total, self.sems = term, passing, total, sems
        self.parts, self.blocks = parts, term.shape[0]
        self.count = self.blocks * parts
        here, tokens = lax.axis_index("heads"), lax.axis_index("tokens")
        self.inner = (here == 1) | (here == 2)
        self.mate = (tokens, jnp.where(here < 2, 1 - here, 5 - here))
        self.across = (tokens, jnp.where(self.inner, 3 - here, here))

    def place(self, i):
        rows = self.term.shape[1] // self.parts
        start = multiple(quotient(i, self.blocks) * rows, rows) if self.parts > 1 else 0
        return remainder(i, self.blocks), pl.ds(start, rows)

    def copy(self, src, dst, kind, i, device):
        block, rows = self.place(i)
        return remote(
            src.at[block, rows],
            dst.at[block, rows],
            self.sems.at[kind, i],
            self.sems.at[kind + 1, i],
            device,
        )

    def out_copy(self, i):
        return self.copy(self.term, self.passing, 0, i, self.mate)

    def across_copy(self, i):
        return self.copy(self.passing, self.total, 2, i, self.across)

    def back_copy(self, i):
        return self.copy(self.total, self.total, 4, i, self.mate)

    def add(self, out, other, i):
        block, rows = self.place(i)
        out[block, rows] = (
            out[block, rows].astype(jnp.float32) + other[block, rows].astype(jnp.float32)
        ).astype(out.dtype)

    def due(self, i, who, job):
        if isinstance(i, int):
            if not 0 <= i < self.count:
                return
        else:
            who = who & (i >= 0) & (i < self.count)

        @pl.when(who)
        def _():
            job()

    def step(self, now):
        i, j = now - self.FIRST, now - self.SECOND

        def pass_on():
            self.out_copy(i).wait_recv()
            self.add(self.passing, self.term, i)
            self.across_copy(i).start()

        def settle():
            self.across_copy(j).wait_recv()
            self.add(self.total, self.passing, j)
            self.back_copy(j).start()

        self.due(now, jnp.logical_not(self.inner), lambda: self.out_copy(now).start())
        self.due(i, self.inner, pass_on)
        self.due(j, self.inner, settle)

    def steps(self):
        return self.count + self.SECOND

    def each(self, who, job):
        @pl.when(who)
        def _():
            @pl.loop(0, self.count)
            def _(i):
                job(i)

    def receive(self, i):
        @pl.when(jnp.logical_not(self.inner))
        def _():
            self.back_copy(i).wait_recv()

    def receive_all(self):
        self.each(jnp.logical_not(self.inner), lambda i: self.back_copy(i).wait_recv())

    def finish(self):
        def sent(i):
            self.across_copy(i).wait_send()
            self.back_copy(i).wait_send()

        self.each(self.inner, sent)
        self.each(jnp.logical_not(self.inner), lambda i: self.out_copy(i).wait_send())


def quotient(a, b):
    return a // b if isinstance(a, int) else lax.div(a, b)


def remainder(a, b):
    return a % b if isinstance(a, int) else lax.rem(a, b)


def multiple(value, of):
    return value if isinstance(value, int) else pl.multiple_of(value, of)


def by_step(now, plan):
    for first, last, stride, job in plan:
        if first == last:

            @pl.when(now == first)
            def _():
                job(0)

        else:
            due = (now >= first) & (now <= last)
            if stride > 1:
                due = due & (lax.rem(now - first, stride) == 0)

            @pl.when(due)
            def _():
                job(lax.div(now - first, stride))


def lanes(shape):
    return lax.broadcasted_iota(jnp.int32, shape, len(shape) - 1)


def turn(vectors, cos_table, sin_table):
    near = jnp.where(
        lanes(vectors.shape) % 64 < 32, pltpu.roll(vectors, 96, 1), pltpu.roll(vectors, 32, 1)
    )
    return vectors * cos_table + near * sin_table


def token_column(row):
    return jnp.broadcast_to(row, (128, row.shape[1])).T


def key_marks(column, first_id):
    lane = lanes(column.shape) % 64
    one_hot = (column - first_id).astype(jnp.int32) == lane
    return jnp.where(one_hot | ((lane >= 4) & (lane < 7)), 1.0, 0.0)


def query_marks(column, first_id):
    lane = lanes(column.shape) % 64
    other = (column - first_id).astype(jnp.int32) != lane
    return jnp.where(other & (lane < 4), -1e30, 0.0)


def nt_dot(left, right):
    return lax.dot_general(
        left, right, (((1,), (1,)), ((), ())), preferred_element_type=jnp.float32
    )


def attend_kernel(
    chain, places, x, small, key_shard, value_shard, inverse, query_shard, out_shard, gate_shard, up_shard,
    down_shard, gate_full, up_full, down_full, query_full, pair_full, out_full, attn_sum, normed_out, query_out,
    pairs, attended_out, log_out, cos_out, sin_out, small_out, gate_here, up_here, down_here, small_all, query_here, pair_here, pair_shard,
    out_here, pre_row, normed, query, attended, log_total, cos_table, sin_table, key_side, value_side, marks,
    scores, peak, mixed, near_pairs, term, passing, total, small_sems, gather_sems, local_sems, pair_sems,
    chain_sems, store_sems, load_sems,
):
    count = term.shape[0] // 2
    tokens = x.shape[0]
    heads = query.shape[1] // 64
    me = lax.axis_index("tokens")
    place = lax.rem(me, places)
    far = place >= 2
    loads = [
        pltpu.make_async_copy(src, dst, load_sems.at[k])
        for k, (src, dst) in enumerate(
            ((gate_shard, gate_here), (up_shard, up_here), (down_shard, down_here))
        )
    ]
    for load in loads:
        load.start()
    greet(range(1, 8), chain)

    def small_copy(flip):
        return remote(
            small,
            small_all.at[me],
            small_sems.at[0, flip - 1],
            small_sems.at[1, flip - 1],
            token_device(flip),
        )

    def gather(k, shard, full, axis, part=(0, 1)):
        return Gather(
            shard, full, axis, gather_sems.at[0, k], gather_sems.at[1, k], local_sems.at[k], part
        )

    gather_query = gather(0, query_shard, query_here, 0)
    gather_pair = gather(1, pair_shard, pair_here, 0)
    gather_out = gather(2, out_shard, out_here, 1)
    half_rows = gate_here.shape[0] // 2
    gate_one, gate_two, up, down = (
        gather(3, gate_here.at[pl.ds(0, half_rows)], gate_full, 0, (0, 2)),
        gather(4, gate_here.at[pl.ds(half_rows, half_rows)], gate_full, 0, (1, 2)),
        gather(5, up_here, up_full, 0),
        gather(6, down_here, down_full, 1),
    )
    stores = []

    def store(src, out):
        copy = pltpu.make_async_copy(src, out, store_sems.at[len(stores)])
        copy.start()
        stores.append(copy)

    for flip in range(1, 8):
        small_copy(flip).start()
    both = jnp.concatenate(
        [key_shard[...].astype(jnp.float32), value_shard[...].astype(jnp.float32)], axis=0
    )
    pair_shard[...] = both.T.astype(jnp.bfloat16)
    gather_pair.start()
    gather_query.start()
    small_all[me] = small[...]
    x_f = x[...].astype(jnp.float32)
    pre_scale = lax.rsqrt(jnp.mean(x_f * x_f, axis=1, keepdims=True) + 1e-05)

    for flip in range(1, 8):
        small_copy(flip).wait_recv()
    store(small_all, small_out)
    width = x.shape[1] // 8
    for k in range(8):
        pre_row[:, k * width : (k + 1) * width] = jnp.broadcast_to(
            small_all[k, 1:2, :width], (8, width)
        )
    gather_pair.relay()
    normed[...] = (x[...].astype(jnp.float32) * pre_scale * pre_row[0:1, :]).astype(jnp.bfloat16)
    store(normed, normed_out)
    first_device = me - place
    first_id = (first_device // places * 4).astype(jnp.float32)
    own = token_column(small_all[me, 0:1, :])
    before = jnp.zeros((tokens, 1), jnp.float32)
    for k in range(places):
        others = small_all[first_device + k, 0:1, :]
        before = before + jnp.sum(
            jnp.where(others < own[:, 0:1], 1.0, 0.0), axis=1, keepdims=True
        )
        column = token_column(others)
        marks[pl.ds(k * tokens, tokens), :] = key_marks(column, first_id)
    row_index = lax.broadcasted_iota(jnp.int32, (tokens, 128), 0) + place * tokens
    turned = (row_index.astype(jnp.float32) - before) * inverse[0:1, :]
    cos_table[...] = jnp.cos(turned)
    sin_signed = jnp.sin(turned)
    sin_table[...] = jnp.where(lanes(sin_signed.shape) % 64 < 32, -sin_signed, sin_signed)
    store(cos_table, cos_out)
    store(sin_table, sin_out)
    gather_query.relay()
    gather_pair.finish_relay()
    gather_pair.finish()

    made = jnp.dot(normed[...], pair_here[...], preferred_element_type=jnp.float32)
    spun = turn(made, cos_table[...], sin_table[...])
    near_pairs[place] = jnp.where(lanes(made.shape) < 64, spun, made).astype(jnp.bfloat16)

    def pair_copy(slot, flip):
        at = place - 2 if slot == 2 else place
        return remote(
            near_pairs.at[at],
            near_pairs.at[at],
            pair_sems.at[0, slot],
            pair_sems.at[1, slot],
            token_device(flip),
        )

    pair_copy(0, 1).start()

    @pl.when(jnp.logical_not(far))
    def _():
        pair_copy(1, 2).start()

    gather_out.start()
    for load in loads:
        load.wait()
    gate_one.start()
    gather_query.finish_relay()
    gather_query.finish()
    for low in range(0, query.shape[1], 256):
        made = jnp.dot(
            normed[...], query_here[:, low : low + 256], preferred_element_type=jnp.float32
        )
        for group in range(low, low + 256, 128):
            spun = turn(made[:, group - low : group - low + 128], cos_table[...], sin_table[...])
            query[:, group : group + 128] = (spun * 0.125).astype(jnp.bfloat16)
    store(query, query_out)
    store(query_here, query_full)
    store(pair_here, pair_full)
    pair_copy(0, 1).wait_recv()

    @pl.when(far)
    def _():
        pair_copy(1, 2).wait_recv()
        pair_copy(2, 1).start()
        pair_copy(2, 1).wait_recv()

    @pl.when(jnp.logical_not(far))
    def _():
        gather_out.relay()

    @pl.when(jnp.logical_not(far))
    def _():
        gate_two.start()

    for k in range(places):

        @pl.when(k <= place)
        def _():
            pair = near_pairs[k].astype(jnp.float32)
            swapped = pltpu.roll(pair, 64, 1)
            lane = lanes(pair.shape)
            mark = marks[pl.ds(k * tokens, tokens), :]
            block = pl.ds(k * tokens, tokens)
            key_side[0, block] = jnp.where(lane < 64, pair, mark).astype(jnp.bfloat16)
            key_side[1, block] = jnp.where(lane < 64, mark, swapped).astype(jnp.bfloat16)
            value_side[0, block] = jnp.where(lane < 64, swapped, 1.0).astype(jnp.bfloat16)
            value_side[1, block] = jnp.where(lane < 64, 1.0, pair).astype(jnp.bfloat16)

    store(near_pairs, pairs)
    lane = lanes((tokens, 128))
    own_marks = query_marks(own, first_id)

    def side_of(group, e):
        at = pl.ds(multiple(group * 128, 128), 128)
        mine = (lane < 64) if e == 0 else (lane >= 64)
        return jnp.where(mine, query[:, at].astype(jnp.float32), own_marks).astype(jnp.bfloat16)

    def keys_at(k):
        return pl.ds(pl.multiple_of(k * tokens, tokens), tokens)

    def look(e, side, k, masked):
        found = nt_dot(side, key_side[e, keys_at(k)])
        if masked:
            rows = lax.broadcasted_iota(jnp.int32, found.shape, 0)
            found = jnp.where(lanes(found.shape) <= rows, found, -1e30)
        scores[e, k] = found
        best = found[:, :128]
        for part in range(128, tokens, 128):
            best = jnp.maximum(best, found[:, part : part + 128])
        peak[e] = best if masked else jnp.maximum(peak[e], best)

    def blend(e, k, first):
        parts = [
            jnp.exp(scores[e, k, :, part : part + 128] - peak[e]).astype(jnp.bfloat16)
            for part in range(0, tokens, 128)
        ]
        made = jnp.dot(
            jnp.concatenate(parts, axis=1),
            value_side[e, keys_at(k)],
            preferred_element_type=jnp.float32,
        )
        mixed[e] = made if first else mixed[e] + made

    def settle(e):
        peak[e] = jnp.broadcast_to(jnp.max(peak[e], axis=1, keepdims=True), lane.shape)

    def finish_head(group, e):
        mine = (lane < 64) if e == 0 else (lane >= 64)
        at = pl.ds(multiple(group * 128, 128), 128)
        out = mixed[e]
        sums = jnp.where(mine, pltpu.roll(out, 64, 1), out)
        share = out / sums
        attended[:, at] = share if e == 0 else jnp.where(lane < 64, attended[:, at], share)
        noted = peak[e] + jnp.log(sums)
        log_total[...] = jnp.where(lane == 2 * group + e, noted, log_total[...])

    def stage(done, begun):
        side = side_of(*begun) if begun else None
        if begun:
            look(begun[1], side, place, True)
        if done:
            blend(done[1], place, True)

        @pl.loop(0, place)
        def _(k):
            if begun:
                look(begun[1], side, k, False)
            if done:
                blend(done[1], k, False)

        if done:
            finish_head(*done)
        if begun:
            settle(begun[1])

    log_total[...] = jnp.zeros(lane.shape, jnp.float32)
    stage(None, (0, 0))
    last = heads // 2 - 1

    @pl.loop(0, last)
    def _(group):
        stage((group, 0), (group, 1))

        @pl.when(far & (group == 0))
        def _():
            gather_out.relay()

        @pl.when(far & (group == 0))
        def _():
            gate_two.start()

        @pl.when(group == 2)
        def _():
            up.start()

        stage((group, 1), (group + 1, 0))

    stage((last, 0), (last, 1))
    stage((last, 1), None)
    store(attended, attended_out)
    store(log_total, log_out)
    gather_out.finish_relay()

    gather_out.finish()
    low = attended[...].astype(jnp.bfloat16)
    each = term.shape[2]

    @pl.loop(0, count)
    def _(k):
        cut = pl.ds(pl.multiple_of(k * 2 * each, 2 * each), 2 * each)
        made = jnp.dot(low, out_here[:, cut], preferred_element_type=jnp.float32).astype(
            jnp.bfloat16
        )
        term[2 * k] = made[:, :each]
        term[2 * k + 1] = made[:, each:]

    store(out_here, out_full)

    down.start()
    line = LineSum(term, passing, total, chain_sems, 2)
    relays = [
        (at, at, 1, lambda _, job=job: job())
        for at, job in (
            (0, gate_one.relay),
            (5, gate_two.relay),
            (13, up.relay),
            (24, down.relay),
            (26, gate_one.finish_relay),
            (28, gate_two.finish_relay),
            (32, up.finish_relay),
        )
    ]

    @pl.loop(0, line.steps())
    def _(now):
        by_step(now, relays)
        line.step(now)

    line.receive_all()
    store(total, attn_sum)
    down.finish_relay()
    line.finish()
    for part in (gate_one, gate_two, up, down):
        part.finish()
    for flip in range(1, 8):
        small_copy(flip).wait_send()
    pair_copy(0, 1).wait_send()

    @pl.when(far)
    def _():
        pair_copy(2, 1).wait_send()

    @pl.when(jnp.logical_not(far))
    def _():
        pair_copy(1, 2).wait_send()

    for copy in stores:
        copy.wait()


def attend(
    chain, places, x, small, key_weight, value_weight, inverse, query_weight, out_weight, gate_weight, up_weight,
    down_weight,
):
    tokens, width = x.shape
    count = 8
    heads_wide = query_weight.shape[1]
    bf16, f32 = jnp.bfloat16, jnp.float32
    row = places * tokens
    each = width // (2 * count)
    anywhere, vmem = pl.BlockSpec(memory_space=pl.ANY), pl.BlockSpec(memory_space=pltpu.VMEM)
    shape = jax.ShapeDtypeStruct
    chunks = (2 * count, tokens, each)
    out_shape = [
        shape((gate_weight.shape[0] * 8, gate_weight.shape[1]), bf16),
        shape((up_weight.shape[0] * 8, up_weight.shape[1]), bf16),
        shape((down_weight.shape[0], down_weight.shape[1] * 8), bf16),
        shape((width, heads_wide), bf16),
        shape((width, 128), bf16),
        shape((heads_wide, width), bf16),
        shape(chunks, bf16),
        shape((tokens, width), bf16),
        shape((tokens, heads_wide), bf16),
        shape((places, tokens, 128), bf16),
        shape((tokens, heads_wide), f32),
        shape((tokens, 128), f32),
        shape((tokens, 128), f32),
        shape((tokens, 128), f32),
        shape((8,) + small.shape, f32),
    ]
    return pl.pallas_call(
        functools.partial(attend_kernel, chain, places),
        out_shape=out_shape,
        in_specs=[vmem] * 5 + [anywhere] * 5,
        out_specs=[anywhere] * len(out_shape),
        scratch_shapes=[
            pltpu.VMEM(gate_weight.shape, bf16),
            pltpu.VMEM(up_weight.shape, bf16),
            pltpu.VMEM(down_weight.shape, bf16),
            pltpu.VMEM((8,) + small.shape, f32),
            pltpu.VMEM((width, heads_wide), bf16),
            pltpu.VMEM((width, 128), bf16),
            pltpu.VMEM((width // 8, 128), bf16),
            pltpu.VMEM((heads_wide, width), bf16),
            pltpu.VMEM((8, width), f32),
            pltpu.VMEM((tokens, width), bf16),
            pltpu.VMEM((tokens, heads_wide), bf16),
            pltpu.VMEM((tokens, heads_wide), f32),
            pltpu.VMEM((tokens, 128), f32),
            pltpu.VMEM((tokens, 128), f32),
            pltpu.VMEM((tokens, 128), f32),
            pltpu.VMEM((2, row, 128), bf16),
            pltpu.VMEM((2, row, 128), bf16),
            pltpu.VMEM((row, 128), f32),
            pltpu.VMEM((2, places, tokens, tokens), f32),
            pltpu.VMEM((2, tokens, 128), f32),
            pltpu.VMEM((2, tokens, 128), f32),
            pltpu.VMEM((places, tokens, 128), bf16),
            pltpu.VMEM(chunks, bf16),
            pltpu.VMEM(chunks, bf16),
            pltpu.VMEM(chunks, bf16),
            pltpu.SemaphoreType.DMA((2, 7)),
            pltpu.SemaphoreType.DMA((2, 7, Gather.COPIES)),
            pltpu.SemaphoreType.DMA((7,)),
            pltpu.SemaphoreType.DMA((2, 3)),
            pltpu.SemaphoreType.DMA((6, 4 * count)),
            pltpu.SemaphoreType.DMA((len(out_shape),)),
            pltpu.SemaphoreType.DMA((3,)),
        ],
        compiler_params=pltpu.CompilerParams(
            collective_id=0, has_side_effects=True, vmem_limit_bytes=VMEM_BYTES
        ),
        name="attend_forward",
    )(
        x, small, key_weight.T, value_weight.T, inverse, query_weight, out_weight, gate_weight, up_weight,
        down_weight,
    )


def greet(flips, chain):
    me, here = lax.axis_index("tokens"), lax.axis_index("heads")
    barrier = pltpu.get_barrier_semaphore()
    for flip in flips:
        pl.semaphore_signal(barrier, inc=1, device_id=token_device(flip), device_id_type=MESH_ID)
    for step in (-1, 1):
        near = here + step

        @pl.when((near >= 0) & (near < chain))
        def _():
            pl.semaphore_signal(barrier, inc=1, device_id=(me, near), device_id_type=MESH_ID)

    edge = (here == 0) | (here == chain - 1)

    @pl.when(edge)
    def _():
        pl.semaphore_wait(barrier, len(flips) + 1)

    @pl.when(jnp.logical_not(edge))
    def _():
        pl.semaphore_wait(barrier, len(flips) + 2)


class Reduce:
    COPIES = 6

    def __init__(self, own, near, sems):
        self.own, self.near, self.sems = own, near, sems

    def copy(self, slot):
        k, half, flip = ((1, 0, 2), (3, 0, 2), (2, 1, 4), (3, 1, 4), (2, 0, 4), (1, 1, 2))[slot]
        rows = self.own.shape[1] // 2
        return remote(
            self.own.at[k, pl.ds(half * rows, rows)],
            self.near.at[slot],
            self.sems.at[0, slot],
            self.sems.at[1, slot],
            token_device(flip),
        )

    def put(self, k, block):
        self.own[k] = block.astype(self.own.dtype)
        self.send(k)

    def send(self, k):
        for which, slots in ((3, (1, 3)), (1, (0,)), (2, (2,))):

            @pl.when(k == which)
            def _():
                for slot in slots:
                    self.copy(slot).start()

    def add_near(self, k, half, slot):
        rows = self.own.shape[1] // 2

        @pl.loop(0, rows // 32)
        def _(i):
            here = pl.ds(pl.multiple_of(i * 32, 32), 32)
            place = pl.ds(pl.multiple_of(half * rows + i * 32, 32), 32)
            self.own[k, place] = (
                self.own[k, place].astype(jnp.float32) + self.near[slot, here].astype(jnp.float32)
            ).astype(self.own.dtype)

    def second(self):
        self.copy(1).wait_recv()
        self.add_near(2, 0, 1)
        self.copy(4).start()
        self.copy(3).wait_recv()
        self.add_near(1, 1, 3)
        self.copy(5).start()

    def finish(self, out):
        rows = self.own.shape[1] // 2
        for half, slots in ((0, (0, 4)), (1, (2, 5))):
            for slot in slots:
                self.copy(slot).wait_recv()

            @pl.loop(0, rows // 32)
            def _(i):
                here = pl.ds(pl.multiple_of(i * 32, 32), 32)
                place = pl.ds(pl.multiple_of(half * rows + i * 32, 32), 32)
                total = self.own[0, place].astype(jnp.float32)
                for slot in slots:
                    total = total + self.near[slot, here].astype(jnp.float32)
                out[place, :] = total

        for slot in range(self.COPIES):
            self.copy(slot).wait_send()


def block_order(i):
    return jnp.where(i == 0, 3, jnp.where(i == 1, 1, jnp.where(i == 2, 2, 0)))


def tn_dot(left, right):
    return lax.dot_general(
        left, right, (((0,), (0,)), ((), ())), preferred_element_type=jnp.float32
    )


def tiles_of(length, size):
    return [(low, min(low + size, length)) for low in range(0, length, size)]


def feed_kernel(
    chain, small_all, x_in, attn_in, cotangent_in, gate_full, up_full, down_full, back_sum, hidden_out, mlp_term,
    scale_out, grad_gate_out, grad_up_out, x, attn_sum, cotangent, hidden, scale, grad_gate, grad_up, gate, up, down, mid_row, normed, back_gate, back_up, term, passing, total,
    own_gate, near_gate, own_up, near_up, load_sems, swap_sems, chain_sems, reduce_sems, store_sems,
):
    count = term.shape[0] // 2
    each = term.shape[2]
    tokens, width = x.shape
    inner = gate.shape[1]
    me = lax.axis_index("tokens")
    tiles = tiles_of(inner, 512)
    early = [
        pltpu.make_async_copy(src, dst, load_sems.at[4, k])
        for k, (src, dst) in enumerate(((x_in, x), (attn_in, attn_sum), (cotangent_in, cotangent)))
    ]
    loads = []
    for k, (low, high) in enumerate(tiles):
        cut = pl.ds(low, high - low)
        loads.append(
            (
                pltpu.make_async_copy(gate_full.at[:, cut], gate.at[:, cut], load_sems.at[0, k]),
                pltpu.make_async_copy(up_full.at[:, cut], up.at[:, cut], load_sems.at[1, k]),
                pltpu.make_async_copy(down_full.at[cut, :], down.at[cut, :], load_sems.at[2, k]),
            )
        )
    for load in early:
        load.start()
    for group in loads:
        for load in group:
            load.start()
    greet((1, 2, 4), chain)

    span = width // 8
    for k in range(8):
        mid_row[:, k * span : (k + 1) * span] = jnp.broadcast_to(
            small_all[k, 1:2, span : 2 * span], (8, span)
        )

    early[0].wait()
    early[1].wait()
    line = LineSum(term, passing, total, chain_sems, 2)
    half = tokens // 2

    def swap(k, ref, row, cut):
        return remote(
            ref.at[pl.ds(multiple(row, half), half), cut],
            ref.at[pl.ds(multiple(tokens + row, half), half), cut],
            swap_sems.at[0, k],
            swap_sems.at[1, k],
            token_device(1),
        )

    def swaps_of(part):
        row = part * half
        found = [swap(part, normed, row, pl.ds(0, width))]
        for k, (low, high) in enumerate(tiles):
            for j, ref in enumerate((back_gate, back_up)):
                found.append(
                    swap(2 + (part * len(tiles) + k) * 2 + j, ref, row, pl.ds(low, high - low))
                )
        return found

    def mid_pair(n, row, rows):
        cut = pl.ds(pl.multiple_of(n * 2 * each, 2 * each), 2 * each)
        place = pl.ds(row, rows)
        made = nt_dot(back_gate[place, :], gate[cut, :]) + nt_dot(back_up[place, :], up[cut, :])
        made = made.astype(jnp.bfloat16)
        term[2 * n, place] = made[:, :each]
        term[2 * n + 1, place] = made[:, each:]

    early[2].wait()

    @pl.loop(0, 2)
    def _(part):
        row = pl.multiple_of(part * half, half)
        rows = pl.ds(row, half)

        def middle_here(c):
            cut = slice(c * each, (c + 1) * each)
            return x[rows, cut].astype(jnp.float32) + attn_sum[c, rows].astype(jnp.float32)

        squares = jnp.zeros((half, each), jnp.float32)
        for c in range(2 * count):
            found = middle_here(c)
            squares = squares + found * found
        mid_scale = lax.rsqrt(jnp.sum(squares, axis=1, keepdims=True) / width + 1e-05)
        scale[rows] = jnp.broadcast_to(mid_scale, (half, scale.shape[1]))
        for c in range(2 * count):
            cut = slice(c * each, (c + 1) * each)
            normed[rows, cut] = (middle_here(c) * mid_scale * mid_row[0:1, cut]).astype(jnp.bfloat16)
        copies = swaps_of(part)
        copies[0].start()
        for k, (low, high) in enumerate(tiles):

            @pl.when(part == 0)
            def _():
                for load in loads[k]:
                    load.wait()

            gate_rows = jnp.dot(
                normed[rows, :], gate[:, low:high], preferred_element_type=jnp.float32
            )
            up_rows = jnp.dot(normed[rows, :], up[:, low:high], preferred_element_type=jnp.float32)
            back_hidden = nt_dot(cotangent[rows, :], down[low:high, :])
            sigmoid = jax.nn.sigmoid(gate_rows)
            silu = gate_rows * sigmoid
            hidden[rows, low:high] = (silu * up_rows).astype(jnp.bfloat16)
            back_gate[rows, low:high] = (
                back_hidden * up_rows * sigmoid * (1.0 + gate_rows * (1.0 - sigmoid))
            ).astype(jnp.bfloat16)
            back_up[rows, low:high] = (back_hidden * silu).astype(jnp.bfloat16)
            for copy in copies[1 + 2 * k : 3 + 2 * k]:
                copy.start()

            @pl.when(part == 1)
            def _():
                line.step(2 * k)
                line.step(2 * k + 1)

        @pl.when(part == 0)
        def _():
            @pl.loop(0, count)
            def _(n):
                mid_pair(n, 0, half)

    stores = []

    def store(src, out):
        copy = pltpu.make_async_copy(src, out, store_sems.at[len(stores)])
        copy.start()
        stores.append(copy)

    store(hidden, hidden_out)
    store(scale, scale_out)

    def mlp_place(n):
        rows = pl.ds(pl.multiple_of(lax.rem(n, 4) * tokens, tokens), tokens)
        return rows, lax.div(n, 4) * 2 * each

    def mlp_stores(n):
        rows, low = mlp_place(n)
        return [
            pltpu.make_async_copy(
                gate.at[rows, pl.ds(pl.multiple_of(low + k * each, each), each)],
                mlp_term.at[2 * n + k],
                load_sems.at[3, 2 * n + k],
            )
            for k in range(2)
        ]

    def mlp_pair(n):
        cut = pl.ds(pl.multiple_of(n * 2 * each, 2 * each), 2 * each)
        made = jnp.dot(hidden[...], down[:, cut], preferred_element_type=jnp.float32)
        rows, low = mlp_place(n)
        gate[rows, pl.ds(pl.multiple_of(low, 2 * each), 2 * each)] = made.astype(jnp.bfloat16)
        for copy in mlp_stores(n):
            copy.start()

    gate_sum = Reduce(own_gate, near_gate, reduce_sems.at[0])
    up_sum = Reduce(own_up, near_up, reduce_sems.at[1])

    def grad_block(part, ref, k):
        index = jnp.bitwise_xor(me, 2 * k)
        cut = pl.ds(pl.multiple_of(index * span, span), span)
        part.put(k, tn_dot(normed[:, cut], ref[...]))

    def received(which):
        for part in range(2):
            for copy in swaps_of(part)[which]:
                copy.wait_recv()

    begun = 2 * len(tiles)
    plan = (
        (begun, begun, 1, lambda _: received(slice(0, 1))),
        (begun, begun, 1, lambda _: received(slice(1, None, 2))),
        (begun, begun + 3, 1, lambda i: grad_block(gate_sum, back_gate, block_order(i))),
        (begun, begun + count - 1, 1, lambda i: mid_pair(i, half, half)),
        (begun + 4, begun + 4, 1, lambda _: received(slice(2, None, 2))),
        (begun + 4, begun + 7, 1, lambda i: grad_block(up_sum, back_up, block_order(i))),
        (begun + 8, begun + 8, 1, lambda _: gate_sum.second()),
        (begun + 9, begun + 2 * count + 7, 2, mlp_pair),
        (begun + 16, begun + 16, 1, lambda _: up_sum.second()),
    )

    @pl.loop(begun, line.steps())
    def _(now):
        by_step(now, plan)
        line.step(now)

    gate_sum.finish(grad_gate)
    store(grad_gate, grad_gate_out)
    line.receive_all()
    store(total, back_sum)
    up_sum.finish(grad_up)
    store(grad_up, grad_up_out)
    line.finish()
    for part in range(2):
        for copy in swaps_of(part):
            copy.wait_send()

    @pl.loop(0, count)
    def _(n):
        for copy in mlp_stores(n):
            copy.wait()

    for copy in stores:
        copy.wait()


def feed(chain, small_all, x, attn_sum, cotangent, gate_full, up_full, down_full):
    tokens, width = x.shape
    inner = gate_full.shape[1]
    count = attn_sum.shape[0] // 2
    span = width // 8
    bf16, f32 = jnp.bfloat16, jnp.float32
    anywhere, vmem = pl.BlockSpec(memory_space=pl.ANY), pl.BlockSpec(memory_space=pltpu.VMEM)
    shape = jax.ShapeDtypeStruct
    tiles = len(tiles_of(inner, 512))
    return pl.pallas_call(
        functools.partial(feed_kernel, chain),
        out_shape=[
            shape(attn_sum.shape, bf16),
            shape((tokens, inner), bf16),
            shape(attn_sum.shape, bf16),
            shape((tokens, 128), f32),
            shape((span, inner), f32),
            shape((span, inner), f32),
        ],
        in_specs=[vmem] + [anywhere] * 6,
        out_specs=[anywhere] * 6,
        scratch_shapes=[
            pltpu.VMEM((tokens, width), bf16),
            pltpu.VMEM(attn_sum.shape, bf16),
            pltpu.VMEM((tokens, width), bf16),
            pltpu.VMEM((tokens, inner), bf16),
            pltpu.VMEM((tokens, 128), f32),
            pltpu.VMEM((span, inner), f32),
            pltpu.VMEM((span, inner), f32),
            pltpu.VMEM((width, inner), bf16),
            pltpu.VMEM((width, inner), bf16),
            pltpu.VMEM((inner, width), bf16),
            pltpu.VMEM((8, width), f32),
            pltpu.VMEM((2 * tokens, width), bf16),
            pltpu.VMEM((2 * tokens, inner), bf16),
            pltpu.VMEM((2 * tokens, inner), bf16),
            pltpu.VMEM(attn_sum.shape, bf16),
            pltpu.VMEM(attn_sum.shape, bf16),
            pltpu.VMEM(attn_sum.shape, bf16),
            pltpu.VMEM((4, span, inner), bf16),
            pltpu.VMEM((6, span // 2, inner), bf16),
            pltpu.VMEM((4, span, inner), bf16),
            pltpu.VMEM((6, span // 2, inner), bf16),
            pltpu.SemaphoreType.DMA((5, max(tiles, 2 * count))),
            pltpu.SemaphoreType.DMA((2, 2 + 4 * tiles)),
            pltpu.SemaphoreType.DMA((6, 4 * count)),
            pltpu.SemaphoreType.DMA((2, 2, Reduce.COPIES)),
            pltpu.SemaphoreType.DMA((5,)),
        ],
        compiler_params=pltpu.CompilerParams(
            collective_id=1, has_side_effects=True, vmem_limit_bytes=VMEM_BYTES
        ),
        name="feed_forward",
    )(small_all, x, attn_sum, cotangent, gate_full, up_full, down_full)


def split_marks(values, at):
    high = values.astype(jnp.bfloat16).astype(jnp.float32)
    rest = values - high
    middle = rest.astype(jnp.bfloat16).astype(jnp.float32)
    low = rest - middle
    return jnp.where(at == 4, high, jnp.where(at == 5, middle, jnp.where(at == 6, low, 0.0)))


def return_kernel(
    chain, places, small_all, query, pairs, log_total, cos_table, sin_table, scale,
    attended_in, x_in, attn_in, back_sum, query_full, pair_full, out_full, mlp_term, hidden_in, cotangent, normed_in, layer_out, grad_input, grad_down_out,
    grad_query, grad_key, grad_value, grad_out_out, gains, mid_part, grad_down, grad_out, pair_back, grad_in, in_here, out_here, key_side, value_side, query_side, back_side, back_att,
    back_rows, back_keys, back_values, pair_out, pair_near, normed, back_attn, hidden, cotangents, att_low,
    back_all, pre_row, pre_part, gains_near, mlp_sum, mlp_passing, mlp_total, term, passing, total, own_down,
    near_down, own_in, near_in, own_out, near_out, load_sems, swap_sems, pair_sems, gain_sems, chain_sems,
    reduce_sems, store_sems,
):
    count = term.shape[0] // 2
    each = term.shape[2]
    tokens, width = x_in.shape
    span = width // 8
    groups = query.shape[1] // 128
    me = lax.axis_index("tokens")
    place = lax.rem(me, places)
    first_device = me - place
    mine, theirs = pl.ds(0, tokens), pl.ds(tokens, tokens)

    def load(k, src, dst):
        copy = pltpu.make_async_copy(src, dst, load_sems.at[k])
        copy.start()
        return copy

    load_mlp = load(5, mlp_term, mlp_sum)
    load_cot = load(2, cotangent, cotangents.at[mine, :])
    attended = back_rows
    load_attended = load(7, attended_in, attended)

    def back_at(side, c):
        row = multiple(remainder(c, 4) * tokens, tokens)
        return side.at[quotient(c, 4), pl.ds(row, tokens), :]

    def attn_at(c):
        row = multiple(quotient(remainder(c, 4), 2) * tokens, tokens)
        low = multiple(remainder(c, 2) * each, each)
        return own_down.at[quotient(c, 4), pl.ds(row, tokens), pl.ds(low, each)]

    loads = []
    for c in range(2 * count):
        side = key_side if c < count else value_side
        loads.append(load(16 + c, back_sum.at[c], back_at(side, c % count)))
        loads.append(load(16 + 2 * count + c, x_in.at[:, pl.ds(c * each, each)], term.at[c]))
        loads.append(load(16 + 4 * count + c, attn_in.at[c], attn_at(c)))
    load_out = load(0, out_full, out_here)
    heads_wide = query.shape[1]
    load_in = load(1, query_full, in_here.at[:, pl.ds(0, heads_wide)])
    load_pair = load(6, pair_full, in_here.at[:, pl.ds(heads_wide, 128)])
    load_hidden = load(3, hidden_in, hidden.at[mine, :])
    load_normed = load(4, normed_in, normed.at[mine, :])
    greet(range(1, 8), chain)

    def swap(k, ref):
        copy = remote(
            ref.at[mine, :],
            ref.at[theirs, :],
            swap_sems.at[0, k],
            swap_sems.at[1, k],
            token_device(1),
        )
        copy.start()
        return copy

    def gain_copy(which, src, flip):
        other = jnp.bitwise_xor(me, flip)
        return remote(
            src.at[:, pl.ds(pl.multiple_of(other * span, span), span)],
            gains_near.at[me, :, pl.ds(which * span, span)],
            gain_sems.at[0, which, flip - 1],
            gain_sems.at[1, which, flip - 1],
            token_device(flip),
        )

    mlp_line = LineSum(mlp_sum, mlp_passing, mlp_total, chain_sems.at[0])
    load_mlp.wait()
    mlp_line.step(0)
    for k in range(8):
        pre_row[:, k * span : (k + 1) * span] = jnp.broadcast_to(
            small_all[k, 1:2, span : 2 * span], (8, span)
        )
    for copy in loads:
        copy.wait()
    load_cot.wait()

    def hat_at(c):
        return (term[c].astype(jnp.float32) + attn_at(c)[...].astype(jnp.float32)) * scale[...]

    def cut_at(c):
        return pl.ds(multiple(c * each, each), each)

    summed_here = back_keys.at[1]
    summed_here[...] = jnp.zeros(summed_here.shape, jnp.float32)
    for base, side in ((0, key_side), (count, value_side)):

        @pl.loop(0, count)
        def _(c):
            cut = cut_at(base + c)
            shared = back_at(side, c)[...].astype(jnp.float32) * hat_at(base + c)
            summed_here[...] += shared * pre_row[0:1, cut]
            mid_part[:, cut] = jnp.broadcast_to(jnp.sum(shared, axis=0, keepdims=True), (8, each))

    mean = jnp.sum(summed_here[...], axis=1, keepdims=True) / width
    summed_here[...] = jnp.broadcast_to(mean, summed_here.shape)
    for flip in range(1, 8):
        gain_copy(1, mid_part, flip).start()
    mlp_line.step(1)
    for base, side in ((0, key_side), (count, value_side)):

        @pl.loop(0, count)
        def _(c):
            cut = cut_at(base + c)
            u = back_at(side, c)[...].astype(jnp.float32) * pre_row[0:1, cut]
            found = scale[...] * (u - hat_at(base + c) * summed_here[...])
            back_attn[mine, cut] = (cotangents[mine, cut].astype(jnp.float32) + found).astype(
                jnp.bfloat16
            )

    mlp_line.step(2)
    load_attended.wait()
    att_low[mine, :] = attended[...].astype(jnp.bfloat16)
    swap_back = swap(0, back_attn)
    swap_att = swap(1, att_low)

    lane = lanes((tokens, 128))
    at = lane % 64
    first_id = (first_device // places * 4).astype(jnp.float32)
    for k in range(places):
        mark = key_marks(token_column(small_all[first_device + k, 0:1, :]), first_id)
        block = pl.ds(k * tokens, tokens)

        @pl.when(k <= place)
        def _():
            pair = pairs[k].astype(jnp.float32)
            swapped = pltpu.roll(pair, 64, 1)
            key_side[0, block] = jnp.where(lane < 64, pair, mark).astype(jnp.bfloat16)
            key_side[1, block] = jnp.where(lane < 64, mark, swapped).astype(jnp.bfloat16)
            value_side[0, block] = jnp.where(lane < 64, swapped, 1.0).astype(jnp.bfloat16)
            value_side[1, block] = jnp.where(lane < 64, 1.0, pair).astype(jnp.bfloat16)

    own_marks = query_marks(token_column(small_all[me, 0:1, :]), first_id)

    load_out.wait()
    back_att[...] = nt_dot(back_attn[mine, :], out_here[...]).astype(jnp.bfloat16)
    swap_cot = swap(2, cotangents)
    mlp_line.step(3)
    load_hidden.wait()
    swap_hidden = swap(3, hidden)

    @pl.loop(0, groups)
    def _(group):
        cut = pl.ds(pl.multiple_of(group * 128, 128), 128)
        back = back_att[:, cut].astype(jnp.float32)
        both = query[:, cut].astype(jnp.float32)
        shared = back * attended[:, cut]
        for e in range(2):
            head = 2 * group + e
            used = (lane < 64) if e == 0 else (lane >= 64)
            delta = jnp.sum(jnp.where(used, shared, 0.0), axis=1, keepdims=True)
            peak = jnp.sum(jnp.where(lane == head, log_total[...], 0.0), axis=1, keepdims=True)
            back_side[head] = jnp.where(
                used, back, split_marks(jnp.broadcast_to(-delta, lane.shape), at)
            ).astype(jnp.bfloat16)
            query_side[head] = jnp.where(
                used, both, own_marks + split_marks(jnp.broadcast_to(-peak, lane.shape), at)
            ).astype(jnp.bfloat16)

    load_normed.wait()
    swap_normed = swap(4, normed)
    load_in.wait()
    load_pair.wait()

    begun = 4
    back_rows[...] = jnp.zeros_like(back_rows)

    def key_step(k, diagonal):
        back_keys[...] = jnp.zeros_like(back_keys)
        back_values[...] = jnp.zeros_like(back_values)

        @pl.loop(0, groups)
        def _(group):
            cut = pl.ds(pl.multiple_of(group * 128, 128), 128)
            for low in (0, tokens // 2):
                keys_here = pl.ds(pl.multiple_of(k * tokens + low, tokens // 2), tokens // 2)
                part = pl.ds(low, tokens // 2)
                first = low if diagonal else 0
                seen = pl.ds(first, tokens - first)
                rows = []
                for e in range(2):
                    head = 2 * group + e
                    found = nt_dot(key_side[e, keys_here], query_side[head, seen])
                    chances = jnp.exp(found)
                    if diagonal:
                        keys = lax.broadcasted_iota(jnp.int32, found.shape, 0) + (low - first)
                        chances = jnp.where(keys <= lanes(found.shape), chances, 0.0)
                    moved = chances * nt_dot(value_side[e, keys_here], back_side[head, seen])
                    chances = chances.astype(jnp.bfloat16)
                    moved = moved.astype(jnp.bfloat16)
                    back_values[e, part] += jnp.dot(
                        chances, back_att[seen, cut], preferred_element_type=jnp.float32
                    )
                    back_keys[e, part] += jnp.dot(
                        moved, query[seen, cut], preferred_element_type=jnp.float32
                    )
                    rows.append(tn_dot(moved, key_side[e, keys_here]))
                back_rows[seen, cut] += jnp.where(lanes(rows[0].shape) < 64, rows[0], rows[1])

            @pl.when(group % 2 == 1)
            def _():
                mlp_line.step(begun + groups // 2 * k + group // 2)

        keys = back_keys[0] + pltpu.roll(back_keys[1], 64, 1)
        values = pltpu.roll(back_values[0], 64, 1) + back_values[1]
        return jnp.where(lane < 64, keys, values)

    def pair_copy(source, target):
        return remote(
            pair_out.at[target],
            pair_near.at[source],
            pair_sems.at[0, target],
            pair_sems.at[1, source],
            (first_device + target, lax.axis_index("heads")),
        )

    @pl.loop(0, place)
    def _(k):
        pair_out[k] = key_step(k, False).astype(jnp.bfloat16)
        pair_copy(place, k).start()

    own_pair = key_step(place, True)
    pair_out[place] = own_pair.astype(jnp.bfloat16)
    early = begun + groups // 2 * places

    @pl.loop(begun + groups // 2 * (place + 1), early)
    def _(now):
        mlp_line.step(now)

    for group in range(groups):
        cut = slice(group * 128, (group + 1) * 128)
        back_all[mine, cut] = (
            turn(back_rows[:, cut], cos_table[...], -sin_table[...]) * 0.125
        ).astype(jnp.bfloat16)
    back_keys[0] = own_pair
    for k in range(1, places):

        @pl.when(k > place)
        def _():
            remote(
                pair_out.at[k],
                pair_near.at[k],
                pair_sems.at[0, k],
                pair_sems.at[1, k],
                (first_device + k, lax.axis_index("heads")),
            ).wait_recv()
            back_keys[0] += pair_near[k].astype(jnp.float32)

    summed = back_keys[0]
    spun = turn(summed, cos_table[...], -sin_table[...])
    back_all[mine, pl.ds(groups * 128, 128)] = jnp.where(lane < 64, spun, summed).astype(
        jnp.bfloat16
    )
    swap_all = swap(5, back_all)

    def pre_pair(n):
        cut = pl.ds(pl.multiple_of(n * 2 * each, 2 * each), 2 * each)
        made = nt_dot(back_all[mine, :], in_here[cut, :]).astype(jnp.bfloat16)
        term[2 * n] = made[:, :each]
        term[2 * n + 1] = made[:, each:]

    def cut_of(k):
        index = jnp.bitwise_xor(me, 2 * k)
        return pl.ds(pl.multiple_of(index * span, span), span)

    down_sum = Reduce(own_down, near_down, reduce_sems.at[0])
    in_sum = Reduce(own_in, near_in, reduce_sems.at[1])
    out_sum = Reduce(own_out, near_out, reduce_sems.at[2])

    def down_block(i):
        k = block_order(i)
        for low, high in tiles_of(hidden.shape[1], 512):
            own_down[k, low:high] = tn_dot(hidden[:, low:high], cotangents[:, cut_of(k)]).astype(
                own_down.dtype
            )
        down_sum.send(k)

    def in_block(i):
        k = block_order(i)
        in_sum.put(k, tn_dot(normed[:, cut_of(k)], back_all[...]))

    def out_block(i):
        k = block_order(i)
        out_sum.put(k, tn_dot(att_low[...], back_attn[:, cut_of(k)]))

    def late_loads():
        copies = [pltpu.make_async_copy(x_in, cotangents.at[theirs, :], load_sems.at[8])]
        for c in range(2 * count):
            copies.append(
                pltpu.make_async_copy(
                    attn_in.at[c],
                    cotangents.at[mine, pl.ds(c * each, each)],
                    load_sems.at[16 + c],
                )
            )
        return copies

    def load_late():
        swap_cot.wait_send()
        for copy in late_loads():
            copy.start()

    def x_at(c):
        return cotangents[theirs, cut_at(c)].astype(jnp.float32)

    def middle_at(c):
        return x_at(c) + cotangents[mine, cut_at(c)].astype(jnp.float32)

    wholes = (
        (grad_down, grad_down_out),
        (grad_out, grad_out_out),
        (grad_in.at[:, pl.ds(0, heads_wide)], grad_query),
        (pair_back.at[pl.ds(0, 64)], grad_key),
        (pair_back.at[pl.ds(64, 64)], grad_value),
    )

    def whole(k):
        return pltpu.make_async_copy(*wholes[k], store_sems.at[4 * count + k])

    def store_block(c, src, out, first):
        return pltpu.make_async_copy(src.at[c], out.at[:, cut_at(c)], store_sems.at[first + c])

    def finish_mlp(_):
        mlp_line.receive_all()
        mlp_line.finish()

        @pl.loop(0, 2 * count)
        def _(c):
            mlp_sum[c] = (middle_at(c) + mlp_total[c].astype(jnp.float32)).astype(jnp.bfloat16)
            store_block(c, mlp_sum, layer_out, 0).start()

    weighed = back_keys.at[1]
    scale_here = back_keys.at[0]

    def scale_rows(_):
        for copy in late_loads():
            copy.wait()
        for k in range(8):
            pre_row[:, k * span : (k + 1) * span] = jnp.broadcast_to(
                small_all[k, 1:2, :span], (8, span)
            )
        scale_here[...] = jnp.zeros(scale_here.shape, jnp.float32)

        @pl.loop(0, 2 * count)
        def _(c):
            part = x_at(c)
            scale_here[...] += part * part

        mean = jnp.sum(scale_here[...], axis=1, keepdims=True) / width
        scale_here[...] = jnp.broadcast_to(lax.rsqrt(mean + 1e-05), scale_here.shape)
        weighed[...] = jnp.zeros(weighed.shape, jnp.float32)

    def weigh(i):
        line.receive(i)
        c, rows = line.place(i)
        size = tokens // line.parts
        first = lax.div(i, line.blocks) * size
        cut = cut_at(c)
        late = pl.ds(pl.multiple_of(tokens + first, size), size)
        hat = cotangents[late, cut].astype(jnp.float32) * scale_here[rows]
        shared = total[c, rows].astype(jnp.float32) * hat
        weighed[rows] += shared * pre_row[0:1, cut]
        summed = jnp.broadcast_to(jnp.sum(shared, axis=0, keepdims=True), (8, each))
        pre_part[:, cut] = jnp.where(i < line.blocks, 0.0, pre_part[:, cut]) + summed

    def finish_in(_):
        in_sum.finish(grad_in)
        pair_back[...] = grad_in[:, heads_wide:].T
        for k in (2, 3, 4):
            whole(k).start()

    def finish_down(_):
        down_sum.finish(grad_down)
        whole(0).start()

    def finish_out(_):
        out_sum.finish(grad_out)
        whole(1).start()

    line = LineSum(term, passing, total, chain_sems.at[1], 2)
    steps = line.steps()
    behind = 14

    def received(*copies):
        def job(_):
            for copy in copies:
                copy.wait_recv()

        return job

    plan = (
        (0, 2 * count - 2, 2, pre_pair),
        (1, 1, 1, received(swap_cot, swap_hidden)),
        (1, 7, 2, down_block),
        (8, 8, 1, lambda _: load_late()),
        (9, 9, 1, received(swap_back, swap_att)),
        (9, 12, 1, out_block),
        (13, 13, 1, received(swap_normed, swap_all)),
        (13, 13, 1, scale_rows),
        (14, 17, 1, in_block),
        (18, 18, 1, lambda _: down_sum.second()),
        (20, 20, 1, finish_mlp),
        (21, 21, 1, lambda _: out_sum.second()),
        (23, 23, 1, lambda _: in_sum.second()),
        (28, 28, 1, finish_down),
        (30, 30, 1, finish_out),
        (32, 32, 1, finish_in),
    )

    @pl.loop(0, steps)
    def _(now):
        by_step(now, plan)

        @pl.when(early + now < mlp_line.steps())
        def _():
            mlp_line.step(early + now)

        line.step(now)

        @pl.when(now >= behind)
        def _():
            weigh(now - behind)

    @pl.loop(steps - behind, line.count)
    def _(i):
        weigh(i)

    for flip in range(1, 8):
        gain_copy(0, pre_part, flip).start()
    mean = jnp.sum(weighed[...], axis=1, keepdims=True) / width
    weighed[...] = jnp.broadcast_to(mean, weighed.shape)
    line.finish()

    @pl.loop(0, 2 * count)
    def _(c):
        cut = cut_at(c)
        u = total[c].astype(jnp.float32) * pre_row[0:1, cut]
        found = scale_here[...] * (u - x_at(c) * scale_here[...] * weighed[...])
        term[c] = (back_attn[mine, cut].astype(jnp.float32) + found).astype(jnp.bfloat16)
        store_block(c, term, grad_input, 2 * count).start()

    own = pl.ds(pl.multiple_of(me * span, span), span)
    gains_near[me, :, :span] = pre_part[:, own]
    gains_near[me, :, span:] = mid_part[:, own]
    for flip in range(1, 8):
        for which, src in enumerate((pre_part, mid_part)):
            gain_copy(which, src, flip).wait_recv()
    gains[...] = jnp.sum(gains_near[...], axis=0)
    for flip in range(1, 8):
        for which, src in enumerate((pre_part, mid_part)):
            gain_copy(which, src, flip).wait_send()
    for copy in (swap_back, swap_att, swap_hidden, swap_normed, swap_all):
        copy.wait_send()

    @pl.loop(0, place)
    def _(k):
        pair_copy(place, k).wait_send()

    for k in range(len(wholes)):
        whole(k).wait()

    @pl.loop(0, 2 * count)
    def _(c):
        store_block(c, mlp_sum, layer_out, 0).wait()
        store_block(c, term, grad_input, 2 * count).wait()


def way_back(
    chain, places, small_all, query, pairs, log_total, cos_table, sin_table, scale, attended, x, attn_sum, back_sum,
    query_full, pair_full, out_full, mlp_term, hidden, cotangent, normed,
):
    tokens, width = x.shape
    inner = hidden.shape[1]
    heads_wide = query.shape[1]
    wide = heads_wide + 128
    chunks = attn_sum.shape
    count = chunks[0] // 2
    span = width // 8
    row = places * tokens
    bf16, f32 = jnp.bfloat16, jnp.float32
    anywhere, vmem = pl.BlockSpec(memory_space=pl.ANY), pl.BlockSpec(memory_space=pltpu.VMEM)
    shape = jax.ShapeDtypeStruct
    return pl.pallas_call(
        functools.partial(return_kernel, chain, places),
        out_shape=[
            shape((tokens, width), bf16),
            shape((tokens, width), bf16),
            shape((inner, span), f32),
            shape((span, heads_wide), f32),
            shape((64, span), f32),
            shape((64, span), f32),
            shape((heads_wide, span), f32),
            shape((8, 2 * span), f32),
        ],
        in_specs=[vmem] * 7 + [anywhere] * 11,
        out_specs=[anywhere] * 7 + [vmem],
        scratch_shapes=[
            pltpu.VMEM((8, width), f32),
            pltpu.VMEM((inner, span), f32),
            pltpu.VMEM((heads_wide, span), f32),
            pltpu.VMEM((128, span), f32),
            pltpu.VMEM((span, wide), f32),
            pltpu.VMEM((width, wide), bf16),
            pltpu.VMEM((heads_wide, width), bf16),
            pltpu.VMEM((2, row, 128), bf16),
            pltpu.VMEM((2, row, 128), bf16),
            pltpu.VMEM((heads_wide // 64, tokens, 128), bf16),
            pltpu.VMEM((heads_wide // 64, tokens, 128), bf16),
            pltpu.VMEM((tokens, heads_wide), bf16),
            pltpu.VMEM((tokens, heads_wide), f32),
            pltpu.VMEM((2, tokens, 128), f32),
            pltpu.VMEM((2, tokens, 128), f32),
            pltpu.VMEM((places, tokens, 128), bf16),
            pltpu.VMEM((places, tokens, 128), bf16),
            pltpu.VMEM((2 * tokens, width), bf16),
            pltpu.VMEM((2 * tokens, width), bf16),
            pltpu.VMEM((2 * tokens, inner), bf16),
            pltpu.VMEM((2 * tokens, width), bf16),
            pltpu.VMEM((2 * tokens, heads_wide), bf16),
            pltpu.VMEM((2 * tokens, wide), bf16),
            pltpu.VMEM((8, width), f32),
            pltpu.VMEM((8, width), f32),
            pltpu.VMEM((8, 8, 2 * span), f32),
            pltpu.VMEM(chunks, bf16),
            pltpu.VMEM(chunks, bf16),
            pltpu.VMEM(chunks, bf16),
            pltpu.VMEM(chunks, bf16),
            pltpu.VMEM(chunks, bf16),
            pltpu.VMEM(chunks, bf16),
            pltpu.VMEM((4, inner, span), bf16),
            pltpu.VMEM((6, inner // 2, span), bf16),
            pltpu.VMEM((4, span, wide), bf16),
            pltpu.VMEM((6, span // 2, wide), bf16),
            pltpu.VMEM((4, heads_wide, span), bf16),
            pltpu.VMEM((6, heads_wide // 2, span), bf16),
            pltpu.SemaphoreType.DMA((16 + 6 * count,)),
            pltpu.SemaphoreType.DMA((2, 6)),
            pltpu.SemaphoreType.DMA((2, places)),
            pltpu.SemaphoreType.DMA((2, 2, 7)),
            pltpu.SemaphoreType.DMA((2, 6, 4 * count)),
            pltpu.SemaphoreType.DMA((3, 2, Reduce.COPIES)),
            pltpu.SemaphoreType.DMA((4 * count + 5,)),
        ],
        compiler_params=pltpu.CompilerParams(
            collective_id=2, has_side_effects=True, vmem_limit_bytes=VMEM_BYTES
        ),
        name="way_back",
    )(
        small_all, query, pairs, log_total, cos_table, sin_table, scale, attended, x, attn_sum, back_sum,
        query_full, pair_full, out_full, mlp_term, hidden, cotangent, normed,
    )


def hand_over_kernel(count, *refs):
    ins, outs, held = refs[:count], refs[count : 2 * count], refs[2 * count : 3 * count]
    sems = refs[3 * count]
    loads = [pltpu.make_async_copy(ins[k], held[k], sems.at[0, k]) for k in range(count)]
    stores = [pltpu.make_async_copy(held[k], outs[k], sems.at[1, k]) for k in range(count)]
    for load in loads:
        load.start()
    for load, store in zip(loads, stores):
        load.wait()
        store.start()
    for store in stores:
        store.wait()


def hand_over(*arrays):
    count = len(arrays)
    anywhere = pl.BlockSpec(memory_space=pl.ANY)
    return pl.pallas_call(
        functools.partial(hand_over_kernel, count),
        out_shape=[jax.ShapeDtypeStruct(array.shape, array.dtype) for array in arrays],
        in_specs=[anywhere] * count,
        out_specs=[anywhere] * count,
        scratch_shapes=[pltpu.VMEM(array.shape, array.dtype) for array in arrays]
        + [pltpu.SemaphoreType.DMA((2, count))],
        compiler_params=pltpu.CompilerParams(vmem_limit_bytes=VMEM_BYTES),
        name="hand_over",
    )(*arrays)


def shards_cube(
    chain,
    inputs,
    segments,
    pre_gain,
    mid_gain,
    query_weight,
    key_weight,
    value_weight,
    out_weight,
    gate_weight,
    up_weight,
    down_weight,
    cotangent,
):
    row_count = inputs.shape[0]
    head_size = key_weight.shape[1]
    query_width = query_weight.shape[1]
    heads_here = query_width // head_size
    places = ROW // row_count
    half = row_count // 2
    gains = jnp.pad(pre_gain.astype(jnp.float32), (0, half)) + jnp.pad(
        mid_gain.astype(jnp.float32), (half, 0)
    )
    sublane = lax.broadcasted_iota(jnp.int32, (8, row_count), 0)
    small = jnp.where(
        sublane == 0, segments.astype(jnp.float32)[None], jnp.where(sublane == 1, gains[None], 0.0)
    )
    half_size = head_size // 2
    inverse = 10000.0 ** (-np.arange(half_size, dtype=np.float32) / half_size)
    inverse = jnp.asarray(np.tile(inverse.astype(np.float32), (8, 128 // half_size)))
    (
        gate_full,
        up_full,
        down_full,
        query_full,
        pair_full,
        out_full,
        attn_sum,
        normed,
        query_rot,
        pairs,
        attended,
        log_total,
        cos_wide,
        sin_wide,
        small_full,
    ) = attend(
        chain,
        places,
        inputs,
        small,
        key_weight,
        value_weight,
        inverse,
        query_weight,
        out_weight,
        gate_weight,
        up_weight,
        down_weight,
    )
    back_sum, hidden, mlp_term, scale, grad_gate, grad_up = feed(
        chain, small_full, inputs, attn_sum, cotangent, gate_full, up_full, down_full
    )
    layer_out, grad_input, grad_down, grad_query, grad_key, grad_value, grad_out, gains = way_back(
        chain,
        places,
        small_full,
        query_rot,
        pairs,
        log_total,
        cos_wide,
        sin_wide,
        scale,
        attended,
        inputs,
        attn_sum,
        back_sum,
        query_full,
        pair_full,
        out_full,
        mlp_term,
        hidden,
        cotangent,
        normed,
    )
    grad_pre, grad_mid = jnp.split(gains[0], 2)
    layer_out, grad_input, grad_query, grad_key, grad_value, grad_out, grad_gate, grad_up, grad_down = hand_over(
        layer_out, grad_input, grad_query, grad_key, grad_value, grad_out, grad_gate, grad_up, grad_down
    )
    grad_key, grad_value = grad_key.T, grad_value.T
    return (
        layer_out,
        grad_input,
        grad_pre,
        grad_mid,
        grad_query,
        grad_key,
        grad_value,
        grad_out,
        grad_gate,
        grad_up,
        grad_down,
    )


def solution(mesh):
    sizes = dict(mesh.shape)
    plan = shards_any
    if sizes["tokens"] == 8 and sizes["heads"] == 4:
        plan = functools.partial(shards_cube, sizes["heads"])
    return jax.shard_map(
        plan,
        mesh=mesh,
        in_specs=(
            P("tokens", None),
            P("tokens"),
            P("tokens"),
            P("tokens"),
            P("tokens", "heads"),
            P("tokens", "heads"),
            P("tokens", "heads"),
            P("heads", "tokens"),
            P("tokens", "heads"),
            P("tokens", "heads"),
            P("heads", "tokens"),
            P("tokens", None),
        ),
        out_specs=(
            P("tokens", None),
            P("tokens", None),
            P("tokens"),
            P("tokens"),
            P("tokens", "heads"),
            P("tokens", "heads"),
            P("tokens", "heads"),
            P("heads", "tokens"),
            P("tokens", "heads"),
            P("tokens", "heads"),
            P("heads", "tokens"),
        ),
        check_vma=False,
    )
```

```python
import functools
import math

import jax
import jax.numpy as jnp
import numpy as np
from jax import lax
from jax.experimental import pallas as pl
from jax.experimental.pallas import tpu as pltpu
from jax.sharding import PartitionSpec as P

ROW = 2048


def rms_scale(vectors):
    return lax.rsqrt(jnp.mean(vectors * vectors, axis=-1, keepdims=True) + 1e-05)


def rotate(vectors, cos_table, sin_table):
    middle_index = vectors.shape[-1] // 2
    former = vectors[..., :middle_index]
    latter = vectors[..., middle_index:]
    return jnp.concatenate(
        [former * cos_table - latter * sin_table, latter * cos_table + former * sin_table], axis=-1
    )


def unrotate(gradient, cos_table, sin_table):
    middle_index = gradient.shape[-1] // 2
    former = gradient[..., :middle_index]
    latter = gradient[..., middle_index:]
    return jnp.concatenate(
        [former * cos_table + latter * sin_table, latter * cos_table - former * sin_table], axis=-1
    )


def norm_back(gradient, vectors, scale_rows, gain_row):
    shaped = vectors * scale_rows
    weighted = gradient * gain_row
    back_vectors = scale_rows * (
        weighted - shaped * jnp.mean(weighted * shaped, axis=-1, keepdims=True)
    )
    return (back_vectors, jnp.sum(gradient * shaped, axis=0))


def shards_any(
    inputs,
    segments,
    pre_gain,
    mid_gain,
    query_weight,
    key_weight,
    value_weight,
    out_weight,
    gate_weight,
    up_weight,
    down_weight,
    cotangent,
):
    row_count = inputs.shape[0]
    head_size = key_weight.shape[1]
    heads_here = query_weight.shape[1] // head_size
    myself = lax.axis_index("tokens")
    gathered = (
        lax.all_gather(pre_gain, "tokens", axis=0, tiled=True),
        lax.all_gather(mid_gain, "tokens", axis=0, tiled=True),
        lax.all_gather(query_weight, "tokens", axis=0, tiled=True),
        lax.all_gather(key_weight, "tokens", axis=0, tiled=True),
        lax.all_gather(value_weight, "tokens", axis=0, tiled=True),
        lax.all_gather(out_weight, "tokens", axis=1, tiled=True),
        lax.all_gather(gate_weight, "tokens", axis=0, tiled=True),
        lax.all_gather(up_weight, "tokens", axis=0, tiled=True),
        lax.all_gather(down_weight, "tokens", axis=1, tiled=True),
    )
    (
        pre_full,
        mid_full,
        query_full,
        key_full,
        value_full,
        out_full,
        gate_full,
        up_full,
        down_full,
    ) = gathered
    pre_row = pre_full.astype(jnp.float32)
    mid_row = mid_full.astype(jnp.float32)
    all_ids = lax.all_gather(segments, "tokens", axis=0, tiled=True)
    length = all_ids.shape[0]
    places = jnp.arange(length, dtype=jnp.int32)
    starts_here = jnp.concatenate([jnp.ones((1,), dtype=jnp.bool_), all_ids[1:] != all_ids[:-1]])
    opening = lax.cummax(jnp.where(starts_here, places, 0), axis=0)
    own_first = myself * row_count
    positions = lax.dynamic_slice_in_dim(places - opening, own_first, row_count)
    own_places = own_first + jnp.arange(row_count, dtype=jnp.int32)
    half_size = head_size // 2
    inverse = 10000.0 ** (-jnp.arange(half_size, dtype=jnp.float32) / half_size)
    turned = positions.astype(jnp.float32)[:, None] * inverse[None, :]
    cos_table = jnp.cos(turned)[:, None, :]
    sin_table = jnp.sin(turned)[:, None, :]
    inputs_f = inputs.astype(jnp.float32)
    pre_scale = rms_scale(inputs_f)
    normed = (inputs_f * pre_scale * pre_row).astype(jnp.bfloat16)
    queries = jnp.dot(normed, query_full, preferred_element_type=jnp.float32).reshape(
        row_count, heads_here, head_size
    )
    query_rot = (rotate(queries, cos_table, sin_table) * head_size ** (-0.5)).astype(jnp.bfloat16)
    key_rows = jnp.dot(normed, key_full, preferred_element_type=jnp.float32)[:, None, :]
    key_rot = rotate(key_rows, cos_table, sin_table)[:, 0, :].astype(jnp.bfloat16)
    value_low = jnp.dot(normed, value_full, preferred_element_type=jnp.float32).astype(jnp.bfloat16)
    key_all, value_all = (
        lax.all_gather(key_rot, "tokens", axis=0, tiled=True),
        lax.all_gather(value_low, "tokens", axis=0, tiled=True),
    )
    span = math.gcd(ROW, 1024)
    row_start = own_first // ROW * ROW
    block_first = row_start // span
    block_total = (own_first + row_count + span - 1) // span

    def key_block(block_index):
        opening_row = block_index * span
        block_keys = lax.dynamic_slice_in_dim(key_all, opening_row, span)
        block_values = lax.dynamic_slice_in_dim(value_all, opening_row, span)
        block_ids = lax.dynamic_slice_in_dim(all_ids, opening_row, span)
        block_places = opening_row + jnp.arange(span, dtype=jnp.int32)
        allowed = (segments[:, None] == block_ids[None, :]) & (
            own_places[:, None] >= block_places[None, :]
        )
        scores = jnp.einsum(
            "qhd,kd->qhk", query_rot, block_keys, preferred_element_type=jnp.float32
        )
        return (opening_row, block_keys, block_values, allowed[:, None, :], scores)

    def forward_step(block_index, state_now):
        row_peak, row_total, running = state_now
        opening_row, block_keys, block_values, allowed, scores = key_block(block_index)
        new_peak = jnp.maximum(row_peak, jnp.max(jnp.where(allowed, scores, -1e30), axis=-1))
        factor = jnp.exp(row_peak - new_peak)
        weights = jnp.where(allowed, jnp.exp(scores - new_peak[..., None]), 0.0)
        row_total = row_total * factor + jnp.sum(weights, axis=-1)
        running = running * factor[..., None] + jnp.einsum(
            "qhk,kd->qhd",
            weights.astype(jnp.bfloat16),
            block_values,
            preferred_element_type=jnp.float32,
        )
        return (new_peak, row_total, running)

    start_state = (
        jnp.full((row_count, heads_here), -1e30, jnp.float32),
        jnp.zeros((row_count, heads_here), jnp.float32),
        jnp.zeros((row_count, heads_here, head_size), jnp.float32),
    )
    row_peak, row_total, running = lax.fori_loop(
        block_first, block_total, forward_step, start_state
    )
    attended = running / row_total[..., None]
    log_total = row_peak + jnp.log(row_total)
    attended_low = attended.astype(jnp.bfloat16).reshape(row_count, heads_here * head_size)
    attn_term = jnp.dot(attended_low, out_full, preferred_element_type=jnp.float32)
    middle = inputs_f + lax.psum(attn_term.astype(jnp.bfloat16), "heads").astype(jnp.float32)
    mid_scale = rms_scale(middle)
    normed_mid = (middle * mid_scale * mid_row).astype(jnp.bfloat16)
    gate_rows = jnp.dot(normed_mid, gate_full, preferred_element_type=jnp.float32)
    up_rows = jnp.dot(normed_mid, up_full, preferred_element_type=jnp.float32)
    sigmoid_rows = jax.nn.sigmoid(gate_rows)
    silu_rows = gate_rows * sigmoid_rows
    hidden = (silu_rows * up_rows).astype(jnp.bfloat16)
    mlp_term = jnp.dot(hidden, down_full, preferred_element_type=jnp.float32)
    layer_out = (
        middle + lax.psum(mlp_term.astype(jnp.bfloat16), "heads").astype(jnp.float32)
    ).astype(jnp.bfloat16)
    grad_down = jnp.einsum("tf,td->fd", hidden, cotangent, preferred_element_type=jnp.float32)
    back_hidden = jnp.einsum("td,fd->tf", cotangent, down_full, preferred_element_type=jnp.float32)
    back_gate = (
        back_hidden * up_rows * sigmoid_rows * (1.0 + gate_rows * (1.0 - sigmoid_rows))
    ).astype(jnp.bfloat16)
    back_up = (back_hidden * silu_rows).astype(jnp.bfloat16)
    grad_gate = jnp.einsum("tc,tf->cf", normed_mid, back_gate, preferred_element_type=jnp.float32)
    grad_up = jnp.einsum("tc,tf->cf", normed_mid, back_up, preferred_element_type=jnp.float32)
    mid_term = jnp.einsum(
        "tf,cf->tc", back_gate, gate_full, preferred_element_type=jnp.float32
    ) + jnp.einsum("tf,cf->tc", back_up, up_full, preferred_element_type=jnp.float32)
    back_normed_mid = lax.psum(mid_term.astype(jnp.bfloat16), "heads").astype(jnp.float32)
    back_middle, grad_mid = norm_back(back_normed_mid, middle, mid_scale, mid_row)
    back_middle = back_middle + cotangent.astype(jnp.float32)
    back_attn = back_middle.astype(jnp.bfloat16)
    grad_out = jnp.einsum("tc,td->cd", attended_low, back_attn, preferred_element_type=jnp.float32)
    back_attended = (
        jnp.einsum("td,cd->tc", back_attn, out_full, preferred_element_type=jnp.float32)
        .astype(jnp.bfloat16)
        .reshape(row_count, heads_here, head_size)
    )
    row_delta = jnp.sum(back_attended.astype(jnp.float32) * attended, axis=-1)

    def backward_step(block_index, state_now):
        back_rows, back_pairs = state_now
        opening_row, block_keys, block_values, allowed, scores = key_block(block_index)
        chances = jnp.where(allowed, jnp.exp(scores - log_total[..., None]), 0.0)
        back_values = jnp.einsum(
            "qhk,qhd->kd",
            chances.astype(jnp.bfloat16),
            back_attended,
            preferred_element_type=jnp.float32,
        )
        back_chances = jnp.einsum(
            "qhd,kd->qhk", back_attended, block_values, preferred_element_type=jnp.float32
        )
        back_scores = (chances * (back_chances - row_delta[..., None])).astype(jnp.bfloat16)
        back_rows = back_rows + jnp.einsum(
            "qhk,kd->qhd", back_scores, block_keys, preferred_element_type=jnp.float32
        )
        back_keys = jnp.einsum(
            "qhk,qhd->kd", back_scores, query_rot, preferred_element_type=jnp.float32
        )
        old_piece = lax.dynamic_slice_in_dim(back_pairs, opening_row, span)
        fresh_piece = old_piece + jnp.concatenate([back_keys, back_values], axis=-1)
        back_pairs = lax.dynamic_update_slice_in_dim(back_pairs, fresh_piece, opening_row, 0)
        return (back_rows, back_pairs)

    start_back = (
        jnp.zeros((row_count, heads_here, head_size), jnp.float32),
        jnp.zeros((length, 2 * head_size), jnp.float32),
    )
    back_rows, back_pairs = lax.fori_loop(block_first, block_total, backward_step, start_back)
    own_pairs = lax.psum_scatter(
        back_pairs.astype(jnp.bfloat16), "tokens", scatter_dimension=0, tiled=True
    ).astype(jnp.float32)
    back_query = (
        (unrotate(back_rows, cos_table, sin_table) * head_size ** (-0.5))
        .astype(jnp.bfloat16)
        .reshape(row_count, heads_here * head_size)
    )
    back_key = unrotate(own_pairs[:, None, :head_size], cos_table, sin_table)[:, 0, :].astype(
        jnp.bfloat16
    )
    back_value = own_pairs[:, head_size:].astype(jnp.bfloat16)
    grad_query = jnp.einsum("tc,tq->cq", normed, back_query, preferred_element_type=jnp.float32)
    grad_key = jnp.einsum("tc,tq->cq", normed, back_key, preferred_element_type=jnp.float32)
    grad_value = jnp.einsum("tc,tq->cq", normed, back_value, preferred_element_type=jnp.float32)
    pre_term = jnp.einsum("tq,cq->tc", back_query, query_full, preferred_element_type=jnp.float32)
    pre_term = pre_term + jnp.einsum(
        "tq,cq->tc", back_key, key_full, preferred_element_type=jnp.float32
    )
    pre_term = pre_term + jnp.einsum(
        "tq,cq->tc", back_value, value_full, preferred_element_type=jnp.float32
    )
    back_normed = lax.psum(pre_term.astype(jnp.bfloat16), "heads").astype(jnp.float32)
    back_inputs, grad_pre = norm_back(back_normed, inputs_f, pre_scale, pre_row)
    grad_input = (back_middle + back_inputs).astype(jnp.bfloat16)
    summed = (
        lax.psum_scatter(
            grad_pre.astype(jnp.bfloat16), "tokens", scatter_dimension=0, tiled=True
        ).astype(jnp.float32),
        lax.psum_scatter(
            grad_mid.astype(jnp.bfloat16), "tokens", scatter_dimension=0, tiled=True
        ).astype(jnp.float32),
        lax.psum_scatter(
            grad_query.astype(jnp.bfloat16), "tokens", scatter_dimension=0, tiled=True
        ).astype(jnp.float32),
        lax.psum_scatter(
            grad_key.astype(jnp.bfloat16), "tokens", scatter_dimension=0, tiled=True
        ).astype(jnp.float32),
        lax.psum_scatter(
            grad_value.astype(jnp.bfloat16), "tokens", scatter_dimension=0, tiled=True
        ).astype(jnp.float32),
        lax.psum_scatter(
            grad_out.astype(jnp.bfloat16), "tokens", scatter_dimension=1, tiled=True
        ).astype(jnp.float32),
        lax.psum_scatter(
            grad_gate.astype(jnp.bfloat16), "tokens", scatter_dimension=0, tiled=True
        ).astype(jnp.float32),
        lax.psum_scatter(
            grad_up.astype(jnp.bfloat16), "tokens", scatter_dimension=0, tiled=True
        ).astype(jnp.float32),
        lax.psum_scatter(
            grad_down.astype(jnp.bfloat16), "tokens", scatter_dimension=1, tiled=True
        ).astype(jnp.float32),
    )
    (
        grad_pre,
        grad_mid,
        grad_query,
        grad_key,
        grad_value,
        grad_out,
        grad_gate,
        grad_up,
        grad_down,
    ) = summed
    return (
        layer_out,
        grad_input,
        grad_pre,
        grad_mid,
        grad_query,
        grad_key,
        grad_value,
        grad_out,
        grad_gate,
        grad_up,
        grad_down,
    )


MESH_ID = pl.DeviceIdType.MESH
VMEM_BYTES = 63 * 2**20
LEAD = 4


def token_device(flip):
    return (jnp.bitwise_xor(lax.axis_index("tokens"), flip), lax.axis_index("heads"))


def remote(src, dst, send, recv, device):
    return pltpu.make_async_remote_copy(
        src_ref=src, dst_ref=dst, send_sem=send, recv_sem=recv, device_id=device, device_id_type=MESH_ID
    )


def block_of(ref, axis, index, half=None, part=(0, 1)):
    size = ref.shape[axis] // 8
    start = pl.multiple_of(index * size, size)
    if axis == 0:
        rows = size // part[1]
        start = pl.multiple_of(start + part[0] * rows, rows)
        if half is None:
            return ref.at[pl.ds(start, rows), :]
        rows //= 2
        return ref.at[pl.ds(pl.multiple_of(start + half * rows, rows), rows), :]
    if half is None:
        return ref.at[:, pl.ds(start, size)]
    rows = ref.shape[0] // 2
    return ref.at[pl.ds(half * rows, rows), pl.ds(start, size)]


def in_order(job):
    @pl.when(lax.axis_index("tokens") >= 0)
    def _():
        job()


class Gather:
    COPIES = 9

    def __init__(self, shard, full, axis, send, recv, local, part=(0, 1)):
        self.shard, self.full, self.axis, self.part = shard, full, axis, part
        self.send, self.recv, self.local = send, recv, local
        self.me = lax.axis_index("tokens")

    def copy(self, slot, flip_block, flip_target, half=None):
        index = jnp.bitwise_xor(self.me, flip_block)
        place = block_of(self.full, self.axis, index, half, self.part)
        return remote(
            self.shard if flip_block == 0 else place,
            place,
            self.send.at[slot],
            self.recv.at[slot],
            token_device(flip_target),
        )

    def copies(self, slot):
        return self.copy(
            slot,
            *(
                (0, 2),
                (0, 4),
                (0, 1),
                (2, 4, 0),
                (4, 2, 1),
                (2, 1),
                (4, 1),
                (6, 1, 0),
                (6, 1, 1),
            )[slot],
        )

    def own_copy(self):
        return pltpu.make_async_copy(
            self.shard, block_of(self.full, self.axis, self.me, None, self.part), self.local
        )

    def start(self):
        def job():
            for slot in (0, 1, 2):
                self.copies(slot).start()
            self.own_copy().start()

        in_order(job)

    def relay_x(self):
        def job():
            self.copies(0).wait_recv()
            self.copies(3).start()
            self.copies(5).start()

        in_order(job)

    def relay_y(self):
        def job():
            self.copies(1).wait_recv()
            self.copies(4).start()
            self.copies(6).start()

        in_order(job)

    def relay(self):
        self.relay_x()
        self.relay_y()

    def finish_relay(self):
        def job():
            self.copies(3).wait_recv()
            self.copies(7).start()
            self.copies(4).wait_recv()
            self.copies(8).start()

        in_order(job)

    def finish(self):
        def job():
            for slot in (2, 5, 6, 7, 8):
                self.copies(slot).wait_recv()
            for slot in range(self.COPIES):
                self.copies(slot).wait_send()
            self.own_copy().wait()

        in_order(job)


class LineSum:
    FIRST, SECOND = 1, 3

    def __init__(self, term, passing, total, sems, parts=1, early=None, given=0):
        self.term, self.passing, self.total, self.sems = term, passing, total, sems
        self.parts, self.blocks = parts, term.shape[0]
        self.count = self.blocks * parts
        self.early = self.count if early is None else early
        self.given = given
        here, tokens = lax.axis_index("heads"), lax.axis_index("tokens")
        self.inner = (here == 1) | (here == 2)
        self.mate = (tokens, jnp.where(here < 2, 1 - here, 5 - here))
        self.across = (tokens, jnp.where(self.inner, 3 - here, here))

    def place(self, i):
        rows = self.term.shape[1] // self.parts
        start = multiple(quotient(i, self.blocks) * rows, rows) if self.parts > 1 else 0
        return remainder(i, self.blocks), pl.ds(start, rows)

    def copy(self, src, dst, send, recv, i, device):
        block, rows = self.place(i)
        return remote(
            src.at[block, rows], dst.at[block, rows], self.sems.at[send, i], self.sems.at[recv, i], device
        )

    def out_copy(self, i):
        return self.copy(self.term, self.passing, 0, 1, i, self.mate)

    def across_copy(self, i, src=None):
        return self.copy(self.passing if src is None else src, self.total, 0, 2, i, self.across)

    def start_given(self):
        @pl.when(self.inner)
        def _():
            for i in range(self.given):
                self.across_copy(i, self.term).start()

    def back_copy(self, i):
        return self.copy(self.total, self.total, 3, 1, i, self.mate)

    def add(self, out, other, i):
        block, rows = self.place(i)
        out[block, rows] = (
            out[block, rows].astype(jnp.float32) + other[block, rows].astype(jnp.float32)
        ).astype(out.dtype)

    def due(self, i, who, job):
        if isinstance(i, int):
            if not 0 <= i < self.count:
                return
        else:
            who = who & (i >= 0) & (i < self.count)

        @pl.when(who)
        def _():
            job()

    def step(self, now):
        i, j = now - self.FIRST, now - self.SECOND

        def pass_on():
            self.out_copy(i).wait_recv()
            self.add(self.passing, self.term, i)
            self.across_copy(i).start()

        def settle(src):
            self.across_copy(j).wait_recv()
            self.add(self.total, src, j)
            self.back_copy(j).start()

        if self.early < self.count:
            end = jnp.logical_not(self.inner) & (now >= self.early)
            self.due(now, end, lambda: self.out_copy(now).start())
        if self.given:
            self.due(i, self.inner & (i >= self.given), pass_on)
            self.due(j, self.inner & (j < self.given), lambda: settle(self.term))
            self.due(j, self.inner & (j >= self.given), lambda: settle(self.passing))
        else:
            self.due(i, self.inner, pass_on)
            self.due(j, self.inner, lambda: settle(self.passing))

    def send(self, first, count):
        @pl.when(jnp.logical_not(self.inner))
        def _():
            @pl.loop(0, count)
            def _(i):
                self.out_copy(first + i).start()

    def steps(self):
        return self.count + self.SECOND

    def each(self, who, job):
        @pl.when(who)
        def _():
            @pl.loop(0, self.count)
            def _(i):
                job(i)

    def receive(self, i):
        @pl.when(jnp.logical_not(self.inner))
        def _():
            self.back_copy(i).wait_recv()

    def receive_all(self):
        self.each(jnp.logical_not(self.inner), lambda i: self.back_copy(i).wait_recv())

    def finish(self):
        def sent(i):
            self.across_copy(i).wait_send()
            self.back_copy(i).wait_send()

        self.each(self.inner, sent)
        @pl.when(jnp.logical_not(self.inner))
        def _():
            @pl.loop(self.given, self.count)
            def _(i):
                self.out_copy(i).wait_send()


def quotient(a, b):
    return a // b if isinstance(a, int) else lax.div(a, b)


def remainder(a, b):
    return a % b if isinstance(a, int) else lax.rem(a, b)


def multiple(value, of):
    return value if isinstance(value, int) else pl.multiple_of(value, of)


def by_step(now, plan):
    for first, last, stride, job in plan:
        if first == last:

            @pl.when(now == first)
            def _():
                job(0)

        else:
            due = (now >= first) & (now <= last)
            if stride > 1:
                due = due & (lax.rem(now - first, stride) == 0)

            @pl.when(due)
            def _():
                job(lax.div(now - first, stride))


def lanes(shape):
    return lax.broadcasted_iota(jnp.int32, shape, len(shape) - 1)


def turn(vectors, cos_table, sin_table):
    near = jnp.where(
        lanes(vectors.shape) % 64 < 32, pltpu.roll(vectors, 96, 1), pltpu.roll(vectors, 32, 1)
    )
    return vectors * cos_table + near * sin_table


def token_column(row):
    return jnp.broadcast_to(row, (128, row.shape[1])).T


def key_marks(column, first_id):
    lane = lanes(column.shape) % 64
    one_hot = (column - first_id).astype(jnp.int32) == lane
    return jnp.where(one_hot | ((lane >= 4) & (lane < 7)), 1.0, 0.0)


def query_marks(column, first_id):
    lane = lanes(column.shape) % 64
    other = (column - first_id).astype(jnp.int32) != lane
    return jnp.where(other & (lane < 4), -1e30, 0.0)


def nt_dot(left, right):
    return lax.dot_general(
        left, right, (((1,), (1,)), ((), ())), preferred_element_type=jnp.float32
    )


def attend_kernel(
    chain, places, x, ids, gains, key_shard, value_shard, inverse, query_shard, out_shard, gate_shard, up_shard,
    down_shard, gate_full, up_full, down_full, query_full, pair_full, out_full, attn_sum, normed_out, query_out,
    pairs, attended_out, log_out, cos_out, sin_out, small_out, small, gate_here, up_here, down_here, small_all, query_here, pair_here, pair_shard,
    out_here, pre_row, normed, query, attended, log_total, cos_table, sin_table, key_side, value_side, marks,
    scores, peak, mixed, near_pairs, term, passing, total, small_sems, gather_sems, local_sems, pair_sems,
    chain_sems, store_sems, load_sems,
):
    count = term.shape[0] // 2
    tokens = x.shape[0]
    heads = query.shape[1] // 64
    me = lax.axis_index("tokens")
    place = lax.rem(me, places)
    far = place >= 2
    loads = [
        pltpu.make_async_copy(src, dst, load_sems.at[k])
        for k, (src, dst) in enumerate(
            ((gate_shard, gate_here), (up_shard, up_here), (down_shard, down_here))
        )
    ]
    for load in loads:
        load.start()
    small[...] = jnp.zeros(small.shape, jnp.float32)
    small[0:1, :] = ids[...].astype(jnp.float32)
    small[1:2, :] = gains[...]
    greet(range(1, 8), chain)

    def small_copy(flip):
        return remote(
            small,
            small_all.at[me],
            small_sems.at[0, flip - 1],
            small_sems.at[1, flip - 1],
            token_device(flip),
        )

    def gather(k, shard, full, axis, part=(0, 1)):
        return Gather(
            shard, full, axis, gather_sems.at[0, k], gather_sems.at[1, k], local_sems.at[k], part
        )

    gather_query = gather(0, query_shard, query_here, 0)
    gather_pair = gather(1, pair_shard, pair_here, 0)
    gather_out = gather(2, out_shard, out_here, 1)
    half_rows = gate_here.shape[0] // 2
    gate_one, gate_two, up, down = (
        gather(3, gate_here.at[pl.ds(0, half_rows)], gate_full, 0, (0, 2)),
        gather(4, gate_here.at[pl.ds(half_rows, half_rows)], gate_full, 0, (1, 2)),
        gather(5, up_here, up_full, 0),
        gather(6, down_here, down_full, 1),
    )
    stores = []

    def store(src, out):
        copy = pltpu.make_async_copy(src, out, store_sems.at[len(stores)])
        copy.start()
        stores.append(copy)

    for flip in range(1, 8):
        small_copy(flip).start()
    both = jnp.concatenate(
        [key_shard[...].astype(jnp.float32), value_shard[...].astype(jnp.float32)], axis=0
    )
    pair_shard[...] = both.T.astype(jnp.bfloat16)
    gather_pair.start()
    gather_query.start()
    small_all[me] = small[...]
    x_f = x[...].astype(jnp.float32)
    pre_scale = lax.rsqrt(jnp.mean(x_f * x_f, axis=1, keepdims=True) + 1e-05)

    for flip in range(1, 8):
        small_copy(flip).wait_recv()
    store(small_all, small_out)
    width = x.shape[1] // 8
    for k in range(8):
        pre_row[:, k * width : (k + 1) * width] = jnp.broadcast_to(
            small_all[k, 1:2, :width], (8, width)
        )
    gather_pair.relay()
    normed[...] = (x[...].astype(jnp.float32) * pre_scale * pre_row[0:1, :]).astype(jnp.bfloat16)
    store(normed, normed_out)
    first_device = me - place
    first_id = (first_device // places * 4).astype(jnp.float32)
    own = token_column(small_all[me, 0:1, :])
    before = jnp.zeros((tokens, 1), jnp.float32)
    for k in range(places):
        others = small_all[first_device + k, 0:1, :]
        before = before + jnp.sum(
            jnp.where(others < own[:, 0:1], 1.0, 0.0), axis=1, keepdims=True
        )
        column = token_column(others)
        marks[pl.ds(k * tokens, tokens), :] = key_marks(column, first_id)
    row_index = lax.broadcasted_iota(jnp.int32, (tokens, 128), 0) + place * tokens
    turned = (row_index.astype(jnp.float32) - before) * inverse[0:1, :]
    cos_table[...] = jnp.cos(turned)
    sin_signed = jnp.sin(turned)
    sin_table[...] = jnp.where(lanes(sin_signed.shape) % 64 < 32, -sin_signed, sin_signed)
    store(cos_table, cos_out)
    store(sin_table, sin_out)
    gather_query.relay()
    gather_pair.finish_relay()
    gather_pair.finish()

    made = jnp.dot(normed[...], pair_here[...], preferred_element_type=jnp.float32)
    spun = turn(made, cos_table[...], sin_table[...])
    near_pairs[place] = jnp.where(lanes(made.shape) < 64, spun, made).astype(jnp.bfloat16)

    def pair_copy(slot, flip):
        at = place - 2 if slot == 2 else place
        return remote(
            near_pairs.at[at],
            near_pairs.at[at],
            pair_sems.at[0, slot],
            pair_sems.at[1, slot],
            token_device(flip),
        )

    pair_copy(0, 1).start()

    @pl.when(jnp.logical_not(far))
    def _():
        pair_copy(1, 2).start()

    gather_out.start()
    for load in loads:
        load.wait()
    gate_one.start()
    gather_query.finish_relay()
    gather_query.finish()
    for low in range(0, query.shape[1], 256):
        made = jnp.dot(
            normed[...], query_here[:, low : low + 256], preferred_element_type=jnp.float32
        )
        for group in range(low, low + 256, 128):
            spun = turn(made[:, group - low : group - low + 128], cos_table[...], sin_table[...])
            query[:, group : group + 128] = (spun * 0.125).astype(jnp.bfloat16)
    store(query, query_out)
    store(query_here, query_full)
    store(pair_here, pair_full)
    pair_copy(0, 1).wait_recv()

    @pl.when(far)
    def _():
        pair_copy(1, 2).wait_recv()
        pair_copy(2, 1).start()
        pair_copy(2, 1).wait_recv()

    @pl.when(jnp.logical_not(far))
    def _():
        gather_out.relay()

    @pl.when(jnp.logical_not(far))
    def _():
        gate_two.start()

    for k in range(places):

        @pl.when(k <= place)
        def _():
            pair = near_pairs[k].astype(jnp.float32)
            swapped = pltpu.roll(pair, 64, 1)
            lane = lanes(pair.shape)
            mark = marks[pl.ds(k * tokens, tokens), :]
            block = pl.ds(k * tokens, tokens)
            key_side[0, block] = jnp.where(lane < 64, pair, mark).astype(jnp.bfloat16)
            key_side[1, block] = jnp.where(lane < 64, mark, swapped).astype(jnp.bfloat16)
            value_side[0, block] = jnp.where(lane < 64, swapped, 1.0).astype(jnp.bfloat16)
            value_side[1, block] = jnp.where(lane < 64, 1.0, pair).astype(jnp.bfloat16)

    store(near_pairs, pairs)
    lane = lanes((tokens, 128))
    own_marks = query_marks(own, first_id)

    def side_of(group, e):
        at = pl.ds(multiple(group * 128, 128), 128)
        mine = (lane < 64) if e == 0 else (lane >= 64)
        return jnp.where(mine, query[:, at].astype(jnp.float32), own_marks).astype(jnp.bfloat16)

    def keys_at(k):
        return pl.ds(pl.multiple_of(k * tokens, tokens), tokens)

    def look(e, side, k, masked):
        found = nt_dot(side, key_side[e, keys_at(k)])
        if masked:
            rows = lax.broadcasted_iota(jnp.int32, found.shape, 0)
            found = jnp.where(lanes(found.shape) <= rows, found, -1e30)
        scores[e, k] = found
        best = found[:, :128]
        for part in range(128, tokens, 128):
            best = jnp.maximum(best, found[:, part : part + 128])
        peak[e] = best if masked else jnp.maximum(peak[e], best)

    def blend(e, k, first):
        parts = [
            jnp.exp(scores[e, k, :, part : part + 128] - peak[e]).astype(jnp.bfloat16)
            for part in range(0, tokens, 128)
        ]
        made = jnp.dot(
            jnp.concatenate(parts, axis=1),
            value_side[e, keys_at(k)],
            preferred_element_type=jnp.float32,
        )
        mixed[e] = made if first else mixed[e] + made

    def settle(e):
        peak[e] = jnp.broadcast_to(jnp.max(peak[e], axis=1, keepdims=True), lane.shape)

    def finish_head(group, e):
        mine = (lane < 64) if e == 0 else (lane >= 64)
        at = pl.ds(multiple(group * 128, 128), 128)
        out = mixed[e]
        sums = jnp.where(mine, pltpu.roll(out, 64, 1), out)
        share = out / sums
        attended[:, at] = share if e == 0 else jnp.where(lane < 64, attended[:, at], share)
        noted = peak[e] + jnp.log(sums)
        log_total[...] = jnp.where(lane == 2 * group + e, noted, log_total[...])

    def stage(done, begun):
        side = side_of(*begun) if begun else None
        if begun:
            look(begun[1], side, place, True)
        if done:
            blend(done[1], place, True)

        @pl.loop(0, place)
        def _(k):
            if begun:
                look(begun[1], side, k, False)
            if done:
                blend(done[1], k, False)

        if done:
            finish_head(*done)
        if begun:
            settle(begun[1])

    log_total[...] = jnp.zeros(lane.shape, jnp.float32)
    stage(None, (0, 0))
    last = heads // 2 - 1

    @pl.loop(0, last)
    def _(group):
        stage((group, 0), (group, 1))

        @pl.when(far & (group == 0))
        def _():
            gather_out.relay()

        @pl.when(far & (group == 0))
        def _():
            gate_two.start()

        @pl.when(group == 2)
        def _():
            up.start()

        stage((group, 1), (group + 1, 0))

    stage((last, 0), (last, 1))
    stage((last, 1), None)
    store(attended, attended_out)
    store(log_total, log_out)
    gather_out.finish_relay()

    gather_out.finish()
    low = attended[...].astype(jnp.bfloat16)
    each = term.shape[2]

    @pl.loop(0, count)
    def _(k):
        cut = pl.ds(pl.multiple_of(k * 2 * each, 2 * each), 2 * each)
        made = jnp.dot(low, out_here[:, cut], preferred_element_type=jnp.float32).astype(
            jnp.bfloat16
        )
        term[2 * k] = made[:, :each]
        term[2 * k + 1] = made[:, each:]

    store(out_here, out_full)

    down.start()
    line = LineSum(term, passing, total, chain_sems, 2)
    line.send(0, line.count)
    relays = [
        (at, at, 1, lambda _, job=job: job())
        for at, job in (
            (0, gate_one.relay),
            (5, gate_two.relay),
            (13, up.relay),
            (24, down.relay),
            (26, gate_one.finish_relay),
            (28, gate_two.finish_relay),
            (32, up.finish_relay),
        )
    ]

    @pl.loop(0, line.steps())
    def _(now):
        by_step(now, relays)
        line.step(now)

    line.receive_all()
    store(total, attn_sum)
    down.finish_relay()
    line.finish()
    for part in (gate_one, gate_two, up, down):
        part.finish()
    for flip in range(1, 8):
        small_copy(flip).wait_send()
    pair_copy(0, 1).wait_send()

    @pl.when(far)
    def _():
        pair_copy(2, 1).wait_send()

    @pl.when(jnp.logical_not(far))
    def _():
        pair_copy(1, 2).wait_send()

    for copy in stores:
        copy.wait()


def attend(
    chain, places, x, ids, gains, key_weight, value_weight, inverse, query_weight, out_weight, gate_weight, up_weight,
    down_weight,
):
    tokens, width = x.shape
    count = 8
    heads_wide = query_weight.shape[1]
    bf16, f32 = jnp.bfloat16, jnp.float32
    row = places * tokens
    each = width // (2 * count)
    small = (8, tokens)
    anywhere, vmem = pl.BlockSpec(memory_space=pl.ANY), pl.BlockSpec(memory_space=pltpu.VMEM)
    shape = jax.ShapeDtypeStruct
    chunks = (2 * count, tokens, each)
    out_shape = [
        shape((gate_weight.shape[0] * 8, gate_weight.shape[1]), bf16),
        shape((up_weight.shape[0] * 8, up_weight.shape[1]), bf16),
        shape((down_weight.shape[0], down_weight.shape[1] * 8), bf16),
        shape((width, heads_wide), bf16),
        shape((width, 128), bf16),
        shape((heads_wide, width), bf16),
        shape(chunks, bf16),
        shape((tokens, width), bf16),
        shape((tokens, heads_wide), bf16),
        shape((places, tokens, 128), bf16),
        shape((tokens, heads_wide), f32),
        shape((tokens, 128), f32),
        shape((tokens, 128), f32),
        shape((tokens, 128), f32),
        shape((8,) + small, f32),
    ]
    return pl.pallas_call(
        functools.partial(attend_kernel, chain, places),
        out_shape=out_shape,
        in_specs=[vmem] * 6 + [anywhere] * 5,
        out_specs=[anywhere] * len(out_shape),
        scratch_shapes=[
            pltpu.VMEM(small, f32),
            pltpu.VMEM(gate_weight.shape, bf16),
            pltpu.VMEM(up_weight.shape, bf16),
            pltpu.VMEM(down_weight.shape, bf16),
            pltpu.VMEM((8,) + small, f32),
            pltpu.VMEM((width, heads_wide), bf16),
            pltpu.VMEM((width, 128), bf16),
            pltpu.VMEM((width // 8, 128), bf16),
            pltpu.VMEM((heads_wide, width), bf16),
            pltpu.VMEM((8, width), f32),
            pltpu.VMEM((tokens, width), bf16),
            pltpu.VMEM((tokens, heads_wide), bf16),
            pltpu.VMEM((tokens, heads_wide), f32),
            pltpu.VMEM((tokens, 128), f32),
            pltpu.VMEM((tokens, 128), f32),
            pltpu.VMEM((tokens, 128), f32),
            pltpu.VMEM((2, row, 128), bf16),
            pltpu.VMEM((2, row, 128), bf16),
            pltpu.VMEM((row, 128), f32),
            pltpu.VMEM((2, places, tokens, tokens), f32),
            pltpu.VMEM((2, tokens, 128), f32),
            pltpu.VMEM((2, tokens, 128), f32),
            pltpu.VMEM((places, tokens, 128), bf16),
            pltpu.VMEM(chunks, bf16),
            pltpu.VMEM(chunks, bf16),
            pltpu.VMEM(chunks, bf16),
            pltpu.SemaphoreType.DMA((2, 7)),
            pltpu.SemaphoreType.DMA((2, 7, Gather.COPIES)),
            pltpu.SemaphoreType.DMA((7,)),
            pltpu.SemaphoreType.DMA((2, 3)),
            pltpu.SemaphoreType.DMA((4, 4 * count)),
            pltpu.SemaphoreType.DMA((len(out_shape),)),
            pltpu.SemaphoreType.DMA((3,)),
        ],
        compiler_params=pltpu.CompilerParams(
            collective_id=0, has_side_effects=True, vmem_limit_bytes=VMEM_BYTES
        ),
        name="attend_forward",
    )(
        x, ids, gains, key_weight.T, value_weight.T, inverse, query_weight, out_weight, gate_weight, up_weight,
        down_weight,
    )


def greet(flips, chain):
    me, here = lax.axis_index("tokens"), lax.axis_index("heads")
    barrier = pltpu.get_barrier_semaphore()
    for flip in flips:
        pl.semaphore_signal(barrier, inc=1, device_id=token_device(flip), device_id_type=MESH_ID)
    for step in (-1, 1):
        near = here + step

        @pl.when((near >= 0) & (near < chain))
        def _():
            pl.semaphore_signal(barrier, inc=1, device_id=(me, near), device_id_type=MESH_ID)

    edge = (here == 0) | (here == chain - 1)

    @pl.when(edge)
    def _():
        pl.semaphore_wait(barrier, len(flips) + 1)

    @pl.when(jnp.logical_not(edge))
    def _():
        pl.semaphore_wait(barrier, len(flips) + 2)


class Reduce:
    COPIES = 6

    def __init__(self, own, near, sems):
        self.own, self.near, self.sems = own, near, sems

    def copy(self, slot):
        k, half, flip = ((1, 0, 2), (3, 0, 2), (2, 1, 4), (3, 1, 4), (2, 0, 4), (1, 1, 2))[slot]
        rows = self.own.shape[1] // 2
        return remote(
            self.own.at[k, pl.ds(half * rows, rows)],
            self.near.at[slot],
            self.sems.at[0, slot],
            self.sems.at[1, slot],
            token_device(flip),
        )

    def put(self, k, block):
        self.own[k] = block.astype(self.own.dtype)
        self.send(k)

    def send(self, k):
        for which, slots in ((3, (1, 3)), (1, (0,)), (2, (2,))):

            @pl.when(k == which)
            def _():
                for slot in slots:
                    self.copy(slot).start()

    def add_near(self, k, half, slot):
        rows = self.own.shape[1] // 2

        @pl.loop(0, rows // 32)
        def _(i):
            here = pl.ds(pl.multiple_of(i * 32, 32), 32)
            place = pl.ds(pl.multiple_of(half * rows + i * 32, 32), 32)
            self.own[k, place] = (
                self.own[k, place].astype(jnp.float32) + self.near[slot, here].astype(jnp.float32)
            ).astype(self.own.dtype)

    def second(self):
        self.copy(1).wait_recv()
        self.add_near(2, 0, 1)
        self.copy(4).start()
        self.copy(3).wait_recv()
        self.add_near(1, 1, 3)
        self.copy(5).start()

    def finish(self, out):
        rows = self.own.shape[1] // 2
        for half, slots in ((0, (0, 4)), (1, (2, 5))):
            for slot in slots:
                self.copy(slot).wait_recv()

            @pl.loop(0, rows // 32)
            def _(i):
                here = pl.ds(pl.multiple_of(i * 32, 32), 32)
                place = pl.ds(pl.multiple_of(half * rows + i * 32, 32), 32)
                total = self.own[0, place].astype(jnp.float32)
                for slot in slots:
                    total = total + self.near[slot, here].astype(jnp.float32)
                out[place, :] = total.astype(out.dtype)

        for slot in range(self.COPIES):
            self.copy(slot).wait_send()

    def halfway(self):
        for slot, (k, half) in enumerate(((0, 0), (2, 0), (0, 1), (1, 1))):
            self.copy(slot).wait_recv()
            self.copy(slot).wait_send()
            self.add_near(k, half, slot)


def block_order(i):
    return jnp.where(i == 0, 3, jnp.where(i == 1, 1, jnp.where(i == 2, 2, 0)))


def tn_dot(left, right):
    return lax.dot_general(
        left, right, (((0,), (0,)), ((), ())), preferred_element_type=jnp.float32
    )


def tiles_of(length, size):
    return [(low, min(low + size, length)) for low in range(0, length, size)]


def feed_kernel(
    chain, small_all, x_in, attn_in, cotangent_in, gate_full, up_full, down_full, back_sum, hidden_out, mlp_term,
    scale_out, grad_gate_out, up_out, x, attn_sum, cotangent, hidden, scale, grad_gate, gate, up, down, mid_row, normed, back_gate, back_up, term, passing, total,
    own_gate, near_gate, own_up, near_up, mlp_near, load_sems, swap_sems, chain_sems, reduce_sems, store_sems,
    lead_sems,
):
    count = term.shape[0] // 2
    each = term.shape[2]
    tokens, width = x.shape
    inner = gate.shape[1]
    me = lax.axis_index("tokens")
    tiles = tiles_of(inner, 512)
    early = [
        pltpu.make_async_copy(src, dst, load_sems.at[k])
        for k, (src, dst) in enumerate(((x_in, x), (attn_in, attn_sum), (cotangent_in, cotangent)))
    ]
    loads = []
    for k, (low, high) in enumerate(tiles):
        cut = pl.ds(low, high - low)
        loads.append(
            (
                pltpu.make_async_copy(gate_full.at[:, cut], gate.at[:, cut], load_sems.at[4 + 3 * k]),
                pltpu.make_async_copy(up_full.at[:, cut], up.at[:, cut], load_sems.at[5 + 3 * k]),
                pltpu.make_async_copy(down_full.at[cut, :], down.at[cut, :], load_sems.at[6 + 3 * k]),
            )
        )
    for load in early:
        load.start()
    for group in loads:
        for load in group:
            load.start()
    greet((1, 2, 4), chain)

    span = width // 8
    for k in range(8):
        mid_row[:, k * span : (k + 1) * span] = jnp.broadcast_to(
            small_all[k, 1:2, span : 2 * span], (8, span)
        )

    early[0].wait()
    early[1].wait()
    line = LineSum(term, passing, total, chain_sems, 2)
    half = tokens // 2

    def swap(k, ref, row, cut):
        return remote(
            ref.at[pl.ds(multiple(row, half), half), cut],
            ref.at[pl.ds(multiple(tokens + row, half), half), cut],
            swap_sems.at[0, k],
            swap_sems.at[1, k],
            token_device(1),
        )

    def swaps_of(part):
        row = part * half
        found = [swap(part, normed, row, pl.ds(0, width))]
        for k, (low, high) in enumerate(tiles):
            for j, ref in enumerate((back_gate, back_up)):
                found.append(
                    swap(2 + (part * len(tiles) + k) * 2 + j, ref, row, pl.ds(low, high - low))
                )
        return found

    ahead = 3

    def mid_pair(n, row):
        cut = pl.ds(pl.multiple_of(n * 2 * each, 2 * each), 2 * each)
        place = pl.ds(row, half)
        made = nt_dot(back_gate[place, :], gate[cut, :]) + nt_dot(back_up[place, :], up[cut, :])
        made = made.astype(jnp.bfloat16)
        term[2 * n, place] = made[:, :each]
        term[2 * n + 1, place] = made[:, each:]

    early[2].wait()

    @pl.loop(0, 2)
    def _(part):
        row = pl.multiple_of(part * half, half)
        rows = pl.ds(row, half)

        def middle_here(c):
            cut = slice(c * each, (c + 1) * each)
            return x[rows, cut].astype(jnp.float32) + attn_sum[c, rows].astype(jnp.float32)

        squares = jnp.zeros((half, each), jnp.float32)
        for c in range(2 * count):
            found = middle_here(c)
            squares = squares + found * found
        mid_scale = lax.rsqrt(jnp.sum(squares, axis=1, keepdims=True) / width + 1e-05)
        scale[rows] = jnp.broadcast_to(mid_scale, (half, scale.shape[1]))
        for c in range(2 * count):
            cut = slice(c * each, (c + 1) * each)
            normed[rows, cut] = (middle_here(c) * mid_scale * mid_row[0:1, cut]).astype(jnp.bfloat16)
        copies = swaps_of(part)
        copies[0].start()
        for k, (low, high) in enumerate(tiles):

            @pl.when(part == 0)
            def _():
                for load in loads[k]:
                    load.wait()

            gate_rows = jnp.dot(
                normed[rows, :], gate[:, low:high], preferred_element_type=jnp.float32
            )
            up_rows = jnp.dot(normed[rows, :], up[:, low:high], preferred_element_type=jnp.float32)
            back_hidden = nt_dot(cotangent[rows, :], down[low:high, :])
            sigmoid = jax.nn.sigmoid(gate_rows)
            silu = gate_rows * sigmoid
            hidden[rows, low:high] = (silu * up_rows).astype(jnp.bfloat16)
            back_gate[rows, low:high] = (
                back_hidden * up_rows * sigmoid * (1.0 + gate_rows * (1.0 - sigmoid))
            ).astype(jnp.bfloat16)
            back_up[rows, low:high] = (back_hidden * silu).astype(jnp.bfloat16)
            for copy in copies[1 + 2 * k : 3 + 2 * k]:
                copy.start()

            @pl.when(part == 1)
            def _():
                line.step(2 * k)
                line.step(2 * k + 1)

        @pl.when(part == 0)
        def _():
            @pl.loop(0, ahead)
            def _(n):
                mid_pair(n, 0)
                line.send(2 * n, 2)

    stores = []

    def store(src, out):
        copy = pltpu.make_async_copy(src, out, store_sems.at[len(stores)])
        copy.start()
        stores.append(copy)

    store(hidden, hidden_out)
    store(scale, scale_out)

    def mlp_place(n):
        rows = pl.ds(multiple(remainder(n, 4) * tokens, tokens), tokens)
        return rows, quotient(n, 4) * 2 * each

    def mlp_at(c):
        rows, low = mlp_place(quotient(c, 2))
        low = low + remainder(c, 2) * each
        return gate.at[rows, pl.ds(multiple(low, each), each)]

    lead = mlp_near.shape[0]

    def lead_copy(c):
        return remote(
            mlp_at(c), mlp_near.at[c], lead_sems.at[0, c], lead_sems.at[1, c], line.mate
        )

    def mlp_pair(n):
        cut = pl.ds(pl.multiple_of(n * 2 * each, 2 * each), 2 * each)
        made = jnp.dot(hidden[...], down[:, cut], preferred_element_type=jnp.float32)
        rows, low = mlp_place(n)
        gate[rows, pl.ds(pl.multiple_of(low, 2 * each), 2 * each)] = made.astype(jnp.bfloat16)

        @pl.when(n >= lead // 2)
        def _():
            for k in range(2):
                pltpu.make_async_copy(
                    mlp_at(2 * n + k), mlp_term.at[2 * n + k], load_sems.at[3]
                ).start()

        @pl.when((n < lead // 2) & jnp.logical_not(line.inner))
        def _():
            for k in range(2):
                lead_copy(2 * n + k).start()

    def lead_store(c):
        return pltpu.make_async_copy(mlp_near.at[c], mlp_term.at[c], lead_sems.at[2, c])

    gate_sum = Reduce(own_gate, near_gate, reduce_sems.at[0])
    up_sum = Reduce(own_up, near_up, reduce_sems.at[1])

    def grad_block(part, ref, k):
        index = jnp.bitwise_xor(me, 2 * k)
        cut = pl.ds(pl.multiple_of(index * span, span), span)
        part.put(k, tn_dot(normed[:, cut], ref[...]))

    def received(which):
        for part in range(2):
            for copy in swaps_of(part)[which]:
                copy.wait_recv()

    def late_pair(i):
        i = i + ahead
        part = jnp.where(i < count, 0, 1)
        n = i - part * count
        mid_pair(n, pl.multiple_of(part * half, half))
        line.send(part * 2 * count + 2 * n, 2)

    def late_pairs(i):
        late_pair(2 * i)

        @pl.when(2 * i + 1 + ahead < 2 * count)
        def _():
            late_pair(2 * i + 1)

    begun = 2 * len(tiles)
    last_pairs = (2 * count - ahead + 1) // 2 - 1
    plan = (
        (0, last_pairs, 1, late_pairs),
        (0, 0, 1, lambda _: received(slice(0, 1))),
        (0, 0, 1, lambda _: received(slice(1, None, 2))),
        (0, 3, 1, lambda i: grad_block(gate_sum, back_gate, block_order(i))),
        (4, 4, 1, lambda _: received(slice(2, None, 2))),
        (4, 7, 1, lambda i: grad_block(up_sum, back_up, block_order(i))),
        (7, 7, 1, lambda _: gate_sum.second()),
        (last_pairs + 1, last_pairs + count, 1, mlp_pair),
    )

    @pl.loop(0, (line.steps() - begun + 1) // 2)
    def _(now):
        by_step(now, plan)
        line.step(begun + 2 * now)
        line.step(begun + 2 * now + 1)

    gate_sum.finish(grad_gate)
    store(grad_gate, grad_gate_out)
    line.receive_all()
    store(total, back_sum)
    @pl.when(line.inner)
    def _():
        for c in range(lead):
            lead_copy(c).wait_recv()
            mlp_near[c] = (
                mlp_near[c].astype(jnp.float32) + mlp_at(c)[...].astype(jnp.float32)
            ).astype(mlp_near.dtype)
            lead_store(c).start()

    up_sum.halfway()
    rows = span // 2
    store(own_up.at[0], up_out.at[pl.ds(0, span), :])
    store(own_up.at[2, pl.ds(0, rows)], up_out.at[pl.ds(span, rows), :])
    store(own_up.at[1, pl.ds(rows, rows)], up_out.at[pl.ds(span + rows, rows), :])
    line.finish()
    for part in range(2):
        for copy in swaps_of(part):
            copy.wait_send()

    rest = pl.ds(lead, 2 * count - lead)
    pltpu.make_async_copy(term.at[rest], total.at[rest], load_sems.at[3]).wait()

    @pl.when(line.inner)
    def _():
        for c in range(lead):
            lead_store(c).wait()

    @pl.when(jnp.logical_not(line.inner))
    def _():
        for c in range(lead):
            lead_copy(c).wait_send()

    for copy in stores:
        copy.wait()


def feed(chain, small_all, x, attn_sum, cotangent, gate_full, up_full, down_full):
    tokens, width = x.shape
    inner = gate_full.shape[1]
    count = attn_sum.shape[0] // 2
    span = width // 8
    bf16, f32 = jnp.bfloat16, jnp.float32
    anywhere, vmem = pl.BlockSpec(memory_space=pl.ANY), pl.BlockSpec(memory_space=pltpu.VMEM)
    shape = jax.ShapeDtypeStruct
    tiles = len(tiles_of(inner, 512))
    return pl.pallas_call(
        functools.partial(feed_kernel, chain),
        out_shape=[
            shape(attn_sum.shape, bf16),
            shape((tokens, inner), bf16),
            shape(attn_sum.shape, bf16),
            shape((tokens, 128), f32),
            shape((span, inner), bf16),
            shape((2 * span, inner), bf16),
        ],
        in_specs=[vmem] + [anywhere] * 6,
        out_specs=[anywhere] * 6,
        scratch_shapes=[
            pltpu.VMEM((tokens, width), bf16),
            pltpu.VMEM(attn_sum.shape, bf16),
            pltpu.VMEM((tokens, width), bf16),
            pltpu.VMEM((tokens, inner), bf16),
            pltpu.VMEM((tokens, 128), f32),
            pltpu.VMEM((span, inner), bf16),
            pltpu.VMEM((width, inner), bf16),
            pltpu.VMEM((width, inner), bf16),
            pltpu.VMEM((inner, width), bf16),
            pltpu.VMEM((8, width), f32),
            pltpu.VMEM((2 * tokens, width), bf16),
            pltpu.VMEM((2 * tokens, inner), bf16),
            pltpu.VMEM((2 * tokens, inner), bf16),
            pltpu.VMEM(attn_sum.shape, bf16),
            pltpu.VMEM(attn_sum.shape, bf16),
            pltpu.VMEM(attn_sum.shape, bf16),
            pltpu.VMEM((4, span, inner), bf16),
            pltpu.VMEM((6, span // 2, inner), bf16),
            pltpu.VMEM((4, span, inner), bf16),
            pltpu.VMEM((6, span // 2, inner), bf16),
            pltpu.VMEM((LEAD, tokens, 128), bf16),
            pltpu.SemaphoreType.DMA((4 + 3 * tiles,)),
            pltpu.SemaphoreType.DMA((2, 2 + 4 * tiles)),
            pltpu.SemaphoreType.DMA((4, 4 * count)),
            pltpu.SemaphoreType.DMA((2, 2, Reduce.COPIES)),
            pltpu.SemaphoreType.DMA((8,)),
            pltpu.SemaphoreType.DMA((3, LEAD)),
        ],
        compiler_params=pltpu.CompilerParams(
            collective_id=1, has_side_effects=True, vmem_limit_bytes=VMEM_BYTES
        ),
        name="feed_forward",
    )(small_all, x, attn_sum, cotangent, gate_full, up_full, down_full)


def split_marks(values, at):
    high = values.astype(jnp.bfloat16).astype(jnp.float32)
    rest = values - high
    middle = rest.astype(jnp.bfloat16).astype(jnp.float32)
    low = rest - middle
    return jnp.where(at == 4, high, jnp.where(at == 5, middle, jnp.where(at == 6, low, 0.0)))


def return_kernel(
    chain, places, small_all, query, pairs, log_total, cos_table, sin_table, scale,
    attended_in, x_in, attn_in, back_sum, query_full, pair_full, out_full, mlp_term, hidden_in, cotangent, normed_in, up_in, layer_out, grad_input, grad_down_out,
    grad_query, grad_key, grad_value, grad_out_out, grad_up_out, gains, mid_part, grad_down, grad_out, pair_back, grad_in, in_here, out_here, key_side, value_side, query_side, back_side, back_att,
    back_rows, back_keys, back_values, pair_out, pair_near, normed, back_attn, hidden, cotangents, att_low,
    back_all, pre_row, pre_part, gains_near, mlp_sum, mlp_passing, mlp_total, term, passing, total, own_down,
    near_down, own_in, near_in, own_out, near_out, load_sems, swap_sems, pair_sems, gain_sems, mlp_sems, chain_sems,
    reduce_sems, store_sems, up_half, up_near, up_sems,
):
    count = term.shape[0] // 2
    each = term.shape[2]
    tokens, width = x_in.shape
    span = width // 8
    groups = query.shape[1] // 128
    me = lax.axis_index("tokens")
    place = lax.rem(me, places)
    first_device = me - place
    mine, theirs = pl.ds(0, tokens), pl.ds(tokens, tokens)

    def load(k, src, dst):
        copy = pltpu.make_async_copy(src, dst, load_sems.at[k])
        copy.start()
        return copy

    load_mlp = load(5, mlp_term, mlp_sum)
    load_cot = load(2, cotangent, cotangents.at[mine, :])
    attended = back_rows
    load_attended = load(7, attended_in, attended)

    def back_at(side, c):
        row = multiple(remainder(c, 4) * tokens, tokens)
        return side.at[quotient(c, 4), pl.ds(row, tokens), :]

    def attn_at(c):
        row = multiple(quotient(remainder(c, 4), 2) * tokens, tokens)
        low = multiple(remainder(c, 2) * each, each)
        return own_down.at[quotient(c, 4), pl.ds(row, tokens), pl.ds(low, each)]

    for c in range(2 * count):
        side = key_side if c < count else value_side
        load(9, back_sum.at[c], back_at(side, c % count))
        load(10, x_in.at[:, pl.ds(c * each, each)], term.at[c])
        load(11, attn_in.at[c], attn_at(c))
    load_out = load(0, out_full, out_here)
    heads_wide = query.shape[1]
    load_in = load(1, query_full, in_here.at[:, pl.ds(0, heads_wide)])
    load_pair = load(6, pair_full, in_here.at[:, pl.ds(heads_wide, 128)])
    load_hidden = load(3, hidden_in, hidden.at[mine, :])
    load_normed = load(4, normed_in, normed.at[mine, :])
    load_up = load(13, up_in, up_half)
    greet(range(1, 8), chain)

    def swap(k, ref):
        copy = remote(
            ref.at[mine, :],
            ref.at[theirs, :],
            swap_sems.at[0, k],
            swap_sems.at[1, k],
            token_device(1),
        )
        copy.start()
        return copy

    def gain_copy(which, src, flip):
        other = jnp.bitwise_xor(me, flip)
        return remote(
            src.at[:, pl.ds(pl.multiple_of(other * span, span), span)],
            gains_near.at[me, :, pl.ds(which * span, span)],
            gain_sems.at[0, which, flip - 1],
            gain_sems.at[1, which, flip - 1],
            token_device(flip),
        )

    mlp_line = LineSum(mlp_sum, mlp_passing, mlp_total, mlp_sems, given=LEAD)
    load_mlp.wait()
    mlp_line.start_given()
    mlp_line.send(LEAD, 2 * count - LEAD)
    rows_up = up_near.shape[1]

    def up_copy(slot):
        return remote(
            up_half.at[pl.ds((2 + slot) * rows_up, rows_up), :],
            up_near.at[slot],
            up_sems.at[0, slot],
            up_sems.at[1, slot],
            token_device((4, 2)[slot]),
        )

    for k in range(8):
        pre_row[:, k * span : (k + 1) * span] = jnp.broadcast_to(
            small_all[k, 1:2, span : 2 * span], (8, span)
        )
    for k in (9, 10, 11):
        pltpu.make_async_copy(attn_in, term, load_sems.at[k]).wait()
    load_cot.wait()

    def hat_at(c):
        return (term[c].astype(jnp.float32) + attn_at(c)[...].astype(jnp.float32)) * scale[...]

    def cut_at(c):
        return pl.ds(multiple(c * each, each), each)

    summed_here = back_keys.at[1]
    summed_here[...] = jnp.zeros(summed_here.shape, jnp.float32)
    for base, side in ((0, key_side), (count, value_side)):

        @pl.loop(0, count)
        def _(c):
            cut = cut_at(base + c)
            shared = back_at(side, c)[...].astype(jnp.float32) * hat_at(base + c)
            summed_here[...] += shared * pre_row[0:1, cut]
            mid_part[:, cut] = jnp.broadcast_to(jnp.sum(shared, axis=0, keepdims=True), (8, each))

    mean = jnp.sum(summed_here[...], axis=1, keepdims=True) / width
    summed_here[...] = jnp.broadcast_to(mean, summed_here.shape)
    for flip in range(1, 8):
        gain_copy(1, mid_part, flip).start()
    mlp_line.step(LineSum.SECOND)
    load_up.wait()
    for slot in range(2):
        up_copy(slot).start()

    for base, side in ((0, key_side), (count, value_side)):

        @pl.loop(0, count)
        def _(c):
            cut = cut_at(base + c)
            u = back_at(side, c)[...].astype(jnp.float32) * pre_row[0:1, cut]
            found = scale[...] * (u - hat_at(base + c) * summed_here[...])
            back_attn[mine, cut] = (cotangents[mine, cut].astype(jnp.float32) + found).astype(
                jnp.bfloat16
            )

    mlp_line.step(LineSum.SECOND + 1)
    load_attended.wait()
    att_low[mine, :] = attended[...].astype(jnp.bfloat16)
    swap_back = swap(0, back_attn)
    swap_att = swap(1, att_low)

    lane = lanes((tokens, 128))
    at = lane % 64
    first_id = (first_device // places * 4).astype(jnp.float32)
    for k in range(places):
        mark = key_marks(token_column(small_all[first_device + k, 0:1, :]), first_id)
        block = pl.ds(k * tokens, tokens)

        @pl.when(k <= place)
        def _():
            pair = pairs[k].astype(jnp.float32)
            swapped = pltpu.roll(pair, 64, 1)
            key_side[0, block] = jnp.where(lane < 64, pair, mark).astype(jnp.bfloat16)
            key_side[1, block] = jnp.where(lane < 64, mark, swapped).astype(jnp.bfloat16)
            value_side[0, block] = jnp.where(lane < 64, swapped, 1.0).astype(jnp.bfloat16)
            value_side[1, block] = jnp.where(lane < 64, 1.0, pair).astype(jnp.bfloat16)

    own_marks = query_marks(token_column(small_all[me, 0:1, :]), first_id)

    load_out.wait()
    back_att[...] = nt_dot(back_attn[mine, :], out_here[...]).astype(jnp.bfloat16)
    swap_cot = swap(2, cotangents)
    mlp_line.step(LineSum.SECOND + 2)
    load_hidden.wait()
    swap_hidden = swap(3, hidden)

    @pl.loop(0, groups)
    def _(group):
        cut = pl.ds(pl.multiple_of(group * 128, 128), 128)
        back = back_att[:, cut].astype(jnp.float32)
        both = query[:, cut].astype(jnp.float32)
        shared = back * attended[:, cut]
        for e in range(2):
            head = 2 * group + e
            used = (lane < 64) if e == 0 else (lane >= 64)
            delta = jnp.sum(jnp.where(used, shared, 0.0), axis=1, keepdims=True)
            peak = jnp.sum(jnp.where(lane == head, log_total[...], 0.0), axis=1, keepdims=True)
            back_side[head] = jnp.where(
                used, back, split_marks(jnp.broadcast_to(-delta, lane.shape), at)
            ).astype(jnp.bfloat16)
            query_side[head] = jnp.where(
                used, both, own_marks + split_marks(jnp.broadcast_to(-peak, lane.shape), at)
            ).astype(jnp.bfloat16)

    load_normed.wait()
    swap_normed = swap(4, normed)
    load_in.wait()
    load_pair.wait()

    begun = LineSum.SECOND + 3
    back_rows[...] = jnp.zeros_like(back_rows)

    def key_step(k, diagonal):
        back_keys[...] = jnp.zeros_like(back_keys)
        back_values[...] = jnp.zeros_like(back_values)

        @pl.loop(0, groups)
        def _(group):
            cut = pl.ds(pl.multiple_of(group * 128, 128), 128)
            for low in (0, tokens // 2):
                keys_here = pl.ds(pl.multiple_of(k * tokens + low, tokens // 2), tokens // 2)
                part = pl.ds(low, tokens // 2)
                first = low if diagonal else 0
                seen = pl.ds(first, tokens - first)
                rows = []
                for e in range(2):
                    head = 2 * group + e
                    found = nt_dot(key_side[e, keys_here], query_side[head, seen])
                    chances = jnp.exp(found)
                    if diagonal:
                        keys = lax.broadcasted_iota(jnp.int32, found.shape, 0) + (low - first)
                        chances = jnp.where(keys <= lanes(found.shape), chances, 0.0)
                    moved = chances * nt_dot(value_side[e, keys_here], back_side[head, seen])
                    chances = chances.astype(jnp.bfloat16)
                    moved = moved.astype(jnp.bfloat16)
                    back_values[e, part] += jnp.dot(
                        chances, back_att[seen, cut], preferred_element_type=jnp.float32
                    )
                    back_keys[e, part] += jnp.dot(
                        moved, query[seen, cut], preferred_element_type=jnp.float32
                    )
                    rows.append(tn_dot(moved, key_side[e, keys_here]))
                back_rows[seen, cut] += jnp.where(lanes(rows[0].shape) < 64, rows[0], rows[1])

            @pl.when(group % 2 == 1)
            def _():
                mlp_line.step(begun + groups // 2 * k + group // 2)

        keys = back_keys[0] + pltpu.roll(back_keys[1], 64, 1)
        values = pltpu.roll(back_values[0], 64, 1) + back_values[1]
        return jnp.where(lane < 64, keys, values)

    def pair_copy(source, target):
        return remote(
            pair_out.at[target],
            pair_near.at[source],
            pair_sems.at[0, target],
            pair_sems.at[1, source],
            (first_device + target, lax.axis_index("heads")),
        )

    @pl.loop(0, place)
    def _(k):
        pair_out[k] = key_step(k, False).astype(jnp.bfloat16)
        pair_copy(place, k).start()

    own_pair = key_step(place, True)
    pair_out[place] = own_pair.astype(jnp.bfloat16)
    early = begun + groups // 2 * places

    @pl.loop(begun + groups // 2 * (place + 1), early)
    def _(now):
        mlp_line.step(now)

    for group in range(groups):
        cut = slice(group * 128, (group + 1) * 128)
        back_all[mine, cut] = (
            turn(back_rows[:, cut], cos_table[...], -sin_table[...]) * 0.125
        ).astype(jnp.bfloat16)
    back_keys[0] = own_pair
    for k in range(1, places):

        @pl.when(k > place)
        def _():
            remote(
                pair_out.at[k],
                pair_near.at[k],
                pair_sems.at[0, k],
                pair_sems.at[1, k],
                (first_device + k, lax.axis_index("heads")),
            ).wait_recv()
            back_keys[0] += pair_near[k].astype(jnp.float32)

    summed = back_keys[0]
    spun = turn(summed, cos_table[...], -sin_table[...])
    back_all[mine, pl.ds(groups * 128, 128)] = jnp.where(lane < 64, spun, summed).astype(
        jnp.bfloat16
    )
    swap_all = swap(5, back_all)

    def pre_pair(n):
        cut = pl.ds(pl.multiple_of(n * 2 * each, 2 * each), 2 * each)
        made = nt_dot(back_all[mine, :], in_here[cut, :]).astype(jnp.bfloat16)
        term[2 * n] = made[:, :each]
        term[2 * n + 1] = made[:, each:]
        line.send(2 * n, 2)

    def cut_of(k):
        index = jnp.bitwise_xor(me, 2 * k)
        return pl.ds(pl.multiple_of(index * span, span), span)

    down_sum = Reduce(own_down, near_down, reduce_sems.at[0])
    in_sum = Reduce(own_in, near_in, reduce_sems.at[1])
    out_sum = Reduce(own_out, near_out, reduce_sems.at[2])

    def down_block(i):
        k = block_order(i)
        for low, high in tiles_of(hidden.shape[1], 512):
            own_down[k, low:high] = tn_dot(hidden[:, low:high], cotangents[:, cut_of(k)]).astype(
                own_down.dtype
            )
        down_sum.send(k)

    def in_block(i):
        k = block_order(i)
        in_sum.put(k, tn_dot(normed[:, cut_of(k)], back_all[...]))

    def out_block(i):
        k = block_order(i)
        out_sum.put(k, tn_dot(att_low[...], back_attn[:, cut_of(k)]))

    def load_late():
        swap_cot.wait_send()
        load(8, x_in, cotangents.at[theirs, :])
        for c in range(2 * count):
            load(12, attn_in.at[c], cotangents.at[mine, pl.ds(c * each, each)])

    def wait_late():
        for k in (8, 12):
            pltpu.make_async_copy(x_in, cotangents.at[mine, :], load_sems.at[k]).wait()

    def x_at(c):
        return cotangents[theirs, cut_at(c)].astype(jnp.float32)

    def middle_at(c):
        return x_at(c) + cotangents[mine, cut_at(c)].astype(jnp.float32)

    wholes = (
        (grad_down, grad_down_out),
        (grad_out, grad_out_out),
        (grad_in.at[:, pl.ds(0, heads_wide)], grad_query),
        (pair_back.at[pl.ds(0, 64)], grad_key),
        (pair_back.at[pl.ds(64, 64)], grad_value),
        (up_half.at[pl.ds(0, 2 * rows_up), :], grad_up_out),
    )

    def whole(k):
        return pltpu.make_async_copy(*wholes[k], store_sems.at[2 + k])

    def store_block(c, src, out, sem):
        return pltpu.make_async_copy(src.at[c], out.at[:, cut_at(c)], store_sems.at[sem])

    def finish_mlp(_):
        mlp_line.receive_all()
        mlp_line.finish()

        @pl.loop(0, 2 * count)
        def _(c):
            mlp_sum[c] = (middle_at(c) + mlp_total[c].astype(jnp.float32)).astype(jnp.bfloat16)
            store_block(c, mlp_sum, layer_out, 0).start()

    weighed = back_keys.at[1]
    scale_here = back_keys.at[0]

    def scale_rows(_):
        wait_late()
        for k in range(8):
            pre_row[:, k * span : (k + 1) * span] = jnp.broadcast_to(
                small_all[k, 1:2, :span], (8, span)
            )
        scale_here[...] = jnp.zeros(scale_here.shape, jnp.float32)

        @pl.loop(0, 2 * count)
        def _(c):
            part = x_at(c)
            scale_here[...] += part * part

        mean = jnp.sum(scale_here[...], axis=1, keepdims=True) / width
        scale_here[...] = jnp.broadcast_to(lax.rsqrt(mean + 1e-05), scale_here.shape)
        weighed[...] = jnp.zeros(weighed.shape, jnp.float32)

    def weigh(i):
        line.receive(i)
        c, rows = line.place(i)
        size = tokens // line.parts
        first = lax.div(i, line.blocks) * size
        cut = cut_at(c)
        late = pl.ds(pl.multiple_of(tokens + first, size), size)
        hat = cotangents[late, cut].astype(jnp.float32) * scale_here[rows]
        shared = total[c, rows].astype(jnp.float32) * hat
        weighed[rows] += shared * pre_row[0:1, cut]
        summed = jnp.broadcast_to(jnp.sum(shared, axis=0, keepdims=True), (8, each))
        pre_part[:, cut] = jnp.where(i < line.blocks, 0.0, pre_part[:, cut]) + summed

    def finish_in(_):
        in_sum.finish(grad_in)
        pair_back[...] = grad_in[:, heads_wide:].astype(jnp.float32).T
        for k in (2, 3, 4):
            whole(k).start()

    def finish_up(_):
        for slot in range(2):
            up_copy(slot).wait()

            @pl.loop(0, rows_up // 32)
            def _(i):
                here = pl.ds(pl.multiple_of(i * 32, 32), 32)
                place = pl.ds(pl.multiple_of(slot * rows_up + i * 32, 32), 32)
                up_half[place, :] = (
                    up_half[place, :].astype(jnp.float32) + up_near[slot, here].astype(jnp.float32)
                ).astype(up_half.dtype)

        whole(5).start()

    def finish_down(_):
        down_sum.finish(grad_down)
        whole(0).start()

    def finish_out(_):
        out_sum.finish(grad_out)
        whole(1).start()

    line = LineSum(term, passing, total, chain_sems, 2, 2 * count)
    steps = line.steps()
    behind = 14

    def received(*copies):
        def job(_):
            for copy in copies:
                copy.wait_recv()

        return job

    plan = (
        (0, 2 * count - 2, 2, pre_pair),
        (1, 1, 1, received(swap_cot, swap_hidden)),
        (1, 7, 2, down_block),
        (8, 8, 1, lambda _: load_late()),
        (9, 9, 1, received(swap_back, swap_att)),
        (9, 12, 1, out_block),
        (13, 13, 1, received(swap_normed, swap_all)),
        (13, 13, 1, scale_rows),
        (14, 17, 1, in_block),
        (18, 18, 1, lambda _: down_sum.second()),
        (20, 20, 1, finish_mlp),
        (21, 21, 1, lambda _: out_sum.second()),
        (23, 23, 1, lambda _: in_sum.second()),
        (26, 26, 1, finish_up),
        (28, 28, 1, finish_down),
        (30, 30, 1, finish_out),
        (32, 32, 1, finish_in),
    )

    @pl.loop(0, steps)
    def _(now):
        by_step(now, plan)

        @pl.when(early + now < mlp_line.steps())
        def _():
            mlp_line.step(early + now)

        line.step(now)

        @pl.when(now >= behind)
        def _():
            weigh(now - behind)

    @pl.loop(steps - behind, line.count)
    def _(i):
        weigh(i)

    for flip in range(1, 8):
        gain_copy(0, pre_part, flip).start()
    mean = jnp.sum(weighed[...], axis=1, keepdims=True) / width
    weighed[...] = jnp.broadcast_to(mean, weighed.shape)
    line.finish()

    @pl.loop(0, 2 * count)
    def _(c):
        cut = cut_at(c)
        u = total[c].astype(jnp.float32) * pre_row[0:1, cut]
        found = scale_here[...] * (u - x_at(c) * scale_here[...] * weighed[...])
        term[c] = (back_attn[mine, cut].astype(jnp.float32) + found).astype(jnp.bfloat16)
        store_block(c, term, grad_input, 1).start()

    own = pl.ds(pl.multiple_of(me * span, span), span)
    gains_near[me, :, :span] = pre_part[:, own]
    gains_near[me, :, span:] = mid_part[:, own]
    for flip in range(1, 8):
        for which, src in enumerate((pre_part, mid_part)):
            gain_copy(which, src, flip).wait_recv()
    gains[...] = jnp.sum(gains_near[...], axis=0)
    for flip in range(1, 8):
        for which, src in enumerate((pre_part, mid_part)):
            gain_copy(which, src, flip).wait_send()
    for copy in (swap_back, swap_att, swap_hidden, swap_normed, swap_all):
        copy.wait_send()

    @pl.loop(0, place)
    def _(k):
        pair_copy(place, k).wait_send()

    for k in range(len(wholes)):
        whole(k).wait()

    for k in range(2):
        pltpu.make_async_copy(mlp_sum, term, store_sems.at[k]).wait()


def way_back(
    chain, places, small_all, query, pairs, log_total, cos_table, sin_table, scale, attended, x, attn_sum, back_sum,
    query_full, pair_full, out_full, mlp_term, hidden, cotangent, normed, up_half,
):
    tokens, width = x.shape
    inner = hidden.shape[1]
    heads_wide = query.shape[1]
    wide = heads_wide + 128
    chunks = attn_sum.shape
    count = chunks[0] // 2
    span = width // 8
    row = places * tokens
    bf16, f32 = jnp.bfloat16, jnp.float32
    anywhere, vmem = pl.BlockSpec(memory_space=pl.ANY), pl.BlockSpec(memory_space=pltpu.VMEM)
    shape = jax.ShapeDtypeStruct
    return pl.pallas_call(
        functools.partial(return_kernel, chain, places),
        out_shape=[
            shape((tokens, width), bf16),
            shape((tokens, width), bf16),
            shape((inner, span), bf16),
            shape((span, heads_wide), bf16),
            shape((64, span), f32),
            shape((64, span), f32),
            shape((heads_wide, span), bf16),
            shape((span, inner), bf16),
            shape((8, 2 * span), f32),
        ],
        in_specs=[vmem] * 7 + [anywhere] * 12,
        out_specs=[anywhere] * 8 + [vmem],
        scratch_shapes=[
            pltpu.VMEM((8, width), f32),
            pltpu.VMEM((inner, span), bf16),
            pltpu.VMEM((heads_wide, span), bf16),
            pltpu.VMEM((128, span), f32),
            pltpu.VMEM((span, wide), bf16),
            pltpu.VMEM((width, wide), bf16),
            pltpu.VMEM((heads_wide, width), bf16),
            pltpu.VMEM((2, row, 128), bf16),
            pltpu.VMEM((2, row, 128), bf16),
            pltpu.VMEM((heads_wide // 64, tokens, 128), bf16),
            pltpu.VMEM((heads_wide // 64, tokens, 128), bf16),
            pltpu.VMEM((tokens, heads_wide), bf16),
            pltpu.VMEM((tokens, heads_wide), f32),
            pltpu.VMEM((2, tokens, 128), f32),
            pltpu.VMEM((2, tokens, 128), f32),
            pltpu.VMEM((places, tokens, 128), bf16),
            pltpu.VMEM((places, tokens, 128), bf16),
            pltpu.VMEM((2 * tokens, width), bf16),
            pltpu.VMEM((2 * tokens, width), bf16),
            pltpu.VMEM((2 * tokens, inner), bf16),
            pltpu.VMEM((2 * tokens, width), bf16),
            pltpu.VMEM((2 * tokens, heads_wide), bf16),
            pltpu.VMEM((2 * tokens, wide), bf16),
            pltpu.VMEM((8, width), f32),
            pltpu.VMEM((8, width), f32),
            pltpu.VMEM((8, 8, 2 * span), f32),
            pltpu.VMEM(chunks, bf16),
            pltpu.VMEM(chunks, bf16),
            pltpu.VMEM(chunks, bf16),
            pltpu.VMEM(chunks, bf16),
            pltpu.VMEM(chunks, bf16),
            pltpu.VMEM(chunks, bf16),
            pltpu.VMEM((4, inner, span), bf16),
            pltpu.VMEM((6, inner // 2, span), bf16),
            pltpu.VMEM((4, span, wide), bf16),
            pltpu.VMEM((6, span // 2, wide), bf16),
            pltpu.VMEM((4, heads_wide, span), bf16),
            pltpu.VMEM((6, heads_wide // 2, span), bf16),
            pltpu.SemaphoreType.DMA((14,)),
            pltpu.SemaphoreType.DMA((2, 6)),
            pltpu.SemaphoreType.DMA((2, places)),
            pltpu.SemaphoreType.DMA((2, 2, 7)),
            pltpu.SemaphoreType.DMA((4, 2 * count)),
            pltpu.SemaphoreType.DMA((4, 4 * count)),
            pltpu.SemaphoreType.DMA((3, 2, Reduce.COPIES)),
            pltpu.SemaphoreType.DMA((8,)),
            pltpu.VMEM((2 * span, inner), bf16),
            pltpu.VMEM((2, span // 2, inner), bf16),
            pltpu.SemaphoreType.DMA((2, 2)),
        ],
        compiler_params=pltpu.CompilerParams(
            collective_id=2, has_side_effects=True, vmem_limit_bytes=VMEM_BYTES
        ),
        name="way_back",
    )(
        small_all, query, pairs, log_total, cos_table, sin_table, scale, attended, x, attn_sum, back_sum,
        query_full, pair_full, out_full, mlp_term, hidden, cotangent, normed, up_half,
    )


def hand_over_kernel(count, gains, *refs):
    ins, outs = refs[:count], refs[count : 2 * count]
    grad_pre, grad_mid = refs[2 * count : 2 * count + 2]
    held, wide, sems = refs[2 * count + 2 : 3 * count + 2], refs[3 * count + 2 : -1], refs[-1]
    loads = [pltpu.make_async_copy(ins[k], held[k], sems.at[0, k]) for k in range(count)]
    for load in loads:
        load.start()
    span = gains.shape[1] // 2
    grad_pre[...] = gains[0:1, :span]
    grad_mid[...] = gains[0:1, span:]
    stores = []
    wide = list(wide)
    for k, load in enumerate(loads):
        load.wait()
        ready = held[k]
        if outs[k].dtype != ready.dtype:
            ready = wide.pop(0)

            @pl.loop(0, ready.shape[0] // 32)
            def _(i):
                here = pl.ds(pl.multiple_of(i * 32, 32), 32)
                ready[here, :] = held[k][here, :].astype(ready.dtype)

        stores.append(pltpu.make_async_copy(ready, outs[k], sems.at[1, k]))
        stores[-1].start()
    for store in stores:
        store.wait()


def hand_over(gains, *arrays):
    count = len(arrays)
    anywhere, vmem = pl.BlockSpec(memory_space=pl.ANY), pl.BlockSpec(memory_space=pltpu.VMEM)
    half = jax.ShapeDtypeStruct((1, gains.shape[1] // 2), gains.dtype)
    types = [array.dtype if k < 2 else jnp.dtype(jnp.float32) for k, array in enumerate(arrays)]
    return pl.pallas_call(
        functools.partial(hand_over_kernel, count),
        out_shape=[jax.ShapeDtypeStruct(array.shape, kind) for array, kind in zip(arrays, types)]
        + [half, half],
        in_specs=[vmem] + [anywhere] * count,
        out_specs=[anywhere] * count + [vmem, vmem],
        scratch_shapes=[pltpu.VMEM(array.shape, array.dtype) for array in arrays]
        + [
            pltpu.VMEM(array.shape, kind)
            for array, kind in zip(arrays, types)
            if kind != array.dtype
        ]
        + [pltpu.SemaphoreType.DMA((2, count))],
        compiler_params=pltpu.CompilerParams(vmem_limit_bytes=VMEM_BYTES),
        name="hand_over",
    )(gains, *arrays)


def shards_cube(
    chain,
    inputs,
    segments,
    pre_gain,
    mid_gain,
    query_weight,
    key_weight,
    value_weight,
    out_weight,
    gate_weight,
    up_weight,
    down_weight,
    cotangent,
):
    row_count = inputs.shape[0]
    head_size = key_weight.shape[1]
    query_width = query_weight.shape[1]
    heads_here = query_width // head_size
    places = ROW // row_count
    gains = jnp.concatenate([pre_gain, mid_gain]).astype(jnp.float32)[None]
    half_size = head_size // 2
    inverse = 10000.0 ** (-np.arange(half_size, dtype=np.float32) / half_size)
    inverse = jnp.asarray(np.tile(inverse.astype(np.float32), (8, 128 // half_size)))
    (
        gate_full,
        up_full,
        down_full,
        query_full,
        pair_full,
        out_full,
        attn_sum,
        normed,
        query_rot,
        pairs,
        attended,
        log_total,
        cos_wide,
        sin_wide,
        small_full,
    ) = attend(
        chain,
        places,
        inputs,
        segments[None],
        gains,
        key_weight,
        value_weight,
        inverse,
        query_weight,
        out_weight,
        gate_weight,
        up_weight,
        down_weight,
    )
    back_sum, hidden, mlp_term, scale, grad_gate, up_half = feed(
        chain, small_full, inputs, attn_sum, cotangent, gate_full, up_full, down_full
    )
    layer_out, grad_input, grad_down, grad_query, grad_key, grad_value, grad_out, grad_up, gains = way_back(
        chain,
        places,
        small_full,
        query_rot,
        pairs,
        log_total,
        cos_wide,
        sin_wide,
        scale,
        attended,
        inputs,
        attn_sum,
        back_sum,
        query_full,
        pair_full,
        out_full,
        mlp_term,
        hidden,
        cotangent,
        normed,
        up_half,
    )
    (
        layer_out,
        grad_input,
        grad_query,
        grad_key,
        grad_value,
        grad_out,
        grad_gate,
        grad_up,
        grad_down,
        grad_pre,
        grad_mid,
    ) = hand_over(
        gains,
        layer_out,
        grad_input,
        grad_query,
        grad_key,
        grad_value,
        grad_out,
        grad_gate,
        grad_up,
        grad_down,
    )
    grad_pre, grad_mid = grad_pre[0], grad_mid[0]
    grad_key, grad_value = grad_key.T, grad_value.T
    return (
        layer_out,
        grad_input,
        grad_pre,
        grad_mid,
        grad_query,
        grad_key,
        grad_value,
        grad_out,
        grad_gate,
        grad_up,
        grad_down,
    )


def solution(mesh):
    sizes = dict(mesh.shape)
    plan = shards_any
    if sizes["tokens"] == 8 and sizes["heads"] == 4:
        plan = functools.partial(shards_cube, sizes["heads"])
    return jax.shard_map(
        plan,
        mesh=mesh,
        in_specs=(
            P("tokens", None),
            P("tokens"),
            P("tokens"),
            P("tokens"),
            P("tokens", "heads"),
            P("tokens", "heads"),
            P("tokens", "heads"),
            P("heads", "tokens"),
            P("tokens", "heads"),
            P("tokens", "heads"),
            P("heads", "tokens"),
            P("tokens", None),
        ),
        out_specs=(
            P("tokens", None),
            P("tokens", None),
            P("tokens"),
            P("tokens"),
            P("tokens", "heads"),
            P("tokens", "heads"),
            P("tokens", "heads"),
            P("heads", "tokens"),
            P("tokens", "heads"),
            P("tokens", "heads"),
            P("heads", "tokens"),
        ),
        check_vma=False,
    )
```

```python
import functools
import math

import jax
import jax.numpy as jnp
import numpy as np
from jax import lax
from jax.experimental import pallas as pl
from jax.experimental.pallas import tpu as pltpu
from jax.sharding import PartitionSpec as P

ROW = 2048


def rms_scale(vectors):
    return lax.rsqrt(jnp.mean(vectors * vectors, axis=-1, keepdims=True) + 1e-05)


def rotate(vectors, cos_table, sin_table):
    middle_index = vectors.shape[-1] // 2
    former = vectors[..., :middle_index]
    latter = vectors[..., middle_index:]
    return jnp.concatenate(
        [former * cos_table - latter * sin_table, latter * cos_table + former * sin_table], axis=-1
    )


def unrotate(gradient, cos_table, sin_table):
    middle_index = gradient.shape[-1] // 2
    former = gradient[..., :middle_index]
    latter = gradient[..., middle_index:]
    return jnp.concatenate(
        [former * cos_table + latter * sin_table, latter * cos_table - former * sin_table], axis=-1
    )


def norm_back(gradient, vectors, scale_rows, gain_row):
    shaped = vectors * scale_rows
    weighted = gradient * gain_row
    back_vectors = scale_rows * (
        weighted - shaped * jnp.mean(weighted * shaped, axis=-1, keepdims=True)
    )
    return (back_vectors, jnp.sum(gradient * shaped, axis=0))


def shards_any(
    inputs,
    segments,
    pre_gain,
    mid_gain,
    query_weight,
    key_weight,
    value_weight,
    out_weight,
    gate_weight,
    up_weight,
    down_weight,
    cotangent,
):
    row_count = inputs.shape[0]
    head_size = key_weight.shape[1]
    heads_here = query_weight.shape[1] // head_size
    myself = lax.axis_index("tokens")
    gathered = (
        lax.all_gather(pre_gain, "tokens", axis=0, tiled=True),
        lax.all_gather(mid_gain, "tokens", axis=0, tiled=True),
        lax.all_gather(query_weight, "tokens", axis=0, tiled=True),
        lax.all_gather(key_weight, "tokens", axis=0, tiled=True),
        lax.all_gather(value_weight, "tokens", axis=0, tiled=True),
        lax.all_gather(out_weight, "tokens", axis=1, tiled=True),
        lax.all_gather(gate_weight, "tokens", axis=0, tiled=True),
        lax.all_gather(up_weight, "tokens", axis=0, tiled=True),
        lax.all_gather(down_weight, "tokens", axis=1, tiled=True),
    )
    (
        pre_full,
        mid_full,
        query_full,
        key_full,
        value_full,
        out_full,
        gate_full,
        up_full,
        down_full,
    ) = gathered
    pre_row = pre_full.astype(jnp.float32)
    mid_row = mid_full.astype(jnp.float32)
    all_ids = lax.all_gather(segments, "tokens", axis=0, tiled=True)
    length = all_ids.shape[0]
    places = jnp.arange(length, dtype=jnp.int32)
    starts_here = jnp.concatenate([jnp.ones((1,), dtype=jnp.bool_), all_ids[1:] != all_ids[:-1]])
    opening = lax.cummax(jnp.where(starts_here, places, 0), axis=0)
    own_first = myself * row_count
    positions = lax.dynamic_slice_in_dim(places - opening, own_first, row_count)
    own_places = own_first + jnp.arange(row_count, dtype=jnp.int32)
    half_size = head_size // 2
    inverse = 10000.0 ** (-jnp.arange(half_size, dtype=jnp.float32) / half_size)
    turned = positions.astype(jnp.float32)[:, None] * inverse[None, :]
    cos_table = jnp.cos(turned)[:, None, :]
    sin_table = jnp.sin(turned)[:, None, :]
    inputs_f = inputs.astype(jnp.float32)
    pre_scale = rms_scale(inputs_f)
    normed = (inputs_f * pre_scale * pre_row).astype(jnp.bfloat16)
    queries = jnp.dot(normed, query_full, preferred_element_type=jnp.float32).reshape(
        row_count, heads_here, head_size
    )
    query_rot = (rotate(queries, cos_table, sin_table) * head_size ** (-0.5)).astype(jnp.bfloat16)
    key_rows = jnp.dot(normed, key_full, preferred_element_type=jnp.float32)[:, None, :]
    key_rot = rotate(key_rows, cos_table, sin_table)[:, 0, :].astype(jnp.bfloat16)
    value_low = jnp.dot(normed, value_full, preferred_element_type=jnp.float32).astype(jnp.bfloat16)
    key_all, value_all = (
        lax.all_gather(key_rot, "tokens", axis=0, tiled=True),
        lax.all_gather(value_low, "tokens", axis=0, tiled=True),
    )
    span = math.gcd(ROW, 1024)
    row_start = own_first // ROW * ROW
    block_first = row_start // span
    block_total = (own_first + row_count + span - 1) // span

    def key_block(block_index):
        opening_row = block_index * span
        block_keys = lax.dynamic_slice_in_dim(key_all, opening_row, span)
        block_values = lax.dynamic_slice_in_dim(value_all, opening_row, span)
        block_ids = lax.dynamic_slice_in_dim(all_ids, opening_row, span)
        block_places = opening_row + jnp.arange(span, dtype=jnp.int32)
        allowed = (segments[:, None] == block_ids[None, :]) & (
            own_places[:, None] >= block_places[None, :]
        )
        scores = jnp.einsum(
            "qhd,kd->qhk", query_rot, block_keys, preferred_element_type=jnp.float32
        )
        return (opening_row, block_keys, block_values, allowed[:, None, :], scores)

    def forward_step(block_index, state_now):
        row_peak, row_total, running = state_now
        opening_row, block_keys, block_values, allowed, scores = key_block(block_index)
        new_peak = jnp.maximum(row_peak, jnp.max(jnp.where(allowed, scores, -1e30), axis=-1))
        factor = jnp.exp(row_peak - new_peak)
        weights = jnp.where(allowed, jnp.exp(scores - new_peak[..., None]), 0.0)
        row_total = row_total * factor + jnp.sum(weights, axis=-1)
        running = running * factor[..., None] + jnp.einsum(
            "qhk,kd->qhd",
            weights.astype(jnp.bfloat16),
            block_values,
            preferred_element_type=jnp.float32,
        )
        return (new_peak, row_total, running)

    start_state = (
        jnp.full((row_count, heads_here), -1e30, jnp.float32),
        jnp.zeros((row_count, heads_here), jnp.float32),
        jnp.zeros((row_count, heads_here, head_size), jnp.float32),
    )
    row_peak, row_total, running = lax.fori_loop(
        block_first, block_total, forward_step, start_state
    )
    attended = running / row_total[..., None]
    log_total = row_peak + jnp.log(row_total)
    attended_low = attended.astype(jnp.bfloat16).reshape(row_count, heads_here * head_size)
    attn_term = jnp.dot(attended_low, out_full, preferred_element_type=jnp.float32)
    middle = inputs_f + lax.psum(attn_term.astype(jnp.bfloat16), "heads").astype(jnp.float32)
    mid_scale = rms_scale(middle)
    normed_mid = (middle * mid_scale * mid_row).astype(jnp.bfloat16)
    gate_rows = jnp.dot(normed_mid, gate_full, preferred_element_type=jnp.float32)
    up_rows = jnp.dot(normed_mid, up_full, preferred_element_type=jnp.float32)
    sigmoid_rows = jax.nn.sigmoid(gate_rows)
    silu_rows = gate_rows * sigmoid_rows
    hidden = (silu_rows * up_rows).astype(jnp.bfloat16)
    mlp_term = jnp.dot(hidden, down_full, preferred_element_type=jnp.float32)
    layer_out = (
        middle + lax.psum(mlp_term.astype(jnp.bfloat16), "heads").astype(jnp.float32)
    ).astype(jnp.bfloat16)
    grad_down = jnp.einsum("tf,td->fd", hidden, cotangent, preferred_element_type=jnp.float32)
    back_hidden = jnp.einsum("td,fd->tf", cotangent, down_full, preferred_element_type=jnp.float32)
    back_gate = (
        back_hidden * up_rows * sigmoid_rows * (1.0 + gate_rows * (1.0 - sigmoid_rows))
    ).astype(jnp.bfloat16)
    back_up = (back_hidden * silu_rows).astype(jnp.bfloat16)
    grad_gate = jnp.einsum("tc,tf->cf", normed_mid, back_gate, preferred_element_type=jnp.float32)
    grad_up = jnp.einsum("tc,tf->cf", normed_mid, back_up, preferred_element_type=jnp.float32)
    mid_term = jnp.einsum(
        "tf,cf->tc", back_gate, gate_full, preferred_element_type=jnp.float32
    ) + jnp.einsum("tf,cf->tc", back_up, up_full, preferred_element_type=jnp.float32)
    back_normed_mid = lax.psum(mid_term.astype(jnp.bfloat16), "heads").astype(jnp.float32)
    back_middle, grad_mid = norm_back(back_normed_mid, middle, mid_scale, mid_row)
    back_middle = back_middle + cotangent.astype(jnp.float32)
    back_attn = back_middle.astype(jnp.bfloat16)
    grad_out = jnp.einsum("tc,td->cd", attended_low, back_attn, preferred_element_type=jnp.float32)
    back_attended = (
        jnp.einsum("td,cd->tc", back_attn, out_full, preferred_element_type=jnp.float32)
        .astype(jnp.bfloat16)
        .reshape(row_count, heads_here, head_size)
    )
    row_delta = jnp.sum(back_attended.astype(jnp.float32) * attended, axis=-1)

    def backward_step(block_index, state_now):
        back_rows, back_pairs = state_now
        opening_row, block_keys, block_values, allowed, scores = key_block(block_index)
        chances = jnp.where(allowed, jnp.exp(scores - log_total[..., None]), 0.0)
        back_values = jnp.einsum(
            "qhk,qhd->kd",
            chances.astype(jnp.bfloat16),
            back_attended,
            preferred_element_type=jnp.float32,
        )
        back_chances = jnp.einsum(
            "qhd,kd->qhk", back_attended, block_values, preferred_element_type=jnp.float32
        )
        back_scores = (chances * (back_chances - row_delta[..., None])).astype(jnp.bfloat16)
        back_rows = back_rows + jnp.einsum(
            "qhk,kd->qhd", back_scores, block_keys, preferred_element_type=jnp.float32
        )
        back_keys = jnp.einsum(
            "qhk,qhd->kd", back_scores, query_rot, preferred_element_type=jnp.float32
        )
        old_piece = lax.dynamic_slice_in_dim(back_pairs, opening_row, span)
        fresh_piece = old_piece + jnp.concatenate([back_keys, back_values], axis=-1)
        back_pairs = lax.dynamic_update_slice_in_dim(back_pairs, fresh_piece, opening_row, 0)
        return (back_rows, back_pairs)

    start_back = (
        jnp.zeros((row_count, heads_here, head_size), jnp.float32),
        jnp.zeros((length, 2 * head_size), jnp.float32),
    )
    back_rows, back_pairs = lax.fori_loop(block_first, block_total, backward_step, start_back)
    own_pairs = lax.psum_scatter(
        back_pairs.astype(jnp.bfloat16), "tokens", scatter_dimension=0, tiled=True
    ).astype(jnp.float32)
    back_query = (
        (unrotate(back_rows, cos_table, sin_table) * head_size ** (-0.5))
        .astype(jnp.bfloat16)
        .reshape(row_count, heads_here * head_size)
    )
    back_key = unrotate(own_pairs[:, None, :head_size], cos_table, sin_table)[:, 0, :].astype(
        jnp.bfloat16
    )
    back_value = own_pairs[:, head_size:].astype(jnp.bfloat16)
    grad_query = jnp.einsum("tc,tq->cq", normed, back_query, preferred_element_type=jnp.float32)
    grad_key = jnp.einsum("tc,tq->cq", normed, back_key, preferred_element_type=jnp.float32)
    grad_value = jnp.einsum("tc,tq->cq", normed, back_value, preferred_element_type=jnp.float32)
    pre_term = jnp.einsum("tq,cq->tc", back_query, query_full, preferred_element_type=jnp.float32)
    pre_term = pre_term + jnp.einsum(
        "tq,cq->tc", back_key, key_full, preferred_element_type=jnp.float32
    )
    pre_term = pre_term + jnp.einsum(
        "tq,cq->tc", back_value, value_full, preferred_element_type=jnp.float32
    )
    back_normed = lax.psum(pre_term.astype(jnp.bfloat16), "heads").astype(jnp.float32)
    back_inputs, grad_pre = norm_back(back_normed, inputs_f, pre_scale, pre_row)
    grad_input = (back_middle + back_inputs).astype(jnp.bfloat16)
    summed = (
        lax.psum_scatter(
            grad_pre.astype(jnp.bfloat16), "tokens", scatter_dimension=0, tiled=True
        ).astype(jnp.float32),
        lax.psum_scatter(
            grad_mid.astype(jnp.bfloat16), "tokens", scatter_dimension=0, tiled=True
        ).astype(jnp.float32),
        lax.psum_scatter(
            grad_query.astype(jnp.bfloat16), "tokens", scatter_dimension=0, tiled=True
        ).astype(jnp.float32),
        lax.psum_scatter(
            grad_key.astype(jnp.bfloat16), "tokens", scatter_dimension=0, tiled=True
        ).astype(jnp.float32),
        lax.psum_scatter(
            grad_value.astype(jnp.bfloat16), "tokens", scatter_dimension=0, tiled=True
        ).astype(jnp.float32),
        lax.psum_scatter(
            grad_out.astype(jnp.bfloat16), "tokens", scatter_dimension=1, tiled=True
        ).astype(jnp.float32),
        lax.psum_scatter(
            grad_gate.astype(jnp.bfloat16), "tokens", scatter_dimension=0, tiled=True
        ).astype(jnp.float32),
        lax.psum_scatter(
            grad_up.astype(jnp.bfloat16), "tokens", scatter_dimension=0, tiled=True
        ).astype(jnp.float32),
        lax.psum_scatter(
            grad_down.astype(jnp.bfloat16), "tokens", scatter_dimension=1, tiled=True
        ).astype(jnp.float32),
    )
    (
        grad_pre,
        grad_mid,
        grad_query,
        grad_key,
        grad_value,
        grad_out,
        grad_gate,
        grad_up,
        grad_down,
    ) = summed
    return (
        layer_out,
        grad_input,
        grad_pre,
        grad_mid,
        grad_query,
        grad_key,
        grad_value,
        grad_out,
        grad_gate,
        grad_up,
        grad_down,
    )


MESH_ID = pl.DeviceIdType.MESH
VMEM_BYTES = 63 * 2**20
LEAD = 2


def token_device(flip):
    return (jnp.bitwise_xor(lax.axis_index("tokens"), flip), lax.axis_index("heads"))


def remote(src, dst, send, recv, device):
    return pltpu.make_async_remote_copy(
        src_ref=src, dst_ref=dst, send_sem=send, recv_sem=recv, device_id=device, device_id_type=MESH_ID
    )


def block_of(ref, axis, index, half=None, part=(0, 1)):
    size = ref.shape[axis] // 8
    start = pl.multiple_of(index * size, size)
    if axis == 0:
        rows = size // part[1]
        start = pl.multiple_of(start + part[0] * rows, rows)
        if half is None:
            return ref.at[pl.ds(start, rows), :]
        rows //= 2
        return ref.at[pl.ds(pl.multiple_of(start + half * rows, rows), rows), :]
    if half is None:
        return ref.at[:, pl.ds(start, size)]
    rows = ref.shape[0] // 2
    return ref.at[pl.ds(half * rows, rows), pl.ds(start, size)]


def in_order(job):
    @pl.when(lax.axis_index("tokens") >= 0)
    def _():
        job()


class Gather:
    COPIES = 9

    def __init__(self, shard, full, axis, send, recv, local, part=(0, 1)):
        self.shard, self.full, self.axis, self.part = shard, full, axis, part
        self.send, self.recv, self.local = send, recv, local
        self.me = lax.axis_index("tokens")

    def copy(self, slot, flip_block, flip_target, half=None):
        index = jnp.bitwise_xor(self.me, flip_block)
        place = block_of(self.full, self.axis, index, half, self.part)
        return remote(
            self.shard if flip_block == 0 else place,
            place,
            self.send.at[slot],
            self.recv.at[slot],
            token_device(flip_target),
        )

    def copies(self, slot):
        return self.copy(
            slot,
            *(
                (0, 2),
                (0, 4),
                (0, 1),
                (2, 4, 0),
                (4, 2, 1),
                (2, 1),
                (4, 1),
                (6, 1, 0),
                (6, 1, 1),
            )[slot],
        )

    def own_copy(self):
        return pltpu.make_async_copy(
            self.shard, block_of(self.full, self.axis, self.me, None, self.part), self.local
        )

    def start(self):
        def job():
            for slot in (0, 1, 2):
                self.copies(slot).start()
            self.own_copy().start()

        in_order(job)

    def relay_x(self):
        def job():
            self.copies(0).wait_recv()
            self.copies(3).start()
            self.copies(5).start()

        in_order(job)

    def relay_y(self):
        def job():
            self.copies(1).wait_recv()
            self.copies(4).start()
            self.copies(6).start()

        in_order(job)

    def relay(self):
        self.relay_x()
        self.relay_y()

    def finish_relay(self):
        def job():
            self.copies(3).wait_recv()
            self.copies(7).start()
            self.copies(4).wait_recv()
            self.copies(8).start()

        in_order(job)

    def finish(self):
        def job():
            for slot in (2, 5, 6, 7, 8):
                self.copies(slot).wait_recv()
            for slot in range(self.COPIES):
                self.copies(slot).wait_send()
            self.own_copy().wait()

        in_order(job)


class LineSum:
    FIRST = 1

    def __init__(self, term, passing, total, sems, parts=1, early=None, given=0, second=5):
        self.term, self.passing, self.total, self.sems = term, passing, total, sems
        self.parts, self.blocks = parts, term.shape[0]
        self.count = self.blocks * parts
        self.early = self.count if early is None else early
        self.given = given
        self.second = second
        here, tokens = lax.axis_index("heads"), lax.axis_index("tokens")
        self.inner = (here == 1) | (here == 2)
        self.mate = (tokens, jnp.where(here < 2, 1 - here, 5 - here))
        self.across = (tokens, jnp.where(self.inner, 3 - here, here))

    def place(self, i):
        rows = self.term.shape[1] // self.parts
        start = multiple(quotient(i, self.blocks) * rows, rows) if self.parts > 1 else 0
        return remainder(i, self.blocks), pl.ds(start, rows)

    def copy(self, src, dst, send, recv, i, device):
        block, rows = self.place(i)
        return remote(
            src.at[block, rows], dst.at[block, rows], self.sems.at[send, i], self.sems.at[recv, i], device
        )

    def out_copy(self, i):
        return self.copy(self.term, self.passing, 0, 1, i, self.mate)

    def across_copy(self, i, src=None):
        return self.copy(self.passing if src is None else src, self.total, 0, 2, i, self.across)

    def start_given(self):
        @pl.when(self.inner)
        def _():
            for i in range(self.given):
                self.across_copy(i, self.term).start()

    def back_copy(self, i):
        return self.copy(self.total, self.total, 3, 1, i, self.mate)

    def add(self, out, other, i):
        block, rows = self.place(i)
        out[block, rows] = out[block, rows] + other[block, rows]

    def due(self, i, who, job):
        if isinstance(i, int):
            if not 0 <= i < self.count:
                return
        else:
            who = who & (i >= 0) & (i < self.count)

        @pl.when(who)
        def _():
            job()

    def step(self, now):
        i, j = now - self.FIRST, now - self.second

        def pass_on():
            self.out_copy(i).wait_recv()
            self.add(self.passing, self.term, i)
            self.across_copy(i).start()

        def settle(src):
            self.across_copy(j).wait_recv()
            self.add(self.total, src, j)
            self.back_copy(j).start()

        if self.early < self.count:
            end = jnp.logical_not(self.inner) & (now >= self.early)
            self.due(now, end, lambda: self.out_copy(now).start())
        if self.given:
            self.due(j, self.inner & (j < self.given), lambda: settle(self.term))
            self.due(j, self.inner & (j >= self.given), lambda: settle(self.passing))
            self.due(i, self.inner & (i >= self.given), pass_on)
        else:
            self.due(i, self.inner, pass_on)
            self.due(j, self.inner, lambda: settle(self.passing))

    def send(self, first, count):
        @pl.when(jnp.logical_not(self.inner))
        def _():
            @pl.loop(0, count)
            def _(i):
                self.out_copy(first + i).start()

    def steps(self):
        return self.count + self.second

    def each(self, who, job):
        @pl.when(who)
        def _():
            @pl.loop(0, self.count)
            def _(i):
                job(i)

    def receive(self, i):
        @pl.when(jnp.logical_not(self.inner))
        def _():
            self.back_copy(i).wait_recv()

    def receive_all(self):
        self.each(jnp.logical_not(self.inner), lambda i: self.back_copy(i).wait_recv())

    def collect(self, out, sem):
        @pl.loop(0, self.count)
        def _(i):
            self.receive(i)
            block, rows = self.place(i)
            pltpu.make_async_copy(self.total.at[block, rows], out.at[block, rows], sem).start()

        return pltpu.make_async_copy(self.total, out, sem)

    def finish_ends(self):
        @pl.when(jnp.logical_not(self.inner))
        def _():
            @pl.loop(self.given, self.count)
            def _(i):
                self.out_copy(i).wait_send()

    def finish_inner(self):
        def sent(i):
            self.across_copy(i).wait_send()
            self.back_copy(i).wait_send()

        self.each(self.inner, sent)

    def finish(self):
        self.finish_inner()
        self.finish_ends()


def quotient(a, b):
    return a // b if isinstance(a, int) else lax.div(a, b)


def remainder(a, b):
    return a % b if isinstance(a, int) else lax.rem(a, b)


def multiple(value, of):
    return value if isinstance(value, int) else pl.multiple_of(value, of)


def by_step(now, plan):
    for first, last, stride, job in plan:
        if first == last:

            @pl.when(now == first)
            def _():
                job(0)

        else:
            due = (now >= first) & (now <= last)
            if stride > 1:
                due = due & (lax.rem(now - first, stride) == 0)

            @pl.when(due)
            def _():
                job(lax.div(now - first, stride))


def lanes(shape):
    return lax.broadcasted_iota(jnp.int32, shape, len(shape) - 1)


def turn(vectors, cos_table, sin_table):
    near = jnp.where(
        lanes(vectors.shape) % 64 < 32, pltpu.roll(vectors, 96, 1), pltpu.roll(vectors, 32, 1)
    )
    return vectors * cos_table + near * sin_table


def token_column(row):
    return jnp.broadcast_to(row, (128, row.shape[1])).T


def key_marks(column, first_id):
    lane = lanes(column.shape) % 64
    one_hot = (column - first_id).astype(jnp.int32) == lane
    return jnp.where(one_hot | ((lane >= 4) & (lane < 7)), 1.0, 0.0)


def query_marks(column, first_id):
    lane = lanes(column.shape) % 64
    other = (column - first_id).astype(jnp.int32) != lane
    return jnp.where(other & (lane < 4), -1e30, 0.0)


def nt_dot(left, right):
    return lax.dot_general(
        left, right, (((1,), (1,)), ((), ())), preferred_element_type=jnp.float32
    )


def attend_kernel(
    chain, places, x, ids, gains, key_shard, value_shard, inverse, query_shard, out_shard, gate_shard, up_shard,
    down_shard, gate_full, up_full, down_full, query_full, pair_full, out_full, attn_sum, normed_out, query_out,
    pairs, attended_out, log_out, cos_out, sin_out, small_out, small, gate_here, up_here, down_here, small_all, query_here, pair_here, pair_shard,
    out_here, pre_row, normed, query, attended, log_total, cos_table, sin_table, key_side, value_side, marks,
    scores, peak, mixed, near_pairs, term, passing, total, small_sems, gather_sems, local_sems, pair_sems,
    chain_sems, store_sems, load_sems,
):
    count = term.shape[0] // 2
    tokens = x.shape[0]
    heads = query.shape[1] // 64
    me = lax.axis_index("tokens")
    place = lax.rem(me, places)
    far = place >= 2
    loads = [
        pltpu.make_async_copy(src, dst, load_sems.at[k])
        for k, (src, dst) in enumerate(
            ((gate_shard, gate_here), (up_shard, up_here), (down_shard, down_here))
        )
    ]
    for load in loads:
        load.start()
    small[...] = jnp.zeros(small.shape, jnp.float32)
    small[0:1, :] = ids[...].astype(jnp.float32)
    small[1:2, :] = gains[...]
    greet(range(1, 8), chain)

    def small_copy(flip):
        return remote(
            small,
            small_all.at[me],
            small_sems.at[0, flip - 1],
            small_sems.at[1, flip - 1],
            token_device(flip),
        )

    def gather(k, shard, full, axis, part=(0, 1)):
        return Gather(
            shard, full, axis, gather_sems.at[0, k], gather_sems.at[1, k], local_sems.at[k], part
        )

    gather_query = gather(0, query_shard, query_here, 0)
    gather_pair = gather(1, pair_shard, pair_here, 0)
    gather_out = gather(2, out_shard, out_here, 1)
    half_rows = gate_here.shape[0] // 2
    gate_one, gate_two, up, down = (
        gather(3, gate_here.at[pl.ds(0, half_rows)], gate_full, 0, (0, 2)),
        gather(4, gate_here.at[pl.ds(half_rows, half_rows)], gate_full, 0, (1, 2)),
        gather(5, up_here, up_full, 0),
        gather(6, down_here, down_full, 1),
    )
    stores = []

    def store(src, out):
        copy = pltpu.make_async_copy(src, out, store_sems.at[len(stores)])
        copy.start()
        stores.append(copy)

    for flip in range(1, 8):
        small_copy(flip).start()
    both = jnp.concatenate(
        [key_shard[...].astype(jnp.float32), value_shard[...].astype(jnp.float32)], axis=0
    )
    pair_shard[...] = both.T.astype(jnp.bfloat16)
    gather_pair.start()
    gather_query.start()
    small_all[me] = small[...]
    x_f = x[...].astype(jnp.float32)
    pre_scale = lax.rsqrt(jnp.mean(x_f * x_f, axis=1, keepdims=True) + 1e-05)

    for flip in range(1, 8):
        small_copy(flip).wait_recv()
    store(small_all, small_out)
    width = x.shape[1] // 8
    for k in range(8):
        pre_row[:, k * width : (k + 1) * width] = jnp.broadcast_to(
            small_all[k, 1:2, :width], (8, width)
        )
    gather_pair.relay()
    normed[...] = (x[...].astype(jnp.float32) * pre_scale * pre_row[0:1, :]).astype(jnp.bfloat16)
    store(normed, normed_out)
    first_device = me - place
    first_id = (first_device // places * 4).astype(jnp.float32)
    own = token_column(small_all[me, 0:1, :])
    before = jnp.zeros((tokens, 1), jnp.float32)
    for k in range(places):
        others = small_all[first_device + k, 0:1, :]
        before = before + jnp.sum(
            jnp.where(others < own[:, 0:1], 1.0, 0.0), axis=1, keepdims=True
        )
        column = token_column(others)
        marks[pl.ds(k * tokens, tokens), :] = key_marks(column, first_id)
    row_index = lax.broadcasted_iota(jnp.int32, (tokens, 128), 0) + place * tokens
    turned = (row_index.astype(jnp.float32) - before) * inverse[0:1, :]
    cos_table[...] = jnp.cos(turned)
    sin_signed = jnp.sin(turned)
    sin_table[...] = jnp.where(lanes(sin_signed.shape) % 64 < 32, -sin_signed, sin_signed)
    store(cos_table, cos_out)
    store(sin_table, sin_out)
    gather_query.relay()
    gather_pair.finish_relay()
    gather_pair.finish()

    made = jnp.dot(normed[...], pair_here[...], preferred_element_type=jnp.float32)
    spun = turn(made, cos_table[...], sin_table[...])
    near_pairs[place] = jnp.where(lanes(made.shape) < 64, spun, made).astype(jnp.bfloat16)

    def pair_copy(slot, flip):
        at = place - 2 if slot == 2 else place
        return remote(
            near_pairs.at[at],
            near_pairs.at[at],
            pair_sems.at[0, slot],
            pair_sems.at[1, slot],
            token_device(flip),
        )

    pair_copy(0, 1).start()

    @pl.when(jnp.logical_not(far))
    def _():
        pair_copy(1, 2).start()

    gather_out.start()
    for load in loads:
        load.wait()
    gate_one.start()
    gather_query.finish_relay()
    gather_query.finish()
    for low in range(0, query.shape[1], 256):
        made = jnp.dot(
            normed[...], query_here[:, low : low + 256], preferred_element_type=jnp.float32
        )
        for group in range(low, low + 256, 128):
            spun = turn(made[:, group - low : group - low + 128], cos_table[...], sin_table[...])
            query[:, group : group + 128] = (spun * 0.125).astype(jnp.bfloat16)
    store(query, query_out)
    store(query_here, query_full)
    store(pair_here, pair_full)
    pair_copy(0, 1).wait_recv()

    @pl.when(far)
    def _():
        pair_copy(1, 2).wait_recv()
        pair_copy(2, 1).start()
        pair_copy(2, 1).wait_recv()

    @pl.when(jnp.logical_not(far))
    def _():
        gather_out.relay()

    @pl.when(jnp.logical_not(far))
    def _():
        gate_two.start()

    for k in range(places):

        @pl.when(k <= place)
        def _():
            pair = near_pairs[k].astype(jnp.float32)
            swapped = pltpu.roll(pair, 64, 1)
            lane = lanes(pair.shape)
            mark = marks[pl.ds(k * tokens, tokens), :]
            block = pl.ds(k * tokens, tokens)
            key_side[0, block] = jnp.where(lane < 64, pair, mark).astype(jnp.bfloat16)
            key_side[1, block] = jnp.where(lane < 64, mark, swapped).astype(jnp.bfloat16)
            value_side[0, block] = jnp.where(lane < 64, swapped, 1.0).astype(jnp.bfloat16)
            value_side[1, block] = jnp.where(lane < 64, 1.0, pair).astype(jnp.bfloat16)

    store(near_pairs, pairs)
    lane = lanes((tokens, 128))
    own_marks = query_marks(own, first_id)

    def side_of(group, e):
        at = pl.ds(multiple(group * 128, 128), 128)
        mine = (lane < 64) if e == 0 else (lane >= 64)
        return jnp.where(mine, query[:, at].astype(jnp.float32), own_marks).astype(jnp.bfloat16)

    def keys_at(k):
        return pl.ds(pl.multiple_of(k * tokens, tokens), tokens)

    def look(e, side, k, masked):
        found = nt_dot(side, key_side[e, keys_at(k)])
        if masked:
            rows = lax.broadcasted_iota(jnp.int32, found.shape, 0)
            found = jnp.where(lanes(found.shape) <= rows, found, -1e30)
        scores[e, k] = found
        best = found[:, :128]
        for part in range(128, tokens, 128):
            best = jnp.maximum(best, found[:, part : part + 128])
        peak[e] = best if masked else jnp.maximum(peak[e], best)

    def blend(e, k, first):
        parts = [
            jnp.exp(scores[e, k, :, part : part + 128] - peak[e]).astype(jnp.bfloat16)
            for part in range(0, tokens, 128)
        ]
        made = jnp.dot(
            jnp.concatenate(parts, axis=1),
            value_side[e, keys_at(k)],
            preferred_element_type=jnp.float32,
        )
        mixed[e] = made if first else mixed[e] + made

    def settle(e):
        peak[e] = jnp.broadcast_to(jnp.max(peak[e], axis=1, keepdims=True), lane.shape)

    def finish_head(group, e):
        mine = (lane < 64) if e == 0 else (lane >= 64)
        at = pl.ds(multiple(group * 128, 128), 128)
        out = mixed[e]
        sums = jnp.where(mine, pltpu.roll(out, 64, 1), out)
        share = out / sums
        attended[:, at] = share if e == 0 else jnp.where(lane < 64, attended[:, at], share)
        noted = peak[e] + jnp.log(sums)
        log_total[...] = jnp.where(lane == 2 * group + e, noted, log_total[...])

    def stage(done, begun):
        side = side_of(*begun) if begun else None
        if begun:
            look(begun[1], side, place, True)
        if done:
            blend(done[1], place, True)

        @pl.loop(0, place)
        def _(k):
            if begun:
                look(begun[1], side, k, False)
            if done:
                blend(done[1], k, False)

        if done:
            finish_head(*done)
        if begun:
            settle(begun[1])

    log_total[...] = jnp.zeros(lane.shape, jnp.float32)
    stage(None, (0, 0))
    last = heads // 2 - 1

    @pl.loop(0, last)
    def _(group):
        stage((group, 0), (group, 1))

        @pl.when(far & (group == 0))
        def _():
            gather_out.relay()

        @pl.when(far & (group == 0))
        def _():
            gate_two.start()

        @pl.when(group == 2)
        def _():
            up.start()

        stage((group, 1), (group + 1, 0))

    stage((last, 0), (last, 1))
    stage((last, 1), None)
    store(attended, attended_out)
    store(log_total, log_out)
    gather_out.finish_relay()

    gather_out.finish()
    low = attended[...].astype(jnp.bfloat16)
    each = term.shape[2]
    line = LineSum(term, passing, total, chain_sems, 2, second=3)

    @pl.loop(0, count)
    def _(k):
        cut = pl.ds(pl.multiple_of(k * 2 * each, 2 * each), 2 * each)
        made = jnp.dot(low, out_here[:, cut], preferred_element_type=jnp.float32).astype(
            jnp.bfloat16
        )
        term[2 * k] = made[:, :each]
        term[2 * k + 1] = made[:, each:]
        line.send(2 * k, 2)

    line.send(2 * count, 2 * count)
    store(out_here, out_full)

    down.start()
    relays = [
        (at, at, 1, lambda _, job=job: job())
        for at, job in (
            (0, gate_one.relay),
            (5, gate_two.relay),
            (13, up.relay),
            (24, down.relay),
            (26, gate_one.finish_relay),
            (28, gate_two.finish_relay),
            (32, up.finish_relay),
        )
    ]

    @pl.loop(0, line.steps())
    def _(now):
        by_step(now, relays)
        line.step(now)

    collected = line.collect(attn_sum, load_sems.at[3])
    down.finish_relay()
    line.finish()
    for part in (gate_one, gate_two, up, down):
        part.finish()
    for flip in range(1, 8):
        small_copy(flip).wait_send()
    pair_copy(0, 1).wait_send()

    @pl.when(far)
    def _():
        pair_copy(2, 1).wait_send()

    @pl.when(jnp.logical_not(far))
    def _():
        pair_copy(1, 2).wait_send()

    for copy in stores:
        copy.wait()
    collected.wait()


def attend(
    chain, places, x, ids, gains, key_weight, value_weight, inverse, query_weight, out_weight, gate_weight, up_weight,
    down_weight,
):
    tokens, width = x.shape
    count = 8
    heads_wide = query_weight.shape[1]
    bf16, f32 = jnp.bfloat16, jnp.float32
    row = places * tokens
    each = width // (2 * count)
    small = (8, tokens)
    anywhere, vmem = pl.BlockSpec(memory_space=pl.ANY), pl.BlockSpec(memory_space=pltpu.VMEM)
    shape = jax.ShapeDtypeStruct
    chunks = (2 * count, tokens, each)
    out_shape = [
        shape((gate_weight.shape[0] * 8, gate_weight.shape[1]), bf16),
        shape((up_weight.shape[0] * 8, up_weight.shape[1]), bf16),
        shape((down_weight.shape[0], down_weight.shape[1] * 8), bf16),
        shape((width, heads_wide), bf16),
        shape((width, 128), bf16),
        shape((heads_wide, width), bf16),
        shape(chunks, bf16),
        shape((tokens, width), bf16),
        shape((tokens, heads_wide), bf16),
        shape((places, tokens, 128), bf16),
        shape((tokens, heads_wide), f32),
        shape((tokens, 128), f32),
        shape((tokens, 128), f32),
        shape((tokens, 128), f32),
        shape((8,) + small, f32),
    ]
    return pl.pallas_call(
        functools.partial(attend_kernel, chain, places),
        out_shape=out_shape,
        in_specs=[vmem] * 6 + [anywhere] * 5,
        out_specs=[anywhere] * len(out_shape),
        scratch_shapes=[
            pltpu.VMEM(small, f32),
            pltpu.VMEM(gate_weight.shape, bf16),
            pltpu.VMEM(up_weight.shape, bf16),
            pltpu.VMEM(down_weight.shape, bf16),
            pltpu.VMEM((8,) + small, f32),
            pltpu.VMEM((width, heads_wide), bf16),
            pltpu.VMEM((width, 128), bf16),
            pltpu.VMEM((width // 8, 128), bf16),
            pltpu.VMEM((heads_wide, width), bf16),
            pltpu.VMEM((8, width), f32),
            pltpu.VMEM((tokens, width), bf16),
            pltpu.VMEM((tokens, heads_wide), bf16),
            pltpu.VMEM((tokens, heads_wide), f32),
            pltpu.VMEM((tokens, 128), f32),
            pltpu.VMEM((tokens, 128), f32),
            pltpu.VMEM((tokens, 128), f32),
            pltpu.VMEM((2, row, 128), bf16),
            pltpu.VMEM((2, row, 128), bf16),
            pltpu.VMEM((row, 128), f32),
            pltpu.VMEM((2, places, tokens, tokens), f32),
            pltpu.VMEM((2, tokens, 128), f32),
            pltpu.VMEM((2, tokens, 128), f32),
            pltpu.VMEM((places, tokens, 128), bf16),
            pltpu.VMEM(chunks, bf16),
            pltpu.VMEM(chunks, bf16),
            pltpu.VMEM(chunks, bf16),
            pltpu.SemaphoreType.DMA((2, 7)),
            pltpu.SemaphoreType.DMA((2, 7, Gather.COPIES)),
            pltpu.SemaphoreType.DMA((7,)),
            pltpu.SemaphoreType.DMA((2, 3)),
            pltpu.SemaphoreType.DMA((4, 4 * count)),
            pltpu.SemaphoreType.DMA((len(out_shape),)),
            pltpu.SemaphoreType.DMA((4,)),
        ],
        compiler_params=pltpu.CompilerParams(
            collective_id=0, has_side_effects=True, vmem_limit_bytes=VMEM_BYTES
        ),
        name="attend_forward",
    )(
        x, ids, gains, key_weight.T, value_weight.T, inverse, query_weight, out_weight, gate_weight, up_weight,
        down_weight,
    )


def greet(flips, chain):
    me, here = lax.axis_index("tokens"), lax.axis_index("heads")
    barrier = pltpu.get_barrier_semaphore()
    for flip in flips:
        pl.semaphore_signal(barrier, inc=1, device_id=token_device(flip), device_id_type=MESH_ID)
    for step in (-1, 1):
        near = here + step

        @pl.when((near >= 0) & (near < chain))
        def _():
            pl.semaphore_signal(barrier, inc=1, device_id=(me, near), device_id_type=MESH_ID)

    edge = (here == 0) | (here == chain - 1)

    @pl.when(edge)
    def _():
        pl.semaphore_wait(barrier, len(flips) + 1)

    @pl.when(jnp.logical_not(edge))
    def _():
        pl.semaphore_wait(barrier, len(flips) + 2)


class Reduce:
    COPIES = 6

    def __init__(self, own, near, sems):
        self.own, self.near, self.sems = own, near, sems

    def copy(self, slot):
        k, half, flip = ((1, 0, 2), (3, 0, 2), (2, 1, 4), (3, 1, 4), (2, 0, 4), (1, 1, 2))[slot]
        rows = self.own.shape[1] // 2
        return remote(
            self.own.at[k, pl.ds(half * rows, rows)],
            self.near.at[slot],
            self.sems.at[0, slot],
            self.sems.at[1, slot],
            token_device(flip),
        )

    def put(self, k, block):
        self.own[k] = block.astype(self.own.dtype)
        self.send(k)

    def send(self, k):
        for which, slots in ((3, (1, 3)), (1, (0,)), (2, (2,))):

            @pl.when(k == which)
            def _():
                for slot in slots:
                    self.copy(slot).start()

    def add_near(self, k, half, slot):
        rows = self.own.shape[1] // 2

        @pl.loop(0, rows // 32)
        def _(i):
            here = pl.ds(pl.multiple_of(i * 32, 32), 32)
            place = pl.ds(pl.multiple_of(half * rows + i * 32, 32), 32)
            self.own[k, place] = (
                self.own[k, place].astype(jnp.float32) + self.near[slot, here].astype(jnp.float32)
            ).astype(self.own.dtype)

    def second(self):
        self.copy(1).wait_recv()
        self.add_near(2, 0, 1)
        self.copy(4).start()
        self.copy(3).wait_recv()
        self.add_near(1, 1, 3)
        self.copy(5).start()

    def finish(self, out):
        rows = self.own.shape[1] // 2
        for half, slots in ((0, (0, 4)), (1, (2, 5))):
            for slot in slots:
                self.copy(slot).wait_recv()

            @pl.loop(0, rows // 32)
            def _(i):
                here = pl.ds(pl.multiple_of(i * 32, 32), 32)
                place = pl.ds(pl.multiple_of(half * rows + i * 32, 32), 32)
                total = self.own[0, place].astype(jnp.float32)
                for slot in slots:
                    total = total + self.near[slot, here].astype(jnp.float32)
                out[place, :] = total.astype(out.dtype)

        for slot in range(self.COPIES):
            self.copy(slot).wait_send()

    def halfway(self):
        for slot, (k, half) in enumerate(((0, 0), (2, 0), (0, 1), (1, 1))):
            self.copy(slot).wait_recv()
            self.copy(slot).wait_send()
            self.add_near(k, half, slot)


def block_order(i):
    return jnp.where(i == 0, 3, jnp.where(i == 1, 1, jnp.where(i == 2, 2, 0)))


def tn_dot(left, right):
    return lax.dot_general(
        left, right, (((0,), (0,)), ((), ())), preferred_element_type=jnp.float32
    )


def tiles_of(length, size):
    return [(low, min(low + size, length)) for low in range(0, length, size)]


def feed_kernel(
    chain, small_all, x_in, attn_in, cotangent_in, gate_full, up_full, down_full, back_sum, hidden_out, mlp_term,
    scale_out, grad_gate_out, up_out, x, attn_sum, cotangent, hidden, scale, grad_gate, gate, up, down, mid_row, normed, back_gate, back_up, term, passing, total,
    own_gate, near_gate, own_up, near_up, mlp_near, load_sems, swap_sems, chain_sems, reduce_sems, store_sems,
    lead_sems,
):
    count = term.shape[0] // 2
    each = term.shape[2]
    tokens, width = x.shape
    inner = gate.shape[1]
    me = lax.axis_index("tokens")
    tiles = tiles_of(inner, 512)
    early = [
        pltpu.make_async_copy(src, dst, load_sems.at[k])
        for k, (src, dst) in enumerate(((x_in, x), (attn_in, attn_sum), (cotangent_in, cotangent)))
    ]
    loads = []
    for k, (low, high) in enumerate(tiles):
        cut = pl.ds(low, high - low)
        loads.append(
            (
                pltpu.make_async_copy(gate_full.at[:, cut], gate.at[:, cut], load_sems.at[4 + 3 * k]),
                pltpu.make_async_copy(up_full.at[:, cut], up.at[:, cut], load_sems.at[5 + 3 * k]),
                pltpu.make_async_copy(down_full.at[cut, :], down.at[cut, :], load_sems.at[6 + 3 * k]),
            )
        )
    for load in early:
        load.start()
    for group in loads:
        for load in group:
            load.start()
    greet((1, 2, 4), chain)

    span = width // 8
    for k in range(8):
        mid_row[:, k * span : (k + 1) * span] = jnp.broadcast_to(
            small_all[k, 1:2, span : 2 * span], (8, span)
        )

    early[0].wait()
    early[1].wait()
    line = LineSum(term, passing, total, chain_sems, 2)
    half = tokens // 2

    def swap(k, ref, row, cut):
        return remote(
            ref.at[pl.ds(multiple(row, half), half), cut],
            ref.at[pl.ds(multiple(tokens + row, half), half), cut],
            swap_sems.at[0, k],
            swap_sems.at[1, k],
            token_device(1),
        )

    def swaps_of(part):
        row = part * half
        found = [swap(part, normed, row, pl.ds(0, width))]
        for k, (low, high) in enumerate(tiles):
            for j, ref in enumerate((back_gate, back_up)):
                found.append(
                    swap(2 + (part * len(tiles) + k) * 2 + j, ref, row, pl.ds(low, high - low))
                )
        return found

    ahead = 4

    def mid_pair(n, row):
        cut = pl.ds(pl.multiple_of(n * 2 * each, 2 * each), 2 * each)
        place = pl.ds(row, half)
        made = nt_dot(back_gate[place, :], gate[cut, :]) + nt_dot(back_up[place, :], up[cut, :])
        made = made.astype(jnp.bfloat16)
        term[2 * n, place] = made[:, :each]
        term[2 * n + 1, place] = made[:, each:]

    early[2].wait()

    @pl.loop(0, 2)
    def _(part):
        row = pl.multiple_of(part * half, half)
        rows = pl.ds(row, half)

        def middle_here(c):
            cut = slice(c * each, (c + 1) * each)
            return x[rows, cut].astype(jnp.float32) + attn_sum[c, rows].astype(jnp.float32)

        squares = jnp.zeros((half, each), jnp.float32)
        for c in range(2 * count):
            found = middle_here(c)
            squares = squares + found * found
        mid_scale = lax.rsqrt(jnp.sum(squares, axis=1, keepdims=True) / width + 1e-05)
        scale[rows] = jnp.broadcast_to(mid_scale, (half, scale.shape[1]))
        for c in range(2 * count):
            cut = slice(c * each, (c + 1) * each)
            normed[rows, cut] = (middle_here(c) * mid_scale * mid_row[0:1, cut]).astype(jnp.bfloat16)
        copies = swaps_of(part)
        copies[0].start()
        for k, (low, high) in enumerate(tiles):

            @pl.when(part == 0)
            def _():
                for load in loads[k]:
                    load.wait()

            gate_rows = jnp.dot(
                normed[rows, :], gate[:, low:high], preferred_element_type=jnp.float32
            )
            up_rows = jnp.dot(normed[rows, :], up[:, low:high], preferred_element_type=jnp.float32)
            back_hidden = nt_dot(cotangent[rows, :], down[low:high, :])
            sigmoid = jax.nn.sigmoid(gate_rows)
            silu = gate_rows * sigmoid
            hidden[rows, low:high] = (silu * up_rows).astype(jnp.bfloat16)
            back_gate[rows, low:high] = (
                back_hidden * up_rows * sigmoid * (1.0 + gate_rows * (1.0 - sigmoid))
            ).astype(jnp.bfloat16)
            back_up[rows, low:high] = (back_hidden * silu).astype(jnp.bfloat16)
            for copy in copies[1 + 2 * k : 3 + 2 * k]:
                copy.start()

            @pl.when(part == 1)
            def _():
                line.step(2 * k)
                line.step(2 * k + 1)

        @pl.when(part == 0)
        def _():
            @pl.loop(0, ahead)
            def _(n):
                mid_pair(n, 0)
                line.send(2 * n, 2)

    stores = []

    def store(src, out):
        copy = pltpu.make_async_copy(src, out, store_sems.at[len(stores)])
        copy.start()
        stores.append(copy)

    store(hidden, hidden_out)
    store(scale, scale_out)

    def mlp_place(n):
        rows = pl.ds(multiple(remainder(n, 4) * tokens, tokens), tokens)
        return rows, quotient(n, 4) * 2 * each

    def mlp_at(c):
        rows, low = mlp_place(quotient(c, 2))
        low = low + remainder(c, 2) * each
        return gate.at[rows, pl.ds(multiple(low, each), each)]

    lead = mlp_near.shape[0]

    def lead_copy(c):
        return remote(
            mlp_at(c), mlp_near.at[c], lead_sems.at[0, c], lead_sems.at[1, c], line.mate
        )

    def mlp_pair(n):
        cut = pl.ds(pl.multiple_of(n * 2 * each, 2 * each), 2 * each)
        made = jnp.dot(hidden[...], down[:, cut], preferred_element_type=jnp.float32)
        rows, low = mlp_place(n)
        gate[rows, pl.ds(pl.multiple_of(low, 2 * each), 2 * each)] = made.astype(jnp.bfloat16)

        @pl.when(n >= lead // 2)
        def _():
            for k in range(2):
                pltpu.make_async_copy(
                    mlp_at(2 * n + k), mlp_term.at[2 * n + k], load_sems.at[3]
                ).start()

        @pl.when((n < lead // 2) & jnp.logical_not(line.inner))
        def _():
            for k in range(2):
                lead_copy(2 * n + k).start()

    def lead_store(c):
        return pltpu.make_async_copy(mlp_near.at[c], mlp_term.at[c], lead_sems.at[2, c])

    gate_sum = Reduce(own_gate, near_gate, reduce_sems.at[0])
    up_sum = Reduce(own_up, near_up, reduce_sems.at[1])

    def grad_block(part, ref, k):
        index = jnp.bitwise_xor(me, 2 * k)
        cut = pl.ds(pl.multiple_of(index * span, span), span)
        part.put(k, tn_dot(normed[:, cut], ref[...]))

    def received(which):
        for part in range(2):
            for copy in swaps_of(part)[which]:
                copy.wait_recv()

    def late_pair(i):
        i = i + ahead
        part = jnp.where(i < count, 0, 1)
        n = i - part * count
        mid_pair(n, pl.multiple_of(part * half, half))
        line.send(part * 2 * count + 2 * n, 2)

    def late_pairs(i):
        late_pair(2 * i)

        @pl.when(2 * i + 1 + ahead < 2 * count)
        def _():
            late_pair(2 * i + 1)

    begun = 2 * len(tiles)
    last_pairs = (2 * count - ahead + 1) // 2 - 1
    plan = (
        (0, last_pairs, 1, late_pairs),
        (0, 0, 1, lambda _: received(slice(0, 1))),
        (0, 0, 1, lambda _: received(slice(1, None, 2))),
        (0, 3, 1, lambda i: grad_block(gate_sum, back_gate, block_order(i))),
        (4, 4, 1, lambda _: received(slice(2, None, 2))),
        (4, 7, 1, lambda i: grad_block(up_sum, back_up, block_order(i))),
        (7, 7, 1, lambda _: gate_sum.second()),
        (last_pairs + 1, last_pairs + count, 1, mlp_pair),
    )

    @pl.loop(0, (line.steps() - begun + 1) // 2)
    def _(now):
        by_step(now, plan)
        line.step(begun + 2 * now)
        line.step(begun + 2 * now + 1)

    gate_sum.finish(grad_gate)
    store(grad_gate, grad_gate_out)
    @pl.when(line.inner)
    def _():
        for c in range(lead):
            lead_copy(c).wait_recv()
            mlp_near[c] = (
                mlp_near[c].astype(jnp.float32) + mlp_at(c)[...].astype(jnp.float32)
            ).astype(mlp_near.dtype)
            lead_store(c).start()

    up_sum.halfway()
    rows = span // 2
    store(own_up.at[0], up_out.at[pl.ds(0, span), :])
    store(own_up.at[2, pl.ds(0, rows)], up_out.at[pl.ds(span, rows), :])
    store(own_up.at[1, pl.ds(rows, rows)], up_out.at[pl.ds(span + rows, rows), :])
    collected = line.collect(back_sum, store_sems.at[7])
    line.finish()
    for part in range(2):
        for copy in swaps_of(part):
            copy.wait_send()

    rest = pl.ds(lead, 2 * count - lead)
    pltpu.make_async_copy(term.at[rest], total.at[rest], load_sems.at[3]).wait()

    @pl.when(line.inner)
    def _():
        for c in range(lead):
            lead_store(c).wait()

    @pl.when(jnp.logical_not(line.inner))
    def _():
        for c in range(lead):
            lead_copy(c).wait_send()

    for copy in stores:
        copy.wait()
    collected.wait()


def feed(chain, small_all, x, attn_sum, cotangent, gate_full, up_full, down_full):
    tokens, width = x.shape
    inner = gate_full.shape[1]
    count = attn_sum.shape[0] // 2
    span = width // 8
    bf16, f32 = jnp.bfloat16, jnp.float32
    anywhere, vmem = pl.BlockSpec(memory_space=pl.ANY), pl.BlockSpec(memory_space=pltpu.VMEM)
    shape = jax.ShapeDtypeStruct
    tiles = len(tiles_of(inner, 512))
    return pl.pallas_call(
        functools.partial(feed_kernel, chain),
        out_shape=[
            shape(attn_sum.shape, bf16),
            shape((tokens, inner), bf16),
            shape(attn_sum.shape, bf16),
            shape((tokens, 128), f32),
            shape((span, inner), bf16),
            shape((2 * span, inner), bf16),
        ],
        in_specs=[vmem] + [anywhere] * 6,
        out_specs=[anywhere] * 6,
        scratch_shapes=[
            pltpu.VMEM((tokens, width), bf16),
            pltpu.VMEM(attn_sum.shape, bf16),
            pltpu.VMEM((tokens, width), bf16),
            pltpu.VMEM((tokens, inner), bf16),
            pltpu.VMEM((tokens, 128), f32),
            pltpu.VMEM((span, inner), bf16),
            pltpu.VMEM((width, inner), bf16),
            pltpu.VMEM((width, inner), bf16),
            pltpu.VMEM((inner, width), bf16),
            pltpu.VMEM((8, width), f32),
            pltpu.VMEM((2 * tokens, width), bf16),
            pltpu.VMEM((2 * tokens, inner), bf16),
            pltpu.VMEM((2 * tokens, inner), bf16),
            pltpu.VMEM(attn_sum.shape, bf16),
            pltpu.VMEM(attn_sum.shape, bf16),
            pltpu.VMEM(attn_sum.shape, bf16),
            pltpu.VMEM((4, span, inner), bf16),
            pltpu.VMEM((6, span // 2, inner), bf16),
            pltpu.VMEM((4, span, inner), bf16),
            pltpu.VMEM((6, span // 2, inner), bf16),
            pltpu.VMEM((LEAD, tokens, 128), bf16),
            pltpu.SemaphoreType.DMA((4 + 3 * tiles,)),
            pltpu.SemaphoreType.DMA((2, 2 + 4 * tiles)),
            pltpu.SemaphoreType.DMA((4, 4 * count)),
            pltpu.SemaphoreType.DMA((2, 2, Reduce.COPIES)),
            pltpu.SemaphoreType.DMA((8,)),
            pltpu.SemaphoreType.DMA((3, LEAD)),
        ],
        compiler_params=pltpu.CompilerParams(
            collective_id=1, has_side_effects=True, vmem_limit_bytes=VMEM_BYTES
        ),
        name="feed_forward",
    )(small_all, x, attn_sum, cotangent, gate_full, up_full, down_full)


def split_marks(values, at):
    high = values.astype(jnp.bfloat16).astype(jnp.float32)
    rest = values - high
    middle = rest.astype(jnp.bfloat16).astype(jnp.float32)
    low = rest - middle
    return jnp.where(at == 4, high, jnp.where(at == 5, middle, jnp.where(at == 6, low, 0.0)))


def return_kernel(
    chain, places, small_all, query, pairs, log_total, cos_table, sin_table, scale,
    attended_in, x_in, attn_in, back_sum, query_full, pair_full, out_full, mlp_term, hidden_in, cotangent, normed_in, up_in, layer_out, grad_input, grad_down_out,
    grad_query, grad_key, grad_value, grad_out_out, grad_up_out, gains, mid_part, grad_down, grad_out, pair_back, grad_in, in_here, out_here, key_side, value_side, query_side, back_side, back_att,
    back_rows, back_keys, back_values, pair_out, pair_near, normed, back_attn, hidden, cotangents, att_low,
    back_all, pre_row, pre_part, gains_near, mlp_sum, mlp_passing, mlp_total, term, passing, total, own_down,
    near_down, own_in, near_in, own_out, near_out, load_sems, swap_sems, pair_sems, gain_sems, mlp_sems, chain_sems,
    reduce_sems, store_sems, up_half, up_near, up_sems,
):
    count = term.shape[0] // 2
    each = term.shape[2]
    tokens, width = x_in.shape
    span = width // 8
    groups = query.shape[1] // 128
    me = lax.axis_index("tokens")
    place = lax.rem(me, places)
    first_device = me - place
    mine, theirs = pl.ds(0, tokens), pl.ds(tokens, tokens)

    def load(k, src, dst):
        copy = pltpu.make_async_copy(src, dst, load_sems.at[k])
        copy.start()
        return copy

    load_mlp = load(5, mlp_term, mlp_sum)
    load_cot = load(2, cotangent, cotangents.at[mine, :])
    attended = back_rows
    load_attended = load(7, attended_in, attended)

    def back_at(side, c):
        row = multiple(remainder(c, 4) * tokens, tokens)
        return side.at[quotient(c, 4), pl.ds(row, tokens), :]

    def attn_at(c):
        row = multiple(quotient(remainder(c, 4), 2) * tokens, tokens)
        low = multiple(remainder(c, 2) * each, each)
        return own_down.at[quotient(c, 4), pl.ds(row, tokens), pl.ds(low, each)]

    for c in range(2 * count):
        side = key_side if c < count else value_side
        load(9, back_sum.at[c], back_at(side, c % count))
        load(10, x_in.at[:, pl.ds(c * each, each)], term.at[c])
        load(11, attn_in.at[c], attn_at(c))
    load_out = load(0, out_full, out_here)
    heads_wide = query.shape[1]
    load_in = load(1, query_full, in_here.at[:, pl.ds(0, heads_wide)])
    load_pair = load(6, pair_full, in_here.at[:, pl.ds(heads_wide, 128)])
    load_hidden = load(3, hidden_in, hidden.at[mine, :])
    load_normed = load(4, normed_in, normed.at[mine, :])
    load_up = load(13, up_in, up_half)
    greet(range(1, 8), chain)

    def swap(k, ref):
        copy = remote(
            ref.at[mine, :],
            ref.at[theirs, :],
            swap_sems.at[0, k],
            swap_sems.at[1, k],
            token_device(1),
        )
        copy.start()
        return copy

    def gain_copy(which, src, flip):
        other = jnp.bitwise_xor(me, flip)
        return remote(
            src.at[:, pl.ds(pl.multiple_of(other * span, span), span)],
            gains_near.at[me, :, pl.ds(which * span, span)],
            gain_sems.at[0, which, flip - 1],
            gain_sems.at[1, which, flip - 1],
            token_device(flip),
        )

    mlp_line = LineSum(mlp_sum, mlp_passing, mlp_total, mlp_sems, given=LEAD, second=LEAD + 1)
    load_mlp.wait()
    mlp_line.start_given()
    mlp_line.send(LEAD, 2 * count - LEAD)
    rows_up = up_near.shape[1]

    def up_copy(slot):
        return remote(
            up_half.at[pl.ds((2 + slot) * rows_up, rows_up), :],
            up_near.at[slot],
            up_sems.at[0, slot],
            up_sems.at[1, slot],
            token_device((4, 2)[slot]),
        )

    for k in range(8):
        pre_row[:, k * span : (k + 1) * span] = jnp.broadcast_to(
            small_all[k, 1:2, span : 2 * span], (8, span)
        )
    for k in (9, 10, 11):
        pltpu.make_async_copy(attn_in, term, load_sems.at[k]).wait()
    load_cot.wait()

    def hat_at(c):
        return (term[c].astype(jnp.float32) + attn_at(c)[...].astype(jnp.float32)) * scale[...]

    def cut_at(c):
        return pl.ds(multiple(c * each, each), each)

    summed_here = back_keys.at[1]
    summed_here[...] = jnp.zeros(summed_here.shape, jnp.float32)
    for base, side in ((0, key_side), (count, value_side)):

        @pl.loop(0, count)
        def _(c):
            cut = cut_at(base + c)
            shared = back_at(side, c)[...].astype(jnp.float32) * hat_at(base + c)
            summed_here[...] += shared * pre_row[0:1, cut]
            mid_part[:, cut] = jnp.broadcast_to(jnp.sum(shared, axis=0, keepdims=True), (8, each))

    mean = jnp.sum(summed_here[...], axis=1, keepdims=True) / width
    summed_here[...] = jnp.broadcast_to(mean, summed_here.shape)
    for flip in range(1, 8):
        gain_copy(1, mid_part, flip).start()
    mlp_line.step(mlp_line.second)
    load_up.wait()
    for slot in range(2):
        up_copy(slot).start()

    for base, side in ((0, key_side), (count, value_side)):

        @pl.loop(0, count)
        def _(c):
            cut = cut_at(base + c)
            u = back_at(side, c)[...].astype(jnp.float32) * pre_row[0:1, cut]
            found = scale[...] * (u - hat_at(base + c) * summed_here[...])
            back_attn[mine, cut] = (cotangents[mine, cut].astype(jnp.float32) + found).astype(
                jnp.bfloat16
            )

    mlp_line.step(mlp_line.second + 1)
    load_attended.wait()
    att_low[mine, :] = attended[...].astype(jnp.bfloat16)
    swap_back = swap(0, back_attn)
    swap_att = swap(1, att_low)

    lane = lanes((tokens, 128))
    at = lane % 64
    first_id = (first_device // places * 4).astype(jnp.float32)
    for k in range(places):
        mark = key_marks(token_column(small_all[first_device + k, 0:1, :]), first_id)
        block = pl.ds(k * tokens, tokens)

        @pl.when(k <= place)
        def _():
            pair = pairs[k].astype(jnp.float32)
            swapped = pltpu.roll(pair, 64, 1)
            key_side[0, block] = jnp.where(lane < 64, pair, mark).astype(jnp.bfloat16)
            key_side[1, block] = jnp.where(lane < 64, mark, swapped).astype(jnp.bfloat16)
            value_side[0, block] = jnp.where(lane < 64, swapped, 1.0).astype(jnp.bfloat16)
            value_side[1, block] = jnp.where(lane < 64, 1.0, pair).astype(jnp.bfloat16)

    own_marks = query_marks(token_column(small_all[me, 0:1, :]), first_id)

    load_out.wait()
    back_att[...] = nt_dot(back_attn[mine, :], out_here[...]).astype(jnp.bfloat16)
    swap_cot = swap(2, cotangents)
    mlp_line.step(mlp_line.second + 2)
    load_hidden.wait()
    swap_hidden = swap(3, hidden)

    @pl.loop(0, groups)
    def _(group):
        cut = pl.ds(pl.multiple_of(group * 128, 128), 128)
        back = back_att[:, cut].astype(jnp.float32)
        both = query[:, cut].astype(jnp.float32)
        shared = back * attended[:, cut]
        for e in range(2):
            head = 2 * group + e
            used = (lane < 64) if e == 0 else (lane >= 64)
            delta = jnp.sum(jnp.where(used, shared, 0.0), axis=1, keepdims=True)
            peak = jnp.sum(jnp.where(lane == head, log_total[...], 0.0), axis=1, keepdims=True)
            back_side[head] = jnp.where(
                used, back, split_marks(jnp.broadcast_to(-delta, lane.shape), at)
            ).astype(jnp.bfloat16)
            query_side[head] = jnp.where(
                used, both, own_marks + split_marks(jnp.broadcast_to(-peak, lane.shape), at)
            ).astype(jnp.bfloat16)

    mlp_line.step(mlp_line.second + 3)
    load_normed.wait()
    swap_normed = swap(4, normed)
    load_in.wait()
    load_pair.wait()

    begun = mlp_line.second + 4
    back_rows[...] = jnp.zeros_like(back_rows)

    def key_step(k, diagonal):
        back_keys[...] = jnp.zeros_like(back_keys)
        back_values[...] = jnp.zeros_like(back_values)

        @pl.loop(0, groups)
        def _(group):
            cut = pl.ds(pl.multiple_of(group * 128, 128), 128)
            for low in (0, tokens // 2):
                keys_here = pl.ds(pl.multiple_of(k * tokens + low, tokens // 2), tokens // 2)
                part = pl.ds(low, tokens // 2)
                first = low if diagonal else 0
                seen = pl.ds(first, tokens - first)
                rows = []
                for e in range(2):
                    head = 2 * group + e
                    found = nt_dot(key_side[e, keys_here], query_side[head, seen])
                    chances = jnp.exp(found)
                    if diagonal:
                        keys = lax.broadcasted_iota(jnp.int32, found.shape, 0) + (low - first)
                        chances = jnp.where(keys <= lanes(found.shape), chances, 0.0)
                    moved = chances * nt_dot(value_side[e, keys_here], back_side[head, seen])
                    chances = chances.astype(jnp.bfloat16)
                    moved = moved.astype(jnp.bfloat16)
                    back_values[e, part] += jnp.dot(
                        chances, back_att[seen, cut], preferred_element_type=jnp.float32
                    )
                    back_keys[e, part] += jnp.dot(
                        moved, query[seen, cut], preferred_element_type=jnp.float32
                    )
                    rows.append(tn_dot(moved, key_side[e, keys_here]))
                back_rows[seen, cut] += jnp.where(lanes(rows[0].shape) < 64, rows[0], rows[1])

            @pl.when(group % 2 == 1)
            def _():
                mlp_line.step(begun + groups // 2 * k + group // 2)

        keys = back_keys[0] + pltpu.roll(back_keys[1], 64, 1)
        values = pltpu.roll(back_values[0], 64, 1) + back_values[1]
        return jnp.where(lane < 64, keys, values)

    def pair_copy(source, target):
        return remote(
            pair_out.at[target],
            pair_near.at[source],
            pair_sems.at[0, target],
            pair_sems.at[1, source],
            (first_device + target, lax.axis_index("heads")),
        )

    @pl.loop(0, place)
    def _(k):
        pair_out[k] = key_step(k, False).astype(jnp.bfloat16)
        pair_copy(place, k).start()

    own_pair = key_step(place, True)
    pair_out[place] = own_pair.astype(jnp.bfloat16)
    early = begun + groups // 2 * places

    @pl.loop(begun + groups // 2 * (place + 1), early)
    def _(now):
        mlp_line.step(now)

    for group in range(groups):
        cut = slice(group * 128, (group + 1) * 128)
        back_all[mine, cut] = (
            turn(back_rows[:, cut], cos_table[...], -sin_table[...]) * 0.125
        ).astype(jnp.bfloat16)
    back_keys[0] = own_pair
    for k in range(1, places):

        @pl.when(k > place)
        def _():
            remote(
                pair_out.at[k],
                pair_near.at[k],
                pair_sems.at[0, k],
                pair_sems.at[1, k],
                (first_device + k, lax.axis_index("heads")),
            ).wait_recv()
            back_keys[0] += pair_near[k].astype(jnp.float32)

    summed = back_keys[0]
    spun = turn(summed, cos_table[...], -sin_table[...])
    back_all[mine, pl.ds(groups * 128, 128)] = jnp.where(lane < 64, spun, summed).astype(
        jnp.bfloat16
    )
    swap_all = swap(5, back_all)

    def pre_pair(n):
        cut = pl.ds(pl.multiple_of(n * 2 * each, 2 * each), 2 * each)
        made = nt_dot(back_all[mine, :], in_here[cut, :]).astype(jnp.bfloat16)
        term[2 * n] = made[:, :each]
        term[2 * n + 1] = made[:, each:]
        line.send(2 * n, 2)

    def cut_of(k):
        index = jnp.bitwise_xor(me, 2 * k)
        return pl.ds(pl.multiple_of(index * span, span), span)

    down_sum = Reduce(own_down, near_down, reduce_sems.at[0])
    in_sum = Reduce(own_in, near_in, reduce_sems.at[1])
    out_sum = Reduce(own_out, near_out, reduce_sems.at[2])

    def down_block(i):
        k = block_order(i)
        for low, high in tiles_of(hidden.shape[1], 512):
            own_down[k, low:high] = tn_dot(hidden[:, low:high], cotangents[:, cut_of(k)]).astype(
                own_down.dtype
            )
        down_sum.send(k)

    def in_block(i):
        k = block_order(i)
        in_sum.put(k, tn_dot(normed[:, cut_of(k)], back_all[...]))

    def out_block(i):
        k = block_order(i)
        out_sum.put(k, tn_dot(att_low[...], back_attn[:, cut_of(k)]))

    def load_late():
        swap_cot.wait_send()
        load(8, x_in, cotangents.at[theirs, :])
        for c in range(2 * count):
            load(12, attn_in.at[c], cotangents.at[mine, pl.ds(c * each, each)])

    def wait_late():
        for k in (8, 12):
            pltpu.make_async_copy(x_in, cotangents.at[mine, :], load_sems.at[k]).wait()

    def x_at(c):
        return cotangents[theirs, cut_at(c)].astype(jnp.float32)

    def middle_at(c):
        return x_at(c) + cotangents[mine, cut_at(c)].astype(jnp.float32)

    wholes = (
        (grad_down, grad_down_out),
        (grad_out, grad_out_out),
        (grad_in.at[:, pl.ds(0, heads_wide)], grad_query),
        (pair_back.at[pl.ds(0, 64)], grad_key),
        (pair_back.at[pl.ds(64, 64)], grad_value),
        (up_half.at[pl.ds(0, 2 * rows_up), :], grad_up_out),
    )

    def whole(k):
        return pltpu.make_async_copy(*wholes[k], store_sems.at[2 + k])

    def store_block(c, src, out, sem):
        return pltpu.make_async_copy(src.at[c], out.at[:, cut_at(c)], store_sems.at[sem])

    def finish_mlp(_):
        mlp_line.receive_all()
        mlp_line.finish()

        @pl.loop(0, 2 * count)
        def _(c):
            mlp_sum[c] = (middle_at(c) + mlp_total[c].astype(jnp.float32)).astype(jnp.bfloat16)
            store_block(c, mlp_sum, layer_out, 0).start()

    weighed = back_keys.at[1]
    scale_here = back_keys.at[0]

    def scale_rows(_):
        wait_late()
        for k in range(8):
            pre_row[:, k * span : (k + 1) * span] = jnp.broadcast_to(
                small_all[k, 1:2, :span], (8, span)
            )
        scale_here[...] = jnp.zeros(scale_here.shape, jnp.float32)

        @pl.loop(0, 2 * count)
        def _(c):
            part = x_at(c)
            scale_here[...] += part * part

        mean = jnp.sum(scale_here[...], axis=1, keepdims=True) / width
        scale_here[...] = jnp.broadcast_to(lax.rsqrt(mean + 1e-05), scale_here.shape)
        weighed[...] = jnp.zeros(weighed.shape, jnp.float32)

    def weigh(i):
        line.receive(i)
        c, rows = line.place(i)
        size = tokens // line.parts
        first = lax.div(i, line.blocks) * size
        cut = cut_at(c)
        late = pl.ds(pl.multiple_of(tokens + first, size), size)
        hat = cotangents[late, cut].astype(jnp.float32) * scale_here[rows]
        shared = total[c, rows].astype(jnp.float32) * hat
        weighed[rows] += shared * pre_row[0:1, cut]
        summed = jnp.broadcast_to(jnp.sum(shared, axis=0, keepdims=True), (8, each))
        pre_part[:, cut] = jnp.where(i < line.blocks, 0.0, pre_part[:, cut]) + summed

    def finish_in(_):
        in_sum.finish(grad_in)
        pair_back[...] = grad_in[:, heads_wide:].astype(jnp.float32).T
        for k in (2, 3, 4):
            whole(k).start()

    def finish_up(_):
        for slot in range(2):
            up_copy(slot).wait()

            @pl.loop(0, rows_up // 32)
            def _(i):
                here = pl.ds(pl.multiple_of(i * 32, 32), 32)
                place = pl.ds(pl.multiple_of(slot * rows_up + i * 32, 32), 32)
                up_half[place, :] = (
                    up_half[place, :].astype(jnp.float32) + up_near[slot, here].astype(jnp.float32)
                ).astype(up_half.dtype)

        whole(5).start()

    def finish_down(_):
        down_sum.finish(grad_down)
        whole(0).start()

    def finish_out(_):
        out_sum.finish(grad_out)
        whole(1).start()

    line = LineSum(term, passing, total, chain_sems, 2, 2 * count)
    steps = line.steps()
    behind = 14

    def received(*copies):
        def job(_):
            for copy in copies:
                copy.wait_recv()

        return job

    plan = (
        (0, 2 * count - 2, 2, pre_pair),
        (1, 1, 1, received(swap_cot, swap_hidden)),
        (1, 7, 2, down_block),
        (8, 8, 1, lambda _: load_late()),
        (9, 9, 1, received(swap_back, swap_att)),
        (9, 12, 1, out_block),
        (13, 13, 1, received(swap_normed, swap_all)),
        (13, 13, 1, scale_rows),
        (14, 17, 1, in_block),
        (18, 18, 1, lambda _: down_sum.second()),
        (20, 20, 1, finish_mlp),
        (21, 21, 1, lambda _: out_sum.second()),
        (23, 23, 1, lambda _: in_sum.second()),
        (26, 26, 1, finish_up),
        (28, 28, 1, finish_down),
        (30, 30, 1, finish_out),
        (32, 32, 1, finish_in),
    )

    @pl.loop(0, steps)
    def _(now):
        by_step(now, plan)

        @pl.when(early + now < mlp_line.steps())
        def _():
            mlp_line.step(early + now)

        line.step(now)

        @pl.when(now >= behind)
        def _():
            weigh(now - behind)

    @pl.loop(steps - behind, line.count)
    def _(i):
        weigh(i)

    for flip in range(1, 8):
        gain_copy(0, pre_part, flip).start()
    mean = jnp.sum(weighed[...], axis=1, keepdims=True) / width
    weighed[...] = jnp.broadcast_to(mean, weighed.shape)
    line.finish_ends()

    @pl.loop(0, 2 * count)
    def _(c):
        cut = cut_at(c)
        u = total[c].astype(jnp.float32) * pre_row[0:1, cut]
        found = scale_here[...] * (u - x_at(c) * scale_here[...] * weighed[...])
        term[c] = (back_attn[mine, cut].astype(jnp.float32) + found).astype(jnp.bfloat16)
        store_block(c, term, grad_input, 1).start()

    own = pl.ds(pl.multiple_of(me * span, span), span)
    gains_near[me, :, :span] = pre_part[:, own]
    gains_near[me, :, span:] = mid_part[:, own]
    for flip in range(1, 8):
        for which, src in enumerate((pre_part, mid_part)):
            gain_copy(which, src, flip).wait_recv()
    gains[...] = jnp.sum(gains_near[...], axis=0)
    for flip in range(1, 8):
        for which, src in enumerate((pre_part, mid_part)):
            gain_copy(which, src, flip).wait_send()
    line.finish_inner()
    for copy in (swap_back, swap_att, swap_hidden, swap_normed, swap_all):
        copy.wait_send()

    @pl.loop(0, place)
    def _(k):
        pair_copy(place, k).wait_send()

    for k in range(len(wholes)):
        whole(k).wait()

    for k in range(2):
        pltpu.make_async_copy(mlp_sum, term, store_sems.at[k]).wait()


def way_back(
    chain, places, small_all, query, pairs, log_total, cos_table, sin_table, scale, attended, x, attn_sum, back_sum,
    query_full, pair_full, out_full, mlp_term, hidden, cotangent, normed, up_half,
):
    tokens, width = x.shape
    inner = hidden.shape[1]
    heads_wide = query.shape[1]
    wide = heads_wide + 128
    chunks = attn_sum.shape
    count = chunks[0] // 2
    span = width // 8
    row = places * tokens
    bf16, f32 = jnp.bfloat16, jnp.float32
    anywhere, vmem = pl.BlockSpec(memory_space=pl.ANY), pl.BlockSpec(memory_space=pltpu.VMEM)
    shape = jax.ShapeDtypeStruct
    return pl.pallas_call(
        functools.partial(return_kernel, chain, places),
        out_shape=[
            shape((tokens, width), bf16),
            shape((tokens, width), bf16),
            shape((inner, span), bf16),
            shape((span, heads_wide), bf16),
            shape((64, span), f32),
            shape((64, span), f32),
            shape((heads_wide, span), bf16),
            shape((span, inner), bf16),
            shape((8, 2 * span), f32),
        ],
        in_specs=[vmem] * 7 + [anywhere] * 12,
        out_specs=[anywhere] * 8 + [vmem],
        scratch_shapes=[
            pltpu.VMEM((8, width), f32),
            pltpu.VMEM((inner, span), bf16),
            pltpu.VMEM((heads_wide, span), bf16),
            pltpu.VMEM((128, span), f32),
            pltpu.VMEM((span, wide), bf16),
            pltpu.VMEM((width, wide), bf16),
            pltpu.VMEM((heads_wide, width), bf16),
            pltpu.VMEM((2, row, 128), bf16),
            pltpu.VMEM((2, row, 128), bf16),
            pltpu.VMEM((heads_wide // 64, tokens, 128), bf16),
            pltpu.VMEM((heads_wide // 64, tokens, 128), bf16),
            pltpu.VMEM((tokens, heads_wide), bf16),
            pltpu.VMEM((tokens, heads_wide), f32),
            pltpu.VMEM((2, tokens, 128), f32),
            pltpu.VMEM((2, tokens, 128), f32),
            pltpu.VMEM((places, tokens, 128), bf16),
            pltpu.VMEM((places, tokens, 128), bf16),
            pltpu.VMEM((2 * tokens, width), bf16),
            pltpu.VMEM((2 * tokens, width), bf16),
            pltpu.VMEM((2 * tokens, inner), bf16),
            pltpu.VMEM((2 * tokens, width), bf16),
            pltpu.VMEM((2 * tokens, heads_wide), bf16),
            pltpu.VMEM((2 * tokens, wide), bf16),
            pltpu.VMEM((8, width), f32),
            pltpu.VMEM((8, width), f32),
            pltpu.VMEM((8, 8, 2 * span), f32),
            pltpu.VMEM(chunks, bf16),
            pltpu.VMEM(chunks, bf16),
            pltpu.VMEM(chunks, bf16),
            pltpu.VMEM(chunks, bf16),
            pltpu.VMEM(chunks, bf16),
            pltpu.VMEM(chunks, bf16),
            pltpu.VMEM((4, inner, span), bf16),
            pltpu.VMEM((6, inner // 2, span), bf16),
            pltpu.VMEM((4, span, wide), bf16),
            pltpu.VMEM((6, span // 2, wide), bf16),
            pltpu.VMEM((4, heads_wide, span), bf16),
            pltpu.VMEM((6, heads_wide // 2, span), bf16),
            pltpu.SemaphoreType.DMA((14,)),
            pltpu.SemaphoreType.DMA((2, 6)),
            pltpu.SemaphoreType.DMA((2, places)),
            pltpu.SemaphoreType.DMA((2, 2, 7)),
            pltpu.SemaphoreType.DMA((4, 2 * count)),
            pltpu.SemaphoreType.DMA((4, 4 * count)),
            pltpu.SemaphoreType.DMA((3, 2, Reduce.COPIES)),
            pltpu.SemaphoreType.DMA((8,)),
            pltpu.VMEM((2 * span, inner), bf16),
            pltpu.VMEM((2, span // 2, inner), bf16),
            pltpu.SemaphoreType.DMA((2, 2)),
        ],
        compiler_params=pltpu.CompilerParams(
            collective_id=2, has_side_effects=True, vmem_limit_bytes=VMEM_BYTES
        ),
        name="way_back",
    )(
        small_all, query, pairs, log_total, cos_table, sin_table, scale, attended, x, attn_sum, back_sum,
        query_full, pair_full, out_full, mlp_term, hidden, cotangent, normed, up_half,
    )


def hand_over_kernel(count, gains, *refs):
    ins, outs = refs[:count], refs[count : 2 * count]
    grad_pre, grad_mid = refs[2 * count : 2 * count + 2]
    held, wide, sems = refs[2 * count + 2 : 3 * count + 2], refs[3 * count + 2 : -1], refs[-1]
    loads = [pltpu.make_async_copy(ins[k], held[k], sems.at[0, k]) for k in range(count)]
    for load in loads:
        load.start()
    span = gains.shape[1] // 2
    grad_pre[...] = gains[0:1, :span]
    grad_mid[...] = gains[0:1, span:]
    stores = []
    wide = list(wide)
    for k, load in enumerate(loads):
        load.wait()
        ready = held[k]
        if outs[k].dtype != ready.dtype:
            ready = wide.pop(0)

            @pl.loop(0, ready.shape[0] // 32)
            def _(i):
                here = pl.ds(pl.multiple_of(i * 32, 32), 32)
                ready[here, :] = held[k][here, :].astype(ready.dtype)

        stores.append(pltpu.make_async_copy(ready, outs[k], sems.at[1, k]))
        stores[-1].start()
    for store in stores:
        store.wait()


def hand_over(gains, *arrays):
    count = len(arrays)
    anywhere, vmem = pl.BlockSpec(memory_space=pl.ANY), pl.BlockSpec(memory_space=pltpu.VMEM)
    half = jax.ShapeDtypeStruct((1, gains.shape[1] // 2), gains.dtype)
    types = [array.dtype if k < 2 else jnp.dtype(jnp.float32) for k, array in enumerate(arrays)]
    return pl.pallas_call(
        functools.partial(hand_over_kernel, count),
        out_shape=[jax.ShapeDtypeStruct(array.shape, kind) for array, kind in zip(arrays, types)]
        + [half, half],
        in_specs=[vmem] + [anywhere] * count,
        out_specs=[anywhere] * count + [vmem, vmem],
        scratch_shapes=[pltpu.VMEM(array.shape, array.dtype) for array in arrays]
        + [
            pltpu.VMEM(array.shape, kind)
            for array, kind in zip(arrays, types)
            if kind != array.dtype
        ]
        + [pltpu.SemaphoreType.DMA((2, count))],
        compiler_params=pltpu.CompilerParams(vmem_limit_bytes=VMEM_BYTES),
        name="hand_over",
    )(gains, *arrays)


def shards_cube(
    chain,
    inputs,
    segments,
    pre_gain,
    mid_gain,
    query_weight,
    key_weight,
    value_weight,
    out_weight,
    gate_weight,
    up_weight,
    down_weight,
    cotangent,
):
    row_count = inputs.shape[0]
    head_size = key_weight.shape[1]
    query_width = query_weight.shape[1]
    heads_here = query_width // head_size
    places = ROW // row_count
    half = pre_gain.shape[0]
    gains = jnp.pad(pre_gain.astype(jnp.float32), (0, half)) + jnp.pad(
        mid_gain.astype(jnp.float32), (half, 0)
    )
    half_size = head_size // 2
    inverse = 10000.0 ** (-np.arange(half_size, dtype=np.float32) / half_size)
    inverse = jnp.asarray(np.tile(inverse.astype(np.float32), (8, 128 // half_size)))
    (
        gate_full,
        up_full,
        down_full,
        query_full,
        pair_full,
        out_full,
        attn_sum,
        normed,
        query_rot,
        pairs,
        attended,
        log_total,
        cos_wide,
        sin_wide,
        small_full,
    ) = attend(
        chain,
        places,
        inputs,
        segments[None],
        gains[None],
        key_weight,
        value_weight,
        inverse,
        query_weight,
        out_weight,
        gate_weight,
        up_weight,
        down_weight,
    )
    back_sum, hidden, mlp_term, scale, grad_gate, up_half = feed(
        chain, small_full, inputs, attn_sum, cotangent, gate_full, up_full, down_full
    )
    layer_out, grad_input, grad_down, grad_query, grad_key, grad_value, grad_out, grad_up, gains = way_back(
        chain,
        places,
        small_full,
        query_rot,
        pairs,
        log_total,
        cos_wide,
        sin_wide,
        scale,
        attended,
        inputs,
        attn_sum,
        back_sum,
        query_full,
        pair_full,
        out_full,
        mlp_term,
        hidden,
        cotangent,
        normed,
        up_half,
    )
    (
        layer_out,
        grad_input,
        grad_query,
        grad_key,
        grad_value,
        grad_out,
        grad_gate,
        grad_up,
        grad_down,
        grad_pre,
        grad_mid,
    ) = hand_over(
        gains,
        layer_out,
        grad_input,
        grad_query,
        grad_key,
        grad_value,
        grad_out,
        grad_gate,
        grad_up,
        grad_down,
    )
    grad_pre, grad_mid = grad_pre[0], grad_mid[0]
    grad_key, grad_value = grad_key.T, grad_value.T
    return (
        layer_out,
        grad_input,
        grad_pre,
        grad_mid,
        grad_query,
        grad_key,
        grad_value,
        grad_out,
        grad_gate,
        grad_up,
        grad_down,
    )


def solution(mesh):
    sizes = dict(mesh.shape)
    plan = shards_any
    if sizes["tokens"] == 8 and sizes["heads"] == 4:
        plan = functools.partial(shards_cube, sizes["heads"])
    return jax.shard_map(
        plan,
        mesh=mesh,
        in_specs=(
            P("tokens", None),
            P("tokens"),
            P("tokens"),
            P("tokens"),
            P("tokens", "heads"),
            P("tokens", "heads"),
            P("tokens", "heads"),
            P("heads", "tokens"),
            P("tokens", "heads"),
            P("tokens", "heads"),
            P("heads", "tokens"),
            P("tokens", None),
        ),
        out_specs=(
            P("tokens", None),
            P("tokens", None),
            P("tokens"),
            P("tokens"),
            P("tokens", "heads"),
            P("tokens", "heads"),
            P("tokens", "heads"),
            P("heads", "tokens"),
            P("tokens", "heads"),
            P("tokens", "heads"),
            P("heads", "tokens"),
        ),
        check_vma=False,
    )
```

```python
import functools
import math

import jax
import jax.numpy as jnp
import numpy as np
from jax import lax
from jax.experimental import pallas as pl
from jax.experimental.pallas import tpu as pltpu
from jax.sharding import PartitionSpec as P

ROW = 2048


def rms_scale(vectors):
    return lax.rsqrt(jnp.mean(vectors * vectors, axis=-1, keepdims=True) + 1e-05)


def rotate(vectors, cos_table, sin_table):
    middle_index = vectors.shape[-1] // 2
    former = vectors[..., :middle_index]
    latter = vectors[..., middle_index:]
    return jnp.concatenate(
        [former * cos_table - latter * sin_table, latter * cos_table + former * sin_table], axis=-1
    )


def unrotate(gradient, cos_table, sin_table):
    middle_index = gradient.shape[-1] // 2
    former = gradient[..., :middle_index]
    latter = gradient[..., middle_index:]
    return jnp.concatenate(
        [former * cos_table + latter * sin_table, latter * cos_table - former * sin_table], axis=-1
    )


def norm_back(gradient, vectors, scale_rows, gain_row):
    shaped = vectors * scale_rows
    weighted = gradient * gain_row
    back_vectors = scale_rows * (
        weighted - shaped * jnp.mean(weighted * shaped, axis=-1, keepdims=True)
    )
    return (back_vectors, jnp.sum(gradient * shaped, axis=0))


def shards_any(
    inputs,
    segments,
    pre_gain,
    mid_gain,
    query_weight,
    key_weight,
    value_weight,
    out_weight,
    gate_weight,
    up_weight,
    down_weight,
    cotangent,
):
    row_count = inputs.shape[0]
    head_size = key_weight.shape[1]
    heads_here = query_weight.shape[1] // head_size
    myself = lax.axis_index("tokens")
    gathered = (
        lax.all_gather(pre_gain, "tokens", axis=0, tiled=True),
        lax.all_gather(mid_gain, "tokens", axis=0, tiled=True),
        lax.all_gather(query_weight, "tokens", axis=0, tiled=True),
        lax.all_gather(key_weight, "tokens", axis=0, tiled=True),
        lax.all_gather(value_weight, "tokens", axis=0, tiled=True),
        lax.all_gather(out_weight, "tokens", axis=1, tiled=True),
        lax.all_gather(gate_weight, "tokens", axis=0, tiled=True),
        lax.all_gather(up_weight, "tokens", axis=0, tiled=True),
        lax.all_gather(down_weight, "tokens", axis=1, tiled=True),
    )
    (
        pre_full,
        mid_full,
        query_full,
        key_full,
        value_full,
        out_full,
        gate_full,
        up_full,
        down_full,
    ) = gathered
    pre_row = pre_full.astype(jnp.float32)
    mid_row = mid_full.astype(jnp.float32)
    all_ids = lax.all_gather(segments, "tokens", axis=0, tiled=True)
    length = all_ids.shape[0]
    places = jnp.arange(length, dtype=jnp.int32)
    starts_here = jnp.concatenate([jnp.ones((1,), dtype=jnp.bool_), all_ids[1:] != all_ids[:-1]])
    opening = lax.cummax(jnp.where(starts_here, places, 0), axis=0)
    own_first = myself * row_count
    positions = lax.dynamic_slice_in_dim(places - opening, own_first, row_count)
    own_places = own_first + jnp.arange(row_count, dtype=jnp.int32)
    half_size = head_size // 2
    inverse = 10000.0 ** (-jnp.arange(half_size, dtype=jnp.float32) / half_size)
    turned = positions.astype(jnp.float32)[:, None] * inverse[None, :]
    cos_table = jnp.cos(turned)[:, None, :]
    sin_table = jnp.sin(turned)[:, None, :]
    inputs_f = inputs.astype(jnp.float32)
    pre_scale = rms_scale(inputs_f)
    normed = (inputs_f * pre_scale * pre_row).astype(jnp.bfloat16)
    queries = jnp.dot(normed, query_full, preferred_element_type=jnp.float32).reshape(
        row_count, heads_here, head_size
    )
    query_rot = (rotate(queries, cos_table, sin_table) * head_size ** (-0.5)).astype(jnp.bfloat16)
    key_rows = jnp.dot(normed, key_full, preferred_element_type=jnp.float32)[:, None, :]
    key_rot = rotate(key_rows, cos_table, sin_table)[:, 0, :].astype(jnp.bfloat16)
    value_low = jnp.dot(normed, value_full, preferred_element_type=jnp.float32).astype(jnp.bfloat16)
    key_all, value_all = (
        lax.all_gather(key_rot, "tokens", axis=0, tiled=True),
        lax.all_gather(value_low, "tokens", axis=0, tiled=True),
    )
    span = math.gcd(ROW, 1024)
    row_start = own_first // ROW * ROW
    block_first = row_start // span
    block_total = (own_first + row_count + span - 1) // span

    def key_block(block_index):
        opening_row = block_index * span
        block_keys = lax.dynamic_slice_in_dim(key_all, opening_row, span)
        block_values = lax.dynamic_slice_in_dim(value_all, opening_row, span)
        block_ids = lax.dynamic_slice_in_dim(all_ids, opening_row, span)
        block_places = opening_row + jnp.arange(span, dtype=jnp.int32)
        allowed = (segments[:, None] == block_ids[None, :]) & (
            own_places[:, None] >= block_places[None, :]
        )
        scores = jnp.einsum(
            "qhd,kd->qhk", query_rot, block_keys, preferred_element_type=jnp.float32
        )
        return (opening_row, block_keys, block_values, allowed[:, None, :], scores)

    def forward_step(block_index, state_now):
        row_peak, row_total, running = state_now
        opening_row, block_keys, block_values, allowed, scores = key_block(block_index)
        new_peak = jnp.maximum(row_peak, jnp.max(jnp.where(allowed, scores, -1e30), axis=-1))
        factor = jnp.exp(row_peak - new_peak)
        weights = jnp.where(allowed, jnp.exp(scores - new_peak[..., None]), 0.0)
        row_total = row_total * factor + jnp.sum(weights, axis=-1)
        running = running * factor[..., None] + jnp.einsum(
            "qhk,kd->qhd",
            weights.astype(jnp.bfloat16),
            block_values,
            preferred_element_type=jnp.float32,
        )
        return (new_peak, row_total, running)

    start_state = (
        jnp.full((row_count, heads_here), -1e30, jnp.float32),
        jnp.zeros((row_count, heads_here), jnp.float32),
        jnp.zeros((row_count, heads_here, head_size), jnp.float32),
    )
    row_peak, row_total, running = lax.fori_loop(
        block_first, block_total, forward_step, start_state
    )
    attended = running / row_total[..., None]
    log_total = row_peak + jnp.log(row_total)
    attended_low = attended.astype(jnp.bfloat16).reshape(row_count, heads_here * head_size)
    attn_term = jnp.dot(attended_low, out_full, preferred_element_type=jnp.float32)
    middle = inputs_f + lax.psum(attn_term.astype(jnp.bfloat16), "heads").astype(jnp.float32)
    mid_scale = rms_scale(middle)
    normed_mid = (middle * mid_scale * mid_row).astype(jnp.bfloat16)
    gate_rows = jnp.dot(normed_mid, gate_full, preferred_element_type=jnp.float32)
    up_rows = jnp.dot(normed_mid, up_full, preferred_element_type=jnp.float32)
    sigmoid_rows = jax.nn.sigmoid(gate_rows)
    silu_rows = gate_rows * sigmoid_rows
    hidden = (silu_rows * up_rows).astype(jnp.bfloat16)
    mlp_term = jnp.dot(hidden, down_full, preferred_element_type=jnp.float32)
    layer_out = (
        middle + lax.psum(mlp_term.astype(jnp.bfloat16), "heads").astype(jnp.float32)
    ).astype(jnp.bfloat16)
    grad_down = jnp.einsum("tf,td->fd", hidden, cotangent, preferred_element_type=jnp.float32)
    back_hidden = jnp.einsum("td,fd->tf", cotangent, down_full, preferred_element_type=jnp.float32)
    back_gate = (
        back_hidden * up_rows * sigmoid_rows * (1.0 + gate_rows * (1.0 - sigmoid_rows))
    ).astype(jnp.bfloat16)
    back_up = (back_hidden * silu_rows).astype(jnp.bfloat16)
    grad_gate = jnp.einsum("tc,tf->cf", normed_mid, back_gate, preferred_element_type=jnp.float32)
    grad_up = jnp.einsum("tc,tf->cf", normed_mid, back_up, preferred_element_type=jnp.float32)
    mid_term = jnp.einsum(
        "tf,cf->tc", back_gate, gate_full, preferred_element_type=jnp.float32
    ) + jnp.einsum("tf,cf->tc", back_up, up_full, preferred_element_type=jnp.float32)
    back_normed_mid = lax.psum(mid_term.astype(jnp.bfloat16), "heads").astype(jnp.float32)
    back_middle, grad_mid = norm_back(back_normed_mid, middle, mid_scale, mid_row)
    back_middle = back_middle + cotangent.astype(jnp.float32)
    back_attn = back_middle.astype(jnp.bfloat16)
    grad_out = jnp.einsum("tc,td->cd", attended_low, back_attn, preferred_element_type=jnp.float32)
    back_attended = (
        jnp.einsum("td,cd->tc", back_attn, out_full, preferred_element_type=jnp.float32)
        .astype(jnp.bfloat16)
        .reshape(row_count, heads_here, head_size)
    )
    row_delta = jnp.sum(back_attended.astype(jnp.float32) * attended, axis=-1)

    def backward_step(block_index, state_now):
        back_rows, back_pairs = state_now
        opening_row, block_keys, block_values, allowed, scores = key_block(block_index)
        chances = jnp.where(allowed, jnp.exp(scores - log_total[..., None]), 0.0)
        back_values = jnp.einsum(
            "qhk,qhd->kd",
            chances.astype(jnp.bfloat16),
            back_attended,
            preferred_element_type=jnp.float32,
        )
        back_chances = jnp.einsum(
            "qhd,kd->qhk", back_attended, block_values, preferred_element_type=jnp.float32
        )
        back_scores = (chances * (back_chances - row_delta[..., None])).astype(jnp.bfloat16)
        back_rows = back_rows + jnp.einsum(
            "qhk,kd->qhd", back_scores, block_keys, preferred_element_type=jnp.float32
        )
        back_keys = jnp.einsum(
            "qhk,qhd->kd", back_scores, query_rot, preferred_element_type=jnp.float32
        )
        old_piece = lax.dynamic_slice_in_dim(back_pairs, opening_row, span)
        fresh_piece = old_piece + jnp.concatenate([back_keys, back_values], axis=-1)
        back_pairs = lax.dynamic_update_slice_in_dim(back_pairs, fresh_piece, opening_row, 0)
        return (back_rows, back_pairs)

    start_back = (
        jnp.zeros((row_count, heads_here, head_size), jnp.float32),
        jnp.zeros((length, 2 * head_size), jnp.float32),
    )
    back_rows, back_pairs = lax.fori_loop(block_first, block_total, backward_step, start_back)
    own_pairs = lax.psum_scatter(
        back_pairs.astype(jnp.bfloat16), "tokens", scatter_dimension=0, tiled=True
    ).astype(jnp.float32)
    back_query = (
        (unrotate(back_rows, cos_table, sin_table) * head_size ** (-0.5))
        .astype(jnp.bfloat16)
        .reshape(row_count, heads_here * head_size)
    )
    back_key = unrotate(own_pairs[:, None, :head_size], cos_table, sin_table)[:, 0, :].astype(
        jnp.bfloat16
    )
    back_value = own_pairs[:, head_size:].astype(jnp.bfloat16)
    grad_query = jnp.einsum("tc,tq->cq", normed, back_query, preferred_element_type=jnp.float32)
    grad_key = jnp.einsum("tc,tq->cq", normed, back_key, preferred_element_type=jnp.float32)
    grad_value = jnp.einsum("tc,tq->cq", normed, back_value, preferred_element_type=jnp.float32)
    pre_term = jnp.einsum("tq,cq->tc", back_query, query_full, preferred_element_type=jnp.float32)
    pre_term = pre_term + jnp.einsum(
        "tq,cq->tc", back_key, key_full, preferred_element_type=jnp.float32
    )
    pre_term = pre_term + jnp.einsum(
        "tq,cq->tc", back_value, value_full, preferred_element_type=jnp.float32
    )
    back_normed = lax.psum(pre_term.astype(jnp.bfloat16), "heads").astype(jnp.float32)
    back_inputs, grad_pre = norm_back(back_normed, inputs_f, pre_scale, pre_row)
    grad_input = (back_middle + back_inputs).astype(jnp.bfloat16)
    summed = (
        lax.psum_scatter(
            grad_pre.astype(jnp.bfloat16), "tokens", scatter_dimension=0, tiled=True
        ).astype(jnp.float32),
        lax.psum_scatter(
            grad_mid.astype(jnp.bfloat16), "tokens", scatter_dimension=0, tiled=True
        ).astype(jnp.float32),
        lax.psum_scatter(
            grad_query.astype(jnp.bfloat16), "tokens", scatter_dimension=0, tiled=True
        ).astype(jnp.float32),
        lax.psum_scatter(
            grad_key.astype(jnp.bfloat16), "tokens", scatter_dimension=0, tiled=True
        ).astype(jnp.float32),
        lax.psum_scatter(
            grad_value.astype(jnp.bfloat16), "tokens", scatter_dimension=0, tiled=True
        ).astype(jnp.float32),
        lax.psum_scatter(
            grad_out.astype(jnp.bfloat16), "tokens", scatter_dimension=1, tiled=True
        ).astype(jnp.float32),
        lax.psum_scatter(
            grad_gate.astype(jnp.bfloat16), "tokens", scatter_dimension=0, tiled=True
        ).astype(jnp.float32),
        lax.psum_scatter(
            grad_up.astype(jnp.bfloat16), "tokens", scatter_dimension=0, tiled=True
        ).astype(jnp.float32),
        lax.psum_scatter(
            grad_down.astype(jnp.bfloat16), "tokens", scatter_dimension=1, tiled=True
        ).astype(jnp.float32),
    )
    (
        grad_pre,
        grad_mid,
        grad_query,
        grad_key,
        grad_value,
        grad_out,
        grad_gate,
        grad_up,
        grad_down,
    ) = summed
    return (
        layer_out,
        grad_input,
        grad_pre,
        grad_mid,
        grad_query,
        grad_key,
        grad_value,
        grad_out,
        grad_gate,
        grad_up,
        grad_down,
    )


MESH_ID = pl.DeviceIdType.MESH
VMEM_BYTES = 63 * 2**20
LEAD = 2


def token_device(flip):
    return (jnp.bitwise_xor(lax.axis_index("tokens"), flip), lax.axis_index("heads"))


def remote(src, dst, send, recv, device):
    return pltpu.make_async_remote_copy(
        src_ref=src, dst_ref=dst, send_sem=send, recv_sem=recv, device_id=device, device_id_type=MESH_ID
    )


def block_of(ref, axis, index, half=None, part=(0, 1)):
    size = ref.shape[axis] // 8
    start = pl.multiple_of(index * size, size)
    if axis == 0:
        rows = size // part[1]
        start = pl.multiple_of(start + part[0] * rows, rows)
        if half is None:
            return ref.at[pl.ds(start, rows), :]
        rows //= 2
        return ref.at[pl.ds(pl.multiple_of(start + half * rows, rows), rows), :]
    if half is None:
        return ref.at[:, pl.ds(start, size)]
    rows = ref.shape[0] // 2
    return ref.at[pl.ds(half * rows, rows), pl.ds(start, size)]


def in_order(job):
    @pl.when(lax.axis_index("tokens") >= 0)
    def _():
        job()


class Gather:
    COPIES = 9

    def __init__(self, shard, full, axis, send, recv, local, part=(0, 1)):
        self.shard, self.full, self.axis, self.part = shard, full, axis, part
        self.send, self.recv, self.local = send, recv, local
        self.me = lax.axis_index("tokens")

    def copy(self, slot, flip_block, flip_target, half=None):
        index = jnp.bitwise_xor(self.me, flip_block)
        place = block_of(self.full, self.axis, index, half, self.part)
        return remote(
            self.shard if flip_block == 0 else place,
            place,
            self.send.at[slot],
            self.recv.at[slot],
            token_device(flip_target),
        )

    def copies(self, slot):
        return self.copy(
            slot,
            *(
                (0, 2),
                (0, 4),
                (0, 1),
                (2, 4, 0),
                (4, 2, 1),
                (2, 1),
                (4, 1),
                (6, 1, 0),
                (6, 1, 1),
            )[slot],
        )

    def own_copy(self):
        return pltpu.make_async_copy(
            self.shard, block_of(self.full, self.axis, self.me, None, self.part), self.local
        )

    def start(self):
        def job():
            for slot in (0, 1, 2):
                self.copies(slot).start()
            self.own_copy().start()

        in_order(job)

    def relay_x(self):
        def job():
            self.copies(0).wait_recv()
            self.copies(3).start()
            self.copies(5).start()

        in_order(job)

    def relay_y(self):
        def job():
            self.copies(1).wait_recv()
            self.copies(4).start()
            self.copies(6).start()

        in_order(job)

    def relay(self):
        self.relay_x()
        self.relay_y()

    def finish_relay(self):
        def job():
            self.copies(3).wait_recv()
            self.copies(7).start()
            self.copies(4).wait_recv()
            self.copies(8).start()

        in_order(job)

    def finish(self):
        def job():
            for slot in (2, 5, 6, 7, 8):
                self.copies(slot).wait_recv()
            for slot in range(self.COPIES):
                self.copies(slot).wait_send()
            self.own_copy().wait()

        in_order(job)


class LineSum:
    FIRST = 1

    def __init__(self, term, passing, total, sems, parts=1, early=None, given=0, second=5):
        self.term, self.passing, self.total, self.sems = term, passing, total, sems
        self.parts, self.blocks = parts, term.shape[0]
        self.count = self.blocks * parts
        self.early = self.count if early is None else early
        self.given = given
        self.second = second
        here, tokens = lax.axis_index("heads"), lax.axis_index("tokens")
        self.inner = (here == 1) | (here == 2)
        self.mate = (tokens, jnp.where(here < 2, 1 - here, 5 - here))
        self.across = (tokens, jnp.where(self.inner, 3 - here, here))

    def place(self, i):
        rows = self.term.shape[1] // self.parts
        start = multiple(quotient(i, self.blocks) * rows, rows) if self.parts > 1 else 0
        return remainder(i, self.blocks), pl.ds(start, rows)

    def copy(self, src, dst, send, recv, i, device):
        block, rows = self.place(i)
        return remote(
            src.at[block, rows], dst.at[block, rows], self.sems.at[send, i], self.sems.at[recv, i], device
        )

    def out_copy(self, i):
        return self.copy(self.term, self.passing, 0, 1, i, self.mate)

    def across_copy(self, i, src=None):
        return self.copy(self.passing if src is None else src, self.total, 0, 2, i, self.across)

    def start_given(self):
        @pl.when(self.inner)
        def _():
            for i in range(self.given):
                self.across_copy(i, self.term).start()

    def back_copy(self, i):
        return self.copy(self.total, self.total, 3, 1, i, self.mate)

    def add(self, out, other, i):
        block, rows = self.place(i)
        out[block, rows] = out[block, rows] + other[block, rows]

    def due(self, i, who, job):
        if isinstance(i, int):
            if not 0 <= i < self.count:
                return
        else:
            who = who & (i >= 0) & (i < self.count)

        @pl.when(who)
        def _():
            job()

    def step(self, now):
        i, j = now - self.FIRST, now - self.second

        def pass_on():
            self.out_copy(i).wait_recv()
            self.add(self.passing, self.term, i)
            self.across_copy(i).start()

        def settle(src):
            self.across_copy(j).wait_recv()
            self.add(self.total, src, j)
            self.back_copy(j).start()

        if self.early < self.count:
            end = jnp.logical_not(self.inner) & (now >= self.early)
            self.due(now, end, lambda: self.out_copy(now).start())
        if self.given:
            self.due(j, self.inner & (j < self.given), lambda: settle(self.term))
            self.due(j, self.inner & (j >= self.given), lambda: settle(self.passing))
            self.due(i, self.inner & (i >= self.given), pass_on)
        else:
            self.due(i, self.inner, pass_on)
            self.due(j, self.inner, lambda: settle(self.passing))

    def send(self, first, count):
        @pl.when(jnp.logical_not(self.inner))
        def _():
            @pl.loop(0, count)
            def _(i):
                self.out_copy(first + i).start()

    def steps(self):
        return self.count + self.second

    def each(self, who, job):
        @pl.when(who)
        def _():
            @pl.loop(0, self.count)
            def _(i):
                job(i)

    def receive(self, i):
        @pl.when(jnp.logical_not(self.inner))
        def _():
            self.back_copy(i).wait_recv()

    def receive_all(self):
        self.each(jnp.logical_not(self.inner), lambda i: self.back_copy(i).wait_recv())

    def collect(self, out, sem):
        @pl.loop(0, self.count)
        def _(i):
            self.receive(i)
            block, rows = self.place(i)
            pltpu.make_async_copy(self.total.at[block, rows], out.at[block, rows], sem).start()

        return pltpu.make_async_copy(self.total, out, sem)

    def finish_ends(self):
        @pl.when(jnp.logical_not(self.inner))
        def _():
            @pl.loop(self.given, self.count)
            def _(i):
                self.out_copy(i).wait_send()

    def finish_inner(self):
        def sent(i):
            self.across_copy(i).wait_send()
            self.back_copy(i).wait_send()

        self.each(self.inner, sent)

    def finish(self):
        self.finish_inner()
        self.finish_ends()


def quotient(a, b):
    return a // b if isinstance(a, int) else lax.div(a, b)


def remainder(a, b):
    return a % b if isinstance(a, int) else lax.rem(a, b)


def multiple(value, of):
    return value if isinstance(value, int) else pl.multiple_of(value, of)


def by_step(now, plan):
    for first, last, stride, job in plan:
        if first == last:

            @pl.when(now == first)
            def _():
                job(0)

        else:
            due = (now >= first) & (now <= last)
            if stride > 1:
                due = due & (lax.rem(now - first, stride) == 0)

            @pl.when(due)
            def _():
                job(lax.div(now - first, stride))


def lanes(shape):
    return lax.broadcasted_iota(jnp.int32, shape, len(shape) - 1)


def turn(vectors, cos_table, sin_table):
    near = jnp.where(
        lanes(vectors.shape) % 64 < 32, pltpu.roll(vectors, 96, 1), pltpu.roll(vectors, 32, 1)
    )
    return vectors * cos_table + near * sin_table


def token_column(row):
    return jnp.broadcast_to(row, (128, row.shape[1])).T


def key_marks(column, first_id):
    lane = lanes(column.shape) % 64
    one_hot = (column - first_id).astype(jnp.int32) == lane
    return jnp.where(one_hot | ((lane >= 4) & (lane < 7)), 1.0, 0.0)


def query_marks(column, first_id):
    lane = lanes(column.shape) % 64
    other = (column - first_id).astype(jnp.int32) != lane
    return jnp.where(other & (lane < 4), -1e30, 0.0)


def nt_dot(left, right):
    return lax.dot_general(
        left, right, (((1,), (1,)), ((), ())), preferred_element_type=jnp.float32
    )


def attend_kernel(
    chain, places, x_in, ids, gains, key_shard, value_shard, inverse, query_shard, out_shard, gate_shard, up_shard,
    down_shard, gate_full, up_full, down_full, query_full, pair_full, out_full, attn_sum, normed_out, query_out,
    pairs, attended_out, log_out, cos_out, sin_out, small_out, x, small, gate_here, up_here, down_here, small_all, query_here, pair_here, pair_shard,
    out_here, pre_row, normed, query, attended, log_total, cos_table, sin_table, key_side, value_side, marks,
    scores, peak, mixed, near_pairs, term, passing, total, small_sems, gather_sems, local_sems, pair_sems,
    chain_sems, store_sems, load_sems,
):
    count = term.shape[0] // 2
    tokens = x.shape[0]
    heads = query.shape[1] // 64
    me = lax.axis_index("tokens")
    place = lax.rem(me, places)
    far = place >= 2
    load_x = pltpu.make_async_copy(x_in, x, load_sems.at[4])
    load_x.start()
    loads = [
        pltpu.make_async_copy(src, dst, load_sems.at[k])
        for k, (src, dst) in enumerate(
            ((gate_shard, gate_here), (up_shard, up_here), (down_shard, down_here))
        )
    ]
    for load in loads:
        load.start()
    small[...] = jnp.zeros(small.shape, jnp.float32)
    small[0:1, :] = ids[...].astype(jnp.float32)
    small[1:2, :] = gains[...]
    greet(range(1, 8), chain)

    def small_copy(flip):
        return remote(
            small,
            small_all.at[me],
            small_sems.at[0, flip - 1],
            small_sems.at[1, flip - 1],
            token_device(flip),
        )

    def gather(k, shard, full, axis, part=(0, 1)):
        return Gather(
            shard, full, axis, gather_sems.at[0, k], gather_sems.at[1, k], local_sems.at[k], part
        )

    gather_query = gather(0, query_shard, query_here, 0)
    gather_pair = gather(1, pair_shard, pair_here, 0)
    gather_out = gather(2, out_shard, out_here, 1)
    half_rows = gate_here.shape[0] // 2
    gate_one, gate_two, up, down = (
        gather(3, gate_here.at[pl.ds(0, half_rows)], gate_full, 0, (0, 2)),
        gather(4, gate_here.at[pl.ds(half_rows, half_rows)], gate_full, 0, (1, 2)),
        gather(5, up_here, up_full, 0),
        gather(6, down_here, down_full, 1),
    )
    stores = []

    def store(src, out):
        copy = pltpu.make_async_copy(src, out, store_sems.at[len(stores)])
        copy.start()
        stores.append(copy)

    for flip in range(1, 8):
        small_copy(flip).start()
    both = jnp.concatenate(
        [key_shard[...].astype(jnp.float32), value_shard[...].astype(jnp.float32)], axis=0
    )
    pair_shard[...] = both.T.astype(jnp.bfloat16)
    gather_pair.start()
    gather_query.start()
    small_all[me] = small[...]
    load_x.wait()
    x_f = x[...].astype(jnp.float32)
    pre_scale = lax.rsqrt(jnp.mean(x_f * x_f, axis=1, keepdims=True) + 1e-05)

    for flip in range(1, 8):
        small_copy(flip).wait_recv()
    store(small_all, small_out)
    width = x.shape[1] // 8
    for k in range(8):
        pre_row[:, k * width : (k + 1) * width] = jnp.broadcast_to(
            small_all[k, 1:2, :width], (8, width)
        )
    gather_pair.relay()
    normed[...] = (x[...].astype(jnp.float32) * pre_scale * pre_row[0:1, :]).astype(jnp.bfloat16)
    store(normed, normed_out)
    first_device = me - place
    first_id = (first_device // places * 4).astype(jnp.float32)
    own = token_column(small_all[me, 0:1, :])
    before = jnp.zeros((tokens, 1), jnp.float32)
    for k in range(places):
        others = small_all[first_device + k, 0:1, :]
        before = before + jnp.sum(
            jnp.where(others < own[:, 0:1], 1.0, 0.0), axis=1, keepdims=True
        )
        column = token_column(others)
        marks[pl.ds(k * tokens, tokens), :] = key_marks(column, first_id)
    row_index = lax.broadcasted_iota(jnp.int32, (tokens, 128), 0) + place * tokens
    turned = (row_index.astype(jnp.float32) - before) * inverse[0:1, :]
    cos_table[...] = jnp.cos(turned)
    sin_signed = jnp.sin(turned)
    sin_table[...] = jnp.where(lanes(sin_signed.shape) % 64 < 32, -sin_signed, sin_signed)
    store(cos_table, cos_out)
    store(sin_table, sin_out)
    gather_query.relay()
    gather_pair.finish_relay()
    gather_pair.finish()

    made = jnp.dot(normed[...], pair_here[...], preferred_element_type=jnp.float32)
    spun = turn(made, cos_table[...], sin_table[...])
    near_pairs[place] = jnp.where(lanes(made.shape) < 64, spun, made).astype(jnp.bfloat16)

    def pair_copy(slot, flip):
        at = place - 2 if slot == 2 else place
        return remote(
            near_pairs.at[at],
            near_pairs.at[at],
            pair_sems.at[0, slot],
            pair_sems.at[1, slot],
            token_device(flip),
        )

    pair_copy(0, 1).start()

    @pl.when(jnp.logical_not(far))
    def _():
        pair_copy(1, 2).start()

    gather_out.start()
    for load in loads:
        load.wait()
    gate_one.start()
    gather_query.finish_relay()
    gather_query.finish()
    for low in range(0, query.shape[1], 256):
        made = jnp.dot(
            normed[...], query_here[:, low : low + 256], preferred_element_type=jnp.float32
        )
        for group in range(low, low + 256, 128):
            spun = turn(made[:, group - low : group - low + 128], cos_table[...], sin_table[...])
            query[:, group : group + 128] = (spun * 0.125).astype(jnp.bfloat16)
    store(query, query_out)
    store(query_here, query_full)
    store(pair_here, pair_full)
    pair_copy(0, 1).wait_recv()

    @pl.when(far)
    def _():
        pair_copy(1, 2).wait_recv()
        pair_copy(2, 1).start()
        pair_copy(2, 1).wait_recv()

    @pl.when(jnp.logical_not(far))
    def _():
        gather_out.relay()

    @pl.when(jnp.logical_not(far))
    def _():
        gate_two.start()

    for k in range(places):

        @pl.when(k <= place)
        def _():
            pair = near_pairs[k].astype(jnp.float32)
            swapped = pltpu.roll(pair, 64, 1)
            lane = lanes(pair.shape)
            mark = marks[pl.ds(k * tokens, tokens), :]
            block = pl.ds(k * tokens, tokens)
            key_side[0, block] = jnp.where(lane < 64, pair, mark).astype(jnp.bfloat16)
            key_side[1, block] = jnp.where(lane < 64, mark, swapped).astype(jnp.bfloat16)
            value_side[0, block] = jnp.where(lane < 64, swapped, 1.0).astype(jnp.bfloat16)
            value_side[1, block] = jnp.where(lane < 64, 1.0, pair).astype(jnp.bfloat16)

    store(near_pairs, pairs)
    lane = lanes((tokens, 128))
    own_marks = query_marks(own, first_id)

    def side_of(group, e):
        at = pl.ds(multiple(group * 128, 128), 128)
        mine = (lane < 64) if e == 0 else (lane >= 64)
        return jnp.where(mine, query[:, at].astype(jnp.float32), own_marks).astype(jnp.bfloat16)

    def keys_at(k):
        return pl.ds(pl.multiple_of(k * tokens, tokens), tokens)

    def look(e, side, k, masked):
        found = nt_dot(side, key_side[e, keys_at(k)])
        if masked:
            rows = lax.broadcasted_iota(jnp.int32, found.shape, 0)
            found = jnp.where(lanes(found.shape) <= rows, found, -1e30)
        scores[e, k] = found
        best = found[:, :128]
        for part in range(128, tokens, 128):
            best = jnp.maximum(best, found[:, part : part + 128])
        peak[e] = best if masked else jnp.maximum(peak[e], best)

    def blend(e, k, first):
        parts = [
            jnp.exp(scores[e, k, :, part : part + 128] - peak[e]).astype(jnp.bfloat16)
            for part in range(0, tokens, 128)
        ]
        made = jnp.dot(
            jnp.concatenate(parts, axis=1),
            value_side[e, keys_at(k)],
            preferred_element_type=jnp.float32,
        )
        mixed[e] = made if first else mixed[e] + made

    def settle(e):
        peak[e] = jnp.broadcast_to(jnp.max(peak[e], axis=1, keepdims=True), lane.shape)

    def finish_head(group, e):
        mine = (lane < 64) if e == 0 else (lane >= 64)
        at = pl.ds(multiple(group * 128, 128), 128)
        out = mixed[e]
        sums = jnp.where(mine, pltpu.roll(out, 64, 1), out)
        share = out / sums
        attended[:, at] = share if e == 0 else jnp.where(lane < 64, attended[:, at], share)
        noted = peak[e] + jnp.log(sums)
        log_total[...] = jnp.where(lane == 2 * group + e, noted, log_total[...])

    def stage(done, begun):
        side = side_of(*begun) if begun else None
        if begun:
            look(begun[1], side, place, True)
        if done:
            blend(done[1], place, True)

        @pl.loop(0, place)
        def _(k):
            if begun:
                look(begun[1], side, k, False)
            if done:
                blend(done[1], k, False)

        if done:
            finish_head(*done)
        if begun:
            settle(begun[1])

    log_total[...] = jnp.zeros(lane.shape, jnp.float32)
    stage(None, (0, 0))
    last = heads // 2 - 1

    @pl.loop(0, last)
    def _(group):
        stage((group, 0), (group, 1))

        @pl.when(far & (group == 0))
        def _():
            gather_out.relay()

        @pl.when(far & (group == 0))
        def _():
            gate_two.start()

        @pl.when(group == 2)
        def _():
            up.start()

        stage((group, 1), (group + 1, 0))

    stage((last, 0), (last, 1))
    stage((last, 1), None)
    store(attended, attended_out)
    store(log_total, log_out)
    gather_out.finish_relay()

    gather_out.finish()
    low = attended[...].astype(jnp.bfloat16)
    each = term.shape[2]
    line = LineSum(term, passing, total, chain_sems, 2, second=3)

    @pl.loop(0, count)
    def _(k):
        cut = pl.ds(pl.multiple_of(k * 2 * each, 2 * each), 2 * each)
        made = jnp.dot(low, out_here[:, cut], preferred_element_type=jnp.float32).astype(
            jnp.bfloat16
        )
        term[2 * k] = made[:, :each]
        term[2 * k + 1] = made[:, each:]
        line.send(2 * k, 2)

    line.send(2 * count, 2 * count)
    store(out_here, out_full)

    down.start()
    relays = [
        (at, at, 1, lambda _, job=job: job())
        for at, job in (
            (0, gate_one.relay),
            (5, gate_two.relay),
            (13, up.relay),
            (24, down.relay),
            (26, gate_one.finish_relay),
            (28, gate_two.finish_relay),
            (32, up.finish_relay),
        )
    ]

    @pl.loop(0, line.steps())
    def _(now):
        by_step(now, relays)
        line.step(now)

    collected = line.collect(attn_sum, load_sems.at[3])
    down.finish_relay()
    line.finish()
    for part in (gate_one, gate_two, up, down):
        part.finish()
    for flip in range(1, 8):
        small_copy(flip).wait_send()
    pair_copy(0, 1).wait_send()

    @pl.when(far)
    def _():
        pair_copy(2, 1).wait_send()

    @pl.when(jnp.logical_not(far))
    def _():
        pair_copy(1, 2).wait_send()

    for copy in stores:
        copy.wait()
    collected.wait()


def attend(
    chain, places, x, ids, gains, key_weight, value_weight, inverse, query_weight, out_weight, gate_weight, up_weight,
    down_weight,
):
    tokens, width = x.shape
    count = 8
    heads_wide = query_weight.shape[1]
    bf16, f32 = jnp.bfloat16, jnp.float32
    row = places * tokens
    each = width // (2 * count)
    small = (8, tokens)
    anywhere, vmem = pl.BlockSpec(memory_space=pl.ANY), pl.BlockSpec(memory_space=pltpu.VMEM)
    shape = jax.ShapeDtypeStruct
    chunks = (2 * count, tokens, each)
    out_shape = [
        shape((gate_weight.shape[0] * 8, gate_weight.shape[1]), bf16),
        shape((up_weight.shape[0] * 8, up_weight.shape[1]), bf16),
        shape((down_weight.shape[0], down_weight.shape[1] * 8), bf16),
        shape((width, heads_wide), bf16),
        shape((width, 128), bf16),
        shape((heads_wide, width), bf16),
        shape(chunks, bf16),
        shape((tokens, width), bf16),
        shape((tokens, heads_wide), bf16),
        shape((places, tokens, 128), bf16),
        shape((tokens, heads_wide), f32),
        shape((tokens, 128), f32),
        shape((tokens, 128), f32),
        shape((tokens, 128), f32),
        shape((8,) + small, f32),
    ]
    return pl.pallas_call(
        functools.partial(attend_kernel, chain, places),
        out_shape=out_shape,
        in_specs=[anywhere] + [vmem] * 5 + [anywhere] * 5,
        out_specs=[anywhere] * len(out_shape),
        scratch_shapes=[
            pltpu.VMEM((tokens, width), bf16),
            pltpu.VMEM(small, f32),
            pltpu.VMEM(gate_weight.shape, bf16),
            pltpu.VMEM(up_weight.shape, bf16),
            pltpu.VMEM(down_weight.shape, bf16),
            pltpu.VMEM((8,) + small, f32),
            pltpu.VMEM((width, heads_wide), bf16),
            pltpu.VMEM((width, 128), bf16),
            pltpu.VMEM((width // 8, 128), bf16),
            pltpu.VMEM((heads_wide, width), bf16),
            pltpu.VMEM((8, width), f32),
            pltpu.VMEM((tokens, width), bf16),
            pltpu.VMEM((tokens, heads_wide), bf16),
            pltpu.VMEM((tokens, heads_wide), f32),
            pltpu.VMEM((tokens, 128), f32),
            pltpu.VMEM((tokens, 128), f32),
            pltpu.VMEM((tokens, 128), f32),
            pltpu.VMEM((2, row, 128), bf16),
            pltpu.VMEM((2, row, 128), bf16),
            pltpu.VMEM((row, 128), f32),
            pltpu.VMEM((2, places, tokens, tokens), f32),
            pltpu.VMEM((2, tokens, 128), f32),
            pltpu.VMEM((2, tokens, 128), f32),
            pltpu.VMEM((places, tokens, 128), bf16),
            pltpu.VMEM(chunks, bf16),
            pltpu.VMEM(chunks, bf16),
            pltpu.VMEM(chunks, bf16),
            pltpu.SemaphoreType.DMA((2, 7)),
            pltpu.SemaphoreType.DMA((2, 7, Gather.COPIES)),
            pltpu.SemaphoreType.DMA((7,)),
            pltpu.SemaphoreType.DMA((2, 3)),
            pltpu.SemaphoreType.DMA((4, 4 * count)),
            pltpu.SemaphoreType.DMA((len(out_shape),)),
            pltpu.SemaphoreType.DMA((5,)),
        ],
        compiler_params=pltpu.CompilerParams(
            collective_id=0, has_side_effects=True, vmem_limit_bytes=VMEM_BYTES
        ),
        name="attend_forward",
    )(
        x, ids, gains, key_weight.T, value_weight.T, inverse, query_weight, out_weight, gate_weight, up_weight,
        down_weight,
    )


def greet(flips, chain):
    me, here = lax.axis_index("tokens"), lax.axis_index("heads")
    barrier = pltpu.get_barrier_semaphore()
    for flip in flips:
        pl.semaphore_signal(barrier, inc=1, device_id=token_device(flip), device_id_type=MESH_ID)
    for step in (-1, 1):
        near = here + step

        @pl.when((near >= 0) & (near < chain))
        def _():
            pl.semaphore_signal(barrier, inc=1, device_id=(me, near), device_id_type=MESH_ID)

    edge = (here == 0) | (here == chain - 1)

    @pl.when(edge)
    def _():
        pl.semaphore_wait(barrier, len(flips) + 1)

    @pl.when(jnp.logical_not(edge))
    def _():
        pl.semaphore_wait(barrier, len(flips) + 2)


class Reduce:
    COPIES = 6

    def __init__(self, own, near, sems):
        self.own, self.near, self.sems = own, near, sems

    def copy(self, slot):
        k, half, flip = ((1, 0, 2), (3, 0, 2), (2, 1, 4), (3, 1, 4), (2, 0, 4), (1, 1, 2))[slot]
        rows = self.own.shape[1] // 2
        return remote(
            self.own.at[k, pl.ds(half * rows, rows)],
            self.near.at[slot],
            self.sems.at[0, slot],
            self.sems.at[1, slot],
            token_device(flip),
        )

    def put(self, k, block):
        self.own[k] = block.astype(self.own.dtype)
        self.send(k)

    def send(self, k):
        for which, slots in ((3, (1, 3)), (1, (0,)), (2, (2,))):

            @pl.when(k == which)
            def _():
                for slot in slots:
                    self.copy(slot).start()

    def add_near(self, k, half, slot):
        rows = self.own.shape[1] // 2

        @pl.loop(0, rows // 32)
        def _(i):
            here = pl.ds(pl.multiple_of(i * 32, 32), 32)
            place = pl.ds(pl.multiple_of(half * rows + i * 32, 32), 32)
            self.own[k, place] = (
                self.own[k, place].astype(jnp.float32) + self.near[slot, here].astype(jnp.float32)
            ).astype(self.own.dtype)

    def second(self):
        self.copy(1).wait_recv()
        self.add_near(2, 0, 1)
        self.copy(4).start()
        self.copy(3).wait_recv()
        self.add_near(1, 1, 3)
        self.copy(5).start()

    def finish(self, out):
        rows = self.own.shape[1] // 2
        for half, slots in ((0, (0, 4)), (1, (2, 5))):
            for slot in slots:
                self.copy(slot).wait_recv()

            @pl.loop(0, rows // 32)
            def _(i):
                here = pl.ds(pl.multiple_of(i * 32, 32), 32)
                place = pl.ds(pl.multiple_of(half * rows + i * 32, 32), 32)
                total = self.own[0, place].astype(jnp.float32)
                for slot in slots:
                    total = total + self.near[slot, here].astype(jnp.float32)
                out[place, :] = total.astype(out.dtype)

        for slot in range(self.COPIES):
            self.copy(slot).wait_send()

    def halfway(self):
        for slot, (k, half) in enumerate(((0, 0), (2, 0), (0, 1), (1, 1))):
            self.copy(slot).wait_recv()
            self.copy(slot).wait_send()
            self.add_near(k, half, slot)


def block_order(i):
    return jnp.where(i == 0, 3, jnp.where(i == 1, 1, jnp.where(i == 2, 2, 0)))


def tn_dot(left, right):
    return lax.dot_general(
        left, right, (((0,), (0,)), ((), ())), preferred_element_type=jnp.float32
    )


def tiles_of(length, size):
    return [(low, min(low + size, length)) for low in range(0, length, size)]


def feed_kernel(
    chain, small_all, x_in, attn_in, cotangent_in, gate_full, up_full, down_full, back_sum, hidden_out, mlp_term,
    scale_out, grad_gate_out, up_out, x, attn_sum, cotangent, hidden, scale, grad_gate, gate, up, down, mid_row, normed, back_gate, back_up, term, passing, total,
    own_gate, near_gate, own_up, near_up, mlp_near, load_sems, swap_sems, chain_sems, reduce_sems, store_sems,
    lead_sems,
):
    count = term.shape[0] // 2
    each = term.shape[2]
    tokens, width = x.shape
    inner = gate.shape[1]
    me = lax.axis_index("tokens")
    tiles = tiles_of(inner, 512)
    early = [
        pltpu.make_async_copy(src, dst, load_sems.at[k])
        for k, (src, dst) in enumerate(((x_in, x), (attn_in, attn_sum), (cotangent_in, cotangent)))
    ]
    loads = []
    for k, (low, high) in enumerate(tiles):
        cut = pl.ds(low, high - low)
        loads.append(
            (
                pltpu.make_async_copy(gate_full.at[:, cut], gate.at[:, cut], load_sems.at[4 + 3 * k]),
                pltpu.make_async_copy(up_full.at[:, cut], up.at[:, cut], load_sems.at[5 + 3 * k]),
                pltpu.make_async_copy(down_full.at[cut, :], down.at[cut, :], load_sems.at[6 + 3 * k]),
            )
        )
    for load in early:
        load.start()
    for group in loads:
        for load in group:
            load.start()
    greet((1, 2, 4), chain)

    span = width // 8
    for k in range(8):
        mid_row[:, k * span : (k + 1) * span] = jnp.broadcast_to(
            small_all[k, 1:2, span : 2 * span], (8, span)
        )

    early[0].wait()
    early[1].wait()
    line = LineSum(term, passing, total, chain_sems, 2)
    half = tokens // 2

    def swap(k, ref, row, cut):
        return remote(
            ref.at[pl.ds(multiple(row, half), half), cut],
            ref.at[pl.ds(multiple(tokens + row, half), half), cut],
            swap_sems.at[0, k],
            swap_sems.at[1, k],
            token_device(1),
        )

    def swaps_of(part):
        row = part * half
        found = [swap(part, normed, row, pl.ds(0, width))]
        for k, (low, high) in enumerate(tiles):
            for j, ref in enumerate((back_gate, back_up)):
                found.append(
                    swap(2 + (part * len(tiles) + k) * 2 + j, ref, row, pl.ds(low, high - low))
                )
        return found

    ahead = 4

    def mid_pair(n, row):
        cut = pl.ds(pl.multiple_of(n * 2 * each, 2 * each), 2 * each)
        place = pl.ds(row, half)
        made = nt_dot(back_gate[place, :], gate[cut, :]) + nt_dot(back_up[place, :], up[cut, :])
        made = made.astype(jnp.bfloat16)
        term[2 * n, place] = made[:, :each]
        term[2 * n + 1, place] = made[:, each:]

    early[2].wait()

    @pl.loop(0, 2)
    def _(part):
        row = pl.multiple_of(part * half, half)
        rows = pl.ds(row, half)

        def middle_here(c):
            cut = slice(c * each, (c + 1) * each)
            return x[rows, cut].astype(jnp.float32) + attn_sum[c, rows].astype(jnp.float32)

        squares = jnp.zeros((half, each), jnp.float32)
        for c in range(2 * count):
            found = middle_here(c)
            squares = squares + found * found
        mid_scale = lax.rsqrt(jnp.sum(squares, axis=1, keepdims=True) / width + 1e-05)
        scale[rows] = jnp.broadcast_to(mid_scale, (half, scale.shape[1]))
        for c in range(2 * count):
            cut = slice(c * each, (c + 1) * each)
            normed[rows, cut] = (middle_here(c) * mid_scale * mid_row[0:1, cut]).astype(jnp.bfloat16)
        copies = swaps_of(part)
        copies[0].start()
        for k, (low, high) in enumerate(tiles):

            @pl.when(part == 0)
            def _():
                for load in loads[k]:
                    load.wait()

            gate_rows = jnp.dot(
                normed[rows, :], gate[:, low:high], preferred_element_type=jnp.float32
            )
            up_rows = jnp.dot(normed[rows, :], up[:, low:high], preferred_element_type=jnp.float32)
            back_hidden = nt_dot(cotangent[rows, :], down[low:high, :])
            sigmoid = jax.nn.sigmoid(gate_rows)
            silu = gate_rows * sigmoid
            hidden[rows, low:high] = (silu * up_rows).astype(jnp.bfloat16)
            back_gate[rows, low:high] = (
                back_hidden * up_rows * sigmoid * (1.0 + gate_rows * (1.0 - sigmoid))
            ).astype(jnp.bfloat16)
            back_up[rows, low:high] = (back_hidden * silu).astype(jnp.bfloat16)
            for copy in copies[1 + 2 * k : 3 + 2 * k]:
                copy.start()

            @pl.when(part == 1)
            def _():
                line.step(2 * k)
                line.step(2 * k + 1)

        @pl.when(part == 0)
        def _():
            @pl.loop(0, ahead)
            def _(n):
                mid_pair(n, 0)
                line.send(2 * n, 2)

    stores = []

    def store(src, out):
        copy = pltpu.make_async_copy(src, out, store_sems.at[len(stores)])
        copy.start()
        stores.append(copy)

    store(hidden, hidden_out)
    store(scale, scale_out)

    def mlp_place(n):
        rows = pl.ds(multiple(remainder(n, 4) * tokens, tokens), tokens)
        return rows, quotient(n, 4) * 2 * each

    def mlp_at(c):
        rows, low = mlp_place(quotient(c, 2))
        low = low + remainder(c, 2) * each
        return gate.at[rows, pl.ds(multiple(low, each), each)]

    lead = mlp_near.shape[0]

    def lead_copy(c):
        return remote(
            mlp_at(c), mlp_near.at[c], lead_sems.at[0, c], lead_sems.at[1, c], line.mate
        )

    def mlp_pair(n):
        cut = pl.ds(pl.multiple_of(n * 2 * each, 2 * each), 2 * each)
        made = jnp.dot(hidden[...], down[:, cut], preferred_element_type=jnp.float32)
        rows, low = mlp_place(n)
        gate[rows, pl.ds(pl.multiple_of(low, 2 * each), 2 * each)] = made.astype(jnp.bfloat16)

        @pl.when(n >= lead // 2)
        def _():
            for k in range(2):
                pltpu.make_async_copy(
                    mlp_at(2 * n + k), mlp_term.at[2 * n + k], load_sems.at[3]
                ).start()

        @pl.when((n < lead // 2) & jnp.logical_not(line.inner))
        def _():
            for k in range(2):
                lead_copy(2 * n + k).start()

    def lead_store(c):
        return pltpu.make_async_copy(mlp_near.at[c], mlp_term.at[c], lead_sems.at[2, c])

    gate_sum = Reduce(own_gate, near_gate, reduce_sems.at[0])
    up_sum = Reduce(own_up, near_up, reduce_sems.at[1])

    def grad_block(part, ref, k):
        index = jnp.bitwise_xor(me, 2 * k)
        cut = pl.ds(pl.multiple_of(index * span, span), span)
        part.put(k, tn_dot(normed[:, cut], ref[...]))

    def received(which):
        for part in range(2):
            for copy in swaps_of(part)[which]:
                copy.wait_recv()

    def late_pair(i):
        i = i + ahead
        part = jnp.where(i < count, 0, 1)
        n = i - part * count
        mid_pair(n, pl.multiple_of(part * half, half))
        line.send(part * 2 * count + 2 * n, 2)

    def late_pairs(i):
        late_pair(2 * i)

        @pl.when(2 * i + 1 + ahead < 2 * count)
        def _():
            late_pair(2 * i + 1)

    begun = 2 * len(tiles)
    last_pairs = (2 * count - ahead + 1) // 2 - 1
    plan = (
        (0, last_pairs, 1, late_pairs),
        (0, 0, 1, lambda _: received(slice(0, 1))),
        (0, 0, 1, lambda _: received(slice(1, None, 2))),
        (0, 3, 1, lambda i: grad_block(gate_sum, back_gate, block_order(i))),
        (4, 4, 1, lambda _: received(slice(2, None, 2))),
        (4, 7, 1, lambda i: grad_block(up_sum, back_up, block_order(i))),
        (7, 7, 1, lambda _: gate_sum.second()),
        (last_pairs + 1, last_pairs + count, 1, mlp_pair),
    )

    @pl.loop(0, (line.steps() - begun + 1) // 2)
    def _(now):
        by_step(now, plan)
        line.step(begun + 2 * now)
        line.step(begun + 2 * now + 1)

    gate_sum.finish(grad_gate)
    store(grad_gate, grad_gate_out)
    @pl.when(line.inner)
    def _():
        for c in range(lead):
            lead_copy(c).wait_recv()
            mlp_near[c] = (
                mlp_near[c].astype(jnp.float32) + mlp_at(c)[...].astype(jnp.float32)
            ).astype(mlp_near.dtype)
            lead_store(c).start()

    up_sum.halfway()
    rows = span // 2
    store(own_up.at[0], up_out.at[pl.ds(0, span), :])
    store(own_up.at[2, pl.ds(0, rows)], up_out.at[pl.ds(span, rows), :])
    store(own_up.at[1, pl.ds(rows, rows)], up_out.at[pl.ds(span + rows, rows), :])
    collected = line.collect(back_sum, store_sems.at[7])
    line.finish()
    for part in range(2):
        for copy in swaps_of(part):
            copy.wait_send()

    rest = pl.ds(lead, 2 * count - lead)
    pltpu.make_async_copy(term.at[rest], total.at[rest], load_sems.at[3]).wait()

    @pl.when(line.inner)
    def _():
        for c in range(lead):
            lead_store(c).wait()

    @pl.when(jnp.logical_not(line.inner))
    def _():
        for c in range(lead):
            lead_copy(c).wait_send()

    for copy in stores:
        copy.wait()
    collected.wait()


def feed(chain, small_all, x, attn_sum, cotangent, gate_full, up_full, down_full):
    tokens, width = x.shape
    inner = gate_full.shape[1]
    count = attn_sum.shape[0] // 2
    span = width // 8
    bf16, f32 = jnp.bfloat16, jnp.float32
    anywhere, vmem = pl.BlockSpec(memory_space=pl.ANY), pl.BlockSpec(memory_space=pltpu.VMEM)
    shape = jax.ShapeDtypeStruct
    tiles = len(tiles_of(inner, 512))
    return pl.pallas_call(
        functools.partial(feed_kernel, chain),
        out_shape=[
            shape(attn_sum.shape, bf16),
            shape((tokens, inner), bf16),
            shape(attn_sum.shape, bf16),
            shape((tokens, 128), f32),
            shape((span, inner), bf16),
            shape((2 * span, inner), bf16),
        ],
        in_specs=[vmem] + [anywhere] * 6,
        out_specs=[anywhere] * 6,
        scratch_shapes=[
            pltpu.VMEM((tokens, width), bf16),
            pltpu.VMEM(attn_sum.shape, bf16),
            pltpu.VMEM((tokens, width), bf16),
            pltpu.VMEM((tokens, inner), bf16),
            pltpu.VMEM((tokens, 128), f32),
            pltpu.VMEM((span, inner), bf16),
            pltpu.VMEM((width, inner), bf16),
            pltpu.VMEM((width, inner), bf16),
            pltpu.VMEM((inner, width), bf16),
            pltpu.VMEM((8, width), f32),
            pltpu.VMEM((2 * tokens, width), bf16),
            pltpu.VMEM((2 * tokens, inner), bf16),
            pltpu.VMEM((2 * tokens, inner), bf16),
            pltpu.VMEM(attn_sum.shape, bf16),
            pltpu.VMEM(attn_sum.shape, bf16),
            pltpu.VMEM(attn_sum.shape, bf16),
            pltpu.VMEM((4, span, inner), bf16),
            pltpu.VMEM((6, span // 2, inner), bf16),
            pltpu.VMEM((4, span, inner), bf16),
            pltpu.VMEM((6, span // 2, inner), bf16),
            pltpu.VMEM((LEAD, tokens, 128), bf16),
            pltpu.SemaphoreType.DMA((4 + 3 * tiles,)),
            pltpu.SemaphoreType.DMA((2, 2 + 4 * tiles)),
            pltpu.SemaphoreType.DMA((4, 4 * count)),
            pltpu.SemaphoreType.DMA((2, 2, Reduce.COPIES)),
            pltpu.SemaphoreType.DMA((8,)),
            pltpu.SemaphoreType.DMA((3, LEAD)),
        ],
        compiler_params=pltpu.CompilerParams(
            collective_id=1, has_side_effects=True, vmem_limit_bytes=VMEM_BYTES
        ),
        name="feed_forward",
    )(small_all, x, attn_sum, cotangent, gate_full, up_full, down_full)


def split_marks(values, at):
    high = values.astype(jnp.bfloat16).astype(jnp.float32)
    rest = values - high
    middle = rest.astype(jnp.bfloat16).astype(jnp.float32)
    low = rest - middle
    return jnp.where(at == 4, high, jnp.where(at == 5, middle, jnp.where(at == 6, low, 0.0)))


def return_kernel(
    chain, places, small_in, query_in, pairs_in, log_in, cos_in, sin_in, scale_in,
    attended_in, x_in, attn_in, back_sum, query_full, pair_full, out_full, mlp_term, hidden_in, cotangent, normed_in, up_in, layer_out, grad_input, grad_down_out,
    grad_query, grad_key, grad_value, grad_out_out, grad_up_out, gains, mid_part, grad_down, grad_out, pair_back, grad_in, in_here, out_here, key_side, value_side, query_side, back_side, back_att,
    back_rows, back_keys, back_values, pair_out, pair_near, normed, back_attn, hidden, cotangents, att_low,
    back_all, pre_row, pre_part, gains_near, mlp_sum, mlp_passing, mlp_total, term, passing, total, own_down,
    near_down, own_in, near_in, own_out, near_out, load_sems, swap_sems, pair_sems, gain_sems, mlp_sems, chain_sems,
    reduce_sems, store_sems, up_half, up_near, up_sems, small_all, query, pairs, log_total, cos_table, sin_table, scale,
    table_sems,
):
    count = term.shape[0] // 2
    each = term.shape[2]
    tokens, width = x_in.shape
    span = width // 8
    groups = query.shape[1] // 128
    me = lax.axis_index("tokens")
    place = lax.rem(me, places)
    first_device = me - place
    mine, theirs = pl.ds(0, tokens), pl.ds(tokens, tokens)

    def load(k, src, dst):
        copy = pltpu.make_async_copy(src, dst, load_sems.at[k])
        copy.start()
        return copy

    load_mlp = load(5, mlp_term, mlp_sum)
    tables = [
        pltpu.make_async_copy(src, dst, table_sems.at[k])
        for k, (src, dst) in enumerate(
            (
                (small_in, small_all),
                (scale_in, scale),
                (query_in, query),
                (pairs_in, pairs),
                (log_in, log_total),
                (cos_in, cos_table),
                (sin_in, sin_table),
            )
        )
    ]
    for table in tables:
        table.start()
    load_cot = load(2, cotangent, cotangents.at[mine, :])
    attended = back_rows
    load_attended = load(7, attended_in, attended)

    def back_at(side, c):
        row = multiple(remainder(c, 4) * tokens, tokens)
        return side.at[quotient(c, 4), pl.ds(row, tokens), :]

    def attn_at(c):
        row = multiple(quotient(remainder(c, 4), 2) * tokens, tokens)
        low = multiple(remainder(c, 2) * each, each)
        return own_down.at[quotient(c, 4), pl.ds(row, tokens), pl.ds(low, each)]

    for c in range(2 * count):
        side = key_side if c < count else value_side
        load(9, back_sum.at[c], back_at(side, c % count))
        load(10, x_in.at[:, pl.ds(c * each, each)], term.at[c])
        load(11, attn_in.at[c], attn_at(c))
    load_out = load(0, out_full, out_here)
    heads_wide = query.shape[1]
    load_in = load(1, query_full, in_here.at[:, pl.ds(0, heads_wide)])
    load_pair = load(6, pair_full, in_here.at[:, pl.ds(heads_wide, 128)])
    load_hidden = load(3, hidden_in, hidden.at[mine, :])
    load_normed = load(4, normed_in, normed.at[mine, :])
    load_up = load(13, up_in, up_half)
    greet(range(1, 8), chain)

    def swap(k, ref):
        copy = remote(
            ref.at[mine, :],
            ref.at[theirs, :],
            swap_sems.at[0, k],
            swap_sems.at[1, k],
            token_device(1),
        )
        copy.start()
        return copy

    def gain_copy(which, src, flip):
        other = jnp.bitwise_xor(me, flip)
        return remote(
            src.at[:, pl.ds(pl.multiple_of(other * span, span), span)],
            gains_near.at[me, :, pl.ds(which * span, span)],
            gain_sems.at[0, which, flip - 1],
            gain_sems.at[1, which, flip - 1],
            token_device(flip),
        )

    mlp_line = LineSum(mlp_sum, mlp_passing, mlp_total, mlp_sems, given=LEAD, second=LEAD + 1)
    load_mlp.wait()
    mlp_line.start_given()
    mlp_line.send(LEAD, 2 * count - LEAD)
    rows_up = up_near.shape[1]

    def up_copy(slot):
        return remote(
            up_half.at[pl.ds((2 + slot) * rows_up, rows_up), :],
            up_near.at[slot],
            up_sems.at[0, slot],
            up_sems.at[1, slot],
            token_device((4, 2)[slot]),
        )

    tables[0].wait()
    tables[1].wait()
    for k in range(8):
        pre_row[:, k * span : (k + 1) * span] = jnp.broadcast_to(
            small_all[k, 1:2, span : 2 * span], (8, span)
        )
    for k in (9, 10, 11):
        pltpu.make_async_copy(attn_in, term, load_sems.at[k]).wait()
    load_cot.wait()

    def hat_at(c):
        return (term[c].astype(jnp.float32) + attn_at(c)[...].astype(jnp.float32)) * scale[...]

    def cut_at(c):
        return pl.ds(multiple(c * each, each), each)

    summed_here = back_keys.at[1]
    summed_here[...] = jnp.zeros(summed_here.shape, jnp.float32)
    for base, side in ((0, key_side), (count, value_side)):

        @pl.loop(0, count)
        def _(c):
            cut = cut_at(base + c)
            shared = back_at(side, c)[...].astype(jnp.float32) * hat_at(base + c)
            summed_here[...] += shared * pre_row[0:1, cut]
            mid_part[:, cut] = jnp.broadcast_to(jnp.sum(shared, axis=0, keepdims=True), (8, each))

    mean = jnp.sum(summed_here[...], axis=1, keepdims=True) / width
    summed_here[...] = jnp.broadcast_to(mean, summed_here.shape)
    for flip in range(1, 8):
        gain_copy(1, mid_part, flip).start()
    mlp_line.step(mlp_line.second)
    load_up.wait()
    for slot in range(2):
        up_copy(slot).start()

    for base, side in ((0, key_side), (count, value_side)):

        @pl.loop(0, count)
        def _(c):
            cut = cut_at(base + c)
            u = back_at(side, c)[...].astype(jnp.float32) * pre_row[0:1, cut]
            found = scale[...] * (u - hat_at(base + c) * summed_here[...])
            back_attn[mine, cut] = (cotangents[mine, cut].astype(jnp.float32) + found).astype(
                jnp.bfloat16
            )

    mlp_line.step(mlp_line.second + 1)
    load_attended.wait()
    att_low[mine, :] = attended[...].astype(jnp.bfloat16)
    swap_back = swap(0, back_attn)
    swap_att = swap(1, att_low)

    for table in tables[2:]:
        table.wait()
    lane = lanes((tokens, 128))
    at = lane % 64
    first_id = (first_device // places * 4).astype(jnp.float32)
    for k in range(places):
        mark = key_marks(token_column(small_all[first_device + k, 0:1, :]), first_id)
        block = pl.ds(k * tokens, tokens)

        @pl.when(k <= place)
        def _():
            pair = pairs[k].astype(jnp.float32)
            swapped = pltpu.roll(pair, 64, 1)
            key_side[0, block] = jnp.where(lane < 64, pair, mark).astype(jnp.bfloat16)
            key_side[1, block] = jnp.where(lane < 64, mark, swapped).astype(jnp.bfloat16)
            value_side[0, block] = jnp.where(lane < 64, swapped, 1.0).astype(jnp.bfloat16)
            value_side[1, block] = jnp.where(lane < 64, 1.0, pair).astype(jnp.bfloat16)

    own_marks = query_marks(token_column(small_all[me, 0:1, :]), first_id)

    load_out.wait()
    back_att[...] = nt_dot(back_attn[mine, :], out_here[...]).astype(jnp.bfloat16)
    swap_cot = swap(2, cotangents)
    mlp_line.step(mlp_line.second + 2)
    load_hidden.wait()
    swap_hidden = swap(3, hidden)

    @pl.loop(0, groups)
    def _(group):
        cut = pl.ds(pl.multiple_of(group * 128, 128), 128)
        back = back_att[:, cut].astype(jnp.float32)
        both = query[:, cut].astype(jnp.float32)
        shared = back * attended[:, cut]
        for e in range(2):
            head = 2 * group + e
            used = (lane < 64) if e == 0 else (lane >= 64)
            delta = jnp.sum(jnp.where(used, shared, 0.0), axis=1, keepdims=True)
            peak = jnp.sum(jnp.where(lane == head, log_total[...], 0.0), axis=1, keepdims=True)
            back_side[head] = jnp.where(
                used, back, split_marks(jnp.broadcast_to(-delta, lane.shape), at)
            ).astype(jnp.bfloat16)
            query_side[head] = jnp.where(
                used, both, own_marks + split_marks(jnp.broadcast_to(-peak, lane.shape), at)
            ).astype(jnp.bfloat16)

    mlp_line.step(mlp_line.second + 3)
    load_normed.wait()
    swap_normed = swap(4, normed)
    load_in.wait()
    load_pair.wait()

    begun = mlp_line.second + 4
    back_rows[...] = jnp.zeros_like(back_rows)

    def key_step(k, diagonal):
        back_keys[...] = jnp.zeros_like(back_keys)
        back_values[...] = jnp.zeros_like(back_values)

        @pl.loop(0, groups)
        def _(group):
            cut = pl.ds(pl.multiple_of(group * 128, 128), 128)
            for low in (0, tokens // 2):
                keys_here = pl.ds(pl.multiple_of(k * tokens + low, tokens // 2), tokens // 2)
                part = pl.ds(low, tokens // 2)
                first = low if diagonal else 0
                seen = pl.ds(first, tokens - first)
                rows = []
                for e in range(2):
                    head = 2 * group + e
                    found = nt_dot(key_side[e, keys_here], query_side[head, seen])
                    chances = jnp.exp(found)
                    if diagonal:
                        keys = lax.broadcasted_iota(jnp.int32, found.shape, 0) + (low - first)
                        chances = jnp.where(keys <= lanes(found.shape), chances, 0.0)
                    moved = chances * nt_dot(value_side[e, keys_here], back_side[head, seen])
                    chances = chances.astype(jnp.bfloat16)
                    moved = moved.astype(jnp.bfloat16)
                    back_values[e, part] += jnp.dot(
                        chances, back_att[seen, cut], preferred_element_type=jnp.float32
                    )
                    back_keys[e, part] += jnp.dot(
                        moved, query[seen, cut], preferred_element_type=jnp.float32
                    )
                    rows.append(tn_dot(moved, key_side[e, keys_here]))
                back_rows[seen, cut] += jnp.where(lanes(rows[0].shape) < 64, rows[0], rows[1])

            @pl.when(group % 2 == 1)
            def _():
                mlp_line.step(begun + groups // 2 * k + group // 2)

        keys = back_keys[0] + pltpu.roll(back_keys[1], 64, 1)
        values = pltpu.roll(back_values[0], 64, 1) + back_values[1]
        return jnp.where(lane < 64, keys, values)

    def pair_copy(source, target):
        return remote(
            pair_out.at[target],
            pair_near.at[source],
            pair_sems.at[0, target],
            pair_sems.at[1, source],
            (first_device + target, lax.axis_index("heads")),
        )

    @pl.loop(0, place)
    def _(k):
        pair_out[k] = key_step(k, False).astype(jnp.bfloat16)
        pair_copy(place, k).start()

    own_pair = key_step(place, True)
    pair_out[place] = own_pair.astype(jnp.bfloat16)
    early = begun + groups // 2 * places

    @pl.loop(begun + groups // 2 * (place + 1), early)
    def _(now):
        mlp_line.step(now)

    for group in range(groups):
        cut = slice(group * 128, (group + 1) * 128)
        back_all[mine, cut] = (
            turn(back_rows[:, cut], cos_table[...], -sin_table[...]) * 0.125
        ).astype(jnp.bfloat16)
    back_keys[0] = own_pair
    for k in range(1, places):

        @pl.when(k > place)
        def _():
            remote(
                pair_out.at[k],
                pair_near.at[k],
                pair_sems.at[0, k],
                pair_sems.at[1, k],
                (first_device + k, lax.axis_index("heads")),
            ).wait_recv()
            back_keys[0] += pair_near[k].astype(jnp.float32)

    summed = back_keys[0]
    spun = turn(summed, cos_table[...], -sin_table[...])
    back_all[mine, pl.ds(groups * 128, 128)] = jnp.where(lane < 64, spun, summed).astype(
        jnp.bfloat16
    )
    swap_all = swap(5, back_all)

    def pre_pair(n):
        cut = pl.ds(pl.multiple_of(n * 2 * each, 2 * each), 2 * each)
        made = nt_dot(back_all[mine, :], in_here[cut, :]).astype(jnp.bfloat16)
        term[2 * n] = made[:, :each]
        term[2 * n + 1] = made[:, each:]
        line.send(2 * n, 2)

    def cut_of(k):
        index = jnp.bitwise_xor(me, 2 * k)
        return pl.ds(pl.multiple_of(index * span, span), span)

    down_sum = Reduce(own_down, near_down, reduce_sems.at[0])
    in_sum = Reduce(own_in, near_in, reduce_sems.at[1])
    out_sum = Reduce(own_out, near_out, reduce_sems.at[2])

    def down_block(i):
        k = block_order(i)
        for low, high in tiles_of(hidden.shape[1], 512):
            own_down[k, low:high] = tn_dot(hidden[:, low:high], cotangents[:, cut_of(k)]).astype(
                own_down.dtype
            )
        down_sum.send(k)

    def in_block(i):
        k = block_order(i)
        in_sum.put(k, tn_dot(normed[:, cut_of(k)], back_all[...]))

    def out_block(i):
        k = block_order(i)
        out_sum.put(k, tn_dot(att_low[...], back_attn[:, cut_of(k)]))

    def load_late():
        swap_cot.wait_send()
        load(8, x_in, cotangents.at[theirs, :])
        for c in range(2 * count):
            load(12, attn_in.at[c], cotangents.at[mine, pl.ds(c * each, each)])

    def wait_late():
        for k in (8, 12):
            pltpu.make_async_copy(x_in, cotangents.at[mine, :], load_sems.at[k]).wait()

    def x_at(c):
        return cotangents[theirs, cut_at(c)].astype(jnp.float32)

    def middle_at(c):
        return x_at(c) + cotangents[mine, cut_at(c)].astype(jnp.float32)

    wholes = (
        (grad_down, grad_down_out),
        (grad_out, grad_out_out),
        (grad_in.at[:, pl.ds(0, heads_wide)], grad_query),
        (pair_back.at[pl.ds(0, 64)], grad_key),
        (pair_back.at[pl.ds(64, 64)], grad_value),
        (up_half.at[pl.ds(0, 2 * rows_up), :], grad_up_out),
    )

    def whole(k):
        return pltpu.make_async_copy(*wholes[k], store_sems.at[2 + k])

    def store_block(c, src, out, sem):
        return pltpu.make_async_copy(src.at[c], out.at[:, cut_at(c)], store_sems.at[sem])

    def finish_mlp(_):
        mlp_line.receive_all()
        mlp_line.finish()

        @pl.loop(0, 2 * count)
        def _(c):
            mlp_sum[c] = (middle_at(c) + mlp_total[c].astype(jnp.float32)).astype(jnp.bfloat16)
            store_block(c, mlp_sum, layer_out, 0).start()

    weighed = back_keys.at[1]
    scale_here = back_keys.at[0]

    def scale_rows(_):
        wait_late()
        for k in range(8):
            pre_row[:, k * span : (k + 1) * span] = jnp.broadcast_to(
                small_all[k, 1:2, :span], (8, span)
            )
        scale_here[...] = jnp.zeros(scale_here.shape, jnp.float32)

        @pl.loop(0, 2 * count)
        def _(c):
            part = x_at(c)
            scale_here[...] += part * part

        mean = jnp.sum(scale_here[...], axis=1, keepdims=True) / width
        scale_here[...] = jnp.broadcast_to(lax.rsqrt(mean + 1e-05), scale_here.shape)
        weighed[...] = jnp.zeros(weighed.shape, jnp.float32)

    def weigh(i):
        line.receive(i)
        c, rows = line.place(i)
        size = tokens // line.parts
        first = lax.div(i, line.blocks) * size
        cut = cut_at(c)
        late = pl.ds(pl.multiple_of(tokens + first, size), size)
        hat = cotangents[late, cut].astype(jnp.float32) * scale_here[rows]
        shared = total[c, rows].astype(jnp.float32) * hat
        weighed[rows] += shared * pre_row[0:1, cut]
        summed = jnp.broadcast_to(jnp.sum(shared, axis=0, keepdims=True), (8, each))
        pre_part[:, cut] = jnp.where(i < line.blocks, 0.0, pre_part[:, cut]) + summed

    def finish_in(_):
        in_sum.finish(grad_in)
        pair_back[...] = grad_in[:, heads_wide:].astype(jnp.float32).T
        for k in (2, 3, 4):
            whole(k).start()

    def finish_up(_):
        for slot in range(2):
            up_copy(slot).wait()

            @pl.loop(0, rows_up // 32)
            def _(i):
                here = pl.ds(pl.multiple_of(i * 32, 32), 32)
                place = pl.ds(pl.multiple_of(slot * rows_up + i * 32, 32), 32)
                up_half[place, :] = (
                    up_half[place, :].astype(jnp.float32) + up_near[slot, here].astype(jnp.float32)
                ).astype(up_half.dtype)

        whole(5).start()

    def finish_down(_):
        down_sum.finish(grad_down)
        whole(0).start()

    def finish_out(_):
        out_sum.finish(grad_out)
        whole(1).start()

    line = LineSum(term, passing, total, chain_sems, 2, 2 * count)
    steps = line.steps()
    behind = 14

    def received(*copies):
        def job(_):
            for copy in copies:
                copy.wait_recv()

        return job

    plan = (
        (0, 2 * count - 2, 2, pre_pair),
        (1, 1, 1, received(swap_cot, swap_hidden)),
        (1, 7, 2, down_block),
        (8, 8, 1, lambda _: load_late()),
        (9, 9, 1, received(swap_back, swap_att)),
        (9, 12, 1, out_block),
        (13, 13, 1, received(swap_normed, swap_all)),
        (13, 13, 1, scale_rows),
        (14, 17, 1, in_block),
        (18, 18, 1, lambda _: down_sum.second()),
        (20, 20, 1, finish_mlp),
        (21, 21, 1, lambda _: out_sum.second()),
        (23, 23, 1, lambda _: in_sum.second()),
        (26, 26, 1, finish_up),
        (28, 28, 1, finish_down),
        (30, 30, 1, finish_out),
        (32, 32, 1, finish_in),
    )

    @pl.loop(0, steps)
    def _(now):
        by_step(now, plan)

        @pl.when(early + now < mlp_line.steps())
        def _():
            mlp_line.step(early + now)

        line.step(now)

        @pl.when(now >= behind)
        def _():
            weigh(now - behind)

    @pl.loop(steps - behind, line.count)
    def _(i):
        weigh(i)

    for flip in range(1, 8):
        gain_copy(0, pre_part, flip).start()
    mean = jnp.sum(weighed[...], axis=1, keepdims=True) / width
    weighed[...] = jnp.broadcast_to(mean, weighed.shape)
    line.finish_ends()

    @pl.loop(0, 2 * count)
    def _(c):
        cut = cut_at(c)
        u = total[c].astype(jnp.float32) * pre_row[0:1, cut]
        found = scale_here[...] * (u - x_at(c) * scale_here[...] * weighed[...])
        term[c] = (back_attn[mine, cut].astype(jnp.float32) + found).astype(jnp.bfloat16)
        store_block(c, term, grad_input, 1).start()

    own = pl.ds(pl.multiple_of(me * span, span), span)
    gains_near[me, :, :span] = pre_part[:, own]
    gains_near[me, :, span:] = mid_part[:, own]
    for flip in range(1, 8):
        for which, src in enumerate((pre_part, mid_part)):
            gain_copy(which, src, flip).wait_recv()
    gains[...] = jnp.sum(gains_near[...], axis=0)
    for flip in range(1, 8):
        for which, src in enumerate((pre_part, mid_part)):
            gain_copy(which, src, flip).wait_send()
    line.finish_inner()
    for copy in (swap_back, swap_att, swap_hidden, swap_normed, swap_all):
        copy.wait_send()

    @pl.loop(0, place)
    def _(k):
        pair_copy(place, k).wait_send()

    for k in range(len(wholes)):
        whole(k).wait()

    for k in range(2):
        pltpu.make_async_copy(mlp_sum, term, store_sems.at[k]).wait()


def way_back(
    chain, places, small_all, query, pairs, log_total, cos_table, sin_table, scale, attended, x, attn_sum, back_sum,
    query_full, pair_full, out_full, mlp_term, hidden, cotangent, normed, up_half,
):
    tokens, width = x.shape
    inner = hidden.shape[1]
    heads_wide = query.shape[1]
    wide = heads_wide + 128
    chunks = attn_sum.shape
    count = chunks[0] // 2
    span = width // 8
    row = places * tokens
    bf16, f32 = jnp.bfloat16, jnp.float32
    anywhere, vmem = pl.BlockSpec(memory_space=pl.ANY), pl.BlockSpec(memory_space=pltpu.VMEM)
    shape = jax.ShapeDtypeStruct
    return pl.pallas_call(
        functools.partial(return_kernel, chain, places),
        out_shape=[
            shape((tokens, width), bf16),
            shape((tokens, width), bf16),
            shape((inner, span), bf16),
            shape((span, heads_wide), bf16),
            shape((64, span), f32),
            shape((64, span), f32),
            shape((heads_wide, span), bf16),
            shape((span, inner), bf16),
            shape((8, 2 * span), f32),
        ],
        in_specs=[anywhere] * 19,
        out_specs=[anywhere] * 8 + [vmem],
        scratch_shapes=[
            pltpu.VMEM((8, width), f32),
            pltpu.VMEM((inner, span), bf16),
            pltpu.VMEM((heads_wide, span), bf16),
            pltpu.VMEM((128, span), f32),
            pltpu.VMEM((span, wide), bf16),
            pltpu.VMEM((width, wide), bf16),
            pltpu.VMEM((heads_wide, width), bf16),
            pltpu.VMEM((2, row, 128), bf16),
            pltpu.VMEM((2, row, 128), bf16),
            pltpu.VMEM((heads_wide // 64, tokens, 128), bf16),
            pltpu.VMEM((heads_wide // 64, tokens, 128), bf16),
            pltpu.VMEM((tokens, heads_wide), bf16),
            pltpu.VMEM((tokens, heads_wide), f32),
            pltpu.VMEM((2, tokens, 128), f32),
            pltpu.VMEM((2, tokens, 128), f32),
            pltpu.VMEM((places, tokens, 128), bf16),
            pltpu.VMEM((places, tokens, 128), bf16),
            pltpu.VMEM((2 * tokens, width), bf16),
            pltpu.VMEM((2 * tokens, width), bf16),
            pltpu.VMEM((2 * tokens, inner), bf16),
            pltpu.VMEM((2 * tokens, width), bf16),
            pltpu.VMEM((2 * tokens, heads_wide), bf16),
            pltpu.VMEM((2 * tokens, wide), bf16),
            pltpu.VMEM((8, width), f32),
            pltpu.VMEM((8, width), f32),
            pltpu.VMEM((8, 8, 2 * span), f32),
            pltpu.VMEM(chunks, bf16),
            pltpu.VMEM(chunks, bf16),
            pltpu.VMEM(chunks, bf16),
            pltpu.VMEM(chunks, bf16),
            pltpu.VMEM(chunks, bf16),
            pltpu.VMEM(chunks, bf16),
            pltpu.VMEM((4, inner, span), bf16),
            pltpu.VMEM((6, inner // 2, span), bf16),
            pltpu.VMEM((4, span, wide), bf16),
            pltpu.VMEM((6, span // 2, wide), bf16),
            pltpu.VMEM((4, heads_wide, span), bf16),
            pltpu.VMEM((6, heads_wide // 2, span), bf16),
            pltpu.SemaphoreType.DMA((14,)),
            pltpu.SemaphoreType.DMA((2, 6)),
            pltpu.SemaphoreType.DMA((2, places)),
            pltpu.SemaphoreType.DMA((2, 2, 7)),
            pltpu.SemaphoreType.DMA((4, 2 * count)),
            pltpu.SemaphoreType.DMA((4, 4 * count)),
            pltpu.SemaphoreType.DMA((3, 2, Reduce.COPIES)),
            pltpu.SemaphoreType.DMA((8,)),
            pltpu.VMEM((2 * span, inner), bf16),
            pltpu.VMEM((2, span // 2, inner), bf16),
            pltpu.SemaphoreType.DMA((2, 2)),
            pltpu.VMEM(small_all.shape, f32),
            pltpu.VMEM(query.shape, bf16),
            pltpu.VMEM(pairs.shape, bf16),
            pltpu.VMEM(log_total.shape, f32),
            pltpu.VMEM(cos_table.shape, f32),
            pltpu.VMEM(sin_table.shape, f32),
            pltpu.VMEM(scale.shape, f32),
            pltpu.SemaphoreType.DMA((7,)),
        ],
        compiler_params=pltpu.CompilerParams(
            collective_id=2, has_side_effects=True, vmem_limit_bytes=VMEM_BYTES
        ),
        name="way_back",
    )(
        small_all, query, pairs, log_total, cos_table, sin_table, scale, attended, x, attn_sum, back_sum,
        query_full, pair_full, out_full, mlp_term, hidden, cotangent, normed, up_half,
    )


def hand_over_kernel(count, gains, *refs):
    ins, outs = refs[:count], refs[count : 2 * count]
    grad_pre, grad_mid = refs[2 * count : 2 * count + 2]
    held, wide, sems = refs[2 * count + 2 : 3 * count + 2], refs[3 * count + 2 : -1], refs[-1]
    loads = [pltpu.make_async_copy(ins[k], held[k], sems.at[0, k]) for k in range(count)]
    for load in loads:
        load.start()
    span = gains.shape[1] // 2
    grad_pre[...] = gains[0:1, :span]
    grad_mid[...] = gains[0:1, span:]
    stores = []
    wide = list(wide)
    for k, load in enumerate(loads):
        load.wait()
        ready = held[k]
        if outs[k].dtype != ready.dtype:
            ready = wide.pop(0)

            @pl.loop(0, ready.shape[0] // 32)
            def _(i):
                here = pl.ds(pl.multiple_of(i * 32, 32), 32)
                ready[here, :] = held[k][here, :].astype(ready.dtype)

        stores.append(pltpu.make_async_copy(ready, outs[k], sems.at[1, k]))
        stores[-1].start()
    for store in stores:
        store.wait()


def hand_over(gains, *arrays):
    count = len(arrays)
    anywhere, vmem = pl.BlockSpec(memory_space=pl.ANY), pl.BlockSpec(memory_space=pltpu.VMEM)
    half = jax.ShapeDtypeStruct((1, gains.shape[1] // 2), gains.dtype)
    types = [array.dtype if k < 2 else jnp.dtype(jnp.float32) for k, array in enumerate(arrays)]
    return pl.pallas_call(
        functools.partial(hand_over_kernel, count),
        out_shape=[jax.ShapeDtypeStruct(array.shape, kind) for array, kind in zip(arrays, types)]
        + [half, half],
        in_specs=[vmem] + [anywhere] * count,
        out_specs=[anywhere] * count + [vmem, vmem],
        scratch_shapes=[pltpu.VMEM(array.shape, array.dtype) for array in arrays]
        + [
            pltpu.VMEM(array.shape, kind)
            for array, kind in zip(arrays, types)
            if kind != array.dtype
        ]
        + [pltpu.SemaphoreType.DMA((2, count))],
        compiler_params=pltpu.CompilerParams(vmem_limit_bytes=VMEM_BYTES),
        name="hand_over",
    )(gains, *arrays)


def shards_cube(
    chain,
    inputs,
    segments,
    pre_gain,
    mid_gain,
    query_weight,
    key_weight,
    value_weight,
    out_weight,
    gate_weight,
    up_weight,
    down_weight,
    cotangent,
):
    row_count = inputs.shape[0]
    head_size = key_weight.shape[1]
    query_width = query_weight.shape[1]
    heads_here = query_width // head_size
    places = ROW // row_count
    half = pre_gain.shape[0]
    gains = jnp.pad(pre_gain.astype(jnp.float32), (0, half)) + jnp.pad(
        mid_gain.astype(jnp.float32), (half, 0)
    )
    half_size = head_size // 2
    inverse = 10000.0 ** (-np.arange(half_size, dtype=np.float32) / half_size)
    inverse = jnp.asarray(np.tile(inverse.astype(np.float32), (8, 128 // half_size)))
    (
        gate_full,
        up_full,
        down_full,
        query_full,
        pair_full,
        out_full,
        attn_sum,
        normed,
        query_rot,
        pairs,
        attended,
        log_total,
        cos_wide,
        sin_wide,
        small_full,
    ) = attend(
        chain,
        places,
        inputs,
        segments[None],
        gains[None],
        key_weight,
        value_weight,
        inverse,
        query_weight,
        out_weight,
        gate_weight,
        up_weight,
        down_weight,
    )
    back_sum, hidden, mlp_term, scale, grad_gate, up_half = feed(
        chain, small_full, inputs, attn_sum, cotangent, gate_full, up_full, down_full
    )
    layer_out, grad_input, grad_down, grad_query, grad_key, grad_value, grad_out, grad_up, gains = way_back(
        chain,
        places,
        small_full,
        query_rot,
        pairs,
        log_total,
        cos_wide,
        sin_wide,
        scale,
        attended,
        inputs,
        attn_sum,
        back_sum,
        query_full,
        pair_full,
        out_full,
        mlp_term,
        hidden,
        cotangent,
        normed,
        up_half,
    )
    (
        layer_out,
        grad_input,
        grad_query,
        grad_key,
        grad_value,
        grad_out,
        grad_gate,
        grad_up,
        grad_down,
        grad_pre,
        grad_mid,
    ) = hand_over(
        gains,
        layer_out,
        grad_input,
        grad_query,
        grad_key,
        grad_value,
        grad_out,
        grad_gate,
        grad_up,
        grad_down,
    )
    grad_pre, grad_mid = grad_pre[0], grad_mid[0]
    grad_key, grad_value = grad_key.T, grad_value.T
    return (
        layer_out,
        grad_input,
        grad_pre,
        grad_mid,
        grad_query,
        grad_key,
        grad_value,
        grad_out,
        grad_gate,
        grad_up,
        grad_down,
    )


def solution(mesh):
    sizes = dict(mesh.shape)
    plan = shards_any
    if sizes["tokens"] == 8 and sizes["heads"] == 4:
        plan = functools.partial(shards_cube, sizes["heads"])
    return jax.shard_map(
        plan,
        mesh=mesh,
        in_specs=(
            P("tokens", None),
            P("tokens"),
            P("tokens"),
            P("tokens"),
            P("tokens", "heads"),
            P("tokens", "heads"),
            P("tokens", "heads"),
            P("heads", "tokens"),
            P("tokens", "heads"),
            P("tokens", "heads"),
            P("heads", "tokens"),
            P("tokens", None),
        ),
        out_specs=(
            P("tokens", None),
            P("tokens", None),
            P("tokens"),
            P("tokens"),
            P("tokens", "heads"),
            P("tokens", "heads"),
            P("tokens", "heads"),
            P("heads", "tokens"),
            P("tokens", "heads"),
            P("tokens", "heads"),
            P("heads", "tokens"),
        ),
        check_vma=False,
    )
```
